32 devices in a mesh: rep: 4 (over z), ctx: 8 (over y, x, core).
Axes of the slice: x: 2, y: 2, z: 4, core: 2. Of those that a mesh axis runs over, the one named last changes fastest.
Arguments:
- query_rows: bfloat16 [4, 1024, 32, 128], P('rep', 'ctx'), may hold values from -17 to 17
- key_rows: bfloat16 [4, 1024, 4, 128], P('rep', 'ctx'), may hold values from -17 to 17
- value_matrix: bfloat16 [4, 1024, 4, 128], P('rep', 'ctx'), may hold values from -6 to 6
- cotangent: bfloat16 [4, 1024, 32, 128], P('rep', 'ctx'), may hold values from -6 to 6
- rotation: bfloat16 [16, 4, 32, 128], replicated, may hold values from -0.29882812 to 0.29882812
- projection: bfloat16 [16, 4, 32, 128], replicated, may hold values from -0.29882812 to 0.29882812
- shift_bias: float32 [16, 4], replicated, may hold values from -4 to 4
- doc_starts: int32 [4, 1024], P('rep'), may hold values from 0 to 1022, as said below
- tenant_ids: int32 [4, 1024], P('rep'), may hold values from 0 to 15, as said below
Outputs:
- d_queries: bfloat16 [4, 1024, 32, 128], P('rep', 'ctx')
- d_keys: bfloat16 [4, 1024, 4, 128], P('rep', 'ctx')
- d_values: bfloat16 [4, 1024, 4, 128], P('rep', 'ctx')
- grad_rotation: float32 [16, 4, 32, 128], P('rep', None, 'ctx')
- grad_projection: float32 [16, 4, 32, 128], P('rep', None, 'ctx')
The draws below stay inside these ranges and needn't reach their ends.
Inputs may be any that keep to these rules, and one draw needn't show every extreme that they name: doc_starts[r, i] is the first position of the document holding position i of sequence r; documents are consecutive, each of even length 2 to 256; every sequence begins with one of exactly 256 and ends with one of length 2. `tenant_ids`: the tenant of a position's document: equal for all positions of one document.
All inputs are finite; a program needn't handle non-finite values.
Results may differ from the reference program's by a relative error of at most 0.03.
Values may be sent and summed in bfloat16 or wider, within the bound.
No kernel may reach another device: no remote copies, remote signals or barrier semaphores. Data moves between devices by JAX's collectives and lax.ppermute only.
A program may use at most 128 MiB of HBM per device.

```python
import jax
import jax.numpy as jnp
from jax import lax

QUERY_HEADS = 32
KEY_VALUE_HEADS = 4
HEAD_SIZE = 128
RANK = 4
TEN = 16
DOC_MAX = 256
BLK = 512
SEQUENCE_COUNT = 4
SEQUENCE_LENGTH = 1024


def doc_layout(key):
    base_key = jax.random.fold_in(key, 101)
    key_length, key_tenant = jax.random.split(base_key)
    half_len = SEQUENCE_LENGTH // 2
    increments = 2 * jax.random.randint(key_length, (SEQUENCE_COUNT, half_len), 1, DOC_MAX // 2 + 1)
    increments = increments.at[:, 0].set(DOC_MAX)
    bounds = jnp.concatenate([jnp.zeros((SEQUENCE_COUNT, 1), jnp.int32), jnp.cumsum(increments, axis=1).astype(jnp.int32)], axis=1)
    positions = jnp.arange(SEQUENCE_LENGTH, dtype=jnp.int32)
    doc_slot = jax.vmap(lambda bound_row: jnp.searchsorted(bound_row, positions, side='right'))(bounds) - 1
    starts = jnp.take_along_axis(bounds, doc_slot, axis=1)
    tail_mask = positions[None, :] >= SEQUENCE_LENGTH - 2
    starts = jnp.where(tail_mask, SEQUENCE_LENGTH - 2, starts)
    doc_slot = jnp.where(tail_mask, half_len + 1, doc_slot)
    tenant_table = jax.random.randint(key_tenant, (SEQUENCE_COUNT, half_len + 2), 0, TEN)
    tenant_table = tenant_table.at[:, 0].set(TEN - 1).at[:, 1].set(0)
    tenants = jnp.take_along_axis(tenant_table, doc_slot, axis=1)
    return (starts.astype(jnp.int32), tenants.astype(jnp.int32))


def draw_doc_starts(key, part):
    return doc_layout(key)[0]


def draw_tenant_ids(key, part):
    return doc_layout(key)[1]


def draw_query_rows(key, part):
    array_shape = (SEQUENCE_COUNT, SEQUENCE_LENGTH, QUERY_HEADS, HEAD_SIZE)
    values = jax.random.truncated_normal(jax.random.fold_in(key, 1), -4.0, 4.0, array_shape, jnp.float32)
    return values.astype(jnp.bfloat16)


def draw_key_rows(key, part):
    array_shape = (SEQUENCE_COUNT, SEQUENCE_LENGTH, KEY_VALUE_HEADS, HEAD_SIZE)
    values = jax.random.truncated_normal(jax.random.fold_in(key, 2), -4.0, 4.0, array_shape, jnp.float32)
    return values.astype(jnp.bfloat16)


def steps_of(stream_key, shape, cuts, least, high):
    loudness = 1.0
    for axis_at, parts in cuts:
        steps = jax.random.uniform(jax.random.fold_in(jax.random.fold_in(stream_key, 6), axis_at), (parts,), jnp.float32, least / len(cuts), high / len(cuts))
        loudness = loudness * jnp.repeat(jnp.exp(steps), shape[axis_at] // parts).reshape((-1,) + (1,) * (len(shape) - 1 - axis_at))
    return loudness


def bell_draw(rng, extent, spread, reach, cuts=(), kind=jnp.bfloat16):
    drawn = jax.random.normal(rng, extent, jnp.float32) * spread
    if len(cuts) > 0:
        drawn = steps_of(rng, extent, cuts, -0.22, 0.18) * drawn
    return jnp.clip(drawn, min=-reach, max=reach).astype(kind)


def setup_inputs(seed: int = 0) -> dict:
    keys = jax.random.split(jax.random.key(seed), 10)
    return {
        "query_rows": draw_query_rows(jax.random.fold_in(keys[9], 71), 0),
        "key_rows": draw_key_rows(jax.random.fold_in(keys[9], 71), 0),
        "value_matrix": bell_draw(keys[2], (SEQUENCE_COUNT, SEQUENCE_LENGTH, KEY_VALUE_HEADS, HEAD_SIZE), 1.0, 6.0, ((0, 4), (1, 8))),
        "cotangent": bell_draw(keys[3], (SEQUENCE_COUNT, SEQUENCE_LENGTH, QUERY_HEADS, HEAD_SIZE), 1.0, 6.0, ((0, 4), (1, 8))),
        "rotation": bell_draw(keys[4], (TEN, RANK, QUERY_HEADS, HEAD_SIZE), 0.05, 0.29882812),
        "projection": bell_draw(keys[5], (TEN, RANK, QUERY_HEADS, HEAD_SIZE), 0.05, 0.29882812),
        "shift_bias": bell_draw(keys[6], (TEN, RANK), 1.0, 4.0, (), jnp.float32),
        "doc_starts": draw_doc_starts(jax.random.fold_in(keys[9], 71), 0),
        "tenant_ids": draw_tenant_ids(jax.random.fold_in(keys[9], 71), 0),
    }


far_below = -1e30


def masked_scores(query_block, key_window, start_block, row_start):
    scaling = query_block.shape[-1] ** -0.5
    scores = jnp.einsum("qhd,khd->hqk", query_block.astype(jnp.float32), key_window.astype(jnp.float32)) * scaling
    query_place = row_start + jnp.arange(query_block.shape[0], dtype=jnp.int32)
    key_place = row_start + query_block.shape[0] - key_window.shape[0] + jnp.arange(key_window.shape[0], dtype=jnp.int32)
    allowed = (key_place[None, :] >= start_block[:, None]) & (key_place[None, :] <= query_place[:, None])
    return jnp.where(allowed[None], scores, far_below)


def one_sequence(queries, key_set, value_set, upstream, starts, owners, rotation, projection, shift_bias):
    head_count = queries.shape[1]
    kv_count = key_set.shape[1]
    group_size = head_count // kv_count
    head_dim = queries.shape[2]
    length = queries.shape[0]
    scaling = head_dim ** -0.5
    spread_keys = jnp.repeat(key_set, group_size, axis=1)
    spread_values = jnp.repeat(value_set, group_size, axis=1)
    padding = jnp.zeros((DOC_MAX, head_count, head_dim), jnp.bfloat16)
    padded_keys = jnp.concatenate([padding, spread_keys], axis=0)
    padded_values = jnp.concatenate([padding, spread_values], axis=0)
    window = BLK + DOC_MAX
    block_count = length // BLK

    def windows(block_index):
        row_start = block_index * BLK
        return (row_start,
                lax.dynamic_slice_in_dim(queries, row_start, BLK, 0),
                lax.dynamic_slice_in_dim(padded_keys, row_start, window, 0),
                lax.dynamic_slice_in_dim(padded_values, row_start, window, 0),
                lax.dynamic_slice_in_dim(starts, row_start, BLK, 0))

    def forward_block(running, block_index):
        row_start, query_block, key_window, value_window, start_block = windows(block_index)
        scores = masked_scores(query_block, key_window, start_block, row_start)
        row_max = jnp.max(scores, axis=-1)
        weights = jnp.exp(scores - row_max[..., None])
        row_total = jnp.sum(weights, axis=-1)
        weights_low = (weights / row_total[..., None]).astype(jnp.bfloat16)
        outputs = jnp.einsum("hqk,khd->qhd", weights_low.astype(jnp.float32), value_window.astype(jnp.float32)).astype(jnp.bfloat16)
        return running, (row_max, row_total, outputs)

    block_ids = jnp.arange(block_count, dtype=jnp.int32)
    _, (maxima, totals, outputs) = lax.scan(forward_block, jnp.zeros((), jnp.int32), block_ids)
    hidden = outputs.reshape(length, head_count, head_dim)

    tenant_mask = (jnp.arange(rotation.shape[0], dtype=jnp.int32)[:, None] == owners[None, :]).astype(jnp.float32)
    hidden_wide = hidden.astype(jnp.float32)
    upstream_wide = upstream.astype(jnp.float32)
    projection_wide = projection.astype(jnp.float32)
    rotation_wide = rotation.astype(jnp.float32)
    on_projection = jnp.einsum("shd,trhd->trs", hidden_wide, projection_wide)
    on_rotation = jnp.einsum("shd,trhd->trs", hidden_wide, rotation_wide)
    pulled_all = jnp.einsum("shd,trhd->trs", upstream_wide, rotation_wide)
    bias_rows = jnp.sum(shift_bias[:, :, None] * tenant_mask[:, None, :], axis=0)
    lifted = jnp.sum(on_projection * tenant_mask[:, None, :], axis=0) - jnp.sum(on_rotation * tenant_mask[:, None, :], axis=0) + bias_rows
    pulled = jnp.sum(pulled_all * tenant_mask[:, None, :], axis=0)
    lifted_low = lifted.astype(jnp.bfloat16)
    pulled_low = pulled.astype(jnp.bfloat16)
    picked_pull = tenant_mask[:, None, :] * pulled_low.astype(jnp.float32)[None]
    picked_lift = tenant_mask[:, None, :] * lifted_low.astype(jnp.float32)[None]
    grad_projection = jnp.einsum("trs,shd->trhd", picked_pull, hidden_wide)
    grad_rotation = jnp.einsum("trs,shd->trhd", picked_lift, upstream_wide) - grad_projection
    hidden_grad = upstream_wide + jnp.einsum("trs,trhd->shd", picked_pull, projection_wide) - jnp.einsum("trs,trhd->shd", picked_pull, rotation_wide)
    grad_hidden = hidden_grad.astype(jnp.bfloat16)
    row_delta = jnp.sum(grad_hidden.astype(jnp.float32) * hidden_wide, axis=-1)

    def backward_block(running, pieces):
        block_index, row_max, row_total = pieces
        key_total, value_total = running
        row_start, query_block, key_window, value_window, start_block = windows(block_index)
        scores = masked_scores(query_block, key_window, start_block, row_start)
        weights = jnp.exp(scores - row_max[..., None]) / row_total[..., None]
        weights_low = weights.astype(jnp.bfloat16)
        grad_block = lax.dynamic_slice_in_dim(grad_hidden, row_start, BLK, 0).astype(jnp.float32)
        delta_block = lax.dynamic_slice_in_dim(row_delta, row_start, BLK, 0)
        value_grad = jnp.einsum("hqk,qhd->khd", weights_low.astype(jnp.float32), grad_block)
        weight_grad = jnp.einsum("qhd,khd->hqk", grad_block, value_window.astype(jnp.float32))
        score_grad = (weights * (weight_grad - delta_block.T[:, :, None])).astype(jnp.bfloat16).astype(jnp.float32)
        query_grad = jnp.einsum("hqk,khd->qhd", score_grad, key_window.astype(jnp.float32)) * scaling
        key_grad = jnp.einsum("hqk,qhd->khd", score_grad, query_block.astype(jnp.float32)) * scaling
        key_total = lax.dynamic_update_slice_in_dim(key_total, lax.dynamic_slice_in_dim(key_total, row_start, window, 0) + key_grad, row_start, 0)
        value_total = lax.dynamic_update_slice_in_dim(value_total, lax.dynamic_slice_in_dim(value_total, row_start, window, 0) + value_grad, row_start, 0)
        return (key_total, value_total), query_grad.astype(jnp.bfloat16)

    empty_total = jnp.zeros((length + DOC_MAX, head_count, head_dim), jnp.float32)
    (key_total, value_total), query_grads = lax.scan(backward_block, (empty_total, empty_total), (block_ids, maxima, totals))
    d_queries = query_grads.reshape(length, head_count, head_dim)
    head_dkeys = lax.optimization_barrier(key_total[DOC_MAX:].astype(jnp.bfloat16))
    head_dvalues = lax.optimization_barrier(value_total[DOC_MAX:].astype(jnp.bfloat16))
    d_keys = head_dkeys.astype(jnp.float32).reshape(length, kv_count, group_size, head_dim).sum(axis=2).astype(jnp.bfloat16)
    d_values = head_dvalues.astype(jnp.float32).reshape(length, kv_count, group_size, head_dim).sum(axis=2).astype(jnp.bfloat16)
    return d_queries, d_keys, d_values, grad_rotation, grad_projection


def reference(query_rows, key_rows, value_matrix, cotangent, rotation, projection, shift_bias, doc_starts, tenant_ids):
    def per_sequence(sequence):
        queries, key_set, value_set, upstream, starts, owners = sequence
        return one_sequence(queries, key_set, value_set, upstream, starts, owners, rotation, projection, shift_bias)

    d_queries, d_keys, d_values, grad_rotation, grad_projection = lax.map(
        per_sequence, (query_rows, key_rows, value_matrix, cotangent, doc_starts, tenant_ids))
    return d_queries, d_keys, d_values, jnp.sum(grad_rotation, axis=0), jnp.sum(grad_projection, axis=0)
```

```python
import jax
import jax.numpy as jnp
from jax import lax
from jax.experimental import pallas as pl
from jax.experimental.pallas import tpu as pltpu
from jax.sharding import PartitionSpec as P

DOC_MAX = 256
LOW = jnp.bfloat16
WIDE = jnp.float32
far_below = -1e30


def shifted(value, axis, steps):
    count = lax.axis_size(axis)
    first, last = (max(0, -steps), min(count, count - steps))
    return lax.ppermute(value, axis, [(source, source + steps) for source in range(first, last)])


def dot(left, right, left_dim, right_dim, precision=None):
    return lax.dot_general(
        left, right, (((left_dim,), (right_dim,)), ((), ())),
        precision=precision, preferred_element_type=WIDE,
    )


def group_rows(ref, kv_count, group_size):
    rows, _, dim = ref.shape
    wide = 2 * group_size
    parts = []
    for pair in range(kv_count // 2):
        both = ref[:, pair * wide : (pair + 1) * wide, :].astype(WIDE)
        for half in range(2):
            one = both[:, half * group_size : (half + 1) * group_size, :]
            parts.append(one.reshape(rows * group_size, dim).astype(LOW))
    return parts


def lane_head(shape, group_size):
    return lax.broadcasted_iota(jnp.int32, shape, 1) % group_size


def own_terms(maps_by_rows, owner, tenants, low_rank, group_size):
    lanes = maps_by_rows.shape[1]
    same_head = lax.broadcasted_iota(jnp.int32, (group_size, lanes), 0) == lane_head(
        (group_size, lanes), group_size
    )
    span = low_rank * group_size
    total = jnp.zeros((low_rank, group_size, lanes), WIDE)
    for tenant in range(tenants):
        keep = same_head & (owner == tenant)
        block = maps_by_rows[tenant * span : (tenant + 1) * span].reshape(
            low_rank, group_size, lanes
        )
        total = total + jnp.where(keep[None], block, 0.0)
    rows = jnp.sum(total, axis=1)
    rows = jnp.concatenate([rows, rows], axis=0)
    tiles = lanes // 128
    stacked = jnp.concatenate([rows[:, c * 128 : (c + 1) * 128] for c in range(tiles)], axis=0)
    side = lax.broadcasted_iota(jnp.int32, (128, 128), 0) // group_size
    over = lax.broadcasted_iota(jnp.int32, (128, 128), 1) // group_size
    spread = dot(stacked, (side == over).astype(WIDE), 1, 0, lax.Precision.HIGHEST)
    return jnp.concatenate([spread[c * 8 : (c + 1) * 8] for c in range(tiles)], axis=1)


def pull_kernel(cot_ref, rot_ref, proj_ref, meta_ref, gh_ref, diff_ref, pulled_ref, *, kv, group, tenants, rank):
    owner = meta_ref[1:2, :]
    lanes = owner.shape[1]
    cots = group_rows(cot_ref, kv, group)
    rots = group_rows(rot_ref, kv, group)
    projs = group_rows(proj_ref, kv, group)
    on_rot = dot(jnp.concatenate(rots, axis=1), jnp.concatenate(cots, axis=1), 1, 1)
    pulled = own_terms(on_rot, owner, tenants, rank, group).astype(LOW).astype(WIDE)
    pulled_ref[...] = pulled
    same_head = lax.broadcasted_iota(jnp.int32, (group, lanes), 0) == lane_head((group, lanes), group)
    picked = []
    for tenant in range(tenants):
        keep = same_head & (owner == tenant)
        for k in range(rank):
            picked.append(jnp.where(keep, pulled[k : k + 1], 0.0))
    picked = jnp.concatenate(picked, axis=0).T.astype(LOW)
    for g in range(kv):
        diff = (projs[g].astype(WIDE) - rots[g].astype(WIDE)).astype(LOW)
        diff_ref[g] = diff
        gh_ref[g] = (cots[g].astype(WIDE) + dot(picked, diff, 1, 0)).astype(LOW)


def places(lanes, tokens, group):
    key = lax.broadcasted_iota(jnp.int32, (tokens, lanes), 0)
    query = lax.broadcasted_iota(jnp.int32, (tokens, lanes), 1) // group
    return key, key <= query


def forward_kernel(
    bias_ref, q_ref, two_ref, one_ref, own_ref, cot_ref, diff_ref, meta_ref, pulled_ref,
    weights_ref, part_ref, *, kv, group, tenants, rank, scaling,
):
    tokens = own_ref.shape[1]
    first = meta_ref[0:1, :]
    owner = meta_ref[1:2, :]
    lanes = owner.shape[1]
    key, here = places(lanes, tokens, group)
    fold_bias = jnp.where(jnp.where(here, key, key - 2 * tokens) >= first, 0.0, far_below)
    mid_bias = jnp.where(key - tokens >= first, 0.0, far_below)
    queries = group_rows(q_ref, kv, group)
    hidden = []
    for g in range(kv):
        fold = jnp.where(here, dot(own_ref[g], queries[g], 1, 1), dot(two_ref[g], queries[g], 1, 1))
        fold = fold * scaling + fold_bias
        mid = dot(one_ref[g], queries[g], 1, 1) * scaling + mid_bias
        top = jnp.maximum(jnp.max(fold, axis=0, keepdims=True), jnp.max(mid, axis=0, keepdims=True))
        fold = jnp.exp(fold - top)
        mid = jnp.exp(mid - top)
        total = jnp.sum(fold, axis=0, keepdims=True) + jnp.sum(mid, axis=0, keepdims=True)
        share = 1.0 / total
        fold = fold * share
        mid = mid * share
        weights_ref[g, 0:tokens, :] = fold
        weights_ref[g, tokens : 2 * tokens, :] = mid
        low = jnp.concatenate(
            [jnp.where(here, 0.0, fold).astype(LOW), mid.astype(LOW), jnp.where(here, fold, 0.0).astype(LOW)],
            axis=0,
        )
        values = jnp.concatenate([two_ref[kv + g], one_ref[kv + g], own_ref[kv + g]], axis=0)
        hidden.append(dot(values, low, 0, 0).astype(LOW))
    hidden = jnp.concatenate(hidden, axis=0)
    on_diff = dot(jnp.concatenate([diff_ref[g] for g in range(kv)], axis=1), hidden, 1, 0)
    lifted = own_terms(on_diff, owner, tenants, rank, group)
    row = lax.broadcasted_iota(jnp.int32, (8, lanes), 0)
    shift = jnp.zeros((8, lanes), WIDE)
    for tenant in range(tenants):
        column = jnp.zeros((8, 1), WIDE)
        for k in range(rank):
            column = jnp.where(row[:, 0:1] % rank == k, bias_ref[tenant, k], column)
        shift = jnp.where(owner == tenant, column, shift)
    lifted = (lifted + shift).astype(LOW).astype(WIDE)
    pulled = pulled_ref[...]
    span = tenants * rank
    mine = owner == lax.broadcasted_iota(jnp.int32, (span, lanes), 0) // rank
    lift_rows = jnp.where(mine, jnp.concatenate([lifted] * (span // 8), axis=0), 0.0)
    pull_rows = jnp.where(mine, jnp.concatenate([pulled] * (span // 8), axis=0), 0.0)
    head = lane_head((span, lanes), group)
    lift_all = jnp.concatenate([jnp.where(head == h, lift_rows, 0.0).astype(LOW) for h in range(group)], axis=0)
    pull_all = jnp.concatenate([jnp.where(head == h, pull_rows, 0.0).astype(LOW) for h in range(group)], axis=0)
    on_proj = dot(pull_all, hidden, 1, 1)
    on_rot = dot(lift_all, jnp.concatenate(group_rows(cot_ref, kv, group), axis=1), 1, 0) - on_proj
    dim = q_ref.shape[2]
    for g in range(kv):
        for h in range(group):
            rows, columns = slice(h * span, (h + 1) * span), slice(g * dim, (g + 1) * dim)
            part_ref[g * group + h, 0] = on_rot[rows, columns].astype(LOW)
            part_ref[g * group + h, 1] = on_proj[rows, columns].astype(LOW)


def backward_kernel(
    q_ref, gh_ref, two_ref, one_ref, own_ref, weights_ref, dq_ref, back_two_ref, back_one_ref, back_own_ref,
    *, kv, group, scaling,
):
    tokens = own_ref.shape[1]
    lanes = weights_ref.shape[2]
    dim = q_ref.shape[2]
    _, here = places(lanes, tokens, group)
    queries = group_rows(q_ref, kv, group)
    query_grads = []
    for g in range(kv):
        grads = gh_ref[g]
        fold_weights = weights_ref[g, 0:tokens, :]
        mid_weights = weights_ref[g, tokens : 2 * tokens, :]
        fold = jnp.where(here, dot(own_ref[kv + g], grads, 1, 1), dot(two_ref[kv + g], grads, 1, 1))
        mid = dot(one_ref[kv + g], grads, 1, 1)
        delta = jnp.sum(fold * fold_weights, axis=0, keepdims=True) + jnp.sum(
            mid * mid_weights, axis=0, keepdims=True
        )
        fold = fold_weights * (fold - delta)
        mid = mid_weights * (mid - delta)
        score_grad = jnp.concatenate(
            [jnp.where(here, 0.0, fold).astype(LOW), mid.astype(LOW), jnp.where(here, fold, 0.0).astype(LOW)],
            axis=0,
        )
        low = jnp.concatenate(
            [
                jnp.where(here, 0.0, fold_weights).astype(LOW),
                mid_weights.astype(LOW),
                jnp.where(here, fold_weights, 0.0).astype(LOW),
            ],
            axis=0,
        )
        keys = jnp.concatenate([two_ref[g], one_ref[g], own_ref[g]], axis=0)
        key_grad = dot(score_grad, queries[g], 1, 0) * scaling
        value_grad = dot(low, grads, 1, 0)
        for place, grad in ((g, key_grad), (kv + g, value_grad)):
            back_two_ref[place] = grad[0:tokens].astype(LOW)
            back_one_ref[place] = grad[tokens : 2 * tokens].astype(LOW)
            back_own_ref[place] = grad[2 * tokens :]
        query_grad = dot(keys, score_grad, 0, 0) * scaling
        query_grads.append(query_grad.T.reshape(tokens, group, dim))
        if g % 2 == 1:
            both = jnp.concatenate(query_grads[-2:], axis=1).astype(LOW)
            dq_ref[:, (g - 1) * group : (g + 1) * group, :] = both


def on_device(
    query_rows, key_rows, value_matrix, cotangent, rotation, projection, shift_bias, doc_starts, tenant_ids,
):
    queries = query_rows[0]
    upstream = cotangent[0]
    tokens, heads, dim = queries.shape
    kv = key_rows.shape[2]
    group = heads // kv
    scaling = dim ** (-0.5)
    tenants, rank = rotation.shape[0], rotation.shape[1]
    lanes = tokens * group
    ctx = lax.axis_size("ctx")
    rep = lax.axis_size("rep")
    assert 2 * tokens == DOC_MAX

    own = jnp.moveaxis(jnp.concatenate([key_rows[0], value_matrix[0]], axis=1), 1, 0)
    one = shifted(own, "ctx", 1)
    two = shifted(own, "ctx", 2)

    row_first = lax.axis_index("ctx") * tokens
    starts = lax.dynamic_slice_in_dim(doc_starts[0], row_first, tokens, 0) - row_first
    owners = lax.dynamic_slice_in_dim(tenant_ids[0], row_first, tokens, 0)
    meta = jnp.repeat(jnp.stack([starts, owners]), group, axis=1)
    rot = rotation.reshape(tenants * rank, heads, dim)
    proj = projection.reshape(tenants * rank, heads, dim)
    params = pltpu.CompilerParams(vmem_limit_bytes=50 * 1024 * 1024)
    sizes = dict(kv=kv, group=group)

    def call(body, outs, flops, moved, specs=None, **fixed):
        def run(*operands):
            return pl.pallas_call(
                lambda *refs: body(*refs, **fixed),
                out_shape=[jax.ShapeDtypeStruct(*out) for out in outs],
                in_specs=specs or [pl.BlockSpec(memory_space=pltpu.VMEM)] * len(operands),
                out_specs=[pl.BlockSpec(memory_space=pltpu.VMEM)] * len(outs),
                compiler_params=params,
                name=body.__name__,
                cost_estimate=pl.CostEstimate(flops=flops, bytes_accessed=moved, transcendentals=0),
            )(*operands)

        return run

    grad_hidden, diff, pulled = call(
        pull_kernel,
        [((kv, lanes, dim), LOW), ((kv, tenants * rank * group, dim), LOW), ((8, lanes), WIDE)],
        2 * 2**30, 4 * 2**20, tenants=tenants, rank=rank, **sizes,
    )(upstream, rot, proj, meta)
    weights, part = call(
        forward_kernel,
        [((kv, 2 * tokens, lanes), WIDE), ((heads, 2, tenants * rank, dim), LOW)],
        4 * 2**30, 10 * 2**20,
        [pl.BlockSpec(memory_space=pltpu.SMEM)] + [pl.BlockSpec(memory_space=pltpu.VMEM)] * 8,
        tenants=tenants, rank=rank, scaling=scaling, **sizes,
    )(shift_bias, queries, two, one, own, upstream, diff, meta, pulled)
    gathered = lax.all_to_all(part, "ctx", split_axis=0, concat_axis=0, tiled=True)
    d_queries, back_two, back_one, back_own = call(
        backward_kernel,
        [((tokens, heads, dim), LOW), (own.shape, LOW), (own.shape, LOW), (own.shape, WIDE)],
        4 * 2**30, 10 * 2**20, scaling=scaling, **sizes,
    )(queries, grad_hidden, two, one, own, weights)
    from_one = shifted(back_one, "ctx", -1)
    from_two = shifted(back_two, "ctx", -2)

    here = heads // ctx
    by_heads = gathered.reshape(ctx, here, 2, rep, tenants * rank // rep, dim).astype(WIDE).sum(axis=0)
    by_rep = jnp.moveaxis(by_heads.astype(LOW), 2, 0)
    by_rep = lax.all_to_all(by_rep, "rep", split_axis=0, concat_axis=0, tiled=True)
    summed = by_rep.astype(WIDE).sum(axis=0).reshape(here, 2, tenants // rep, rank, dim)
    grads = jnp.moveaxis(summed, 0, 3)
    back = (back_own + from_one.astype(WIDE) + from_two.astype(WIDE)).astype(LOW)
    d_keys = jnp.moveaxis(back[:kv], 0, 1)
    d_values = jnp.moveaxis(back[kv:], 0, 1)
    return (d_queries[None], d_keys[None], d_values[None], grads[0], grads[1])


def solution(mesh):
    rows = P("rep", "ctx", None, None)
    in_specs = (rows, rows, rows, rows, P(), P(), P(), P("rep", None), P("rep", None))
    tenant_rows = P("rep", None, "ctx", None)
    out_specs = (rows, rows, rows, tenant_rows, tenant_rows)
    return jax.shard_map(
        on_device, mesh=mesh, in_specs=in_specs, out_specs=out_specs, check_vma=False
    )
```

```python
import jax
import jax.numpy as jnp
from jax import lax
from jax.experimental import pallas as pl
from jax.experimental.pallas import tpu as pltpu
from jax.sharding import PartitionSpec as P

DOC_MAX = 256
LOW = jnp.bfloat16
WIDE = jnp.float32
far_below = -1e30


def shifted(value, axis, steps):
    count = lax.axis_size(axis)
    first, last = (max(0, -steps), min(count, count - steps))
    return lax.ppermute(value, axis, [(source, source + steps) for source in range(first, last)])


def dot(left, right, left_dim, right_dim, precision=None):
    return lax.dot_general(
        left, right, (((left_dim,), (right_dim,)), ((), ())),
        precision=precision, preferred_element_type=WIDE,
    )


def group_rows(ref, kv_count, group_size):
    rows, _, dim = ref.shape
    wide = 2 * group_size
    parts = []
    for pair in range(kv_count // 2):
        both = ref[:, pair * wide : (pair + 1) * wide, :].astype(WIDE)
        for half in range(2):
            one = both[:, half * group_size : (half + 1) * group_size, :]
            parts.append(one.reshape(rows * group_size, dim).astype(LOW))
    return parts


def lane_head(shape, group_size):
    return lax.broadcasted_iota(jnp.int32, shape, 1) % group_size


def own_terms(maps_by_rows, owner, tenants, low_rank, group_size):
    lanes = maps_by_rows.shape[1]
    same_head = lax.broadcasted_iota(jnp.int32, (group_size, lanes), 0) == lane_head(
        (group_size, lanes), group_size
    )
    span = low_rank * group_size
    total = jnp.zeros((low_rank, group_size, lanes), WIDE)
    for tenant in range(tenants):
        keep = same_head & (owner == tenant)
        block = maps_by_rows[tenant * span : (tenant + 1) * span].reshape(
            low_rank, group_size, lanes
        )
        total = total + jnp.where(keep[None], block, 0.0)
    rows = jnp.sum(total, axis=1)
    rows = jnp.concatenate([rows, rows], axis=0)
    tiles = lanes // 128
    stacked = jnp.concatenate([rows[:, c * 128 : (c + 1) * 128] for c in range(tiles)], axis=0)
    side = lax.broadcasted_iota(jnp.int32, (128, 128), 0) // group_size
    over = lax.broadcasted_iota(jnp.int32, (128, 128), 1) // group_size
    spread = dot(stacked, (side == over).astype(WIDE), 1, 0, lax.Precision.HIGHEST)
    return jnp.concatenate([spread[c * 8 : (c + 1) * 8] for c in range(tiles)], axis=1)


def pull_kernel(
    starts_ref, owners_ref, cot_hbm, rot_hbm, proj_hbm, cots_ref, gh_ref, diff_ref, pulled_ref, meta_ref,
    cot_ref, rot_ref, proj_ref, sems, *, kv, group, tenants, rank,
):
    copies = [
        pltpu.make_async_copy(source, target, sems.at[at])
        for at, (source, target) in enumerate(
            ((cot_hbm, cot_ref), (rot_hbm, rot_ref), (proj_hbm, proj_ref))
        )
    ]
    for copy in copies:
        copy.start()
    lanes = meta_ref.shape[1]
    tokens = lanes // group
    row_first = lax.axis_index("ctx") * tokens
    mine = pl.ds(pl.multiple_of(row_first, tokens), tokens)
    row = lax.broadcasted_iota(jnp.int32, (8, tokens), 0)
    both = jnp.where(row == 0, starts_ref[:, mine] - row_first, owners_ref[:, mine]).astype(WIDE)
    repeat = lax.broadcasted_iota(jnp.int32, (tokens, lanes), 0) == (
        lax.broadcasted_iota(jnp.int32, (tokens, lanes), 1) // group
    )
    meta = dot(both, repeat.astype(WIDE), 1, 0, lax.Precision.HIGHEST).astype(jnp.int32)
    meta_ref[...] = meta
    owner = meta[1:2, :]
    copies[0].wait()
    cots = group_rows(cot_ref, kv, group)
    for g in range(kv):
        cots_ref[g] = cots[g]
    copies[1].wait()
    rots = group_rows(rot_ref, kv, group)
    on_rot = dot(jnp.concatenate(rots, axis=1), jnp.concatenate(cots, axis=1), 1, 1)
    pulled = own_terms(on_rot, owner, tenants, rank, group).astype(LOW).astype(WIDE)
    pulled_ref[...] = pulled
    same_head = lax.broadcasted_iota(jnp.int32, (group, lanes), 0) == lane_head((group, lanes), group)
    picked = []
    for tenant in range(tenants):
        keep = same_head & (owner == tenant)
        for k in range(rank):
            picked.append(jnp.where(keep, pulled[k : k + 1], 0.0))
    picked = jnp.concatenate(picked, axis=0).T.astype(LOW)
    copies[2].wait()
    projs = group_rows(proj_ref, kv, group)
    for g in range(kv):
        diff = (projs[g].astype(WIDE) - rots[g].astype(WIDE)).astype(LOW)
        diff_ref[g] = diff
        gh_ref[g] = (cots[g].astype(WIDE) + dot(picked, diff, 1, 0)).astype(LOW)


def places(lanes, tokens, group):
    key = lax.broadcasted_iota(jnp.int32, (tokens, lanes), 0)
    query = lax.broadcasted_iota(jnp.int32, (tokens, lanes), 1) // group
    return key, key <= query


def forward_kernel(
    bias_ref, q_ref, two_ref, one_ref, own_ref, cots_ref, diff_ref, meta_ref, pulled_ref,
    weights_ref, part_ref, *, kv, group, tenants, rank, scaling, rep, owned,
):
    tokens = own_ref.shape[1]
    first = meta_ref[0:1, :]
    owner = meta_ref[1:2, :]
    lanes = owner.shape[1]
    key, here = places(lanes, tokens, group)
    fold_bias = jnp.where(jnp.where(here, key, key - 2 * tokens) >= first, 0.0, far_below)
    mid_bias = jnp.where(key - tokens >= first, 0.0, far_below)
    queries = group_rows(q_ref, kv, group)
    hidden = []
    for g in range(kv):
        fold = jnp.where(here, dot(own_ref[g], queries[g], 1, 1), dot(two_ref[g], queries[g], 1, 1))
        fold = fold * scaling + fold_bias
        mid = dot(one_ref[g], queries[g], 1, 1) * scaling + mid_bias
        top = jnp.maximum(jnp.max(fold, axis=0, keepdims=True), jnp.max(mid, axis=0, keepdims=True))
        fold = jnp.exp(fold - top)
        mid = jnp.exp(mid - top)
        total = jnp.sum(fold, axis=0, keepdims=True) + jnp.sum(mid, axis=0, keepdims=True)
        share = 1.0 / total
        fold = fold * share
        mid = mid * share
        weights_ref[g, 0:tokens, :] = fold
        weights_ref[g, tokens : 2 * tokens, :] = mid
        low = jnp.concatenate(
            [jnp.where(here, 0.0, fold).astype(LOW), mid.astype(LOW), jnp.where(here, fold, 0.0).astype(LOW)],
            axis=0,
        )
        values = jnp.concatenate([two_ref[kv + g], one_ref[kv + g], own_ref[kv + g]], axis=0)
        hidden.append(dot(values, low, 0, 0).astype(LOW))
    hidden = jnp.concatenate(hidden, axis=0)
    on_diff = dot(jnp.concatenate([diff_ref[g] for g in range(kv)], axis=1), hidden, 1, 0)
    lifted = own_terms(on_diff, owner, tenants, rank, group)
    one_hot = (owner == lax.broadcasted_iota(jnp.int32, (tenants, lanes), 0)).astype(WIDE)
    bias = jnp.concatenate([bias_ref[...]] * (8 // rank), axis=0)
    shift = dot(bias, one_hot, 1, 0, lax.Precision.HIGHEST)
    lifted = (lifted + shift).astype(LOW).astype(WIDE)
    pulled = pulled_ref[...]
    span = tenants * rank
    mine = owner == lax.broadcasted_iota(jnp.int32, (span, lanes), 0) // rank
    lift_rows = jnp.where(mine, jnp.concatenate([lifted] * (span // 8), axis=0), 0.0)
    pull_rows = jnp.where(mine, jnp.concatenate([pulled] * (span // 8), axis=0), 0.0)
    head = lane_head((span, lanes), group)
    lift_all = jnp.concatenate([jnp.where(head == h, lift_rows, 0.0).astype(LOW) for h in range(group)], axis=0)
    pull_all = jnp.concatenate([jnp.where(head == h, pull_rows, 0.0).astype(LOW) for h in range(group)], axis=0)
    on_proj = dot(pull_all, hidden, 1, 1)
    on_rot = dot(lift_all, jnp.concatenate([cots_ref[g] for g in range(kv)], axis=1), 1, 0) - on_proj
    dim = q_ref.shape[2]
    for g in range(kv):
        for h in range(group):
            device, place = (g * group + h) // owned, (g * group + h) % owned
            columns = slice(g * dim, (g + 1) * dim)
            for r in range(rep):
                rows = slice(h * span + r * span // rep, h * span + (r + 1) * span // rep)
                part_ref[device, r, place, 0] = on_rot[rows, columns].astype(LOW)
                part_ref[device, r, place, 1] = on_proj[rows, columns].astype(LOW)


def backward_kernel(
    q_ref, gh_ref, two_ref, one_ref, own_ref, weights_ref, dq_ref, back_two_ref, back_one_ref, back_own_ref,
    *, kv, group, scaling,
):
    tokens = own_ref.shape[1]
    lanes = weights_ref.shape[2]
    dim = q_ref.shape[2]
    _, here = places(lanes, tokens, group)
    queries = group_rows(q_ref, kv, group)
    query_grads = []
    for g in range(kv):
        grads = gh_ref[g]
        fold_weights = weights_ref[g, 0:tokens, :]
        mid_weights = weights_ref[g, tokens : 2 * tokens, :]
        fold = jnp.where(here, dot(own_ref[kv + g], grads, 1, 1), dot(two_ref[kv + g], grads, 1, 1))
        mid = dot(one_ref[kv + g], grads, 1, 1)
        delta = jnp.sum(fold * fold_weights, axis=0, keepdims=True) + jnp.sum(
            mid * mid_weights, axis=0, keepdims=True
        )
        fold = fold_weights * (fold - delta)
        mid = mid_weights * (mid - delta)
        score_grad = jnp.concatenate(
            [jnp.where(here, 0.0, fold).astype(LOW), mid.astype(LOW), jnp.where(here, fold, 0.0).astype(LOW)],
            axis=0,
        )
        low = jnp.concatenate(
            [
                jnp.where(here, 0.0, fold_weights).astype(LOW),
                mid_weights.astype(LOW),
                jnp.where(here, fold_weights, 0.0).astype(LOW),
            ],
            axis=0,
        )
        keys = jnp.concatenate([two_ref[g], one_ref[g], own_ref[g]], axis=0)
        key_grad = dot(score_grad, queries[g], 1, 0) * scaling
        value_grad = dot(low, grads, 1, 0)
        for place, grad in ((g, key_grad), (kv + g, value_grad)):
            back_two_ref[place] = grad[0:tokens].astype(LOW)
            back_one_ref[place] = grad[tokens : 2 * tokens].astype(LOW)
            back_own_ref[place] = grad[2 * tokens :]
        query_grad = dot(keys, score_grad, 0, 0) * scaling
        query_grads.append(query_grad.T.reshape(tokens, group, dim))
        if g % 2 == 1:
            both = jnp.concatenate(query_grads[-2:], axis=1).astype(LOW)
            dq_ref[:, (g - 1) * group : (g + 1) * group, :] = both


def on_device(
    query_rows, key_rows, value_matrix, cotangent, rotation, projection, shift_bias, doc_starts, tenant_ids,
):
    queries = query_rows[0]
    upstream = cotangent[0]
    tokens, heads, dim = queries.shape
    kv = key_rows.shape[2]
    group = heads // kv
    scaling = dim ** (-0.5)
    tenants, rank = rotation.shape[0], rotation.shape[1]
    lanes = tokens * group
    ctx = lax.axis_size("ctx")
    rep = lax.axis_size("rep")
    assert 2 * tokens == DOC_MAX

    own = jnp.moveaxis(jnp.concatenate([key_rows[0], value_matrix[0]], axis=1), 1, 0)
    one = shifted(own, "ctx", 1)
    two = shifted(own, "ctx", 2)

    rot = rotation.reshape(tenants * rank, heads, dim)
    proj = projection.reshape(tenants * rank, heads, dim)
    sizes = dict(kv=kv, group=group)
    vmem = pl.BlockSpec(memory_space=pltpu.VMEM)
    hbm = pl.BlockSpec(memory_space=pltpu.HBM)

    def call(body, outs, flops, moved, specs=None, scratch=(), limit=24, **fixed):
        def run(*operands):
            return pl.pallas_call(
                lambda *refs: body(*refs, **fixed),
                out_shape=[jax.ShapeDtypeStruct(*out) for out in outs],
                in_specs=specs or [vmem] * len(operands),
                out_specs=[vmem] * len(outs),
                scratch_shapes=scratch,
                compiler_params=pltpu.CompilerParams(vmem_limit_bytes=limit * 2**20),
                name=body.__name__,
                cost_estimate=pl.CostEstimate(flops=flops, bytes_accessed=moved, transcendentals=0),
            )(*operands)

        return run

    span = tenants * rank
    in_kernel = rep if span // rep % 16 == 0 else 1
    cots, grad_hidden, diff, pulled, meta = call(
        pull_kernel,
        [
            ((kv, lanes, dim), LOW), ((kv, lanes, dim), LOW), ((kv, span * group, dim), LOW),
            ((8, lanes), WIDE), ((8, lanes), jnp.int32),
        ],
        2 * 2**30, 4 * 2**20, [vmem, vmem, hbm, hbm, hbm],
        [
            pltpu.VMEM((tokens, heads, dim), LOW), pltpu.VMEM((span, heads, dim), LOW),
            pltpu.VMEM((span, heads, dim), LOW), pltpu.SemaphoreType.DMA((3,)),
        ],
        limit=53, tenants=tenants, rank=rank, **sizes,
    )(doc_starts, tenant_ids, upstream, rot, proj)
    here = heads // ctx
    weights, part = call(
        forward_kernel,
        [((kv, 2 * tokens, lanes), WIDE), ((ctx, in_kernel, here, 2, span // in_kernel, dim), LOW)],
        4 * 2**30, 10 * 2**20,
        tenants=tenants, rank=rank, scaling=scaling, rep=in_kernel, owned=here, **sizes,
    )(shift_bias.T, queries, two, one, own, cots, diff, meta, pulled)
    gathered = lax.all_to_all(part, "ctx", split_axis=0, concat_axis=0, tiled=True)
    d_queries, back_two, back_one, back_own = call(
        backward_kernel,
        [((tokens, heads, dim), LOW), (own.shape, LOW), (own.shape, LOW), (own.shape, WIDE)],
        4 * 2**30, 10 * 2**20, scaling=scaling, **sizes,
    )(queries, grad_hidden, two, one, own, weights)
    from_one = shifted(back_one, "ctx", -1)
    from_two = shifted(back_two, "ctx", -2)

    by_rep = gathered.astype(WIDE).sum(axis=0).astype(LOW)
    if in_kernel == 1:
        by_rep = jnp.moveaxis(by_rep.reshape(here, 2, rep, span // rep, dim), 2, 0)
    from_one, from_two, _ = lax.optimization_barrier((from_one, from_two, by_rep))
    by_rep = lax.all_to_all(by_rep, "rep", split_axis=0, concat_axis=0, tiled=True)
    summed = by_rep.astype(WIDE).sum(axis=0).reshape(here, 2, tenants // rep, rank, dim)
    grads = jnp.moveaxis(summed, 0, 3)
    back = (back_own + from_one.astype(WIDE) + from_two.astype(WIDE)).astype(LOW)
    d_keys = jnp.moveaxis(back[:kv], 0, 1)
    d_values = jnp.moveaxis(back[kv:], 0, 1)
    return (d_queries[None], d_keys[None], d_values[None], grads[0], grads[1])


def solution(mesh):
    rows = P("rep", "ctx", None, None)
    in_specs = (rows, rows, rows, rows, P(), P(), P(), P("rep", None), P("rep", None))
    tenant_rows = P("rep", None, "ctx", None)
    out_specs = (rows, rows, rows, tenant_rows, tenant_rows)
    return jax.shard_map(
        on_device, mesh=mesh, in_specs=in_specs, out_specs=out_specs, check_vma=False
    )
```

```python
import jax
import jax.numpy as jnp
from jax import lax
from jax.experimental import pallas as pl
from jax.experimental.pallas import tpu as pltpu
from jax.sharding import PartitionSpec as P

DOC_MAX = 256
LOW = jnp.bfloat16
WIDE = jnp.float32
far_below = -1e30


def shifted(value, axis, steps):
    count = lax.axis_size(axis)
    first, last = (max(0, -steps), min(count, count - steps))
    return lax.ppermute(value, axis, [(source, source + steps) for source in range(first, last)])


def exchanged(value, axis, bit):
    count = lax.axis_size(axis)
    return lax.ppermute(value, axis, [(source, source ^ bit) for source in range(count)])


def halved(keep, axis, bit):
    half = keep.shape[0] // 2
    other = exchanged(keep[half:], axis, bit)
    return keep[:half].astype(WIDE) + other.astype(WIDE)


def reversed_bits(value, bits):
    result = 0 * value
    for bit in range(bits):
        result = result + ((value >> bit) & 1) * (1 << (bits - 1 - bit))
    return result


def dot(left, right, left_dim, right_dim, precision=None):
    return lax.dot_general(
        left, right, (((left_dim,), (right_dim,)), ((), ())),
        precision=precision, preferred_element_type=WIDE,
    )


def group_rows(ref, kv_count, group_size):
    rows, _, dim = ref.shape
    wide = 2 * group_size
    parts = []
    for pair in range(kv_count // 2):
        both = ref[:, pair * wide : (pair + 1) * wide, :].astype(WIDE)
        for half in range(2):
            one = both[:, half * group_size : (half + 1) * group_size, :]
            parts.append(one.reshape(rows * group_size, dim).astype(LOW))
    return parts


def lane_head(shape, group_size):
    return lax.broadcasted_iota(jnp.int32, shape, 1) % group_size


def own_terms(maps_by_rows, owner, tenants, low_rank, group_size):
    lanes = maps_by_rows.shape[1]
    same_head = lax.broadcasted_iota(jnp.int32, (group_size, lanes), 0) == lane_head(
        (group_size, lanes), group_size
    )
    span = low_rank * group_size
    total = jnp.zeros((low_rank, group_size, lanes), WIDE)
    for tenant in range(tenants):
        keep = same_head & (owner == tenant)
        block = maps_by_rows[tenant * span : (tenant + 1) * span].reshape(
            low_rank, group_size, lanes
        )
        total = total + jnp.where(keep[None], block, 0.0)
    rows = jnp.sum(total, axis=1)
    rows = jnp.concatenate([rows, rows], axis=0)
    tiles = lanes // 128
    stacked = jnp.concatenate([rows[:, c * 128 : (c + 1) * 128] for c in range(tiles)], axis=0)
    side = lax.broadcasted_iota(jnp.int32, (128, 128), 0) // group_size
    over = lax.broadcasted_iota(jnp.int32, (128, 128), 1) // group_size
    spread = dot(stacked, (side == over).astype(WIDE), 1, 0, lax.Precision.HIGHEST)
    return jnp.concatenate([spread[c * 8 : (c + 1) * 8] for c in range(tiles)], axis=1)


def pull_kernel(
    starts_hbm, owners_hbm, cot_hbm, rot_hbm, proj_hbm, gh_ref, diff_ref, pulled_ref, meta_ref,
    starts_ref, owners_ref, cot_ref, rot_ref, proj_ref, sems, *, kv, group, tenants, rank,
):
    pairs = (
        (starts_hbm, starts_ref), (owners_hbm, owners_ref), (cot_hbm, cot_ref),
        (rot_hbm, rot_ref), (proj_hbm, proj_ref),
    )
    copies = [
        pltpu.make_async_copy(source, target, sems.at[at])
        for at, (source, target) in enumerate(pairs)
    ]
    for copy in copies:
        copy.start()
    copies[0].wait()
    copies[1].wait()
    lanes = meta_ref.shape[1]
    tokens = lanes // group
    row_first = lax.axis_index("ctx") * tokens
    mine = pl.ds(pl.multiple_of(row_first, tokens), tokens)
    row = lax.broadcasted_iota(jnp.int32, (8, tokens), 0)
    both = jnp.where(row == 0, starts_ref[:, mine] - row_first, owners_ref[:, mine]).astype(WIDE)
    repeat = lax.broadcasted_iota(jnp.int32, (tokens, lanes), 0) == (
        lax.broadcasted_iota(jnp.int32, (tokens, lanes), 1) // group
    )
    meta = dot(both, repeat.astype(WIDE), 1, 0, lax.Precision.HIGHEST).astype(jnp.int32)
    meta_ref[...] = meta
    owner = meta[1:2, :]
    copies[2].wait()
    cots = group_rows(cot_ref, kv, group)
    copies[3].wait()
    rots = group_rows(rot_ref, kv, group)
    on_rot = dot(jnp.concatenate(rots, axis=1), jnp.concatenate(cots, axis=1), 1, 1)
    pulled = own_terms(on_rot, owner, tenants, rank, group).astype(LOW).astype(WIDE)
    pulled_ref[...] = pulled
    same_head = lax.broadcasted_iota(jnp.int32, (group, lanes), 0) == lane_head((group, lanes), group)
    picked = []
    for tenant in range(tenants):
        keep = same_head & (owner == tenant)
        for k in range(rank):
            picked.append(jnp.where(keep, pulled[k : k + 1], 0.0))
    picked = jnp.concatenate(picked, axis=0).T.astype(LOW)
    copies[4].wait()
    projs = group_rows(proj_ref, kv, group)
    for g in range(kv):
        diff = (projs[g].astype(WIDE) - rots[g].astype(WIDE)).astype(LOW)
        diff_ref[g] = diff
        gh_ref[g] = (cots[g].astype(WIDE) + dot(picked, diff, 1, 0)).astype(LOW)


def places(lanes, tokens, group):
    key = lax.broadcasted_iota(jnp.int32, (tokens, lanes), 0)
    query = lax.broadcasted_iota(jnp.int32, (tokens, lanes), 1) // group
    return key, key <= query


def forward_kernel(
    bias_ref, q_ref, two_ref, one_ref, own_ref, cot_hbm, diff_ref, meta_ref, pulled_ref,
    weights_ref, send_ref, keep_ref, cot_ref, sem, *, kv, group, tenants, rank, scaling, owned,
):
    fetch = pltpu.make_async_copy(cot_hbm, cot_ref, sem)
    fetch.start()
    tokens = own_ref.shape[1]
    first = meta_ref[0:1, :]
    owner = meta_ref[1:2, :]
    lanes = owner.shape[1]
    key, here = places(lanes, tokens, group)
    fold_bias = jnp.where(jnp.where(here, key, key - 2 * tokens) >= first, 0.0, far_below)
    mid_bias = jnp.where(key - tokens >= first, 0.0, far_below)
    queries = group_rows(q_ref, kv, group)
    hidden = []
    for g in range(kv):
        fold = jnp.where(here, dot(own_ref[g], queries[g], 1, 1), dot(two_ref[g], queries[g], 1, 1))
        fold = fold * scaling + fold_bias
        mid = dot(one_ref[g], queries[g], 1, 1) * scaling + mid_bias
        top = jnp.maximum(jnp.max(fold, axis=0, keepdims=True), jnp.max(mid, axis=0, keepdims=True))
        fold = jnp.exp(fold - top)
        mid = jnp.exp(mid - top)
        total = jnp.sum(fold, axis=0, keepdims=True) + jnp.sum(mid, axis=0, keepdims=True)
        share = 1.0 / total
        fold = fold * share
        mid = mid * share
        weights_ref[g, 0:tokens, :] = fold
        weights_ref[g, tokens : 2 * tokens, :] = mid
        low = jnp.concatenate(
            [jnp.where(here, 0.0, fold).astype(LOW), mid.astype(LOW), jnp.where(here, fold, 0.0).astype(LOW)],
            axis=0,
        )
        values = jnp.concatenate([two_ref[kv + g], one_ref[kv + g], own_ref[kv + g]], axis=0)
        hidden.append(dot(values, low, 0, 0).astype(LOW))
    hidden = jnp.concatenate(hidden, axis=0)
    on_diff = dot(jnp.concatenate([diff_ref[g] for g in range(kv)], axis=1), hidden, 1, 0)
    lifted = own_terms(on_diff, owner, tenants, rank, group)
    one_hot = (owner == lax.broadcasted_iota(jnp.int32, (tenants, lanes), 0)).astype(WIDE)
    bias = jnp.concatenate([bias_ref[...]] * (8 // rank), axis=0)
    shift = dot(bias, one_hot, 1, 0, lax.Precision.HIGHEST)
    lifted = (lifted + shift).astype(LOW).astype(WIDE)
    pulled = pulled_ref[...]
    ctx, rep = lax.axis_size("ctx"), lax.axis_size("rep")
    me, layer = lax.axis_index("ctx"), lax.axis_index("rep")
    per_group = group // owned
    span = tenants * rank
    tenant_row = lax.broadcasted_iota(jnp.int32, (span, lanes), 0) // rank
    mine = owner == (tenant_row ^ (layer * (tenants // rep)))
    lift_rows = jnp.where(mine, jnp.concatenate([lifted] * (span // 8), axis=0), 0.0)
    pull_rows = jnp.where(mine, jnp.concatenate([pulled] * (span // 8), axis=0), 0.0)
    slot = lane_head((span, lanes), group) ^ ((me % per_group) * owned)
    lift_all = jnp.concatenate([jnp.where(slot == h, lift_rows, 0.0).astype(LOW) for h in range(group)], axis=0)
    pull_all = jnp.concatenate([jnp.where(slot == h, pull_rows, 0.0).astype(LOW) for h in range(group)], axis=0)
    on_proj = dot(pull_all, hidden, 1, 1)
    fetch.wait()
    on_rot = dot(lift_all, jnp.concatenate(group_rows(cot_ref, kv, group), axis=1), 1, 0) - on_proj
    dim = q_ref.shape[2]
    here_rows = span // rep
    bits = ctx.bit_length() - 1
    for g in range(kv):
        columns = slice(g * dim, (g + 1) * dim)
        for low in range(per_group):
            device = (g ^ (me // per_group)) * per_group + low
            place = reversed_bits(device >> 1, bits - 1)
            into = send_ref if low % 2 else keep_ref
            for r in range(rep):
                pieces = []
                for h in range(low * owned, (low + 1) * owned):
                    rows = slice(h * span + r * here_rows, h * span + (r + 1) * here_rows)
                    pieces += [on_rot[rows, columns], on_proj[rows, columns]]
                into[place, reversed_bits(r, rep.bit_length() - 1)] = jnp.concatenate(pieces, axis=0).astype(LOW)


def backward_kernel(
    q_ref, gh_ref, two_ref, one_ref, own_ref, weights_ref, dq_ref, back_two_ref, back_one_ref, back_own_ref,
    *, kv, group, scaling,
):
    tokens = own_ref.shape[1]
    lanes = weights_ref.shape[2]
    dim = q_ref.shape[2]
    _, here = places(lanes, tokens, group)
    queries = group_rows(q_ref, kv, group)
    query_grads = []
    for g in range(kv):
        grads = gh_ref[g]
        fold_weights = weights_ref[g, 0:tokens, :]
        mid_weights = weights_ref[g, tokens : 2 * tokens, :]
        fold = jnp.where(here, dot(own_ref[kv + g], grads, 1, 1), dot(two_ref[kv + g], grads, 1, 1))
        mid = dot(one_ref[kv + g], grads, 1, 1)
        delta = jnp.sum(fold * fold_weights, axis=0, keepdims=True) + jnp.sum(
            mid * mid_weights, axis=0, keepdims=True
        )
        fold = fold_weights * (fold - delta)
        mid = mid_weights * (mid - delta)
        score_grad = jnp.concatenate(
            [jnp.where(here, 0.0, fold).astype(LOW), mid.astype(LOW), jnp.where(here, fold, 0.0).astype(LOW)],
            axis=0,
        )
        low = jnp.concatenate(
            [
                jnp.where(here, 0.0, fold_weights).astype(LOW),
                mid_weights.astype(LOW),
                jnp.where(here, fold_weights, 0.0).astype(LOW),
            ],
            axis=0,
        )
        keys = jnp.concatenate([two_ref[g], one_ref[g], own_ref[g]], axis=0)
        key_grad = dot(score_grad, queries[g], 1, 0) * scaling
        value_grad = dot(low, grads, 1, 0)
        for place, grad in ((g, key_grad), (kv + g, value_grad)):
            back_two_ref[place] = grad[0:tokens].astype(LOW)
            back_one_ref[place] = grad[tokens : 2 * tokens].astype(LOW)
            back_own_ref[place] = grad[2 * tokens :]
        query_grad = dot(keys, score_grad, 0, 0) * scaling
        query_grads.append(query_grad.T.reshape(tokens, group, dim))
        if g % 2 == 1:
            both = jnp.concatenate(query_grads[-2:], axis=1).astype(LOW)
            dq_ref[:, (g - 1) * group : (g + 1) * group, :] = both


def on_device(
    query_rows, key_rows, value_matrix, cotangent, rotation, projection, shift_bias, doc_starts, tenant_ids,
):
    queries = query_rows[0]
    upstream = cotangent[0]
    tokens, heads, dim = queries.shape
    kv = key_rows.shape[2]
    group = heads // kv
    scaling = dim ** (-0.5)
    tenants, rank = rotation.shape[0], rotation.shape[1]
    lanes = tokens * group
    ctx = lax.axis_size("ctx")
    rep = lax.axis_size("rep")
    assert 2 * tokens == DOC_MAX

    own = jnp.moveaxis(jnp.concatenate([key_rows[0], value_matrix[0]], axis=1), 1, 0)
    one = shifted(own, "ctx", 1)
    two = shifted(own, "ctx", 2)

    rot = rotation.reshape(tenants * rank, heads, dim)
    proj = projection.reshape(tenants * rank, heads, dim)
    sizes = dict(kv=kv, group=group)
    vmem = pl.BlockSpec(memory_space=pltpu.VMEM)
    hbm = pl.BlockSpec(memory_space=pltpu.HBM)

    def call(body, outs, flops, moved, specs=None, scratch=(), limit=24, **fixed):
        def run(*operands):
            return pl.pallas_call(
                lambda *refs: body(*refs, **fixed),
                out_shape=[jax.ShapeDtypeStruct(*out) for out in outs],
                in_specs=specs or [vmem] * len(operands),
                out_specs=[vmem] * len(outs),
                scratch_shapes=scratch,
                compiler_params=pltpu.CompilerParams(vmem_limit_bytes=limit * 2**20),
                name=body.__name__,
                cost_estimate=pl.CostEstimate(flops=flops, bytes_accessed=moved, transcendentals=0),
            )(*operands)

        return run

    span = tenants * rank
    here = heads // ctx
    rows = here * 2 * span // rep
    grad_hidden, diff, pulled, meta = call(
        pull_kernel,
        [
            ((kv, lanes, dim), LOW), ((kv, span * group, dim), LOW),
            ((8, lanes), WIDE), ((8, lanes), jnp.int32),
        ],
        2 * 2**30, 4 * 2**20, [hbm] * 5,
        [
            pltpu.VMEM(doc_starts.shape, jnp.int32), pltpu.VMEM(tenant_ids.shape, jnp.int32),
            pltpu.VMEM((tokens, heads, dim), LOW), pltpu.VMEM((span, heads, dim), LOW),
            pltpu.VMEM((span, heads, dim), LOW), pltpu.SemaphoreType.DMA((5,)),
        ],
        limit=53, tenants=tenants, rank=rank, **sizes,
    )(doc_starts, tenant_ids, upstream, rot, proj)
    weights, send, keep = call(
        forward_kernel,
        [((kv, 2 * tokens, lanes), WIDE)] + [((ctx // 2, rep, rows, dim), LOW)] * 2,
        4 * 2**30, 10 * 2**20, [vmem] * 5 + [hbm] + [vmem] * 3,
        [pltpu.VMEM((tokens, heads, dim), LOW), pltpu.SemaphoreType.DMA],
        tenants=tenants, rank=rank, scaling=scaling, owned=here, **sizes,
    )(shift_bias.T, queries, two, one, own, upstream, diff, meta, pulled)
    part = (keep.astype(WIDE) + exchanged(send, "ctx", 1).astype(WIDE)).astype(LOW)
    weights, part = lax.optimization_barrier((weights, part))
    d_queries, back_two, back_one, back_own = call(
        backward_kernel,
        [((tokens, heads, dim), LOW), (own.shape, LOW), (own.shape, LOW), (own.shape, WIDE)],
        4 * 2**30, 10 * 2**20, scaling=scaling, **sizes,
    )(queries, grad_hidden, two, one, own, weights)
    from_one = shifted(back_one, "ctx", -1)
    from_two = shifted(back_two, "ctx", -2)

    bit = 2
    while bit < ctx:
        part = halved(part, "ctx", bit).astype(LOW)
        bit *= 2
    part = part[0]
    bit = 1
    while bit < rep:
        part = part.astype(LOW)
        if 2 * bit == rep:
            from_one, from_two, _ = lax.optimization_barrier((from_one, from_two, part))
        part = halved(part, "rep", bit)
        bit *= 2
    grads = jnp.moveaxis(part.astype(WIDE).reshape(here, 2, tenants // rep, rank, dim), 0, 3)
    back = (back_own + from_one.astype(WIDE) + from_two.astype(WIDE)).astype(LOW)
    d_keys = jnp.moveaxis(back[:kv], 0, 1)
    d_values = jnp.moveaxis(back[kv:], 0, 1)
    return (d_queries[None], d_keys[None], d_values[None], grads[0], grads[1])


def solution(mesh):
    rows = P("rep", "ctx", None, None)
    in_specs = (rows, rows, rows, rows, P(), P(), P(), P("rep", None), P("rep", None))
    tenant_rows = P("rep", None, "ctx", None)
    out_specs = (rows, rows, rows, tenant_rows, tenant_rows)
    return jax.shard_map(
        on_device, mesh=mesh, in_specs=in_specs, out_specs=out_specs, check_vma=False
    )
```

```python
import jax
import jax.numpy as jnp
from jax import lax
from jax.experimental import pallas as pl
from jax.experimental.pallas import tpu as pltpu
from jax.sharding import PartitionSpec as P

DOC_MAX = 256
LOW = jnp.bfloat16
WIDE = jnp.float32
far_below = -1e30


def shifted(value, axis, steps):
    count = lax.axis_size(axis)
    first, last = (max(0, -steps), min(count, count - steps))
    return lax.ppermute(value, axis, [(source, source + steps) for source in range(first, last)])


def exchanged(value, axis, bit):
    count = lax.axis_size(axis)
    return lax.ppermute(value, axis, [(source, source ^ bit) for source in range(count)])


def halved(keep, axis, bit, beside=None):
    half = keep.shape[0] // 2
    other = exchanged(keep[half:], axis, bit)
    if beside is not None:
        other, _ = lax.optimization_barrier((other, beside))
    return keep[:half].astype(WIDE) + other.astype(WIDE)


def reversed_bits(value, bits):
    result = 0 * value
    for bit in range(bits):
        result = result + ((value >> bit) & 1) * (1 << (bits - 1 - bit))
    return result


def dot(left, right, left_dim, right_dim, precision=None):
    return lax.dot_general(
        left, right, (((left_dim,), (right_dim,)), ((), ())),
        precision=precision, preferred_element_type=WIDE,
    )


def group_rows(ref, kv_count, group_size):
    rows, _, dim = ref.shape
    wide = 2 * group_size
    parts = []
    for pair in range(kv_count // 2):
        both = ref[:, pair * wide : (pair + 1) * wide, :].astype(WIDE)
        for half in range(2):
            one = both[:, half * group_size : (half + 1) * group_size, :]
            parts.append(one.reshape(rows * group_size, dim).astype(LOW))
    return parts


def lane_head(shape, group_size):
    return lax.broadcasted_iota(jnp.int32, shape, 1) % group_size


def own_terms(maps_by_rows, owner, tenants, low_rank, group_size):
    lanes = maps_by_rows.shape[1]
    same_head = lax.broadcasted_iota(jnp.int32, (group_size, lanes), 0) == lane_head(
        (group_size, lanes), group_size
    )
    span = low_rank * group_size
    total = jnp.zeros((low_rank, group_size, lanes), WIDE)
    for tenant in range(tenants):
        keep = same_head & (owner == tenant)
        block = maps_by_rows[tenant * span : (tenant + 1) * span].reshape(
            low_rank, group_size, lanes
        )
        total = total + jnp.where(keep[None], block, 0.0)
    rows = jnp.sum(total, axis=1)
    rows = jnp.concatenate([rows, rows], axis=0)
    tiles = lanes // 128
    stacked = jnp.concatenate([rows[:, c * 128 : (c + 1) * 128] for c in range(tiles)], axis=0)
    side = lax.broadcasted_iota(jnp.int32, (128, 128), 0) // group_size
    over = lax.broadcasted_iota(jnp.int32, (128, 128), 1) // group_size
    spread = dot(stacked, (side == over).astype(WIDE), 1, 0, lax.Precision.HIGHEST)
    return jnp.concatenate([spread[c * 8 : (c + 1) * 8] for c in range(tiles)], axis=1)


def pull_kernel(
    starts_hbm, owners_hbm, cot_hbm, rot_hbm, proj_hbm, gh_ref, diff_ref, pulled_ref, meta_ref,
    starts_ref, owners_ref, cot_ref, rot_ref, proj_ref, sems, *, kv, group, tenants, rank,
):
    pairs = (
        (starts_hbm, starts_ref), (owners_hbm, owners_ref), (cot_hbm, cot_ref),
        (rot_hbm, rot_ref), (proj_hbm, proj_ref),
    )
    copies = [
        pltpu.make_async_copy(source, target, sems.at[at])
        for at, (source, target) in enumerate(pairs)
    ]
    for copy in copies:
        copy.start()
    copies[0].wait()
    copies[1].wait()
    lanes = meta_ref.shape[1]
    tokens = lanes // group
    row_first = lax.axis_index("ctx") * tokens
    mine = pl.ds(pl.multiple_of(row_first, tokens), tokens)
    row = lax.broadcasted_iota(jnp.int32, (8, tokens), 0)
    both = jnp.where(row == 0, starts_ref[:, mine] - row_first, owners_ref[:, mine]).astype(WIDE)
    repeat = lax.broadcasted_iota(jnp.int32, (tokens, lanes), 0) == (
        lax.broadcasted_iota(jnp.int32, (tokens, lanes), 1) // group
    )
    meta = dot(both, repeat.astype(WIDE), 1, 0, lax.Precision.HIGHEST).astype(jnp.int32)
    meta_ref[...] = meta
    owner = meta[1:2, :]
    copies[2].wait()
    cots = group_rows(cot_ref, kv, group)
    copies[3].wait()
    rots = group_rows(rot_ref, kv, group)
    on_rot = dot(jnp.concatenate(rots, axis=1), jnp.concatenate(cots, axis=1), 1, 1)
    pulled = own_terms(on_rot, owner, tenants, rank, group).astype(LOW).astype(WIDE)
    pulled_ref[...] = pulled
    same_head = lax.broadcasted_iota(jnp.int32, (group, lanes), 0) == lane_head((group, lanes), group)
    picked = []
    for tenant in range(tenants):
        keep = same_head & (owner == tenant)
        for k in range(rank):
            picked.append(jnp.where(keep, pulled[k : k + 1], 0.0))
    picked = jnp.concatenate(picked, axis=0).T.astype(LOW)
    copies[4].wait()
    projs = group_rows(proj_ref, kv, group)
    for g in range(kv):
        diff = (projs[g].astype(WIDE) - rots[g].astype(WIDE)).astype(LOW)
        diff_ref[g] = diff
        gh_ref[g] = (cots[g].astype(WIDE) + dot(picked, diff, 1, 0)).astype(LOW)


def places(lanes, tokens, group):
    key = lax.broadcasted_iota(jnp.int32, (tokens, lanes), 0)
    query = lax.broadcasted_iota(jnp.int32, (tokens, lanes), 1) // group
    return key, key <= query


def forward_kernel(
    bias_ref, q_ref, two_ref, one_ref, own_ref, cot_hbm, diff_ref, meta_ref, pulled_ref,
    weights_ref, send_ref, keep_ref, cot_ref, sem, *, kv, group, tenants, rank, scaling, owned,
):
    fetch = pltpu.make_async_copy(cot_hbm, cot_ref, sem)
    fetch.start()
    tokens = own_ref.shape[1]
    first = meta_ref[0:1, :]
    owner = meta_ref[1:2, :]
    lanes = owner.shape[1]
    key, here = places(lanes, tokens, group)
    fold_bias = jnp.where(jnp.where(here, key, key - 2 * tokens) >= first, 0.0, far_below)
    mid_bias = jnp.where(key - tokens >= first, 0.0, far_below)
    queries = group_rows(q_ref, kv, group)
    hidden = []
    for g in range(kv):
        fold = jnp.where(here, dot(own_ref[g], queries[g], 1, 1), dot(two_ref[g], queries[g], 1, 1))
        fold = fold * scaling + fold_bias
        mid = dot(one_ref[g], queries[g], 1, 1) * scaling + mid_bias
        top = jnp.maximum(jnp.max(fold, axis=0, keepdims=True), jnp.max(mid, axis=0, keepdims=True))
        fold = jnp.exp(fold - top)
        mid = jnp.exp(mid - top)
        total = jnp.sum(fold, axis=0, keepdims=True) + jnp.sum(mid, axis=0, keepdims=True)
        share = 1.0 / total
        fold = fold * share
        mid = mid * share
        weights_ref[g, 0:tokens, :] = fold
        weights_ref[g, tokens : 2 * tokens, :] = mid
        low = jnp.concatenate(
            [jnp.where(here, 0.0, fold).astype(LOW), mid.astype(LOW), jnp.where(here, fold, 0.0).astype(LOW)],
            axis=0,
        )
        values = jnp.concatenate([two_ref[kv + g], one_ref[kv + g], own_ref[kv + g]], axis=0)
        hidden.append(dot(values, low, 0, 0).astype(LOW))
    hidden = jnp.concatenate(hidden, axis=0)
    on_diff = dot(jnp.concatenate([diff_ref[g] for g in range(kv)], axis=1), hidden, 1, 0)
    lifted = own_terms(on_diff, owner, tenants, rank, group)
    one_hot = (owner == lax.broadcasted_iota(jnp.int32, (tenants, lanes), 0)).astype(WIDE)
    bias = jnp.concatenate([bias_ref[...]] * (8 // rank), axis=0)
    shift = dot(bias, one_hot, 1, 0, lax.Precision.HIGHEST)
    lifted = (lifted + shift).astype(LOW).astype(WIDE)
    pulled = pulled_ref[...]
    ctx, rep = lax.axis_size("ctx"), lax.axis_size("rep")
    me, layer = lax.axis_index("ctx"), lax.axis_index("rep")
    per_group = group // owned
    span = tenants * rank
    tenant_row = lax.broadcasted_iota(jnp.int32, (span, lanes), 0) // rank
    mine = owner == (tenant_row ^ (layer * (tenants // rep)))
    lift_rows = jnp.where(mine, jnp.concatenate([lifted] * (span // 8), axis=0), 0.0)
    pull_rows = jnp.where(mine, jnp.concatenate([pulled] * (span // 8), axis=0), 0.0)
    slot = lane_head((span, lanes), group) ^ ((me % per_group) * owned)
    lift_all = jnp.concatenate([jnp.where(slot == h, lift_rows, 0.0).astype(LOW) for h in range(group)], axis=0)
    pull_all = jnp.concatenate([jnp.where(slot == h, pull_rows, 0.0).astype(LOW) for h in range(group)], axis=0)
    on_proj = dot(pull_all, hidden, 1, 1)
    fetch.wait()
    on_rot = dot(lift_all, jnp.concatenate(group_rows(cot_ref, kv, group), axis=1), 1, 0) - on_proj
    dim = q_ref.shape[2]
    here_rows = span // rep
    bits = ctx.bit_length() - 1
    for g in range(kv):
        columns = slice(g * dim, (g + 1) * dim)
        for low in range(per_group):
            device = (g ^ (me // per_group)) * per_group + low
            place = reversed_bits(device >> 1, bits - 1)
            into = send_ref if low % 2 else keep_ref
            for r in range(rep):
                pieces = []
                for h in range(low * owned, (low + 1) * owned):
                    rows = slice(h * span + r * here_rows, h * span + (r + 1) * here_rows)
                    pieces += [on_rot[rows, columns], on_proj[rows, columns]]
                into[place, reversed_bits(r, rep.bit_length() - 1)] = jnp.concatenate(pieces, axis=0).astype(LOW)


def backward_kernel(
    q_ref, gh_ref, two_ref, one_ref, own_ref, weights_ref, dq_ref, back_two_ref, back_one_ref, back_own_ref,
    *, kv, group, scaling,
):
    tokens = own_ref.shape[1]
    lanes = weights_ref.shape[2]
    dim = q_ref.shape[2]
    _, here = places(lanes, tokens, group)
    queries = group_rows(q_ref, kv, group)
    query_grads = []
    for g in range(kv):
        grads = gh_ref[g]
        fold_weights = weights_ref[g, 0:tokens, :]
        mid_weights = weights_ref[g, tokens : 2 * tokens, :]
        fold = jnp.where(here, dot(own_ref[kv + g], grads, 1, 1), dot(two_ref[kv + g], grads, 1, 1))
        mid = dot(one_ref[kv + g], grads, 1, 1)
        delta = jnp.sum(fold * fold_weights, axis=0, keepdims=True) + jnp.sum(
            mid * mid_weights, axis=0, keepdims=True
        )
        fold = fold_weights * (fold - delta)
        mid = mid_weights * (mid - delta)
        score_grad = jnp.concatenate(
            [jnp.where(here, 0.0, fold).astype(LOW), mid.astype(LOW), jnp.where(here, fold, 0.0).astype(LOW)],
            axis=0,
        )
        low = jnp.concatenate(
            [
                jnp.where(here, 0.0, fold_weights).astype(LOW),
                mid_weights.astype(LOW),
                jnp.where(here, fold_weights, 0.0).astype(LOW),
            ],
            axis=0,
        )
        keys = jnp.concatenate([two_ref[g], one_ref[g], own_ref[g]], axis=0)
        key_grad = dot(score_grad, queries[g], 1, 0) * scaling
        value_grad = dot(low, grads, 1, 0)
        for place, grad in ((g, key_grad), (kv + g, value_grad)):
            back_two_ref[place] = grad[0:tokens].astype(LOW)
            back_one_ref[place] = grad[tokens : 2 * tokens].astype(LOW)
            back_own_ref[place] = grad[2 * tokens :]
        query_grad = dot(keys, score_grad, 0, 0) * scaling
        query_grads.append(query_grad.T.reshape(tokens, group, dim))
        if g % 2 == 1:
            both = jnp.concatenate(query_grads[-2:], axis=1).astype(LOW)
            dq_ref[:, (g - 1) * group : (g + 1) * group, :] = both


def on_device(
    query_rows, key_rows, value_matrix, cotangent, rotation, projection, shift_bias, doc_starts, tenant_ids,
):
    queries = query_rows[0]
    upstream = cotangent[0]
    tokens, heads, dim = queries.shape
    kv = key_rows.shape[2]
    group = heads // kv
    scaling = dim ** (-0.5)
    tenants, rank = rotation.shape[0], rotation.shape[1]
    lanes = tokens * group
    ctx = lax.axis_size("ctx")
    rep = lax.axis_size("rep")
    assert 2 * tokens == DOC_MAX

    own = jnp.moveaxis(jnp.concatenate([key_rows[0], value_matrix[0]], axis=1), 1, 0)
    one = shifted(own, "ctx", 1)
    two = shifted(own, "ctx", 2)

    rot = rotation.reshape(tenants * rank, heads, dim)
    proj = projection.reshape(tenants * rank, heads, dim)
    sizes = dict(kv=kv, group=group)
    vmem = pl.BlockSpec(memory_space=pltpu.VMEM)
    hbm = pl.BlockSpec(memory_space=pltpu.HBM)

    def call(body, outs, flops, moved, specs=None, scratch=(), limit=24, **fixed):
        def run(*operands):
            return pl.pallas_call(
                lambda *refs: body(*refs, **fixed),
                out_shape=[jax.ShapeDtypeStruct(*out) for out in outs],
                in_specs=specs or [vmem] * len(operands),
                out_specs=[vmem] * len(outs),
                scratch_shapes=scratch,
                compiler_params=pltpu.CompilerParams(vmem_limit_bytes=limit * 2**20),
                name=body.__name__,
                cost_estimate=pl.CostEstimate(flops=flops, bytes_accessed=moved, transcendentals=0),
            )(*operands)

        return run

    span = tenants * rank
    here = heads // ctx
    rows = here * 2 * span // rep
    grad_hidden, diff, pulled, meta = call(
        pull_kernel,
        [
            ((kv, lanes, dim), LOW), ((kv, span * group, dim), LOW),
            ((8, lanes), WIDE), ((8, lanes), jnp.int32),
        ],
        2 * 2**30, 4 * 2**20, [hbm] * 5,
        [
            pltpu.VMEM(doc_starts.shape, jnp.int32), pltpu.VMEM(tenant_ids.shape, jnp.int32),
            pltpu.VMEM((tokens, heads, dim), LOW), pltpu.VMEM((span, heads, dim), LOW),
            pltpu.VMEM((span, heads, dim), LOW), pltpu.SemaphoreType.DMA((5,)),
        ],
        limit=53, tenants=tenants, rank=rank, **sizes,
    )(doc_starts, tenant_ids, upstream, rot, proj)
    weights, send, keep = call(
        forward_kernel,
        [((kv, 2 * tokens, lanes), WIDE)] + [((ctx // 2, rep, rows, dim), LOW)] * 2,
        4 * 2**30, 10 * 2**20, [vmem] * 5 + [hbm] + [vmem] * 3,
        [pltpu.VMEM((tokens, heads, dim), LOW), pltpu.SemaphoreType.DMA],
        tenants=tenants, rank=rank, scaling=scaling, owned=here, **sizes,
    )(shift_bias.T, queries, two, one, own, upstream, diff, meta, pulled)
    part = (keep.astype(WIDE) + exchanged(send, "ctx", 1).astype(WIDE)).astype(LOW)
    weights, part = lax.optimization_barrier((weights, part))
    d_queries, back_two, back_one, back_own = call(
        backward_kernel,
        [((tokens, heads, dim), LOW), (own.shape, LOW), (own.shape, LOW), (own.shape, WIDE)],
        4 * 2**30, 10 * 2**20, scaling=scaling, **sizes,
    )(queries, grad_hidden, two, one, own, weights)
    from_one = shifted(back_one, "ctx", -1)
    from_two = shifted(back_two, "ctx", -2)

    bit = 2
    while bit < ctx:
        part = halved(part, "ctx", bit, back_own if bit == 2 else None).astype(LOW)
        bit *= 2
    part = part[0]
    from_one, from_two, _ = lax.optimization_barrier((from_one, from_two, part))
    bit = 1
    while bit < rep:
        part = part.astype(LOW)
        part = halved(part, "rep", bit)
        bit *= 2
    grads = jnp.moveaxis(part.astype(WIDE).reshape(here, 2, tenants // rep, rank, dim), 0, 3)
    back = (back_own + from_one.astype(WIDE) + from_two.astype(WIDE)).astype(LOW)
    d_keys = jnp.moveaxis(back[:kv], 0, 1)
    d_values = jnp.moveaxis(back[kv:], 0, 1)
    return (d_queries[None], d_keys[None], d_values[None], grads[0], grads[1])


def solution(mesh):
    rows = P("rep", "ctx", None, None)
    in_specs = (rows, rows, rows, rows, P(), P(), P(), P("rep", None), P("rep", None))
    tenant_rows = P("rep", None, "ctx", None)
    out_specs = (rows, rows, rows, tenant_rows, tenant_rows)
    return jax.shard_map(
        on_device, mesh=mesh, in_specs=in_specs, out_specs=out_specs, check_vma=False
    )
```

```python
import itertools

import jax
import jax.numpy as jnp
import numpy as np
from jax import lax
from jax.experimental import pallas as pl
from jax.experimental.pallas import tpu as pltpu
from jax.sharding import PartitionSpec as P

DOC_MAX = 256
LOW = jnp.bfloat16
WIDE = jnp.float32
far_below = -1e30


def shifted(value, axis, steps):
    count = lax.axis_size(axis)
    return lax.ppermute(value, axis, [(source, (source + steps) % count) for source in range(count)])


def exchanged(value, bits):
    axes = tuple(bits)
    shape = [lax.axis_size(axis) for axis in axes]
    pairs = []
    for source in np.ndindex(*shape):
        target = [at ^ bits[axis] for at, axis in zip(source, axes)]
        pairs.append((np.ravel_multi_index(source, shape), np.ravel_multi_index(target, shape)))
    return lax.ppermute(value, axes, [(int(source), int(target)) for source, target in pairs])


def reduce_groups():
    ctx, rep = lax.axis_size("ctx"), lax.axis_size("rep")
    over_ctx = [{"ctx": 1 << at} for at in range(ctx.bit_length() - 2, 0, -1)]
    over_rep = [{"rep": 1 << at} for at in range(rep.bit_length() - 1)]
    return [
        [pair for pair in pairs if pair] for pairs in itertools.zip_longest(over_ctx, over_rep)
    ]


def reduce_place(index):
    place = 0
    for bits in itertools.chain(*reduce_groups()):
        for axis, bit in bits.items():
            place = 2 * place + (index[axis] // bit) % 2
    return place


def scattered(part, group, beside=None):
    count = 1 << len(group)
    size = part.shape[0] // count
    others = []
    for j in range(1, count):
        bits = {}
        for at, pair in enumerate(reversed(group)):
            if (j >> at) & 1:
                bits.update(pair)
        others.append(exchanged(part[j * size : (j + 1) * size], bits))
    if beside is not None:
        others = lax.optimization_barrier((others, beside))[0]
    return part[:size].astype(WIDE) + sum(other.astype(WIDE) for other in others)


def dot(left, right, left_dim, right_dim, precision=None):
    return lax.dot_general(
        left, right, (((left_dim,), (right_dim,)), ((), ())),
        precision=precision, preferred_element_type=WIDE,
    )


def group_rows(ref, kv_count, group_size):
    rows, _, dim = ref.shape
    wide = 2 * group_size
    parts = []
    for pair in range(kv_count // 2):
        both = ref[:, pair * wide : (pair + 1) * wide, :].astype(WIDE)
        for half in range(2):
            one = both[:, half * group_size : (half + 1) * group_size, :]
            parts.append(one.reshape(rows * group_size, dim).astype(LOW))
    return parts


def lane_head(shape, group_size):
    return lax.broadcasted_iota(jnp.int32, shape, 1) % group_size


def own_terms(maps_by_rows, owner, tenants, low_rank, group_size):
    lanes = maps_by_rows.shape[1]
    same_head = lax.broadcasted_iota(jnp.int32, (group_size, lanes), 0) == lane_head(
        (group_size, lanes), group_size
    )
    span = low_rank * group_size
    total = jnp.zeros((low_rank, group_size, lanes), WIDE)
    for tenant in range(tenants):
        keep = same_head & (owner == tenant)
        block = maps_by_rows[tenant * span : (tenant + 1) * span].reshape(
            low_rank, group_size, lanes
        )
        total = total + jnp.where(keep[None], block, 0.0)
    rows = jnp.sum(total, axis=1)
    rows = jnp.concatenate([rows, rows], axis=0)
    tiles = lanes // 128
    stacked = jnp.concatenate([rows[:, c * 128 : (c + 1) * 128] for c in range(tiles)], axis=0)
    side = lax.broadcasted_iota(jnp.int32, (128, 128), 0) // group_size
    over = lax.broadcasted_iota(jnp.int32, (128, 128), 1) // group_size
    spread = dot(stacked, (side == over).astype(WIDE), 1, 0, lax.Precision.HIGHEST)
    return jnp.concatenate([spread[c * 8 : (c + 1) * 8] for c in range(tiles)], axis=1)


def pull_kernel(
    starts_hbm, owners_hbm, cot_hbm, rot_hbm, proj_hbm, gh_ref, diff_ref, pulled_ref, meta_ref,
    starts_ref, owners_ref, cot_ref, rot_ref, proj_ref, sems, *, kv, group, tenants, rank,
):
    pairs = (
        (starts_hbm, starts_ref), (owners_hbm, owners_ref), (cot_hbm, cot_ref),
        (rot_hbm, rot_ref), (proj_hbm, proj_ref),
    )
    copies = [
        pltpu.make_async_copy(source, target, sems.at[at])
        for at, (source, target) in enumerate(pairs)
    ]
    for copy in copies:
        copy.start()
    copies[0].wait()
    copies[1].wait()
    lanes = meta_ref.shape[1]
    tokens = lanes // group
    row_first = lax.axis_index("ctx") * tokens
    mine = pl.ds(pl.multiple_of(row_first, tokens), tokens)
    row = lax.broadcasted_iota(jnp.int32, (8, tokens), 0)
    both = jnp.where(row == 0, starts_ref[:, mine] - row_first, owners_ref[:, mine]).astype(WIDE)
    repeat = lax.broadcasted_iota(jnp.int32, (tokens, lanes), 0) == (
        lax.broadcasted_iota(jnp.int32, (tokens, lanes), 1) // group
    )
    meta = dot(both, repeat.astype(WIDE), 1, 0, lax.Precision.HIGHEST).astype(jnp.int32)
    meta_ref[...] = meta
    owner = meta[1:2, :]
    copies[2].wait()
    cots = group_rows(cot_ref, kv, group)
    copies[3].wait()
    rots = group_rows(rot_ref, kv, group)
    on_rot = dot(jnp.concatenate(rots, axis=1), jnp.concatenate(cots, axis=1), 1, 1)
    pulled = own_terms(on_rot, owner, tenants, rank, group).astype(LOW).astype(WIDE)
    pulled_ref[...] = pulled
    same_head = lax.broadcasted_iota(jnp.int32, (group, lanes), 0) == lane_head((group, lanes), group)
    picked = []
    for tenant in range(tenants):
        keep = same_head & (owner == tenant)
        for k in range(rank):
            picked.append(jnp.where(keep, pulled[k : k + 1], 0.0))
    picked = jnp.concatenate(picked, axis=0).T.astype(LOW)
    copies[4].wait()
    projs = group_rows(proj_ref, kv, group)
    for g in range(kv):
        diff = (projs[g].astype(WIDE) - rots[g].astype(WIDE)).astype(LOW)
        diff_ref[g] = diff
        gh_ref[g] = (cots[g].astype(WIDE) + dot(picked, diff, 1, 0)).astype(LOW)


def places(lanes, tokens, group):
    key = lax.broadcasted_iota(jnp.int32, (tokens, lanes), 0)
    query = lax.broadcasted_iota(jnp.int32, (tokens, lanes), 1) // group
    return key, key <= query


def forward_kernel(
    bias_ref, q_ref, two_ref, one_ref, own_ref, cot_hbm, diff_ref, meta_ref, pulled_ref,
    weights_ref, send_ref, keep_ref, cot_ref, sem, *, kv, group, tenants, rank, scaling, owned,
):
    fetch = pltpu.make_async_copy(cot_hbm, cot_ref, sem)
    fetch.start()
    tokens = own_ref.shape[1]
    first = meta_ref[0:1, :]
    owner = meta_ref[1:2, :]
    lanes = owner.shape[1]
    key, here = places(lanes, tokens, group)
    fold_bias = jnp.where(jnp.where(here, key, key - 2 * tokens) >= first, 0.0, far_below)
    mid_bias = jnp.where(key - tokens >= first, 0.0, far_below)
    queries = group_rows(q_ref, kv, group)
    hidden = []
    for g in range(kv):
        fold = jnp.where(here, dot(own_ref[g], queries[g], 1, 1), dot(two_ref[g], queries[g], 1, 1))
        fold = fold * scaling + fold_bias
        mid = dot(one_ref[g], queries[g], 1, 1) * scaling + mid_bias
        top = jnp.maximum(jnp.max(fold, axis=0, keepdims=True), jnp.max(mid, axis=0, keepdims=True))
        fold = jnp.exp(fold - top)
        mid = jnp.exp(mid - top)
        total = jnp.sum(fold, axis=0, keepdims=True) + jnp.sum(mid, axis=0, keepdims=True)
        share = 1.0 / total
        fold = fold * share
        mid = mid * share
        weights_ref[g, 0:tokens, :] = fold
        weights_ref[g, tokens : 2 * tokens, :] = mid
        low = jnp.concatenate(
            [jnp.where(here, 0.0, fold).astype(LOW), mid.astype(LOW), jnp.where(here, fold, 0.0).astype(LOW)],
            axis=0,
        )
        values = jnp.concatenate([two_ref[kv + g], one_ref[kv + g], own_ref[kv + g]], axis=0)
        hidden.append(dot(values, low, 0, 0).astype(LOW))
    hidden = jnp.concatenate(hidden, axis=0)
    on_diff = dot(jnp.concatenate([diff_ref[g] for g in range(kv)], axis=1), hidden, 1, 0)
    lifted = own_terms(on_diff, owner, tenants, rank, group)
    one_hot = (owner == lax.broadcasted_iota(jnp.int32, (tenants, lanes), 0)).astype(WIDE)
    bias = jnp.concatenate([bias_ref[...]] * (8 // rank), axis=0)
    shift = dot(bias, one_hot, 1, 0, lax.Precision.HIGHEST)
    lifted = (lifted + shift).astype(LOW).astype(WIDE)
    pulled = pulled_ref[...]
    ctx, rep = lax.axis_size("ctx"), lax.axis_size("rep")
    me, layer = lax.axis_index("ctx"), lax.axis_index("rep")
    per_group = group // owned
    span = tenants * rank
    tenant_row = lax.broadcasted_iota(jnp.int32, (span, lanes), 0) // rank
    mine = owner == (tenant_row ^ (layer * (tenants // rep)))
    lift_rows = jnp.where(mine, jnp.concatenate([lifted] * (span // 8), axis=0), 0.0)
    pull_rows = jnp.where(mine, jnp.concatenate([pulled] * (span // 8), axis=0), 0.0)
    slot = lane_head((span, lanes), group) ^ ((me % per_group) * owned)
    lift_all = jnp.concatenate([jnp.where(slot == h, lift_rows, 0.0).astype(LOW) for h in range(group)], axis=0)
    pull_all = jnp.concatenate([jnp.where(slot == h, pull_rows, 0.0).astype(LOW) for h in range(group)], axis=0)
    on_proj = dot(pull_all, hidden, 1, 1)
    fetch.wait()
    on_rot = dot(lift_all, jnp.concatenate(group_rows(cot_ref, kv, group), axis=1), 1, 0) - on_proj
    dim = q_ref.shape[2]
    here_rows = span // rep
    for g in range(kv):
        columns = slice(g * dim, (g + 1) * dim)
        for low in range(per_group):
            device = (g ^ (me // per_group)) * per_group + low
            into = send_ref if low % 2 else keep_ref
            for r in range(rep):
                pieces = []
                for h in range(low * owned, (low + 1) * owned):
                    rows = slice(h * span + r * here_rows, h * span + (r + 1) * here_rows)
                    pieces += [on_rot[rows, columns], on_proj[rows, columns]]
                into[reduce_place(dict(ctx=device, rep=r))] = jnp.concatenate(pieces, axis=0).astype(LOW)


def backward_kernel(
    q_ref, gh_ref, two_ref, one_ref, own_ref, weights_ref, dq_ref, back_two_ref, back_one_ref, back_own_ref,
    *, kv, group, scaling,
):
    tokens = own_ref.shape[1]
    lanes = weights_ref.shape[2]
    dim = q_ref.shape[2]
    _, here = places(lanes, tokens, group)
    queries = group_rows(q_ref, kv, group)
    query_grads = []
    for g in range(kv):
        grads = gh_ref[g]
        fold_weights = weights_ref[g, 0:tokens, :]
        mid_weights = weights_ref[g, tokens : 2 * tokens, :]
        fold = jnp.where(here, dot(own_ref[kv + g], grads, 1, 1), dot(two_ref[kv + g], grads, 1, 1))
        mid = dot(one_ref[kv + g], grads, 1, 1)
        delta = jnp.sum(fold * fold_weights, axis=0, keepdims=True) + jnp.sum(
            mid * mid_weights, axis=0, keepdims=True
        )
        fold = fold_weights * (fold - delta)
        mid = mid_weights * (mid - delta)
        score_grad = jnp.concatenate(
            [jnp.where(here, 0.0, fold).astype(LOW), mid.astype(LOW), jnp.where(here, fold, 0.0).astype(LOW)],
            axis=0,
        )
        low = jnp.concatenate(
            [
                jnp.where(here, 0.0, fold_weights).astype(LOW),
                mid_weights.astype(LOW),
                jnp.where(here, fold_weights, 0.0).astype(LOW),
            ],
            axis=0,
        )
        keys = jnp.concatenate([two_ref[g], one_ref[g], own_ref[g]], axis=0)
        key_grad = dot(score_grad, queries[g], 1, 0) * scaling
        value_grad = dot(low, grads, 1, 0)
        for place, grad in ((g, key_grad), (kv + g, value_grad)):
            back_two_ref[place] = grad[0:tokens].astype(LOW)
            back_one_ref[place] = grad[tokens : 2 * tokens].astype(LOW)
            back_own_ref[place] = grad[2 * tokens :]
        query_grad = dot(keys, score_grad, 0, 0) * scaling
        query_grads.append(query_grad.T.reshape(tokens, group, dim))
        if g % 2 == 1:
            both = jnp.concatenate(query_grads[-2:], axis=1).astype(LOW)
            dq_ref[:, (g - 1) * group : (g + 1) * group, :] = both


def on_device(
    query_rows, key_rows, value_matrix, cotangent, rotation, projection, shift_bias, doc_starts, tenant_ids,
):
    queries = query_rows[0]
    upstream = cotangent[0]
    tokens, heads, dim = queries.shape
    kv = key_rows.shape[2]
    group = heads // kv
    scaling = dim ** (-0.5)
    tenants, rank = rotation.shape[0], rotation.shape[1]
    lanes = tokens * group
    ctx = lax.axis_size("ctx")
    rep = lax.axis_size("rep")
    assert 2 * tokens == DOC_MAX

    own = jnp.moveaxis(jnp.concatenate([key_rows[0], value_matrix[0]], axis=1), 1, 0)
    even = lax.axis_index("ctx") % 2 == 0
    two = shifted(own, "ctx", 2)

    rot = rotation.reshape(tenants * rank, heads, dim)
    proj = projection.reshape(tenants * rank, heads, dim)
    sizes = dict(kv=kv, group=group)
    vmem = pl.BlockSpec(memory_space=pltpu.VMEM)
    hbm = pl.BlockSpec(memory_space=pltpu.HBM)

    def call(body, outs, flops, moved, specs=None, scratch=(), limit=24, **fixed):
        def run(*operands):
            return pl.pallas_call(
                lambda *refs: body(*refs, **fixed),
                out_shape=[jax.ShapeDtypeStruct(*out) for out in outs],
                in_specs=specs or [vmem] * len(operands),
                out_specs=[vmem] * len(outs),
                scratch_shapes=scratch,
                compiler_params=pltpu.CompilerParams(vmem_limit_bytes=limit * 2**20),
                name=body.__name__,
                cost_estimate=pl.CostEstimate(flops=flops, bytes_accessed=moved, transcendentals=0),
            )(*operands)

        return run

    span = tenants * rank
    here = heads // ctx
    rows = here * 2 * span // rep
    grad_hidden, diff, pulled, meta = call(
        pull_kernel,
        [
            ((kv, lanes, dim), LOW), ((kv, span * group, dim), LOW),
            ((8, lanes), WIDE), ((8, lanes), jnp.int32),
        ],
        2 * 2**30, 4 * 2**20, [hbm] * 5,
        [
            pltpu.VMEM(doc_starts.shape, jnp.int32), pltpu.VMEM(tenant_ids.shape, jnp.int32),
            pltpu.VMEM((tokens, heads, dim), LOW), pltpu.VMEM((span, heads, dim), LOW),
            pltpu.VMEM((span, heads, dim), LOW), pltpu.SemaphoreType.DMA((5,)),
        ],
        limit=53, tenants=tenants, rank=rank, **sizes,
    )(doc_starts, tenant_ids, upstream, rot, proj)
    two, meta = lax.optimization_barrier((two, meta))
    one = exchanged(jnp.where(even, own, two), {"ctx": 1})
    weights, send, keep = call(
        forward_kernel,
        [((kv, 2 * tokens, lanes), WIDE)] + [((ctx * rep // 2, rows, dim), LOW)] * 2,
        4 * 2**30, 10 * 2**20, [vmem] * 5 + [hbm] + [vmem] * 3,
        [pltpu.VMEM((tokens, heads, dim), LOW), pltpu.SemaphoreType.DMA],
        tenants=tenants, rank=rank, scaling=scaling, owned=here, **sizes,
    )(shift_bias.T, queries, two, one, own, upstream, diff, meta, pulled)
    part = (keep.astype(WIDE) + exchanged(send, {"ctx": 1}).astype(WIDE)).astype(LOW)
    weights, part = lax.optimization_barrier((weights, part))
    d_queries, back_two, back_one, back_own = call(
        backward_kernel,
        [((tokens, heads, dim), LOW), (own.shape, LOW), (own.shape, LOW), (own.shape, WIDE)],
        4 * 2**30, 10 * 2**20, scaling=scaling, **sizes,
    )(queries, grad_hidden, two, one, own, weights)
    from_mate = exchanged(back_one, {"ctx": 1}).astype(WIDE)
    onward = back_two.astype(WIDE) + jnp.where(even, 0.0, from_mate)
    from_two = shifted(onward.astype(LOW), "ctx", -2)

    for at, group_bits in enumerate(reduce_groups()):
        part = scattered(part.astype(LOW), group_bits, back_own if at == 0 else None)
    grads = jnp.moveaxis(part.reshape(here, 2, tenants // rep, rank, dim), 0, 3)
    back = back_own + from_two.astype(WIDE) + jnp.where(even, from_mate, 0.0)
    back = back.astype(LOW)
    d_keys = jnp.moveaxis(back[:kv], 0, 1)
    d_values = jnp.moveaxis(back[kv:], 0, 1)
    return (d_queries[None], d_keys[None], d_values[None], grads[0], grads[1])


def solution(mesh):
    rows = P("rep", "ctx", None, None)
    in_specs = (rows, rows, rows, rows, P(), P(), P(), P("rep", None), P("rep", None))
    tenant_rows = P("rep", None, "ctx", None)
    out_specs = (rows, rows, rows, tenant_rows, tenant_rows)
    return jax.shard_map(
        on_device, mesh=mesh, in_specs=in_specs, out_specs=out_specs, check_vma=False
    )
```

```python
import itertools

import jax
import jax.numpy as jnp
import numpy as np
from jax import lax
from jax.experimental import pallas as pl
from jax.experimental.pallas import tpu as pltpu
from jax.sharding import PartitionSpec as P

DOC_MAX = 256
LOW = jnp.bfloat16
WIDE = jnp.float32
far_below = -1e30


def shifted(value, axis, steps):
    count = lax.axis_size(axis)
    return lax.ppermute(value, axis, [(source, (source + steps) % count) for source in range(count)])


def exchanged(value, bits):
    axes = tuple(bits)
    shape = [lax.axis_size(axis) for axis in axes]
    pairs = []
    for source in np.ndindex(*shape):
        target = [at ^ bits[axis] for at, axis in zip(source, axes)]
        pairs.append((np.ravel_multi_index(source, shape), np.ravel_multi_index(target, shape)))
    return lax.ppermute(value, axes, [(int(source), int(target)) for source, target in pairs])


def reduce_groups():
    ctx, rep = lax.axis_size("ctx"), lax.axis_size("rep")
    over_ctx = [{"ctx": 1 << at} for at in range(ctx.bit_length() - 2, 0, -1)]
    over_rep = [{"rep": 1 << at} for at in range(rep.bit_length() - 1)]
    return [
        [pair for pair in pairs if pair] for pairs in itertools.zip_longest(over_ctx, over_rep)
    ]


def reduce_place(index):
    place = 0
    for bits in itertools.chain(*reduce_groups()):
        for axis, bit in bits.items():
            place = 2 * place + (index[axis] // bit) % 2
    return place


def scattered(part, group, beside=None):
    count = 1 << len(group)
    size = part.shape[0] // count
    others = []
    for j in range(1, count):
        bits = {}
        for at, pair in enumerate(reversed(group)):
            if (j >> at) & 1:
                bits.update(pair)
        others.append(exchanged(part[j * size : (j + 1) * size], bits))
    if beside is not None:
        others = lax.optimization_barrier((others, beside))[0]
    return part[:size], others


def dot(left, right, left_dim, right_dim, precision=None):
    return lax.dot_general(
        left, right, (((left_dim,), (right_dim,)), ((), ())),
        precision=precision, preferred_element_type=WIDE,
    )


def group_rows(ref, kv_count, group_size):
    rows, _, dim = ref.shape
    wide = 2 * group_size
    parts = []
    for pair in range(kv_count // 2):
        both = ref[:, pair * wide : (pair + 1) * wide, :].astype(WIDE)
        for half in range(2):
            one = both[:, half * group_size : (half + 1) * group_size, :]
            parts.append(one.reshape(rows * group_size, dim).astype(LOW))
    return parts


def lane_head(shape, group_size):
    return lax.broadcasted_iota(jnp.int32, shape, 1) % group_size


def own_terms(maps_by_rows, owner, tenants, low_rank, group_size):
    lanes = maps_by_rows.shape[1]
    same_head = lax.broadcasted_iota(jnp.int32, (group_size, lanes), 0) == lane_head(
        (group_size, lanes), group_size
    )
    span = low_rank * group_size
    total = jnp.zeros((low_rank, group_size, lanes), WIDE)
    for tenant in range(tenants):
        keep = same_head & (owner == tenant)
        block = maps_by_rows[tenant * span : (tenant + 1) * span].reshape(
            low_rank, group_size, lanes
        )
        total = total + jnp.where(keep[None], block, 0.0)
    rows = jnp.sum(total, axis=1)
    rows = jnp.concatenate([rows, rows], axis=0)
    tiles = lanes // 128
    stacked = jnp.concatenate([rows[:, c * 128 : (c + 1) * 128] for c in range(tiles)], axis=0)
    side = lax.broadcasted_iota(jnp.int32, (128, 128), 0) // group_size
    over = lax.broadcasted_iota(jnp.int32, (128, 128), 1) // group_size
    spread = dot(stacked, (side == over).astype(WIDE), 1, 0, lax.Precision.HIGHEST)
    return jnp.concatenate([spread[c * 8 : (c + 1) * 8] for c in range(tiles)], axis=1)


def pull_kernel(
    starts_hbm, owners_hbm, cot_hbm, rot_hbm, proj_hbm, gh_ref, diff_ref, pulled_ref, meta_ref,
    starts_ref, owners_ref, cot_ref, rot_ref, proj_ref, sems, *, kv, group, tenants, rank,
):
    pairs = (
        (starts_hbm, starts_ref), (owners_hbm, owners_ref), (cot_hbm, cot_ref),
        (rot_hbm, rot_ref), (proj_hbm, proj_ref),
    )
    copies = [
        pltpu.make_async_copy(source, target, sems.at[at])
        for at, (source, target) in enumerate(pairs)
    ]
    for copy in copies:
        copy.start()
    copies[0].wait()
    copies[1].wait()
    lanes = meta_ref.shape[1]
    tokens = lanes // group
    row_first = lax.axis_index("ctx") * tokens
    mine = pl.ds(pl.multiple_of(row_first, tokens), tokens)
    row = lax.broadcasted_iota(jnp.int32, (8, tokens), 0)
    both = jnp.where(row == 0, starts_ref[:, mine] - row_first, owners_ref[:, mine]).astype(WIDE)
    repeat = lax.broadcasted_iota(jnp.int32, (tokens, lanes), 0) == (
        lax.broadcasted_iota(jnp.int32, (tokens, lanes), 1) // group
    )
    meta = dot(both, repeat.astype(WIDE), 1, 0, lax.Precision.HIGHEST).astype(jnp.int32)
    meta_ref[...] = meta
    owner = meta[1:2, :]
    copies[2].wait()
    cots = group_rows(cot_ref, kv, group)
    copies[3].wait()
    rots = group_rows(rot_ref, kv, group)
    on_rot = dot(jnp.concatenate(rots, axis=1), jnp.concatenate(cots, axis=1), 1, 1)
    pulled = own_terms(on_rot, owner, tenants, rank, group).astype(LOW).astype(WIDE)
    pulled_ref[...] = pulled
    same_head = lax.broadcasted_iota(jnp.int32, (group, lanes), 0) == lane_head((group, lanes), group)
    picked = []
    for tenant in range(tenants):
        keep = same_head & (owner == tenant)
        for k in range(rank):
            picked.append(jnp.where(keep, pulled[k : k + 1], 0.0))
    picked = jnp.concatenate(picked, axis=0).T.astype(LOW)
    copies[4].wait()
    projs = group_rows(proj_ref, kv, group)
    for g in range(kv):
        diff = (projs[g].astype(WIDE) - rots[g].astype(WIDE)).astype(LOW)
        diff_ref[g] = diff
        gh_ref[g] = (cots[g].astype(WIDE) + dot(picked, diff, 1, 0)).astype(LOW)


def places(lanes, tokens, group):
    key = lax.broadcasted_iota(jnp.int32, (tokens, lanes), 0)
    query = lax.broadcasted_iota(jnp.int32, (tokens, lanes), 1) // group
    return key, key <= query


def forward_kernel(
    bias_ref, q_ref, two_ref, one_ref, own_ref, cot_hbm, diff_ref, meta_ref, pulled_ref,
    weights_ref, send_ref, keep_ref, cot_ref, sem, *, kv, group, tenants, rank, scaling, owned,
):
    fetch = pltpu.make_async_copy(cot_hbm, cot_ref, sem)
    fetch.start()
    tokens = own_ref.shape[1]
    first = meta_ref[0:1, :]
    owner = meta_ref[1:2, :]
    lanes = owner.shape[1]
    key, here = places(lanes, tokens, group)
    fold_bias = jnp.where(jnp.where(here, key, key - 2 * tokens) >= first, 0.0, far_below)
    mid_bias = jnp.where(key - tokens >= first, 0.0, far_below)
    queries = group_rows(q_ref, kv, group)
    hidden = []
    for g in range(kv):
        fold = jnp.where(here, dot(own_ref[g], queries[g], 1, 1), dot(two_ref[g], queries[g], 1, 1))
        fold = fold * scaling + fold_bias
        mid = dot(one_ref[g], queries[g], 1, 1) * scaling + mid_bias
        top = jnp.maximum(jnp.max(fold, axis=0, keepdims=True), jnp.max(mid, axis=0, keepdims=True))
        fold = jnp.exp(fold - top)
        mid = jnp.exp(mid - top)
        total = jnp.sum(fold, axis=0, keepdims=True) + jnp.sum(mid, axis=0, keepdims=True)
        share = 1.0 / total
        fold = fold * share
        mid = mid * share
        weights_ref[g, 0:tokens, :] = fold
        weights_ref[g, tokens : 2 * tokens, :] = mid
        low = jnp.concatenate(
            [jnp.where(here, 0.0, fold).astype(LOW), mid.astype(LOW), jnp.where(here, fold, 0.0).astype(LOW)],
            axis=0,
        )
        values = jnp.concatenate([two_ref[kv + g], one_ref[kv + g], own_ref[kv + g]], axis=0)
        hidden.append(dot(values, low, 0, 0).astype(LOW))
    hidden = jnp.concatenate(hidden, axis=0)
    on_diff = dot(jnp.concatenate([diff_ref[g] for g in range(kv)], axis=1), hidden, 1, 0)
    lifted = own_terms(on_diff, owner, tenants, rank, group)
    one_hot = (owner == lax.broadcasted_iota(jnp.int32, (tenants, lanes), 0)).astype(WIDE)
    bias = jnp.concatenate([bias_ref[...]] * (8 // rank), axis=0)
    shift = dot(bias, one_hot, 1, 0, lax.Precision.HIGHEST)
    lifted = (lifted + shift).astype(LOW).astype(WIDE)
    pulled = pulled_ref[...]
    ctx, rep = lax.axis_size("ctx"), lax.axis_size("rep")
    me, layer = lax.axis_index("ctx"), lax.axis_index("rep")
    per_group = group // owned
    span = tenants * rank
    tenant_row = lax.broadcasted_iota(jnp.int32, (span, lanes), 0) // rank
    mine = owner == (tenant_row ^ (layer * (tenants // rep)))
    lift_rows = jnp.where(mine, jnp.concatenate([lifted] * (span // 8), axis=0), 0.0)
    pull_rows = jnp.where(mine, jnp.concatenate([pulled] * (span // 8), axis=0), 0.0)
    slot = lane_head((span, lanes), group) ^ ((me % per_group) * owned)
    lift_all = jnp.concatenate([jnp.where(slot == h, lift_rows, 0.0).astype(LOW) for h in range(group)], axis=0)
    pull_all = jnp.concatenate([jnp.where(slot == h, pull_rows, 0.0).astype(LOW) for h in range(group)], axis=0)
    on_proj = dot(pull_all, hidden, 1, 1)
    fetch.wait()
    on_rot = dot(lift_all, jnp.concatenate(group_rows(cot_ref, kv, group), axis=1), 1, 0) - on_proj
    dim = q_ref.shape[2]
    here_rows = span // rep
    for g in range(kv):
        columns = slice(g * dim, (g + 1) * dim)
        for low in range(per_group):
            device = (g ^ (me // per_group)) * per_group + low
            into = send_ref if low % 2 else keep_ref
            for r in range(rep):
                pieces = []
                for h in range(low * owned, (low + 1) * owned):
                    rows = slice(h * span + r * here_rows, h * span + (r + 1) * here_rows)
                    pieces += [on_rot[rows, columns], on_proj[rows, columns]]
                into[reduce_place(dict(ctx=device, rep=r))] = jnp.concatenate(pieces, axis=0).astype(LOW)


def backward_kernel(
    q_ref, gh_ref, two_ref, one_ref, own_ref, weights_ref, dq_ref, back_two_ref, back_one_ref, back_own_ref,
    *, kv, group, scaling,
):
    tokens = own_ref.shape[1]
    lanes = weights_ref.shape[2]
    dim = q_ref.shape[2]
    _, here = places(lanes, tokens, group)
    queries = group_rows(q_ref, kv, group)
    query_grads = []
    for g in range(kv):
        grads = gh_ref[g]
        fold_weights = weights_ref[g, 0:tokens, :]
        mid_weights = weights_ref[g, tokens : 2 * tokens, :]
        fold = jnp.where(here, dot(own_ref[kv + g], grads, 1, 1), dot(two_ref[kv + g], grads, 1, 1))
        mid = dot(one_ref[kv + g], grads, 1, 1)
        delta = jnp.sum(fold * fold_weights, axis=0, keepdims=True) + jnp.sum(
            mid * mid_weights, axis=0, keepdims=True
        )
        fold = fold_weights * (fold - delta)
        mid = mid_weights * (mid - delta)
        score_grad = jnp.concatenate(
            [jnp.where(here, 0.0, fold).astype(LOW), mid.astype(LOW), jnp.where(here, fold, 0.0).astype(LOW)],
            axis=0,
        )
        low = jnp.concatenate(
            [
                jnp.where(here, 0.0, fold_weights).astype(LOW),
                mid_weights.astype(LOW),
                jnp.where(here, fold_weights, 0.0).astype(LOW),
            ],
            axis=0,
        )
        keys = jnp.concatenate([two_ref[g], one_ref[g], own_ref[g]], axis=0)
        key_grad = dot(score_grad, queries[g], 1, 0) * scaling
        value_grad = dot(low, grads, 1, 0)
        for place, grad in ((g, key_grad), (kv + g, value_grad)):
            back_two_ref[place] = grad[0:tokens].astype(LOW)
            back_one_ref[place] = grad[tokens : 2 * tokens].astype(LOW)
            back_own_ref[place] = grad[2 * tokens :]
        query_grad = dot(keys, score_grad, 0, 0) * scaling
        query_grads.append(query_grad.T.reshape(tokens, group, dim))
        if g % 2 == 1:
            both = jnp.concatenate(query_grads[-2:], axis=1).astype(LOW)
            dq_ref[:, (g - 1) * group : (g + 1) * group, :] = both


def grads_kernel(part_ref, *refs, owned):
    total = part_ref[0].astype(WIDE)
    for other_ref in refs[:-2]:
        total = total + other_ref[0].astype(WIDE)
    size = refs[-1].shape[0]
    for place in range(owned):
        for at in range(2):
            row = (2 * place + at) * size
            refs[at - 2][:, place, :] = total[row : row + size]


def halo_kernel(own_ref, mate_ref, two_ref, keys_ref, values_ref, wide_keys, wide_values, *, kv):
    even = (lax.axis_index("ctx") % 2 == 0).astype(WIDE)
    for at, (wide, out) in enumerate(((wide_keys, keys_ref), (wide_values, values_ref))):
        for m in range(kv):
            place = at * kv + m
            wide[:, m, :] = own_ref[place] + two_ref[place].astype(WIDE) + even * mate_ref[place].astype(WIDE)
        out[...] = wide[...].astype(LOW)


def on_device(
    query_rows, key_rows, value_matrix, cotangent, rotation, projection, shift_bias, doc_starts, tenant_ids,
):
    queries = query_rows[0]
    upstream = cotangent[0]
    tokens, heads, dim = queries.shape
    kv = key_rows.shape[2]
    group = heads // kv
    scaling = dim ** (-0.5)
    tenants, rank = rotation.shape[0], rotation.shape[1]
    lanes = tokens * group
    ctx = lax.axis_size("ctx")
    rep = lax.axis_size("rep")
    assert 2 * tokens == DOC_MAX

    own = jnp.moveaxis(jnp.concatenate([key_rows[0], value_matrix[0]], axis=1), 1, 0)
    even = lax.axis_index("ctx") % 2 == 0
    two = shifted(own, "ctx", 2)

    rot = rotation.reshape(tenants * rank, heads, dim)
    proj = projection.reshape(tenants * rank, heads, dim)
    sizes = dict(kv=kv, group=group)
    vmem = pl.BlockSpec(memory_space=pltpu.VMEM)
    hbm = pl.BlockSpec(memory_space=pltpu.HBM)

    def call(body, outs, flops, moved, specs=None, scratch=(), limit=24, **fixed):
        def run(*operands):
            return pl.pallas_call(
                lambda *refs: body(*refs, **fixed),
                out_shape=[jax.ShapeDtypeStruct(*out) for out in outs],
                in_specs=specs or [vmem] * len(operands),
                out_specs=[vmem] * len(outs),
                scratch_shapes=scratch,
                compiler_params=pltpu.CompilerParams(vmem_limit_bytes=limit * 2**20),
                name=body.__name__,
                cost_estimate=pl.CostEstimate(flops=flops, bytes_accessed=moved, transcendentals=0),
            )(*operands)

        return run

    span = tenants * rank
    here = heads // ctx
    rows = here * 2 * span // rep
    grad_hidden, diff, pulled, meta = call(
        pull_kernel,
        [
            ((kv, lanes, dim), LOW), ((kv, span * group, dim), LOW),
            ((8, lanes), WIDE), ((8, lanes), jnp.int32),
        ],
        2 * 2**30, 4 * 2**20, [hbm] * 5,
        [
            pltpu.VMEM(doc_starts.shape, jnp.int32), pltpu.VMEM(tenant_ids.shape, jnp.int32),
            pltpu.VMEM((tokens, heads, dim), LOW), pltpu.VMEM((span, heads, dim), LOW),
            pltpu.VMEM((span, heads, dim), LOW), pltpu.SemaphoreType.DMA((5,)),
        ],
        limit=53, tenants=tenants, rank=rank, **sizes,
    )(doc_starts, tenant_ids, upstream, rot, proj)
    two, meta = lax.optimization_barrier((two, meta))
    one = exchanged(jnp.where(even, own, two), {"ctx": 1})
    weights, send, keep = call(
        forward_kernel,
        [((kv, 2 * tokens, lanes), WIDE)] + [((ctx * rep // 2, rows, dim), LOW)] * 2,
        4 * 2**30, 10 * 2**20, [vmem] * 5 + [hbm] + [vmem] * 3,
        [pltpu.VMEM((tokens, heads, dim), LOW), pltpu.SemaphoreType.DMA],
        tenants=tenants, rank=rank, scaling=scaling, owned=here, **sizes,
    )(shift_bias.T, queries, two, one, own, upstream, diff, meta, pulled)
    part = (keep.astype(WIDE) + exchanged(send, {"ctx": 1}).astype(WIDE)).astype(LOW)
    weights, part = lax.optimization_barrier((weights, part))
    d_queries, back_two, back_one, back_own = call(
        backward_kernel,
        [((tokens, heads, dim), LOW), (own.shape, LOW), (own.shape, LOW), (own.shape, WIDE)],
        4 * 2**30, 10 * 2**20, scaling=scaling, **sizes,
    )(queries, grad_hidden, two, one, own, weights)
    from_mate = exchanged(back_one, {"ctx": 1})
    onward = back_two.astype(WIDE) + jnp.where(even, 0.0, from_mate.astype(WIDE))
    onward = onward.astype(LOW)

    groups = reduce_groups()
    for at, group_bits in enumerate(groups):
        beside = back_own if at == 0 else None
        if at == len(groups) - 1:
            part, onward = lax.optimization_barrier((part, onward))
            from_two = shifted(onward, "ctx", -2)
            beside = from_two
        part, others = scattered(part, group_bits, beside)
        if at < len(groups) - 1:
            part = part.astype(WIDE) + sum(other.astype(WIDE) for other in others)
            part = part.astype(LOW)
    grads = call(
        grads_kernel, [((span // rep, here, dim), WIDE)] * 2, 2**18, 2**18, owned=here,
    )(part, *others)
    grads = [grad.reshape(tenants // rep, rank, here, dim) for grad in grads]
    d_keys, d_values = call(
        halo_kernel, [((tokens, kv, dim), LOW)] * 2, 2**20, 2**20,
        scratch=[pltpu.VMEM((tokens, kv, dim), WIDE)] * 2, kv=kv,
    )(back_own, from_mate, from_two)
    return (d_queries[None], d_keys[None], d_values[None], grads[0], grads[1])


def solution(mesh):
    rows = P("rep", "ctx", None, None)
    in_specs = (rows, rows, rows, rows, P(), P(), P(), P("rep", None), P("rep", None))
    tenant_rows = P("rep", None, "ctx", None)
    out_specs = (rows, rows, rows, tenant_rows, tenant_rows)
    return jax.shard_map(
        on_device, mesh=mesh, in_specs=in_specs, out_specs=out_specs, check_vma=False
    )
```

```python
import itertools

import jax
import jax.numpy as jnp
import numpy as np
from jax import lax
from jax.experimental import pallas as pl
from jax.experimental.pallas import tpu as pltpu
from jax.sharding import PartitionSpec as P

DOC_MAX = 256
LOW = jnp.bfloat16
WIDE = jnp.float32
far_below = -1e30


def shifted(value, axis, steps):
    count = lax.axis_size(axis)
    return lax.ppermute(value, axis, [(source, (source + steps) % count) for source in range(count)])


def exchanged(value, bits):
    axes = tuple(bits)
    shape = [lax.axis_size(axis) for axis in axes]
    pairs = []
    for source in np.ndindex(*shape):
        target = [at ^ bits[axis] for at, axis in zip(source, axes)]
        pairs.append((np.ravel_multi_index(source, shape), np.ravel_multi_index(target, shape)))
    return lax.ppermute(value, axes, [(int(source), int(target)) for source, target in pairs])


def reduce_groups():
    ctx, rep = lax.axis_size("ctx"), lax.axis_size("rep")
    over_ctx = [{"ctx": 1 << at} for at in range(ctx.bit_length() - 2, 0, -1)]
    over_rep = [{"rep": 1 << at} for at in range(rep.bit_length() - 1)]
    return [
        [pair for pair in pairs if pair] for pairs in itertools.zip_longest(over_ctx, over_rep)
    ]


def reduce_place(index):
    place = 0
    for bits in itertools.chain(*reduce_groups()):
        for axis, bit in bits.items():
            place = 2 * place + (index[axis] // bit) % 2
    return place


def scattered(part, group, beside=None):
    count = 1 << len(group)
    size = part.shape[0] // count
    others = []
    for j in range(1, count):
        bits = {}
        for at, pair in enumerate(reversed(group)):
            if (j >> at) & 1:
                bits.update(pair)
        others.append(exchanged(part[j * size : (j + 1) * size], bits))
    if beside is not None:
        others = lax.optimization_barrier((others, beside))[0]
    return part[:size], others


def dot(left, right, left_dim, right_dim, precision=None):
    return lax.dot_general(
        left, right, (((left_dim,), (right_dim,)), ((), ())),
        precision=precision, preferred_element_type=WIDE,
    )


def group_rows(ref, kv_count, group_size):
    rows, _, dim = ref.shape
    wide = 2 * group_size
    parts = []
    for pair in range(kv_count // 2):
        both = ref[:, pair * wide : (pair + 1) * wide, :].astype(WIDE)
        for half in range(2):
            one = both[:, half * group_size : (half + 1) * group_size, :]
            parts.append(one.reshape(rows * group_size, dim).astype(LOW))
    return parts


def lane_head(shape, group_size):
    return lax.broadcasted_iota(jnp.int32, shape, 1) % group_size


def own_terms(maps_by_rows, owner, tenants, low_rank, group_size):
    lanes = maps_by_rows.shape[1]
    same_head = lax.broadcasted_iota(jnp.int32, (group_size, lanes), 0) == lane_head(
        (group_size, lanes), group_size
    )
    span = low_rank * group_size
    total = jnp.zeros((low_rank, group_size, lanes), WIDE)
    for tenant in range(tenants):
        keep = same_head & (owner == tenant)
        block = maps_by_rows[tenant * span : (tenant + 1) * span].reshape(
            low_rank, group_size, lanes
        )
        total = total + jnp.where(keep[None], block, 0.0)
    rows = jnp.sum(total, axis=1)
    rows = jnp.concatenate([rows, rows], axis=0)
    tiles = lanes // 128
    stacked = jnp.concatenate([rows[:, c * 128 : (c + 1) * 128] for c in range(tiles)], axis=0)
    side = lax.broadcasted_iota(jnp.int32, (128, 128), 0) // group_size
    over = lax.broadcasted_iota(jnp.int32, (128, 128), 1) // group_size
    spread = dot(stacked, (side == over).astype(WIDE), 1, 0, lax.Precision.HIGHEST)
    return jnp.concatenate([spread[c * 8 : (c + 1) * 8] for c in range(tiles)], axis=1)


def place_kernel(starts_ref, owners_ref, meta_ref, bias_ref, *, group):
    lanes = meta_ref.shape[1]
    tokens = lanes // group
    row_first = lax.axis_index("ctx") * tokens
    mine = pl.ds(pl.multiple_of(row_first, tokens), tokens)
    row = lax.broadcasted_iota(jnp.int32, (8, tokens), 0)
    both = jnp.where(row == 0, starts_ref[:, mine] - row_first, owners_ref[:, mine]).astype(WIDE)
    repeat = lax.broadcasted_iota(jnp.int32, (tokens, lanes), 0) == (
        lax.broadcasted_iota(jnp.int32, (tokens, lanes), 1) // group
    )
    meta = dot(both, repeat.astype(WIDE), 1, 0, lax.Precision.HIGHEST).astype(jnp.int32)
    meta_ref[...] = meta
    first = meta[0:1, :]
    key, here = places(lanes, tokens, group)
    bias_ref[0] = jnp.where(jnp.where(here, key, key - 2 * tokens) >= first, 0.0, far_below)
    bias_ref[1] = jnp.where(key - tokens >= first, 0.0, far_below)


def slots_of(lanes, group, owned):
    per_group = group // owned
    head = lane_head((1, lanes), group)
    return head ^ ((lax.axis_index("ctx") % per_group) * owned)


def tenants_of(lanes, tenants, rank):
    row = lax.broadcasted_iota(jnp.int32, (tenants * rank, lanes), 0) // rank
    return row ^ (lax.axis_index("rep") * (tenants // lax.axis_size("rep")))


def picked_rows(rows, owner, slots, tenants, rank, group):
    lanes = owner.shape[1]
    mine = owner == tenants_of(lanes, tenants, rank)
    rows = jnp.where(mine, jnp.concatenate([rows] * (tenants * rank // 8), axis=0), 0.0)
    return [jnp.where(slots == h, rows, 0.0).astype(LOW) for h in range(group)]


def pull_kernel(
    meta_ref, cot_ref, rot_ref, proj_ref, q_ref, gh_ref, diff_ref, cots_ref, queries_ref, pull_ref,
    *, kv, group, tenants, rank, owned,
):
    lanes = meta_ref.shape[1]
    owner = meta_ref[1:2, :]
    cots = group_rows(cot_ref, kv, group)
    rots = group_rows(rot_ref, kv, group)
    on_rot = dot(jnp.concatenate(rots, axis=1), jnp.concatenate(cots, axis=1), 1, 1)
    pulled = own_terms(on_rot, owner, tenants, rank, group).astype(LOW).astype(WIDE)
    same_head = lax.broadcasted_iota(jnp.int32, (group, lanes), 0) == lane_head((group, lanes), group)
    picked = []
    for tenant in range(tenants):
        keep = same_head & (owner == tenant)
        for k in range(rank):
            picked.append(jnp.where(keep, pulled[k : k + 1], 0.0))
    picked = jnp.concatenate(picked, axis=0).T.astype(LOW)
    projs = group_rows(proj_ref, kv, group)
    for g in range(kv):
        diff = (projs[g].astype(WIDE) - rots[g].astype(WIDE)).astype(LOW)
        diff_ref[g] = diff
        gh_ref[g] = (cots[g].astype(WIDE) + dot(picked, diff, 1, 0)).astype(LOW)
        cots_ref[g] = cots[g]
    for g, rows in enumerate(group_rows(q_ref, kv, group)):
        queries_ref[g] = rows
    span = tenants * rank
    slots = slots_of(lanes, group, owned)
    for h, rows in enumerate(picked_rows(pulled, owner, slots, tenants, rank, group)):
        pull_ref[h * span : (h + 1) * span, :] = rows


def places(lanes, tokens, group):
    key = lax.broadcasted_iota(jnp.int32, (tokens, lanes), 0)
    query = lax.broadcasted_iota(jnp.int32, (tokens, lanes), 1) // group
    return key, key <= query


def forward_kernel(
    shift_ref, queries_ref, two_ref, one_ref, own_ref, cots_ref, diff_ref, meta_ref, pull_ref, bias_ref,
    weights_ref, send_ref, keep_ref, *, kv, group, tenants, rank, scaling, owned,
):
    tokens = own_ref.shape[1]
    owner = meta_ref[1:2, :]
    lanes = owner.shape[1]
    _, here = places(lanes, tokens, group)
    hidden = []
    for g in range(kv):
        queries = queries_ref[g]
        fold = jnp.where(here, dot(own_ref[g], queries, 1, 1), dot(two_ref[g], queries, 1, 1))
        fold = fold * scaling + bias_ref[0]
        mid = dot(one_ref[g], queries, 1, 1) * scaling + bias_ref[1]
        top = jnp.maximum(jnp.max(fold, axis=0, keepdims=True), jnp.max(mid, axis=0, keepdims=True))
        fold = jnp.exp(fold - top)
        mid = jnp.exp(mid - top)
        total = jnp.sum(fold, axis=0, keepdims=True) + jnp.sum(mid, axis=0, keepdims=True)
        share = 1.0 / total
        fold = fold * share
        mid = mid * share
        weights_ref[g, 0:tokens, :] = fold
        weights_ref[g, tokens : 2 * tokens, :] = mid
        low = jnp.concatenate(
            [jnp.where(here, 0.0, fold).astype(LOW), mid.astype(LOW), jnp.where(here, fold, 0.0).astype(LOW)],
            axis=0,
        )
        values = jnp.concatenate([two_ref[kv + g], one_ref[kv + g], own_ref[kv + g]], axis=0)
        hidden.append(dot(values, low, 0, 0).astype(LOW))
    hidden = jnp.concatenate(hidden, axis=0)
    on_diff = dot(jnp.concatenate([diff_ref[g] for g in range(kv)], axis=1), hidden, 1, 0)
    lifted = own_terms(on_diff, owner, tenants, rank, group)
    one_hot = (owner == lax.broadcasted_iota(jnp.int32, (tenants, lanes), 0)).astype(WIDE)
    bias = jnp.concatenate([shift_ref[...]] * (8 // rank), axis=0)
    shift = dot(bias, one_hot, 1, 0, lax.Precision.HIGHEST)
    lifted = (lifted + shift).astype(LOW).astype(WIDE)
    rep = lax.axis_size("rep")
    me = lax.axis_index("ctx")
    per_group = group // owned
    span = tenants * rank
    slots = slots_of(lanes, group, owned)
    lift_all = jnp.concatenate(picked_rows(lifted, owner, slots, tenants, rank, group), axis=0)
    on_proj = dot(pull_ref[...], hidden, 1, 1)
    on_rot = dot(lift_all, jnp.concatenate([cots_ref[g] for g in range(kv)], axis=1), 1, 0) - on_proj
    dim = two_ref.shape[2]
    here_rows = span // rep
    for g in range(kv):
        columns = slice(g * dim, (g + 1) * dim)
        for low in range(per_group):
            device = (g ^ (me // per_group)) * per_group + low
            into = send_ref if low % 2 else keep_ref
            for r in range(rep):
                pieces = []
                for h in range(low * owned, (low + 1) * owned):
                    rows = slice(h * span + r * here_rows, h * span + (r + 1) * here_rows)
                    pieces += [on_rot[rows, columns], on_proj[rows, columns]]
                into[reduce_place(dict(ctx=device, rep=r))] = jnp.concatenate(pieces, axis=0).astype(LOW)


def backward_kernel(
    queries_ref, gh_ref, two_ref, one_ref, own_ref, weights_ref, dq_ref, back_two_ref, back_one_ref, back_own_ref,
    *, kv, group, scaling,
):
    tokens = own_ref.shape[1]
    lanes = weights_ref.shape[2]
    dim = queries_ref.shape[2]
    _, here = places(lanes, tokens, group)
    query_grads = []
    for g in range(kv):
        grads = gh_ref[g]
        fold_weights = weights_ref[g, 0:tokens, :]
        mid_weights = weights_ref[g, tokens : 2 * tokens, :]
        fold = jnp.where(here, dot(own_ref[kv + g], grads, 1, 1), dot(two_ref[kv + g], grads, 1, 1))
        mid = dot(one_ref[kv + g], grads, 1, 1)
        delta = jnp.sum(fold * fold_weights, axis=0, keepdims=True) + jnp.sum(
            mid * mid_weights, axis=0, keepdims=True
        )
        fold = fold_weights * (fold - delta)
        mid = mid_weights * (mid - delta)
        score_grad = jnp.concatenate(
            [jnp.where(here, 0.0, fold).astype(LOW), mid.astype(LOW), jnp.where(here, fold, 0.0).astype(LOW)],
            axis=0,
        )
        low = jnp.concatenate(
            [
                jnp.where(here, 0.0, fold_weights).astype(LOW),
                mid_weights.astype(LOW),
                jnp.where(here, fold_weights, 0.0).astype(LOW),
            ],
            axis=0,
        )
        keys = jnp.concatenate([two_ref[g], one_ref[g], own_ref[g]], axis=0)
        key_grad = dot(score_grad, queries_ref[g], 1, 0) * scaling
        value_grad = dot(low, grads, 1, 0)
        for place, grad in ((g, key_grad), (kv + g, value_grad)):
            back_two_ref[place] = grad[0:tokens].astype(LOW)
            back_one_ref[place] = grad[tokens : 2 * tokens].astype(LOW)
            back_own_ref[place] = grad[2 * tokens :]
        query_grad = dot(keys, score_grad, 0, 0) * scaling
        query_grads.append(query_grad.T.reshape(tokens, group, dim))
        if g % 2 == 1:
            both = jnp.concatenate(query_grads[-2:], axis=1).astype(LOW)
            dq_ref[:, (g - 1) * group : (g + 1) * group, :] = both


def grads_kernel(part_ref, *refs, owned):
    total = part_ref[0].astype(WIDE)
    for other_ref in refs[:-2]:
        total = total + other_ref[0].astype(WIDE)
    size = refs[-1].shape[0]
    for place in range(owned):
        for at in range(2):
            row = (2 * place + at) * size
            refs[at - 2][:, place, :] = total[row : row + size]


def halo_kernel(own_ref, mate_ref, two_ref, keys_ref, values_ref, wide_ref, *, kv):
    tokens = own_ref.shape[1]
    even = (lax.axis_index("ctx") % 2 == 0).astype(WIDE)
    for at, out in enumerate((keys_ref, values_ref)):
        for m in range(kv):
            place = at * kv + m
            total = own_ref[place] + two_ref[place].astype(WIDE) + even * mate_ref[place].astype(WIDE)
            wide_ref[at, pl.ds(m, tokens, stride=kv), :] = total
        out[...] = wide_ref[at].astype(LOW)


def on_device(
    query_rows, key_rows, value_matrix, cotangent, rotation, projection, shift_bias, doc_starts, tenant_ids,
):
    queries = query_rows[0]
    upstream = cotangent[0]
    tokens, heads, dim = queries.shape
    kv = key_rows.shape[2]
    group = heads // kv
    scaling = dim ** (-0.5)
    tenants, rank = rotation.shape[0], rotation.shape[1]
    lanes = tokens * group
    ctx = lax.axis_size("ctx")
    rep = lax.axis_size("rep")
    assert 2 * tokens == DOC_MAX


    rot = rotation.reshape(tenants * rank, heads, dim)
    proj = projection.reshape(tenants * rank, heads, dim)
    sizes = dict(kv=kv, group=group)
    vmem = pl.BlockSpec(memory_space=pltpu.VMEM)

    def call(body, outs, flops, moved, specs=None, scratch=(), limit=24, **fixed):
        def run(*operands):
            return pl.pallas_call(
                lambda *refs: body(*refs, **fixed),
                out_shape=[jax.ShapeDtypeStruct(*out) for out in outs],
                in_specs=specs or [vmem] * len(operands),
                out_specs=[vmem] * len(outs),
                scratch_shapes=scratch,
                compiler_params=pltpu.CompilerParams(vmem_limit_bytes=limit * 2**20),
                name=body.__name__,
                cost_estimate=pl.CostEstimate(flops=flops, bytes_accessed=moved, transcendentals=0),
            )(*operands)

        return run

    span = tenants * rank
    here = heads // ctx
    rows = here * 2 * span // rep
    own = jnp.moveaxis(jnp.concatenate([key_rows[0], value_matrix[0]], axis=1), 1, 0)
    even = lax.axis_index("ctx") % 2 == 0
    two = shifted(own, "ctx", 2)
    meta, biases = call(
        place_kernel, [((8, lanes), jnp.int32), ((2, tokens, lanes), WIDE)], 8 * 2**30, 2**20,
        group=group,
    )(doc_starts, tenant_ids)
    grad_hidden, diff, cots, queries, pull = call(
        pull_kernel,
        [
            ((kv, lanes, dim), LOW), ((kv, span * group, dim), LOW), ((kv, lanes, dim), LOW),
            ((kv, lanes, dim), LOW), ((span * group, lanes), LOW),
        ],
        2 * 2**30, 4 * 2**20, tenants=tenants, rank=rank, owned=here, **sizes,
    )(meta, upstream, rot, proj, queries)
    two, pull = lax.optimization_barrier((two, pull))
    one = exchanged(jnp.where(even, own, two), {"ctx": 1})
    weights, send, keep = call(
        forward_kernel,
        [((kv, 2 * tokens, lanes), WIDE)] + [((ctx * rep // 2, rows, dim), LOW)] * 2,
        4 * 2**30, 10 * 2**20,
        tenants=tenants, rank=rank, scaling=scaling, owned=here, **sizes,
    )(shift_bias.T, queries, two, one, own, cots, diff, meta, pull, biases)
    part = (keep.astype(WIDE) + exchanged(send, {"ctx": 1}).astype(WIDE)).astype(LOW)
    weights, part = lax.optimization_barrier((weights, part))
    d_queries, back_two, back_one, back_own = call(
        backward_kernel,
        [((tokens, heads, dim), LOW), (own.shape, LOW), (own.shape, LOW), (own.shape, WIDE)],
        4 * 2**30, 10 * 2**20, scaling=scaling, **sizes,
    )(queries, grad_hidden, two, one, own, weights)
    from_mate = exchanged(back_one, {"ctx": 1})
    onward = back_two.astype(WIDE) + jnp.where(even, 0.0, from_mate.astype(WIDE))
    onward = onward.astype(LOW)

    groups = reduce_groups()
    for at, group_bits in enumerate(groups):
        beside = back_own if at == 0 else None
        if at == len(groups) - 1:
            part, onward = lax.optimization_barrier((part, onward))
            from_two = shifted(onward, "ctx", -2)
            beside = from_two
        part, others = scattered(part, group_bits, beside)
        if at < len(groups) - 1:
            part = part.astype(WIDE) + sum(other.astype(WIDE) for other in others)
            part = part.astype(LOW)
    grads = call(
        grads_kernel, [((span // rep, here, dim), WIDE)] * 2, 2**18, 2**18, owned=here,
    )(part, *others)
    grads = [grad.reshape(tenants // rep, rank, here, dim) for grad in grads]
    d_keys, d_values = call(
        halo_kernel, [((tokens * kv, dim), LOW)] * 2, 2**20, 2**20,
        scratch=[pltpu.VMEM((2, tokens * kv, dim), WIDE)], kv=kv,
    )(back_own, from_mate, from_two)
    d_keys, d_values = (grad.reshape(key_rows.shape) for grad in (d_keys, d_values))
    return (d_queries[None], d_keys, d_values, grads[0], grads[1])


def solution(mesh):
    rows = P("rep", "ctx", None, None)
    in_specs = (rows, rows, rows, rows, P(), P(), P(), P("rep", None), P("rep", None))
    tenant_rows = P("rep", None, "ctx", None)
    out_specs = (rows, rows, rows, tenant_rows, tenant_rows)
    return jax.shard_map(
        on_device, mesh=mesh, in_specs=in_specs, out_specs=out_specs, check_vma=False
    )
```

```python
import itertools

import jax
import jax.numpy as jnp
import numpy as np
from jax import lax
from jax.experimental import pallas as pl
from jax.experimental.pallas import tpu as pltpu
from jax.sharding import PartitionSpec as P

DOC_MAX = 256
LOW = jnp.bfloat16
WIDE = jnp.float32
far_below = -1e30
PIECE = 256


def shifted(value, axis, steps):
    count = lax.axis_size(axis)
    return lax.ppermute(value, axis, [(source, (source + steps) % count) for source in range(count)])


def exchanged(value, bits):
    axes = tuple(bits)
    shape = [lax.axis_size(axis) for axis in axes]
    pairs = []
    for source in np.ndindex(*shape):
        target = [at ^ bits[axis] for at, axis in zip(source, axes)]
        pairs.append((np.ravel_multi_index(source, shape), np.ravel_multi_index(target, shape)))
    return lax.ppermute(value, axes, [(int(source), int(target)) for source, target in pairs])


def reduce_groups():
    ctx, rep = lax.axis_size("ctx"), lax.axis_size("rep")
    over_ctx = [{"ctx": 1 << at} for at in range(ctx.bit_length() - 2, 0, -1)]
    over_rep = [{"rep": 1 << at} for at in range(rep.bit_length() - 1)]
    return [
        [pair for pair in pairs if pair] for pairs in itertools.zip_longest(over_ctx, over_rep)
    ]


def reduce_place(index):
    place = 0
    for bits in itertools.chain(*reduce_groups()):
        for axis, bit in bits.items():
            place = 2 * place + (index[axis] // bit) % 2
    return place


def scattered(part, group, beside=None):
    count = 1 << len(group)
    size = part.shape[0] // count
    others = []
    for j in range(1, count):
        bits = {}
        for at, pair in enumerate(reversed(group)):
            if (j >> at) & 1:
                bits.update(pair)
        others.append(exchanged(part[j * size : (j + 1) * size], bits))
    if beside is not None:
        others = lax.optimization_barrier((others, beside))[0]
    return part[:size], others


def dot(left, right, left_dim, right_dim, precision=None):
    return lax.dot_general(
        left, right, (((left_dim,), (right_dim,)), ((), ())),
        precision=precision, preferred_element_type=WIDE,
    )


def group_rows(ref, kv_count, group_size):
    rows, _, dim = ref.shape
    wide = 2 * group_size
    parts = []
    for pair in range(kv_count // 2):
        both = ref[:, pair * wide : (pair + 1) * wide, :].astype(WIDE)
        for half in range(2):
            one = both[:, half * group_size : (half + 1) * group_size, :]
            parts.append(one.reshape(rows * group_size, dim).astype(LOW))
    return parts


def lane_head(shape, group_size):
    return lax.broadcasted_iota(jnp.int32, shape, 1) % group_size


def own_terms(maps_by_rows, owner, tenants, low_rank, group_size):
    lanes = maps_by_rows.shape[1]
    same_head = lax.broadcasted_iota(jnp.int32, (group_size, lanes), 0) == lane_head(
        (group_size, lanes), group_size
    )
    span = low_rank * group_size
    total = jnp.zeros((low_rank, group_size, lanes), WIDE)
    for tenant in range(tenants):
        keep = same_head & (owner == tenant)
        block = maps_by_rows[tenant * span : (tenant + 1) * span].reshape(
            low_rank, group_size, lanes
        )
        total = total + jnp.where(keep[None], block, 0.0)
    rows = jnp.sum(total, axis=1)
    rows = jnp.concatenate([rows, rows], axis=0)
    tiles = lanes // 128
    stacked = jnp.concatenate([rows[:, c * 128 : (c + 1) * 128] for c in range(tiles)], axis=0)
    side = lax.broadcasted_iota(jnp.int32, (128, 128), 0) // group_size
    over = lax.broadcasted_iota(jnp.int32, (128, 128), 1) // group_size
    spread = dot(stacked, (side == over).astype(WIDE), 1, 0, lax.Precision.HIGHEST)
    return jnp.concatenate([spread[c * 8 : (c + 1) * 8] for c in range(tiles)], axis=1)


def place_kernel(starts_ref, owners_ref, meta_ref, bias_ref, *, group):
    lanes = meta_ref.shape[1]
    tokens = lanes // group
    row_first = lax.axis_index("ctx") * tokens
    mine = pl.ds(pl.multiple_of(row_first, tokens), tokens)
    row = lax.broadcasted_iota(jnp.int32, (8, tokens), 0)
    both = jnp.where(row == 0, starts_ref[:, mine] - row_first, owners_ref[:, mine]).astype(WIDE)
    repeat = lax.broadcasted_iota(jnp.int32, (tokens, lanes), 0) == (
        lax.broadcasted_iota(jnp.int32, (tokens, lanes), 1) // group
    )
    meta = dot(both, repeat.astype(WIDE), 1, 0, lax.Precision.HIGHEST).astype(jnp.int32)
    meta_ref[...] = meta
    first = meta[0:1, :]
    key, here = places(lanes, tokens, group)
    bias_ref[0] = jnp.where(jnp.where(here, key, key - 2 * tokens) >= first, 0.0, far_below)
    bias_ref[1] = jnp.where(key - tokens >= first, 0.0, far_below)


def slots_of(lanes, group, owned):
    per_group = group // owned
    head = lane_head((1, lanes), group)
    return head ^ ((lax.axis_index("ctx") % per_group) * owned)


def tenants_of(lanes, tenants, rank):
    row = lax.broadcasted_iota(jnp.int32, (tenants * rank, lanes), 0) // rank
    return row ^ (lax.axis_index("rep") * (tenants // lax.axis_size("rep")))


def picked_rows(rows, owner, slots, tenants, rank, group):
    lanes = owner.shape[1]
    mine = owner == tenants_of(lanes, tenants, rank)
    rows = jnp.where(mine, jnp.concatenate([rows] * (tenants * rank // 8), axis=0), 0.0)
    return [jnp.where(slots == h, rows, 0.0).astype(LOW) for h in range(group)]


def pull_kernel(
    meta_ref, cot_ref, rot_ref, proj_ref, q_ref, gh_ref, diff_ref, cots_ref, queries_ref, pull_ref,
    *, kv, group, tenants, rank, owned,
):
    lanes = meta_ref.shape[1]
    owner = meta_ref[1:2, :]
    cots = group_rows(cot_ref, kv, group)
    rots = group_rows(rot_ref, kv, group)
    on_rot = dot(jnp.concatenate(rots, axis=1), jnp.concatenate(cots, axis=1), 1, 1)
    pulled = own_terms(on_rot, owner, tenants, rank, group).astype(LOW).astype(WIDE)
    same_head = lax.broadcasted_iota(jnp.int32, (group, lanes), 0) == lane_head((group, lanes), group)
    picked = []
    for tenant in range(tenants):
        keep = same_head & (owner == tenant)
        for k in range(rank):
            picked.append(jnp.where(keep, pulled[k : k + 1], 0.0))
    picked = jnp.concatenate(picked, axis=0).T.astype(LOW)
    projs = group_rows(proj_ref, kv, group)
    for g in range(kv):
        diff = (projs[g].astype(WIDE) - rots[g].astype(WIDE)).astype(LOW)
        diff_ref[g] = diff
        gh_ref[g] = (cots[g].astype(WIDE) + dot(picked, diff, 1, 0)).astype(LOW)
        cots_ref[g] = cots[g]
    for g, rows in enumerate(group_rows(q_ref, kv, group)):
        queries_ref[g] = rows
    span = tenants * rank
    slots = slots_of(lanes, group, owned)
    for h, rows in enumerate(picked_rows(pulled, owner, slots, tenants, rank, group)):
        pull_ref[h * span : (h + 1) * span, :] = rows


def here_of(tokens, group, piece):
    key = lax.broadcasted_iota(jnp.int32, (tokens, PIECE), 0)
    return key <= lax.broadcasted_iota(jnp.int32, (tokens, PIECE), 1) // group + piece * (PIECE // group)


def places(lanes, tokens, group):
    key = lax.broadcasted_iota(jnp.int32, (tokens, lanes), 0)
    query = lax.broadcasted_iota(jnp.int32, (tokens, lanes), 1) // group
    return key, key <= query


def forward_kernel(
    shift_ref, queries_ref, two_ref, one_ref, own_ref, cots_ref, diff_ref, meta_ref, pull_ref, bias_ref,
    low_ref, send_ref, keep_ref, hidden_ref, *, kv, group, tenants, rank, scaling, owned,
):
    tokens = own_ref.shape[1]
    dim = own_ref.shape[2]
    owner = meta_ref[1:2, :]
    lanes = owner.shape[1]
    for g in range(kv):
        values = jnp.concatenate([two_ref[kv + g], one_ref[kv + g], own_ref[kv + g]], axis=0).T
        for piece in range(lanes // PIECE):
            columns = slice(piece * PIECE, (piece + 1) * PIECE)
            here = here_of(tokens, group, piece)
            queries = queries_ref[g, columns, :]
            fold = jnp.where(here, dot(own_ref[g], queries, 1, 1), dot(two_ref[g], queries, 1, 1))
            fold = fold * scaling + bias_ref[0, :, columns]
            mid = dot(one_ref[g], queries, 1, 1) * scaling + bias_ref[1, :, columns]
            top = jnp.max(jnp.maximum(fold, mid), axis=0, keepdims=True)
            fold = jnp.exp(fold - top)
            mid = jnp.exp(mid - top)
            share = 1.0 / jnp.sum(fold + mid, axis=0, keepdims=True)
            fold = fold * share
            low = jnp.concatenate(
                [
                    jnp.where(here, 0.0, fold).astype(LOW),
                    (mid * share).astype(LOW),
                    jnp.where(here, fold, 0.0).astype(LOW),
                ],
                axis=0,
            )
            low_ref[g, :, columns] = low
            hidden_ref[g * dim : (g + 1) * dim, columns] = dot(values, low, 1, 0).astype(LOW)
    hidden = hidden_ref[...]
    on_diff = dot(jnp.concatenate([diff_ref[g] for g in range(kv)], axis=1), hidden, 1, 0)
    lifted = own_terms(on_diff, owner, tenants, rank, group)
    one_hot = (owner == lax.broadcasted_iota(jnp.int32, (tenants, lanes), 0)).astype(WIDE)
    bias = jnp.concatenate([shift_ref[...]] * (8 // rank), axis=0)
    shift = dot(bias, one_hot, 1, 0, lax.Precision.HIGHEST)
    lifted = (lifted + shift).astype(LOW).astype(WIDE)
    rep = lax.axis_size("rep")
    me = lax.axis_index("ctx")
    per_group = group // owned
    span = tenants * rank
    slots = slots_of(lanes, group, owned)
    lift_all = jnp.concatenate(picked_rows(lifted, owner, slots, tenants, rank, group), axis=0)
    on_proj = dot(pull_ref[...], hidden, 1, 1)
    on_rot = dot(lift_all, jnp.concatenate([cots_ref[g] for g in range(kv)], axis=1), 1, 0) - on_proj
    here_rows = span // rep
    for g in range(kv):
        columns = slice(g * dim, (g + 1) * dim)
        for low in range(per_group):
            device = (g ^ (me // per_group)) * per_group + low
            into = send_ref if low % 2 else keep_ref
            for r in range(rep):
                pieces = []
                for h in range(low * owned, (low + 1) * owned):
                    rows = slice(h * span + r * here_rows, h * span + (r + 1) * here_rows)
                    pieces += [on_rot[rows, columns], on_proj[rows, columns]]
                into[reduce_place(dict(ctx=device, rep=r))] = jnp.concatenate(pieces, axis=0).astype(LOW)


def backward_kernel(
    queries_ref, gh_ref, two_ref, one_ref, own_ref, low_ref, dq_hbm, back_two_ref, back_one_ref, back_own_ref,
    grad_ref, dq_ref, sems, *, kv, group, scaling,
):
    tokens, dim = own_ref.shape[1:]
    lanes = low_ref.shape[2]
    rows = PIECE // group
    windows = [
        jnp.concatenate([two_ref[place], one_ref[place], own_ref[place]], axis=0) for place in range(2 * kv)
    ]
    keys = [window.T for window in windows[:kv]]
    copies = []
    for piece in range(lanes // PIECE):
        columns = slice(piece * PIECE, (piece + 1) * PIECE)
        here = slice(piece * rows, (piece + 1) * rows)
        for g in range(kv):
            weights = low_ref[g, :, columns].astype(WIDE)
            weight_grad = dot(windows[kv + g], gh_ref[g, columns, :], 1, 1)
            delta = jnp.sum(weights * weight_grad, axis=0, keepdims=True)
            score_grad = (weights * (weight_grad - delta)).astype(LOW)
            grad_ref[g, :, columns] = score_grad
            query_grad = (dot(keys[g], score_grad, 1, 0) * scaling).T.reshape(rows, group, dim)
            if g % 2 == 1:
                both = jnp.concatenate([before, query_grad], axis=1).astype(LOW)
                dq_ref[here, (g - 1) * group : (g + 1) * group, :] = both
            before = query_grad
        copies.append(pltpu.make_async_copy(dq_ref.at[here], dq_hbm.at[here], sems.at[piece]))
        copies[-1].start()
    for g in range(kv):
        key_grad = dot(grad_ref[g], queries_ref[g], 1, 0) * scaling
        value_grad = dot(low_ref[g], gh_ref[g], 1, 0)
        for place, grad in ((g, key_grad), (kv + g, value_grad)):
            back_two_ref[place] = grad[0:tokens].astype(LOW)
            back_one_ref[place] = grad[tokens : 2 * tokens].astype(LOW)
            back_own_ref[place] = grad[2 * tokens :]
    for copy in copies:
        copy.wait()


def grads_kernel(part_ref, *refs, owned):
    total = part_ref[0].astype(WIDE)
    for other_ref in refs[:-2]:
        total = total + other_ref[0].astype(WIDE)
    size = refs[-1].shape[0]
    for place in range(owned):
        for at in range(2):
            row = (2 * place + at) * size
            refs[at - 2][:, place, :] = total[row : row + size]


def halo_kernel(own_ref, mate_ref, two_ref, keys_ref, values_ref, wide_ref, *, kv):
    tokens = own_ref.shape[1]
    even = (lax.axis_index("ctx") % 2 == 0).astype(WIDE)
    for at, out in enumerate((keys_ref, values_ref)):
        for m in range(kv):
            place = at * kv + m
            total = own_ref[place] + two_ref[place].astype(WIDE) + even * mate_ref[place].astype(WIDE)
            wide_ref[at, pl.ds(m, tokens, stride=kv), :] = total
        out[...] = wide_ref[at].astype(LOW)


def on_device(
    query_rows, key_rows, value_matrix, cotangent, rotation, projection, shift_bias, doc_starts, tenant_ids,
):
    queries = query_rows[0]
    upstream = cotangent[0]
    tokens, heads, dim = queries.shape
    kv = key_rows.shape[2]
    group = heads // kv
    scaling = dim ** (-0.5)
    tenants, rank = rotation.shape[0], rotation.shape[1]
    lanes = tokens * group
    ctx = lax.axis_size("ctx")
    rep = lax.axis_size("rep")
    assert 2 * tokens == DOC_MAX


    rot = rotation.reshape(tenants * rank, heads, dim)
    proj = projection.reshape(tenants * rank, heads, dim)
    sizes = dict(kv=kv, group=group)
    vmem = pl.BlockSpec(memory_space=pltpu.VMEM)

    def call(body, outs, flops, moved, out_specs=None, scratch=(), **fixed):
        def run(*operands):
            return pl.pallas_call(
                lambda *refs: body(*refs, **fixed),
                out_shape=[jax.ShapeDtypeStruct(*out) for out in outs],
                in_specs=[vmem] * len(operands),
                out_specs=out_specs or [vmem] * len(outs),
                scratch_shapes=scratch,
                compiler_params=pltpu.CompilerParams(vmem_limit_bytes=24 * 2**20),
                name=body.__name__,
                cost_estimate=pl.CostEstimate(flops=flops, bytes_accessed=moved, transcendentals=0),
            )(*operands)

        return run

    span = tenants * rank
    here = heads // ctx
    rows = here * 2 * span // rep
    own = jnp.moveaxis(jnp.concatenate([key_rows[0], value_matrix[0]], axis=1), 1, 0)
    even = lax.axis_index("ctx") % 2 == 0
    two = shifted(own, "ctx", 2)
    meta, biases = call(
        place_kernel, [((8, lanes), jnp.int32), ((2, tokens, lanes), WIDE)], 8 * 2**30, 2**20,
        group=group,
    )(doc_starts, tenant_ids)
    grad_hidden, diff, cots, queries, pull = call(
        pull_kernel,
        [
            ((kv, lanes, dim), LOW), ((kv, span * group, dim), LOW), ((kv, lanes, dim), LOW),
            ((kv, lanes, dim), LOW), ((span * group, lanes), LOW),
        ],
        2 * 2**30, 4 * 2**20, tenants=tenants, rank=rank, owned=here, **sizes,
    )(meta, upstream, rot, proj, queries)
    two, pull = lax.optimization_barrier((two, pull))
    one = exchanged(jnp.where(even, own, two), {"ctx": 1})
    low, send, keep = call(
        forward_kernel,
        [((kv, 3 * tokens, lanes), LOW)] + [((ctx * rep // 2, rows, dim), LOW)] * 2,
        4 * 2**30, 10 * 2**20, scratch=[pltpu.VMEM((heads // group * dim, lanes), LOW)],
        tenants=tenants, rank=rank, scaling=scaling, owned=here, **sizes,
    )(shift_bias.T, queries, two, one, own, cots, diff, meta, pull, biases)
    part = (keep.astype(WIDE) + exchanged(send, {"ctx": 1}).astype(WIDE)).astype(LOW)
    low, part = lax.optimization_barrier((low, part))
    d_queries, back_two, back_one, back_own = call(
        backward_kernel,
        [((tokens, heads, dim), LOW), (own.shape, LOW), (own.shape, LOW), (own.shape, WIDE)],
        4 * 2**30, 10 * 2**20,
        scratch=[
            pltpu.VMEM((kv, 3 * tokens, lanes), LOW), pltpu.VMEM((tokens, heads, dim), LOW),
            pltpu.SemaphoreType.DMA((lanes // PIECE,)),
        ],
        out_specs=[pl.BlockSpec(memory_space=pltpu.HBM), vmem, vmem, vmem], scaling=scaling, **sizes,
    )(queries, grad_hidden, two, one, own, low)
    from_mate = exchanged(back_one, {"ctx": 1})
    onward = back_two.astype(WIDE) + jnp.where(even, 0.0, from_mate.astype(WIDE))
    onward = onward.astype(LOW)

    groups = reduce_groups()
    for at, group_bits in enumerate(groups):
        beside = back_own if at == 0 else None
        if at == len(groups) - 1:
            part, onward = lax.optimization_barrier((part, onward))
            from_two = shifted(onward, "ctx", -2)
            beside = from_two
        part, others = scattered(part, group_bits, beside)
        if at < len(groups) - 1:
            part = part.astype(WIDE) + sum(other.astype(WIDE) for other in others)
            part = part.astype(LOW)
    grads = call(
        grads_kernel, [((span // rep, here, dim), WIDE)] * 2, 2**18, 2**18, owned=here,
    )(part, *others)
    grads = [grad.reshape(tenants // rep, rank, here, dim) for grad in grads]
    d_keys, d_values = call(
        halo_kernel, [((tokens * kv, dim), LOW)] * 2, 2**20, 2**20,
        scratch=[pltpu.VMEM((2, tokens * kv, dim), WIDE)], kv=kv,
    )(back_own, from_mate, from_two)
    d_keys, d_values = (grad.reshape(key_rows.shape) for grad in (d_keys, d_values))
    return (d_queries[None], d_keys, d_values, grads[0], grads[1])


def solution(mesh):
    rows = P("rep", "ctx", None, None)
    in_specs = (rows, rows, rows, rows, P(), P(), P(), P("rep", None), P("rep", None))
    tenant_rows = P("rep", None, "ctx", None)
    out_specs = (rows, rows, rows, tenant_rows, tenant_rows)
    return jax.shard_map(
        on_device, mesh=mesh, in_specs=in_specs, out_specs=out_specs, check_vma=False
    )
```

```python
import itertools

import jax
import jax.numpy as jnp
import numpy as np
from jax import lax
from jax.experimental import pallas as pl
from jax.experimental.pallas import tpu as pltpu
from jax.sharding import PartitionSpec as P

DOC_MAX = 256
LOW = jnp.bfloat16
WIDE = jnp.float32
far_below = -1e30


def shifted(value, axis, steps):
    count = lax.axis_size(axis)
    return lax.ppermute(value, axis, [(source, (source + steps) % count) for source in range(count)])


def exchanged(value, bits):
    axes = tuple(bits)
    shape = [lax.axis_size(axis) for axis in axes]
    pairs = []
    for source in np.ndindex(*shape):
        target = [at ^ bits[axis] for at, axis in zip(source, axes)]
        pairs.append((np.ravel_multi_index(source, shape), np.ravel_multi_index(target, shape)))
    return lax.ppermute(value, axes, [(int(source), int(target)) for source, target in pairs])


def reduce_groups():
    ctx, rep = lax.axis_size("ctx"), lax.axis_size("rep")
    over_ctx = [{"ctx": 1 << at} for at in range(ctx.bit_length() - 2, 0, -1)]
    over_rep = [{"rep": 1 << at} for at in range(rep.bit_length() - 1)]
    return [
        [pair for pair in pairs if pair] for pairs in itertools.zip_longest(over_ctx, over_rep)
    ]


def reduce_place(index):
    place = 0
    for bits in itertools.chain(*reduce_groups()):
        for axis, bit in bits.items():
            place = 2 * place + (index[axis] // bit) % 2
    return place


def scattered(part, group, beside=None):
    count = 1 << len(group)
    size = part.shape[0] // count
    others = []
    for j in range(1, count):
        bits = {}
        for at, pair in enumerate(reversed(group)):
            if (j >> at) & 1:
                bits.update(pair)
        others.append(exchanged(part[j * size : (j + 1) * size], bits))
    if beside is not None:
        others = lax.optimization_barrier((others, beside))[0]
    return part[:size], others


def dot(left, right, left_dim, right_dim, precision=None):
    return lax.dot_general(
        left, right, (((left_dim,), (right_dim,)), ((), ())),
        precision=precision, preferred_element_type=WIDE,
    )


def group_rows(ref, kv_count, group_size):
    rows, _, dim = ref.shape
    wide = 2 * group_size
    parts = []
    for pair in range(kv_count // 2):
        both = ref[:, pair * wide : (pair + 1) * wide, :].astype(WIDE)
        for half in range(2):
            one = both[:, half * group_size : (half + 1) * group_size, :]
            parts.append(one.reshape(rows * group_size, dim).astype(LOW))
    return parts


def lane_head(shape, group_size):
    return lax.broadcasted_iota(jnp.int32, shape, 1) % group_size


def own_terms(maps_by_rows, owner, tenants, low_rank, group_size):
    lanes = maps_by_rows.shape[1]
    same_head = lax.broadcasted_iota(jnp.int32, (group_size, lanes), 0) == lane_head(
        (group_size, lanes), group_size
    )
    span = low_rank * group_size
    total = jnp.zeros((low_rank, group_size, lanes), WIDE)
    for tenant in range(tenants):
        keep = same_head & (owner == tenant)
        block = maps_by_rows[tenant * span : (tenant + 1) * span].reshape(
            low_rank, group_size, lanes
        )
        total = total + jnp.where(keep[None], block, 0.0)
    rows = jnp.sum(total, axis=1)
    rows = jnp.concatenate([rows, rows], axis=0)
    tiles = lanes // 128
    stacked = jnp.concatenate([rows[:, c * 128 : (c + 1) * 128] for c in range(tiles)], axis=0)
    side = lax.broadcasted_iota(jnp.int32, (128, 128), 0) // group_size
    over = lax.broadcasted_iota(jnp.int32, (128, 128), 1) // group_size
    spread = dot(stacked, (side == over).astype(WIDE), 1, 0, lax.Precision.HIGHEST)
    return jnp.concatenate([spread[c * 8 : (c + 1) * 8] for c in range(tiles)], axis=1)


def place_kernel(starts_ref, owners_ref, meta_ref, bias_ref, *, group):
    lanes = meta_ref.shape[1]
    tokens = lanes // group
    row_first = lax.axis_index("ctx") * tokens
    mine = pl.ds(pl.multiple_of(row_first, tokens), tokens)
    row = lax.broadcasted_iota(jnp.int32, (8, tokens), 0)
    both = jnp.where(row == 0, starts_ref[:, mine] - row_first, owners_ref[:, mine]).astype(WIDE)
    repeat = lax.broadcasted_iota(jnp.int32, (tokens, lanes), 0) == (
        lax.broadcasted_iota(jnp.int32, (tokens, lanes), 1) // group
    )
    meta = dot(both, repeat.astype(WIDE), 1, 0, lax.Precision.HIGHEST).astype(jnp.int32)
    meta_ref[...] = meta
    first = meta[0:1, :]
    key, here = places(lanes, tokens, group)
    bias_ref[0] = jnp.where(jnp.where(here, key, key - 2 * tokens) >= first, 0.0, far_below)
    bias_ref[1] = jnp.where(key - tokens >= first, 0.0, far_below)


def slots_of(lanes, group, owned):
    per_group = group // owned
    head = lane_head((1, lanes), group)
    return head ^ ((lax.axis_index("ctx") % per_group) * owned)


def tenants_of(lanes, tenants, rank):
    row = lax.broadcasted_iota(jnp.int32, (tenants * rank, lanes), 0) // rank
    return row ^ (lax.axis_index("rep") * (tenants // lax.axis_size("rep")))


def picked_rows(rows, owner, slots, tenants, rank, group):
    lanes = owner.shape[1]
    mine = owner == tenants_of(lanes, tenants, rank)
    rows = jnp.where(mine, jnp.concatenate([rows] * (tenants * rank // 8), axis=0), 0.0)
    return [jnp.where(slots == h, rows, 0.0).astype(LOW) for h in range(group)]


def pull_kernel(
    meta_ref, cot_ref, rot_ref, proj_ref, q_ref, gh_ref, diff_ref, cots_ref, queries_ref, pull_ref,
    *, kv, group, tenants, rank, owned,
):
    lanes = meta_ref.shape[1]
    owner = meta_ref[1:2, :]
    cots = group_rows(cot_ref, kv, group)
    rots = group_rows(rot_ref, kv, group)
    on_rot = dot(jnp.concatenate(rots, axis=1), jnp.concatenate(cots, axis=1), 1, 1)
    pulled = own_terms(on_rot, owner, tenants, rank, group).astype(LOW).astype(WIDE)
    same_head = lax.broadcasted_iota(jnp.int32, (group, lanes), 0) == lane_head((group, lanes), group)
    picked = []
    for tenant in range(tenants):
        keep = same_head & (owner == tenant)
        for k in range(rank):
            picked.append(jnp.where(keep, pulled[k : k + 1], 0.0))
    picked = jnp.concatenate(picked, axis=0).T.astype(LOW)
    projs = group_rows(proj_ref, kv, group)
    for g in range(kv):
        diff = (projs[g].astype(WIDE) - rots[g].astype(WIDE)).astype(LOW)
        diff_ref[g] = diff
        gh_ref[g] = (cots[g].astype(WIDE) + dot(picked, diff, 1, 0)).astype(LOW)
        cots_ref[g] = cots[g]
    for g, rows in enumerate(group_rows(q_ref, kv, group)):
        queries_ref[g] = rows
    span = tenants * rank
    slots = slots_of(lanes, group, owned)
    for h, rows in enumerate(picked_rows(pulled, owner, slots, tenants, rank, group)):
        pull_ref[h * span : (h + 1) * span, :] = rows


def places(lanes, tokens, group):
    key = lax.broadcasted_iota(jnp.int32, (tokens, lanes), 0)
    query = lax.broadcasted_iota(jnp.int32, (tokens, lanes), 1) // group
    return key, key <= query


def forward_kernel(
    shift_ref, queries_ref, two_ref, one_ref, own_ref, cots_ref, diff_ref, meta_ref, pull_ref, bias_ref,
    low_ref, send_ref, keep_ref, hidden_ref, *, kv, group, tenants, rank, scaling, owned,
):
    tokens = own_ref.shape[1]
    dim = own_ref.shape[2]
    owner = meta_ref[1:2, :]
    lanes = owner.shape[1]
    _, here = places(lanes, tokens, group)
    windows = [
        jnp.concatenate([two_ref[place], one_ref[place], own_ref[place]], axis=0) for place in range(2 * kv)
    ]

    def weigh(scores):
        fold = jnp.where(here, scores[2 * tokens :], scores[0:tokens]) * scaling + bias_ref[0]
        mid = scores[tokens : 2 * tokens] * scaling + bias_ref[1]
        top = jnp.max(jnp.maximum(fold, mid), axis=0, keepdims=True)
        fold = jnp.exp(fold - top)
        mid = jnp.exp(mid - top)
        share = 1.0 / jnp.sum(fold + mid, axis=0, keepdims=True)
        fold = fold * share
        pieces = [jnp.where(here, 0.0, fold), mid * share, jnp.where(here, fold, 0.0)]
        return jnp.concatenate([piece.astype(LOW) for piece in pieces], axis=0)

    scores = dot(windows[0], queries_ref[0], 1, 1)
    for g in range(kv):
        ahead = dot(windows[g + 1], queries_ref[g + 1], 1, 1) if g + 1 < kv else None
        low = weigh(scores)
        low_ref[g] = low
        hidden_ref[g * dim : (g + 1) * dim, :] = dot(windows[kv + g], low, 0, 0).astype(LOW)
        scores = ahead
    hidden = hidden_ref[...]
    on_diff = dot(jnp.concatenate([diff_ref[g] for g in range(kv)], axis=1), hidden, 1, 0)
    lifted = own_terms(on_diff, owner, tenants, rank, group)
    one_hot = (owner == lax.broadcasted_iota(jnp.int32, (tenants, lanes), 0)).astype(WIDE)
    bias = jnp.concatenate([shift_ref[...]] * (8 // rank), axis=0)
    shift = dot(bias, one_hot, 1, 0, lax.Precision.HIGHEST)
    lifted = (lifted + shift).astype(LOW).astype(WIDE)
    rep = lax.axis_size("rep")
    me = lax.axis_index("ctx")
    per_group = group // owned
    span = tenants * rank
    slots = slots_of(lanes, group, owned)
    lift_all = jnp.concatenate(picked_rows(lifted, owner, slots, tenants, rank, group), axis=0)
    on_proj = dot(pull_ref[...], hidden, 1, 1)
    on_rot = dot(lift_all, jnp.concatenate([cots_ref[g] for g in range(kv)], axis=1), 1, 0) - on_proj
    here_rows = span // rep
    for g in range(kv):
        columns = slice(g * dim, (g + 1) * dim)
        for low in range(per_group):
            device = (g ^ (me // per_group)) * per_group + low
            into = send_ref if low % 2 else keep_ref
            for r in range(rep):
                pieces = []
                for h in range(low * owned, (low + 1) * owned):
                    rows = slice(h * span + r * here_rows, h * span + (r + 1) * here_rows)
                    pieces += [on_rot[rows, columns], on_proj[rows, columns]]
                into[reduce_place(dict(ctx=device, rep=r))] = jnp.concatenate(pieces, axis=0).astype(LOW)


def backward_kernel(
    queries_ref, gh_ref, two_ref, one_ref, own_ref, low_ref, dq_hbm, back_two_ref, back_one_ref, back_own_ref,
    dq_ref, sems, *, kv, group, scaling,
):
    tokens, dim = own_ref.shape[1:]
    windows = [
        jnp.concatenate([two_ref[place], one_ref[place], own_ref[place]], axis=0) for place in range(2 * kv)
    ]
    copies = []
    weight_grad = dot(windows[kv], gh_ref[0], 1, 1)
    for g in range(kv):
        ahead = dot(windows[kv + g + 1], gh_ref[g + 1], 1, 1) if g + 1 < kv else None
        weights = low_ref[g].astype(WIDE)
        delta = jnp.sum(weights * weight_grad, axis=0, keepdims=True)
        score_grad = (weights * (weight_grad - delta)).astype(LOW)
        query_grad = (dot(windows[g], score_grad, 0, 0) * scaling).T.reshape(tokens, group, dim)
        if g % 2 == 1:
            heads = slice((g - 1) * group, (g + 1) * group)
            dq_ref[:, heads, :] = jnp.concatenate([before, query_grad], axis=1).astype(LOW)
            copies.append(pltpu.make_async_copy(dq_ref.at[:, heads], dq_hbm.at[:, heads], sems.at[g // 2]))
            copies[-1].start()
        before = query_grad
        key_grad = dot(score_grad, queries_ref[g], 1, 0) * scaling
        value_grad = dot(low_ref[g], gh_ref[g], 1, 0)
        for place, grad in ((g, key_grad), (kv + g, value_grad)):
            back_two_ref[place] = grad[0:tokens].astype(LOW)
            back_one_ref[place] = grad[tokens : 2 * tokens].astype(LOW)
            back_own_ref[place] = grad[2 * tokens :]
        weight_grad = ahead
    for copy in copies:
        copy.wait()


def grads_kernel(part_ref, *refs, owned):
    total = part_ref[0].astype(WIDE)
    for other_ref in refs[:-2]:
        total = total + other_ref[0].astype(WIDE)
    size = refs[-1].shape[0]
    for place in range(owned):
        for at in range(2):
            row = (2 * place + at) * size
            refs[at - 2][:, place, :] = total[row : row + size]


def halo_kernel(own_ref, mate_ref, two_ref, keys_ref, values_ref, wide_ref, *, kv):
    tokens = own_ref.shape[1]
    even = (lax.axis_index("ctx") % 2 == 0).astype(WIDE)
    for at, out in enumerate((keys_ref, values_ref)):
        for m in range(kv):
            place = at * kv + m
            total = own_ref[place] + two_ref[place].astype(WIDE) + even * mate_ref[place].astype(WIDE)
            wide_ref[at, pl.ds(m, tokens, stride=kv), :] = total
        out[...] = wide_ref[at].astype(LOW)


def on_device(
    query_rows, key_rows, value_matrix, cotangent, rotation, projection, shift_bias, doc_starts, tenant_ids,
):
    queries = query_rows[0]
    upstream = cotangent[0]
    tokens, heads, dim = queries.shape
    kv = key_rows.shape[2]
    group = heads // kv
    scaling = dim ** (-0.5)
    tenants, rank = rotation.shape[0], rotation.shape[1]
    lanes = tokens * group
    ctx = lax.axis_size("ctx")
    rep = lax.axis_size("rep")
    assert 2 * tokens == DOC_MAX


    rot = rotation.reshape(tenants * rank, heads, dim)
    proj = projection.reshape(tenants * rank, heads, dim)
    sizes = dict(kv=kv, group=group)
    vmem = pl.BlockSpec(memory_space=pltpu.VMEM)

    def call(body, outs, flops, moved, out_specs=None, scratch=(), **fixed):
        def run(*operands):
            return pl.pallas_call(
                lambda *refs: body(*refs, **fixed),
                out_shape=[jax.ShapeDtypeStruct(*out) for out in outs],
                in_specs=[vmem] * len(operands),
                out_specs=out_specs or [vmem] * len(outs),
                scratch_shapes=scratch,
                compiler_params=pltpu.CompilerParams(vmem_limit_bytes=24 * 2**20),
                name=body.__name__,
                cost_estimate=pl.CostEstimate(flops=flops, bytes_accessed=moved, transcendentals=0),
            )(*operands)

        return run

    span = tenants * rank
    here = heads // ctx
    rows = here * 2 * span // rep
    own = jnp.moveaxis(jnp.concatenate([key_rows[0], value_matrix[0]], axis=1), 1, 0)
    even = lax.axis_index("ctx") % 2 == 0
    two = shifted(own, "ctx", 2)
    meta, biases = call(
        place_kernel, [((8, lanes), jnp.int32), ((2, tokens, lanes), WIDE)], 8 * 2**30, 2**20,
        group=group,
    )(doc_starts, tenant_ids)
    grad_hidden, diff, cots, queries, pull = call(
        pull_kernel,
        [
            ((kv, lanes, dim), LOW), ((kv, span * group, dim), LOW), ((kv, lanes, dim), LOW),
            ((kv, lanes, dim), LOW), ((span * group, lanes), LOW),
        ],
        2 * 2**30, 4 * 2**20, tenants=tenants, rank=rank, owned=here, **sizes,
    )(meta, upstream, rot, proj, queries)
    two, pull = lax.optimization_barrier((two, pull))
    one = exchanged(jnp.where(even, own, two), {"ctx": 1})
    low, send, keep = call(
        forward_kernel,
        [((kv, 3 * tokens, lanes), LOW)] + [((ctx * rep // 2, rows, dim), LOW)] * 2,
        4 * 2**30, 10 * 2**20, scratch=[pltpu.VMEM((heads // group * dim, lanes), LOW)],
        tenants=tenants, rank=rank, scaling=scaling, owned=here, **sizes,
    )(shift_bias.T, queries, two, one, own, cots, diff, meta, pull, biases)
    part = (keep.astype(WIDE) + exchanged(send, {"ctx": 1}).astype(WIDE)).astype(LOW)
    low, part = lax.optimization_barrier((low, part))
    d_queries, back_two, back_one, back_own = call(
        backward_kernel,
        [((tokens, heads, dim), LOW), (own.shape, LOW), (own.shape, LOW), (own.shape, WIDE)],
        4 * 2**30, 10 * 2**20,
        scratch=[
            pltpu.VMEM((tokens, heads, dim), LOW), pltpu.SemaphoreType.DMA((kv // 2,)),
        ],
        out_specs=[pl.BlockSpec(memory_space=pltpu.HBM), vmem, vmem, vmem], scaling=scaling, **sizes,
    )(queries, grad_hidden, two, one, own, low)
    from_mate = exchanged(back_one, {"ctx": 1})
    onward = back_two.astype(WIDE) + jnp.where(even, 0.0, from_mate.astype(WIDE))
    onward = onward.astype(LOW)

    groups = reduce_groups()
    for at, group_bits in enumerate(groups):
        beside = back_own if at == 0 else None
        if at == len(groups) - 1:
            part, onward = lax.optimization_barrier((part, onward))
            from_two = shifted(onward, "ctx", -2)
            beside = from_two
        part, others = scattered(part, group_bits, beside)
        if at < len(groups) - 1:
            part = part.astype(WIDE) + sum(other.astype(WIDE) for other in others)
            part = part.astype(LOW)
    grads = call(
        grads_kernel, [((span // rep, here, dim), WIDE)] * 2, 2**18, 2**18, owned=here,
    )(part, *others)
    grads = [grad.reshape(tenants // rep, rank, here, dim) for grad in grads]
    d_keys, d_values = call(
        halo_kernel, [((tokens * kv, dim), LOW)] * 2, 2**20, 2**20,
        scratch=[pltpu.VMEM((2, tokens * kv, dim), WIDE)], kv=kv,
    )(back_own, from_mate, from_two)
    d_keys, d_values = (grad.reshape(key_rows.shape) for grad in (d_keys, d_values))
    return (d_queries[None], d_keys, d_values, grads[0], grads[1])


def solution(mesh):
    rows = P("rep", "ctx", None, None)
    in_specs = (rows, rows, rows, rows, P(), P(), P(), P("rep", None), P("rep", None))
    tenant_rows = P("rep", None, "ctx", None)
    out_specs = (rows, rows, rows, tenant_rows, tenant_rows)
    return jax.shard_map(
        on_device, mesh=mesh, in_specs=in_specs, out_specs=out_specs, check_vma=False
    )
```

```python
import itertools

import jax
import jax.numpy as jnp
import numpy as np
from jax import lax
from jax.experimental import pallas as pl
from jax.experimental.pallas import tpu as pltpu
from jax.sharding import PartitionSpec as P

DOC_MAX = 256
LOW = jnp.bfloat16
WIDE = jnp.float32
far_below = -1e30


def shifted(value, axis, steps):
    count = lax.axis_size(axis)
    return lax.ppermute(value, axis, [(source, (source + steps) % count) for source in range(count)])


def exchanged(value, bits):
    axes = tuple(bits)
    shape = [lax.axis_size(axis) for axis in axes]
    pairs = []
    for source in np.ndindex(*shape):
        target = [at ^ bits[axis] for at, axis in zip(source, axes)]
        pairs.append((np.ravel_multi_index(source, shape), np.ravel_multi_index(target, shape)))
    return lax.ppermute(value, axes, [(int(source), int(target)) for source, target in pairs])


def reduce_groups():
    ctx, rep = lax.axis_size("ctx"), lax.axis_size("rep")
    bits = [{"ctx": 1 << at} for at in range(ctx.bit_length() - 2, 0, -1)]
    bits += [{"rep": 1 << at} for at in range(rep.bit_length() - 1)]
    return [bits[at : at + 2] for at in range(0, len(bits), 2)]


def reduce_place(index):
    place = 0
    for bits in itertools.chain(*reduce_groups()):
        for axis, bit in bits.items():
            place = 2 * place + (index[axis] // bit) % 2
    return place


def scattered(part, group, beside=None):
    count = 1 << len(group)
    size = part.shape[0] // count
    others = []
    for j in range(1, count):
        bits = {}
        for at, pair in enumerate(reversed(group)):
            if (j >> at) & 1:
                bits.update({axis: bits.get(axis, 0) | bit for axis, bit in pair.items()})
        others.append(exchanged(part[j * size : (j + 1) * size], bits))
    if beside is not None:
        others = lax.optimization_barrier((others, beside))[0]
    return part[:size], others


def dot(left, right, left_dim, right_dim, precision=None):
    return lax.dot_general(
        left, right, (((left_dim,), (right_dim,)), ((), ())),
        precision=precision, preferred_element_type=WIDE,
    )


def group_rows(ref, kv_count, group_size):
    rows, _, dim = ref.shape
    wide = 2 * group_size
    parts = []
    for pair in range(kv_count // 2):
        both = ref[:, pair * wide : (pair + 1) * wide, :].astype(WIDE)
        for half in range(2):
            one = both[:, half * group_size : (half + 1) * group_size, :]
            parts.append(one.reshape(rows * group_size, dim).astype(LOW))
    return parts


def lane_head(shape, group_size):
    return lax.broadcasted_iota(jnp.int32, shape, 1) % group_size


def own_terms(maps_by_rows, owner, tenants, low_rank, group_size):
    lanes = maps_by_rows.shape[1]
    same_head = lax.broadcasted_iota(jnp.int32, (group_size, lanes), 0) == lane_head(
        (group_size, lanes), group_size
    )
    span = low_rank * group_size
    total = jnp.zeros((low_rank, group_size, lanes), WIDE)
    for tenant in range(tenants):
        keep = same_head & (owner == tenant)
        block = maps_by_rows[tenant * span : (tenant + 1) * span].reshape(
            low_rank, group_size, lanes
        )
        total = total + jnp.where(keep[None], block, 0.0)
    rows = jnp.sum(total, axis=1)
    rows = jnp.concatenate([rows, rows], axis=0)
    tiles = lanes // 128
    stacked = jnp.concatenate([rows[:, c * 128 : (c + 1) * 128] for c in range(tiles)], axis=0)
    side = lax.broadcasted_iota(jnp.int32, (128, 128), 0) // group_size
    over = lax.broadcasted_iota(jnp.int32, (128, 128), 1) // group_size
    spread = dot(stacked, (side == over).astype(WIDE), 1, 0, lax.Precision.HIGHEST)
    return jnp.concatenate([spread[c * 8 : (c + 1) * 8] for c in range(tiles)], axis=1)


def place_kernel(starts_ref, owners_ref, meta_ref, bias_ref, *, group):
    lanes = meta_ref.shape[1]
    tokens = lanes // group
    row_first = lax.axis_index("ctx") * tokens
    mine = pl.ds(pl.multiple_of(row_first, tokens), tokens)
    row = lax.broadcasted_iota(jnp.int32, (8, tokens), 0)
    both = jnp.where(row == 0, starts_ref[:, mine] - row_first, owners_ref[:, mine]).astype(WIDE)
    repeat = lax.broadcasted_iota(jnp.int32, (tokens, lanes), 0) == (
        lax.broadcasted_iota(jnp.int32, (tokens, lanes), 1) // group
    )
    meta = dot(both, repeat.astype(WIDE), 1, 0, lax.Precision.HIGHEST).astype(jnp.int32)
    meta_ref[...] = meta
    first = meta[0:1, :]
    key, here = places(lanes, tokens, group)
    bias_ref[0] = jnp.where(jnp.where(here, key, key - 2 * tokens) >= first, 0.0, far_below)
    bias_ref[1] = jnp.where(key - tokens >= first, 0.0, far_below)


def slots_of(lanes, group, owned):
    per_group = group // owned
    head = lane_head((1, lanes), group)
    return head ^ ((lax.axis_index("ctx") % per_group) * owned)


def tenants_of(lanes, tenants, rank):
    row = lax.broadcasted_iota(jnp.int32, (tenants * rank, lanes), 0) // rank
    return row ^ (lax.axis_index("rep") * (tenants // lax.axis_size("rep")))


def picked_rows(rows, owner, slots, tenants, rank, group):
    lanes = owner.shape[1]
    mine = owner == tenants_of(lanes, tenants, rank)
    rows = jnp.where(mine, jnp.concatenate([rows] * (tenants * rank // 8), axis=0), 0.0)
    return [jnp.where(slots == h, rows, 0.0).astype(LOW) for h in range(group)]


def pull_kernel(
    meta_ref, cot_ref, rot_ref, proj_ref, q_ref, gh_ref, diff_ref, cots_ref, queries_ref, pull_ref,
    *, kv, group, tenants, rank, owned,
):
    lanes = meta_ref.shape[1]
    owner = meta_ref[1:2, :]
    cots = group_rows(cot_ref, kv, group)
    rots = group_rows(rot_ref, kv, group)
    on_rot = dot(jnp.concatenate(rots, axis=1), jnp.concatenate(cots, axis=1), 1, 1)
    pulled = own_terms(on_rot, owner, tenants, rank, group).astype(LOW).astype(WIDE)
    same_head = lax.broadcasted_iota(jnp.int32, (group, lanes), 0) == lane_head((group, lanes), group)
    picked = []
    for tenant in range(tenants):
        keep = same_head & (owner == tenant)
        for k in range(rank):
            picked.append(jnp.where(keep, pulled[k : k + 1], 0.0))
    picked = jnp.concatenate(picked, axis=0).T.astype(LOW)
    projs = group_rows(proj_ref, kv, group)
    for g in range(kv):
        diff = (projs[g].astype(WIDE) - rots[g].astype(WIDE)).astype(LOW)
        diff_ref[g] = diff
        gh_ref[g] = (cots[g].astype(WIDE) + dot(picked, diff, 1, 0)).astype(LOW)
        cots_ref[g] = cots[g]
    for g, rows in enumerate(group_rows(q_ref, kv, group)):
        queries_ref[g] = rows
    span = tenants * rank
    slots = slots_of(lanes, group, owned)
    for h, rows in enumerate(picked_rows(pulled, owner, slots, tenants, rank, group)):
        pull_ref[h * span : (h + 1) * span, :] = rows


def places(lanes, tokens, group):
    key = lax.broadcasted_iota(jnp.int32, (tokens, lanes), 0)
    query = lax.broadcasted_iota(jnp.int32, (tokens, lanes), 1) // group
    return key, key <= query


def forward_kernel(
    shift_ref, queries_ref, two_ref, one_ref, own_ref, cots_ref, diff_ref, meta_ref, pull_ref, bias_ref,
    low_ref, send_ref, keep_ref, hidden_ref, *, kv, group, tenants, rank, scaling, owned,
):
    tokens = own_ref.shape[1]
    dim = own_ref.shape[2]
    owner = meta_ref[1:2, :]
    lanes = owner.shape[1]
    _, here = places(lanes, tokens, group)
    windows = [
        jnp.concatenate([two_ref[place], one_ref[place], own_ref[place]], axis=0) for place in range(2 * kv)
    ]

    def weigh(scores):
        fold = jnp.where(here, scores[2 * tokens :], scores[0:tokens]) * scaling + bias_ref[0]
        mid = scores[tokens : 2 * tokens] * scaling + bias_ref[1]
        top = jnp.max(jnp.maximum(fold, mid), axis=0, keepdims=True)
        fold = jnp.exp(fold - top)
        mid = jnp.exp(mid - top)
        share = 1.0 / jnp.sum(fold + mid, axis=0, keepdims=True)
        fold = fold * share
        pieces = [jnp.where(here, 0.0, fold), mid * share, jnp.where(here, fold, 0.0)]
        return jnp.concatenate([piece.astype(LOW) for piece in pieces], axis=0)

    scores = dot(windows[0], queries_ref[0], 1, 1)
    for g in range(kv):
        ahead = dot(windows[g + 1], queries_ref[g + 1], 1, 1) if g + 1 < kv else None
        low = weigh(scores)
        low_ref[g] = low
        hidden_ref[g * dim : (g + 1) * dim, :] = dot(windows[kv + g], low, 0, 0).astype(LOW)
        scores = ahead
    hidden = hidden_ref[...]
    on_diff = dot(jnp.concatenate([diff_ref[g] for g in range(kv)], axis=1), hidden, 1, 0)
    lifted = own_terms(on_diff, owner, tenants, rank, group)
    one_hot = (owner == lax.broadcasted_iota(jnp.int32, (tenants, lanes), 0)).astype(WIDE)
    bias = jnp.concatenate([shift_ref[...]] * (8 // rank), axis=0)
    shift = dot(bias, one_hot, 1, 0, lax.Precision.HIGHEST)
    lifted = (lifted + shift).astype(LOW).astype(WIDE)
    rep = lax.axis_size("rep")
    me = lax.axis_index("ctx")
    per_group = group // owned
    span = tenants * rank
    slots = slots_of(lanes, group, owned)
    lift_all = jnp.concatenate(picked_rows(lifted, owner, slots, tenants, rank, group), axis=0)
    on_proj = dot(pull_ref[...], hidden, 1, 1)
    on_rot = dot(lift_all, jnp.concatenate([cots_ref[g] for g in range(kv)], axis=1), 1, 0) - on_proj
    here_rows = span // rep
    for g in range(kv):
        columns = slice(g * dim, (g + 1) * dim)
        for low in range(per_group):
            device = (g ^ (me // per_group)) * per_group + low
            into = send_ref if low % 2 else keep_ref
            for r in range(rep):
                pieces = []
                for h in range(low * owned, (low + 1) * owned):
                    rows = slice(h * span + r * here_rows, h * span + (r + 1) * here_rows)
                    pieces += [on_rot[rows, columns], on_proj[rows, columns]]
                into[reduce_place(dict(ctx=device, rep=r))] = jnp.concatenate(pieces, axis=0).astype(LOW)


def backward_kernel(
    queries_ref, gh_ref, two_ref, one_ref, own_ref, low_ref, dq_hbm, back_two_ref, back_one_ref, back_own_ref,
    dq_ref, sems, *, kv, group, scaling,
):
    tokens, dim = own_ref.shape[1:]
    windows = [
        jnp.concatenate([two_ref[place], one_ref[place], own_ref[place]], axis=0) for place in range(2 * kv)
    ]
    copies = []
    weight_grad = dot(windows[kv], gh_ref[0], 1, 1)
    for g in range(kv):
        ahead = dot(windows[kv + g + 1], gh_ref[g + 1], 1, 1) if g + 1 < kv else None
        weights = low_ref[g].astype(WIDE)
        delta = jnp.sum(weights * weight_grad, axis=0, keepdims=True)
        score_grad = (weights * (weight_grad - delta)).astype(LOW)
        query_grad = (dot(windows[g], score_grad, 0, 0) * scaling).T.reshape(tokens, group, dim)
        if g % 2 == 1:
            heads = slice((g - 1) * group, (g + 1) * group)
            dq_ref[:, heads, :] = jnp.concatenate([before, query_grad], axis=1).astype(LOW)
            copies.append(pltpu.make_async_copy(dq_ref.at[:, heads], dq_hbm.at[:, heads], sems.at[g // 2]))
            copies[-1].start()
        before = query_grad
        key_grad = dot(score_grad, queries_ref[g], 1, 0) * scaling
        value_grad = dot(low_ref[g], gh_ref[g], 1, 0)
        for place, grad in ((g, key_grad), (kv + g, value_grad)):
            back_two_ref[place] = grad[0:tokens].astype(LOW)
            back_one_ref[place] = grad[tokens : 2 * tokens].astype(LOW)
            back_own_ref[place] = grad[2 * tokens :]
        weight_grad = ahead
    for copy in copies:
        copy.wait()


def finish_kernel(
    own_ref, mate_ref, two_ref, part_ref, *refs, kv, owned,
):
    *other_refs, keys_ref, values_ref, rot_ref, proj_ref, wide_ref = refs
    total = part_ref[0].astype(WIDE)
    for other_ref in other_refs:
        total = total + other_ref[0].astype(WIDE)
    size = rot_ref.shape[0]
    for place in range(owned):
        for at, out in enumerate((rot_ref, proj_ref)):
            row = (2 * place + at) * size
            out[:, place, :] = total[row : row + size]
    tokens = own_ref.shape[1]
    even = (lax.axis_index("ctx") % 2 == 0).astype(WIDE)
    for at, out in enumerate((keys_ref, values_ref)):
        for m in range(kv):
            place = at * kv + m
            total = own_ref[place] + two_ref[place].astype(WIDE) + even * mate_ref[place].astype(WIDE)
            wide_ref[at, pl.ds(m, tokens, stride=kv), :] = total
        out[...] = wide_ref[at].astype(LOW)


def on_device(
    query_rows, key_rows, value_matrix, cotangent, rotation, projection, shift_bias, doc_starts, tenant_ids,
):
    queries = query_rows[0]
    upstream = cotangent[0]
    tokens, heads, dim = queries.shape
    kv = key_rows.shape[2]
    group = heads // kv
    scaling = dim ** (-0.5)
    tenants, rank = rotation.shape[0], rotation.shape[1]
    lanes = tokens * group
    ctx = lax.axis_size("ctx")
    rep = lax.axis_size("rep")
    assert 2 * tokens == DOC_MAX


    rot = rotation.reshape(tenants * rank, heads, dim)
    proj = projection.reshape(tenants * rank, heads, dim)
    sizes = dict(kv=kv, group=group)
    vmem = pl.BlockSpec(memory_space=pltpu.VMEM)

    def call(body, outs, flops, moved, out_specs=None, scratch=(), **fixed):
        def run(*operands):
            return pl.pallas_call(
                lambda *refs: body(*refs, **fixed),
                out_shape=[jax.ShapeDtypeStruct(*out) for out in outs],
                in_specs=[vmem] * len(operands),
                out_specs=out_specs or [vmem] * len(outs),
                scratch_shapes=scratch,
                compiler_params=pltpu.CompilerParams(vmem_limit_bytes=24 * 2**20),
                name=body.__name__,
                cost_estimate=pl.CostEstimate(flops=flops, bytes_accessed=moved, transcendentals=0),
            )(*operands)

        return run

    span = tenants * rank
    here = heads // ctx
    rows = here * 2 * span // rep
    own = jnp.moveaxis(jnp.concatenate([key_rows[0], value_matrix[0]], axis=1), 1, 0)
    even = lax.axis_index("ctx") % 2 == 0
    two = shifted(own, "ctx", 2)
    meta, biases = call(
        place_kernel, [((8, lanes), jnp.int32), ((2, tokens, lanes), WIDE)], 8 * 2**30, 2**20,
        group=group,
    )(doc_starts, tenant_ids)
    grad_hidden, diff, cots, queries, pull = call(
        pull_kernel,
        [
            ((kv, lanes, dim), LOW), ((kv, span * group, dim), LOW), ((kv, lanes, dim), LOW),
            ((kv, lanes, dim), LOW), ((span * group, lanes), LOW),
        ],
        2 * 2**30, 4 * 2**20, tenants=tenants, rank=rank, owned=here, **sizes,
    )(meta, upstream, rot, proj, queries)
    two, pull = lax.optimization_barrier((two, pull))
    one = exchanged(jnp.where(even, own, two), {"ctx": 1})
    low, send, keep = call(
        forward_kernel,
        [((kv, 3 * tokens, lanes), LOW)] + [((ctx * rep // 2, rows, dim), LOW)] * 2,
        4 * 2**30, 10 * 2**20, scratch=[pltpu.VMEM((heads // group * dim, lanes), LOW)],
        tenants=tenants, rank=rank, scaling=scaling, owned=here, **sizes,
    )(shift_bias.T, queries, two, one, own, cots, diff, meta, pull, biases)
    part = (keep.astype(WIDE) + exchanged(send, {"ctx": 1}).astype(WIDE)).astype(LOW)
    low, part = lax.optimization_barrier((low, part))
    d_queries, back_two, back_one, back_own = call(
        backward_kernel,
        [((tokens, heads, dim), LOW), (own.shape, LOW), (own.shape, LOW), (own.shape, WIDE)],
        4 * 2**30, 10 * 2**20,
        scratch=[
            pltpu.VMEM((tokens, heads, dim), LOW), pltpu.SemaphoreType.DMA((kv // 2,)),
        ],
        out_specs=[pl.BlockSpec(memory_space=pltpu.HBM), vmem, vmem, vmem], scaling=scaling, **sizes,
    )(queries, grad_hidden, two, one, own, low)
    from_mate = exchanged(back_one, {"ctx": 1})
    onward = back_two.astype(WIDE) + jnp.where(even, 0.0, from_mate.astype(WIDE))
    onward = onward.astype(LOW)

    groups = reduce_groups()
    for at, group_bits in enumerate(groups):
        beside = back_own if at == 0 else None
        if at == len(groups) - 1:
            part, onward = lax.optimization_barrier((part, onward))
            from_two = shifted(onward, "ctx", -2)
            beside = from_two
        part, others = scattered(part, group_bits, beside)
        if at < len(groups) - 1:
            part = part.astype(WIDE) + sum(other.astype(WIDE) for other in others)
            part = part.astype(LOW)
    d_keys, d_values, *grads = call(
        finish_kernel, [((tokens * kv, dim), LOW)] * 2 + [((span // rep, here, dim), WIDE)] * 2, 2**20, 2**20,
        scratch=[pltpu.VMEM((2, tokens * kv, dim), WIDE)], kv=kv, owned=here,
    )(back_own, from_mate, from_two, part, *others)
    grads = [grad.reshape(tenants // rep, rank, here, dim) for grad in grads]
    d_keys, d_values = (grad.reshape(key_rows.shape) for grad in (d_keys, d_values))
    return (d_queries[None], d_keys, d_values, grads[0], grads[1])


def solution(mesh):
    rows = P("rep", "ctx", None, None)
    in_specs = (rows, rows, rows, rows, P(), P(), P(), P("rep", None), P("rep", None))
    tenant_rows = P("rep", None, "ctx", None)
    out_specs = (rows, rows, rows, tenant_rows, tenant_rows)
    return jax.shard_map(
        on_device, mesh=mesh, in_specs=in_specs, out_specs=out_specs, check_vma=False
    )
```

```python
import itertools

import jax
import jax.numpy as jnp
import numpy as np
from jax import lax
from jax.experimental import pallas as pl
from jax.experimental.pallas import tpu as pltpu
from jax.sharding import PartitionSpec as P

DOC_MAX = 256
LOW = jnp.bfloat16
WIDE = jnp.float32
far_below = -1e30


def shifted(value, axis, steps):
    count = lax.axis_size(axis)
    return lax.ppermute(value, axis, [(source, (source + steps) % count) for source in range(count)])


def exchanged(value, bits):
    axes = tuple(bits)
    shape = [lax.axis_size(axis) for axis in axes]
    pairs = []
    for source in np.ndindex(*shape):
        target = [at ^ bits[axis] for at, axis in zip(source, axes)]
        pairs.append((np.ravel_multi_index(source, shape), np.ravel_multi_index(target, shape)))
    return lax.ppermute(value, axes, [(int(source), int(target)) for source, target in pairs])


def reduce_groups():
    ctx, rep = lax.axis_size("ctx"), lax.axis_size("rep")
    bits = [{"ctx": 1 << at} for at in range(ctx.bit_length() - 2, 0, -1)]
    bits += [{"rep": 1 << at} for at in range(rep.bit_length() - 1)]
    return [bits[at : at + 2] for at in range(0, len(bits), 2)]


def reduce_place(index):
    place = 0
    for bits in itertools.chain(*reduce_groups()):
        for axis, bit in bits.items():
            place = 2 * place + (index[axis] // bit) % 2
    return place


def scattered(part, group, beside=None):
    count = 1 << len(group)
    size = part.shape[0] // count
    others = []
    for j in range(1, count):
        bits = {}
        for at, pair in enumerate(reversed(group)):
            if (j >> at) & 1:
                bits.update({axis: bits.get(axis, 0) | bit for axis, bit in pair.items()})
        others.append(exchanged(part[j * size : (j + 1) * size], bits))
    if beside is not None:
        others = lax.optimization_barrier((others, beside))[0]
    return part[:size], others


def dot(left, right, left_dim, right_dim, precision=None):
    return lax.dot_general(
        left, right, (((left_dim,), (right_dim,)), ((), ())),
        precision=precision, preferred_element_type=WIDE,
    )


def group_rows(ref, kv_count, group_size):
    rows, _, dim = ref.shape
    wide = 2 * group_size
    parts = []
    for pair in range(kv_count // 2):
        both = ref[:, pair * wide : (pair + 1) * wide, :].astype(WIDE)
        for half in range(2):
            one = both[:, half * group_size : (half + 1) * group_size, :]
            parts.append(one.reshape(rows * group_size, dim).astype(LOW))
    return parts


def lane_head(shape, group_size):
    return lax.broadcasted_iota(jnp.int32, shape, 1) % group_size


def own_terms(maps_by_rows, owner, tenants, low_rank, group_size):
    lanes = maps_by_rows.shape[1]
    same_head = lax.broadcasted_iota(jnp.int32, (group_size, lanes), 0) == lane_head(
        (group_size, lanes), group_size
    )
    span = low_rank * group_size
    total = jnp.zeros((low_rank, group_size, lanes), WIDE)
    for tenant in range(tenants):
        keep = same_head & (owner == tenant)
        block = maps_by_rows[tenant * span : (tenant + 1) * span].reshape(
            low_rank, group_size, lanes
        )
        total = total + jnp.where(keep[None], block, 0.0)
    rows = jnp.sum(total, axis=1)
    rows = jnp.concatenate([rows, rows], axis=0)
    tiles = lanes // 128
    stacked = jnp.concatenate([rows[:, c * 128 : (c + 1) * 128] for c in range(tiles)], axis=0)
    side = lax.broadcasted_iota(jnp.int32, (128, 128), 0) // group_size
    over = lax.broadcasted_iota(jnp.int32, (128, 128), 1) // group_size
    spread = dot(stacked, (side == over).astype(WIDE), 1, 0, lax.Precision.HIGHEST)
    return jnp.concatenate([spread[c * 8 : (c + 1) * 8] for c in range(tiles)], axis=1)


def place_kernel(starts_ref, owners_ref, meta_ref, bias_ref, *, group):
    lanes = meta_ref.shape[1]
    tokens = lanes // group
    row_first = lax.axis_index("ctx") * tokens
    mine = pl.ds(pl.multiple_of(row_first, tokens), tokens)
    row = lax.broadcasted_iota(jnp.int32, (8, tokens), 0)
    both = jnp.where(row == 0, starts_ref[:, mine] - row_first, owners_ref[:, mine]).astype(WIDE)
    repeat = lax.broadcasted_iota(jnp.int32, (tokens, lanes), 0) == (
        lax.broadcasted_iota(jnp.int32, (tokens, lanes), 1) // group
    )
    meta = dot(both, repeat.astype(WIDE), 1, 0, lax.Precision.HIGHEST).astype(jnp.int32)
    meta_ref[...] = meta
    first = meta[0:1, :]
    key, here = places(lanes, tokens, group)
    bias_ref[0] = jnp.where(jnp.where(here, key, key - 2 * tokens) >= first, 0.0, far_below)
    bias_ref[1] = jnp.where(key - tokens >= first, 0.0, far_below)


def slots_of(lanes, group, owned):
    per_group = group // owned
    head = lane_head((1, lanes), group)
    return head ^ ((lax.axis_index("ctx") % per_group) * owned)


def tenants_of(lanes, tenants, rank):
    row = lax.broadcasted_iota(jnp.int32, (tenants * rank, lanes), 0) // rank
    return row ^ (lax.axis_index("rep") * (tenants // lax.axis_size("rep")))


def picked_rows(rows, owner, slots, tenants, rank, group):
    lanes = owner.shape[1]
    mine = owner == tenants_of(lanes, tenants, rank)
    rows = jnp.where(mine, jnp.concatenate([rows] * (tenants * rank // 8), axis=0), 0.0)
    return [jnp.where(slots == h, rows, 0.0).astype(LOW) for h in range(group)]


def pull_kernel(
    meta_ref, cot_ref, rot_ref, q_ref, cots_ref, queries_ref, pulled_ref, pull_ref,
    *, kv, group, tenants, rank, owned,
):
    owner = meta_ref[1:2, :]
    lanes = owner.shape[1]
    cots = group_rows(cot_ref, kv, group)
    rots = group_rows(rot_ref, kv, group)
    on_rot = dot(jnp.concatenate(rots, axis=1), jnp.concatenate(cots, axis=1), 1, 1)
    pulled = own_terms(on_rot, owner, tenants, rank, group).astype(LOW).astype(WIDE)
    pulled_ref[...] = pulled
    for g, rows in enumerate(group_rows(q_ref, kv, group)):
        queries_ref[g] = rows
        cots_ref[g] = cots[g]
    span = tenants * rank
    slots = slots_of(lanes, group, owned)
    for h, rows in enumerate(picked_rows(pulled, owner, slots, tenants, rank, group)):
        pull_ref[h * span : (h + 1) * span, :] = rows


def hidden_grad_kernel(
    meta_ref, pulled_ref, cots_ref, rot_ref, proj_ref, gh_ref, diff_ref, *, kv, group, tenants, rank,
):
    owner = meta_ref[1:2, :]
    lanes = owner.shape[1]
    dim = cots_ref.shape[2]
    pulled = pulled_ref[...]
    same_head = lax.broadcasted_iota(jnp.int32, (group, lanes), 0) == lane_head((group, lanes), group)
    picked = []
    for tenant in range(tenants):
        keep = same_head & (owner == tenant)
        for k in range(rank):
            picked.append(jnp.where(keep, pulled[k : k + 1], 0.0))
    picked = jnp.concatenate(picked, axis=0).T.astype(LOW)
    rots = group_rows(rot_ref, kv, group)
    projs = group_rows(proj_ref, kv, group)
    diffs = [(proj.astype(WIDE) - rot.astype(WIDE)).astype(LOW) for proj, rot in zip(projs, rots)]
    steered = dot(picked, jnp.concatenate(diffs, axis=1), 1, 0)
    for g in range(kv):
        diff_ref[g] = diffs[g]
        gh_ref[g] = (cots_ref[g].astype(WIDE) + steered[:, g * dim : (g + 1) * dim]).astype(LOW)


def places(lanes, tokens, group):
    key = lax.broadcasted_iota(jnp.int32, (tokens, lanes), 0)
    query = lax.broadcasted_iota(jnp.int32, (tokens, lanes), 1) // group
    return key, key <= query


def window_of(two_ref, one_ref, own_ref, head):
    return jnp.concatenate([two_ref[head], one_ref[head], own_ref[head]], axis=0)


def score_kernel(queries_ref, two_ref, one_ref, own_ref, bias_ref, low_ref, *, group, scaling, first):
    tokens = own_ref.shape[1]
    _, here = places(queries_ref.shape[1], tokens, group)
    count = low_ref.shape[0]

    def scores_of(at):
        return dot(window_of(two_ref, one_ref, own_ref, first + at), queries_ref[first + at], 1, 1)

    scores = scores_of(0)
    for at in range(count):
        ahead = scores_of(at + 1) if at + 1 < count else None
        fold = jnp.where(here, scores[2 * tokens :], scores[0:tokens]) * scaling + bias_ref[0]
        mid = scores[tokens : 2 * tokens] * scaling + bias_ref[1]
        top = jnp.max(jnp.maximum(fold, mid), axis=0, keepdims=True)
        fold = jnp.exp(fold - top)
        mid = jnp.exp(mid - top)
        share = 1.0 / jnp.sum(fold + mid, axis=0, keepdims=True)
        fold = fold * share
        pieces = [jnp.where(here, 0.0, fold), mid * share, jnp.where(here, fold, 0.0)]
        low_ref[at] = jnp.concatenate([piece.astype(LOW) for piece in pieces], axis=0)
        scores = ahead


def forward_kernel(
    shift_ref, near_ref, far_ref, two_ref, one_ref, own_ref, cots_ref, diff_ref, meta_ref, pull_ref,
    send_ref, keep_ref, *, kv, group, tenants, rank, owned,
):
    dim = own_ref.shape[2]
    owner = meta_ref[1:2, :]
    lanes = owner.shape[1]
    hidden = []
    for g in range(kv):
        low = (near_ref if g < kv // 2 else far_ref)[g % (kv // 2)]
        hidden.append(dot(window_of(two_ref, one_ref, own_ref, g), low, 0, 0).astype(LOW))
    hidden = jnp.concatenate(hidden, axis=0)
    on_diff = dot(jnp.concatenate([diff_ref[g] for g in range(kv)], axis=1), hidden, 1, 0)
    lifted = own_terms(on_diff, owner, tenants, rank, group)
    one_hot = (owner == lax.broadcasted_iota(jnp.int32, (tenants, lanes), 0)).astype(WIDE)
    bias = jnp.concatenate([shift_ref[...]] * (8 // rank), axis=0)
    shift = dot(bias, one_hot, 1, 0, lax.Precision.HIGHEST)
    lifted = (lifted + shift).astype(LOW).astype(WIDE)
    rep = lax.axis_size("rep")
    me = lax.axis_index("ctx")
    per_group = group // owned
    span = tenants * rank
    slots = slots_of(lanes, group, owned)
    lift_all = jnp.concatenate(picked_rows(lifted, owner, slots, tenants, rank, group), axis=0)
    on_proj = dot(pull_ref[...], hidden, 1, 1)
    on_rot = dot(lift_all, jnp.concatenate([cots_ref[g] for g in range(kv)], axis=1), 1, 0) - on_proj
    here_rows = span // rep
    for g in range(kv):
        columns = slice(g * dim, (g + 1) * dim)
        for low in range(per_group):
            device = (g ^ (me // per_group)) * per_group + low
            into = send_ref if low % 2 else keep_ref
            for r in range(rep):
                pieces = []
                for h in range(low * owned, (low + 1) * owned):
                    rows = slice(h * span + r * here_rows, h * span + (r + 1) * here_rows)
                    pieces += [on_rot[rows, columns], on_proj[rows, columns]]
                into[reduce_place(dict(ctx=device, rep=r))] = jnp.concatenate(pieces, axis=0).astype(LOW)


def backward_kernel(
    queries_ref, gh_ref, near_ref, far_ref, two_keys, one_keys, own_keys, two_values, one_values, own_values,
    dq_hbm, back_two_ref, back_one_ref, back_own_ref, dq_ref, sems, *, kv, group, scaling,
):
    tokens, dim = own_keys.shape[1:]

    def weight_grad_of(g):
        return dot(window_of(two_values, one_values, own_values, g), gh_ref[g], 1, 1)

    copies = []
    weight_grad = weight_grad_of(0)
    for g in range(kv):
        ahead = weight_grad_of(g + 1) if g + 1 < kv else None
        low = (near_ref if g < kv // 2 else far_ref)[g % (kv // 2)]
        weights = low.astype(WIDE)
        delta = jnp.sum(weights * weight_grad, axis=0, keepdims=True)
        score_grad = (weights * (weight_grad - delta)).astype(LOW)
        query_grad = (dot(window_of(two_keys, one_keys, own_keys, g), score_grad, 0, 0) * scaling).T.reshape(tokens, group, dim)
        if g % 2 == 1:
            heads = slice((g - 1) * group, (g + 1) * group)
            dq_ref[:, heads, :] = jnp.concatenate([before, query_grad], axis=1).astype(LOW)
            copies.append(pltpu.make_async_copy(dq_ref.at[:, heads], dq_hbm.at[:, heads], sems.at[g // 2]))
            copies[-1].start()
        before = query_grad
        key_grad = dot(score_grad, queries_ref[g], 1, 0) * scaling
        value_grad = dot(low, gh_ref[g], 1, 0)
        for place, grad in ((g, key_grad), (kv + g, value_grad)):
            back_two_ref[place] = grad[0:tokens].astype(LOW)
            back_one_ref[place] = grad[tokens : 2 * tokens].astype(LOW)
            back_own_ref[place] = grad[2 * tokens :]
        weight_grad = ahead
    for copy in copies:
        copy.wait()


def finish_kernel(
    own_ref, mate_ref, two_ref, part_ref, *refs, kv, owned,
):
    *other_refs, keys_ref, values_ref, rot_ref, proj_ref, wide_ref = refs
    total = part_ref[0].astype(WIDE)
    for other_ref in other_refs:
        total = total + other_ref[0].astype(WIDE)
    size = rot_ref.shape[0]
    for place in range(owned):
        for at, out in enumerate((rot_ref, proj_ref)):
            row = (2 * place + at) * size
            out[:, place, :] = total[row : row + size]
    tokens = own_ref.shape[1]
    even = (lax.axis_index("ctx") % 2 == 0).astype(WIDE)
    for at, out in enumerate((keys_ref, values_ref)):
        for m in range(kv):
            place = at * kv + m
            total = own_ref[place] + two_ref[place].astype(WIDE) + even * mate_ref[place].astype(WIDE)
            wide_ref[at, pl.ds(m, tokens, stride=kv), :] = total
        out[...] = wide_ref[at].astype(LOW)


def on_device(
    query_rows, key_rows, value_matrix, cotangent, rotation, projection, shift_bias, doc_starts, tenant_ids,
):
    queries = query_rows[0]
    upstream = cotangent[0]
    tokens, heads, dim = queries.shape
    kv = key_rows.shape[2]
    group = heads // kv
    scaling = dim ** (-0.5)
    tenants, rank = rotation.shape[0], rotation.shape[1]
    lanes = tokens * group
    ctx = lax.axis_size("ctx")
    rep = lax.axis_size("rep")
    assert 2 * tokens == DOC_MAX


    rot = rotation.reshape(tenants * rank, heads, dim)
    proj = projection.reshape(tenants * rank, heads, dim)
    sizes = dict(kv=kv, group=group)
    vmem = pl.BlockSpec(memory_space=pltpu.VMEM)

    def call(body, outs, flops, moved, out_specs=None, scratch=(), **fixed):
        def run(*operands):
            return pl.pallas_call(
                lambda *refs: body(*refs, **fixed),
                out_shape=[jax.ShapeDtypeStruct(*out) for out in outs],
                in_specs=[vmem] * len(operands),
                out_specs=out_specs or [vmem] * len(outs),
                scratch_shapes=scratch,
                compiler_params=pltpu.CompilerParams(vmem_limit_bytes=12 * 2**20),
                name=body.__name__,
                cost_estimate=pl.CostEstimate(flops=flops, bytes_accessed=moved, transcendentals=0),
            )(*operands)

        return run

    span = tenants * rank
    here = heads // ctx
    rows = here * 2 * span // rep
    own_keys = lax.optimization_barrier(jnp.moveaxis(key_rows[0], 1, 0))
    even = lax.axis_index("ctx") % 2 == 0
    two_keys = shifted(own_keys, "ctx", 2)
    meta, biases = call(
        place_kernel, [((8, lanes), jnp.int32), ((2, tokens, lanes), WIDE)], 8 * 2**30, 2**20,
        group=group,
    )(doc_starts, tenant_ids)
    own_values, meta = lax.optimization_barrier((jnp.moveaxis(value_matrix[0], 1, 0), meta))
    two_values = shifted(own_values, "ctx", 2)
    cots, queries, pulled, pull = call(
        pull_kernel,
        [((kv, lanes, dim), LOW), ((kv, lanes, dim), LOW), ((8, lanes), WIDE), ((span * group, lanes), LOW)],
        2**30, 4 * 2**20, tenants=tenants, rank=rank, owned=here, **sizes,
    )(meta, upstream, rot, queries)
    two_keys, pulled = lax.optimization_barrier((two_keys, pulled))
    one_keys = exchanged(jnp.where(even, own_keys, two_keys), {"ctx": 1})
    grad_hidden, diff = call(
        hidden_grad_kernel, [((kv, lanes, dim), LOW), ((kv, span * group, dim), LOW)],
        2 * 2**30, 4 * 2**20, tenants=tenants, rank=rank, **sizes,
    )(meta, pulled, cots, rot, proj)
    one_keys, grad_hidden = lax.optimization_barrier((one_keys, grad_hidden))

    def weights_of(first):
        return call(
            score_kernel, [((kv // 2, 3 * tokens, lanes), LOW)], 2 * 2**30, 4 * 2**20,
            group=group, scaling=scaling, first=first,
        )(queries, two_keys, one_keys, own_keys, biases)[0]

    near = weights_of(0)
    two_values, near = lax.optimization_barrier((two_values, near))
    one_values = exchanged(jnp.where(even, own_values, two_values), {"ctx": 1})
    far = weights_of(kv // 2)
    one_values, far = lax.optimization_barrier((one_values, far))
    send, keep = call(
        forward_kernel, [((ctx * rep // 2, rows, dim), LOW)] * 2, 4 * 2**30, 10 * 2**20,
        tenants=tenants, rank=rank, owned=here, **sizes,
    )(shift_bias.T, near, far, two_values, one_values, own_values, cots, diff, meta, pull)
    part = (keep.astype(WIDE) + exchanged(send, {"ctx": 1}).astype(WIDE)).astype(LOW)
    near, part = lax.optimization_barrier((near, part))
    window = (2 * kv, tokens, dim)
    d_queries, back_two, back_one, back_own = call(
        backward_kernel,
        [((tokens, heads, dim), LOW), (window, LOW), (window, LOW), (window, WIDE)],
        4 * 2**30, 10 * 2**20,
        scratch=[
            pltpu.VMEM((tokens, heads, dim), LOW), pltpu.SemaphoreType.DMA((kv // 2,)),
        ],
        out_specs=[pl.BlockSpec(memory_space=pltpu.HBM), vmem, vmem, vmem], scaling=scaling, **sizes,
    )(
        queries, grad_hidden, near, far, two_keys, one_keys, own_keys, two_values, one_values, own_values,
    )
    from_mate = exchanged(back_one, {"ctx": 1})
    onward = back_two.astype(WIDE) + jnp.where(even, 0.0, from_mate.astype(WIDE))
    onward = onward.astype(LOW)

    groups = reduce_groups()
    for at, group_bits in enumerate(groups):
        beside = back_own if at == 0 else None
        if at == len(groups) - 1:
            part, onward = lax.optimization_barrier((part, onward))
            from_two = shifted(onward, "ctx", -2)
            beside = from_two
        part, others = scattered(part, group_bits, beside)
        if at < len(groups) - 1:
            part = part.astype(WIDE) + sum(other.astype(WIDE) for other in others)
            part = part.astype(LOW)
    d_keys, d_values, *grads = call(
        finish_kernel, [((tokens * kv, dim), LOW)] * 2 + [((span // rep, here, dim), WIDE)] * 2, 2**20, 2**20,
        scratch=[pltpu.VMEM((2, tokens * kv, dim), WIDE)], kv=kv, owned=here,
    )(back_own, from_mate, from_two, part, *others)
    grads = [grad.reshape(tenants // rep, rank, here, dim) for grad in grads]
    d_keys, d_values = (grad.reshape(key_rows.shape) for grad in (d_keys, d_values))
    return (d_queries[None], d_keys, d_values, grads[0], grads[1])


def solution(mesh):
    rows = P("rep", "ctx", None, None)
    in_specs = (rows, rows, rows, rows, P(), P(), P(), P("rep", None), P("rep", None))
    tenant_rows = P("rep", None, "ctx", None)
    out_specs = (rows, rows, rows, tenant_rows, tenant_rows)
    return jax.shard_map(
        on_device, mesh=mesh, in_specs=in_specs, out_specs=out_specs, check_vma=False
    )
```

```python
import itertools

import jax
import jax.numpy as jnp
import numpy as np
from jax import lax
from jax.experimental import pallas as pl
from jax.experimental.pallas import tpu as pltpu
from jax.sharding import PartitionSpec as P

DOC_MAX = 256
LOW = jnp.bfloat16
WIDE = jnp.float32
far_below = -1e30


def shifted(value, axis, steps):
    count = lax.axis_size(axis)
    return lax.ppermute(value, axis, [(source, (source + steps) % count) for source in range(count)])


def exchanged(value, bits):
    axes = tuple(bits)
    shape = [lax.axis_size(axis) for axis in axes]
    pairs = []
    for source in np.ndindex(*shape):
        target = [at ^ bits[axis] for at, axis in zip(source, axes)]
        pairs.append((np.ravel_multi_index(source, shape), np.ravel_multi_index(target, shape)))
    return lax.ppermute(value, axes, [(int(source), int(target)) for source, target in pairs])


def reduce_groups():
    ctx, rep = lax.axis_size("ctx"), lax.axis_size("rep")
    bits = [{"ctx": 1 << at} for at in range(ctx.bit_length() - 2, 0, -1)]
    bits += [{"rep": 1 << at} for at in range(rep.bit_length() - 1)]
    return [bits[at : at + 2] for at in range(0, len(bits), 2)]


def reduce_place(index):
    place = 0
    for bits in itertools.chain(*reduce_groups()):
        for axis, bit in bits.items():
            place = 2 * place + (index[axis] // bit) % 2
    return place


def scattered(part, group, beside=None):
    count = 1 << len(group)
    size = part.shape[0] // count
    others = []
    for j in range(1, count):
        bits = {}
        for at, pair in enumerate(reversed(group)):
            if (j >> at) & 1:
                bits.update({axis: bits.get(axis, 0) | bit for axis, bit in pair.items()})
        others.append(exchanged(part[j * size : (j + 1) * size], bits))
    if beside is not None:
        others = lax.optimization_barrier((others, beside))[0]
    return part[:size], others


def dot(left, right, left_dim, right_dim, precision=None):
    return lax.dot_general(
        left, right, (((left_dim,), (right_dim,)), ((), ())),
        precision=precision, preferred_element_type=WIDE,
    )


def group_rows(ref, kv_count, group_size):
    rows, _, dim = ref.shape
    wide = 2 * group_size
    parts = []
    for pair in range(kv_count // 2):
        both = ref[:, pair * wide : (pair + 1) * wide, :].astype(WIDE)
        for half in range(2):
            one = both[:, half * group_size : (half + 1) * group_size, :]
            parts.append(one.reshape(rows * group_size, dim).astype(LOW))
    return parts


def lane_head(shape, group_size):
    return lax.broadcasted_iota(jnp.int32, shape, 1) % group_size


def own_terms(maps_by_rows, owner, tenants, low_rank, group_size):
    lanes = maps_by_rows.shape[1]
    same_head = lax.broadcasted_iota(jnp.int32, (group_size, lanes), 0) == lane_head(
        (group_size, lanes), group_size
    )
    span = low_rank * group_size
    total = jnp.zeros((low_rank, group_size, lanes), WIDE)
    for tenant in range(tenants):
        keep = same_head & (owner == tenant)
        block = maps_by_rows[tenant * span : (tenant + 1) * span].reshape(
            low_rank, group_size, lanes
        )
        total = total + jnp.where(keep[None], block, 0.0)
    rows = jnp.sum(total, axis=1)
    rows = jnp.concatenate([rows, rows], axis=0)
    tiles = lanes // 128
    stacked = jnp.concatenate([rows[:, c * 128 : (c + 1) * 128] for c in range(tiles)], axis=0)
    side = lax.broadcasted_iota(jnp.int32, (128, 128), 0) // group_size
    over = lax.broadcasted_iota(jnp.int32, (128, 128), 1) // group_size
    spread = dot(stacked, (side == over).astype(WIDE), 1, 0, lax.Precision.HIGHEST)
    return jnp.concatenate([spread[c * 8 : (c + 1) * 8] for c in range(tiles)], axis=1)


def place_kernel(rows_ref, meta_ref, bias_ref, *, group):
    lanes = meta_ref.shape[1]
    tokens = lanes // group
    row_first = lax.axis_index("ctx") * tokens
    mine = pl.ds(pl.multiple_of(row_first, tokens), tokens)
    row = lax.broadcasted_iota(jnp.int32, (8, tokens), 0)
    both = jnp.where(row == 0, rows_ref[0:1, mine] - row_first, rows_ref[1:2, mine]).astype(WIDE)
    repeat = lax.broadcasted_iota(jnp.int32, (tokens, lanes), 0) == (
        lax.broadcasted_iota(jnp.int32, (tokens, lanes), 1) // group
    )
    meta = dot(both, repeat.astype(WIDE), 1, 0, lax.Precision.HIGHEST).astype(jnp.int32)
    meta_ref[...] = meta
    first = meta[0:1, :]
    key, here = places(lanes, tokens, group)
    bias_ref[0] = jnp.where(jnp.where(here, key, key - 2 * tokens) >= first, 0.0, far_below)
    bias_ref[1] = jnp.where(key - tokens >= first, 0.0, far_below)


def slots_of(lanes, group, owned):
    per_group = group // owned
    head = lane_head((1, lanes), group)
    return head ^ ((lax.axis_index("ctx") % per_group) * owned)


def tenants_of(lanes, tenants, rank):
    row = lax.broadcasted_iota(jnp.int32, (tenants * rank, lanes), 0) // rank
    return row ^ (lax.axis_index("rep") * (tenants // lax.axis_size("rep")))


def picked_rows(rows, owner, slots, tenants, rank, group):
    lanes = owner.shape[1]
    mine = owner == tenants_of(lanes, tenants, rank)
    rows = jnp.where(mine, jnp.concatenate([rows] * (tenants * rank // 8), axis=0), 0.0)
    return [jnp.where(slots == h, rows, 0.0).astype(LOW) for h in range(group)]


def pull_kernel(
    meta_ref, cot_ref, rot_ref, q_ref, cots_ref, queries_ref, pulled_ref, pull_ref,
    *, kv, group, tenants, rank, owned,
):
    owner = meta_ref[1:2, :]
    lanes = owner.shape[1]
    cots = group_rows(cot_ref, kv, group)
    rots = group_rows(rot_ref, kv, group)
    on_rot = dot(jnp.concatenate(rots, axis=1), jnp.concatenate(cots, axis=1), 1, 1)
    pulled = own_terms(on_rot, owner, tenants, rank, group).astype(LOW).astype(WIDE)
    pulled_ref[...] = pulled
    for g, rows in enumerate(group_rows(q_ref, kv, group)):
        queries_ref[g] = rows
        cots_ref[g] = cots[g]
    span = tenants * rank
    slots = slots_of(lanes, group, owned)
    for h, rows in enumerate(picked_rows(pulled, owner, slots, tenants, rank, group)):
        pull_ref[h * span : (h + 1) * span, :] = rows


def hidden_grad_kernel(
    meta_ref, pulled_ref, cots_ref, rot_ref, proj_ref, gh_ref, diff_ref, *, kv, group, tenants, rank,
):
    owner = meta_ref[1:2, :]
    lanes = owner.shape[1]
    dim = cots_ref.shape[2]
    pulled = pulled_ref[...]
    same_head = lax.broadcasted_iota(jnp.int32, (group, lanes), 0) == lane_head((group, lanes), group)
    picked = []
    for tenant in range(tenants):
        keep = same_head & (owner == tenant)
        for k in range(rank):
            picked.append(jnp.where(keep, pulled[k : k + 1], 0.0))
    picked = jnp.concatenate(picked, axis=0).T.astype(LOW)
    rots = group_rows(rot_ref, kv, group)
    projs = group_rows(proj_ref, kv, group)
    diffs = [(proj.astype(WIDE) - rot.astype(WIDE)).astype(LOW) for proj, rot in zip(projs, rots)]
    steered = dot(picked, jnp.concatenate(diffs, axis=1), 1, 0)
    for g in range(kv):
        diff_ref[g] = diffs[g]
        gh_ref[g] = (cots_ref[g].astype(WIDE) + steered[:, g * dim : (g + 1) * dim]).astype(LOW)


def places(lanes, tokens, group):
    key = lax.broadcasted_iota(jnp.int32, (tokens, lanes), 0)
    query = lax.broadcasted_iota(jnp.int32, (tokens, lanes), 1) // group
    return key, key <= query


def window_of(two_ref, one_ref, own_ref, head):
    return jnp.concatenate([two_ref[head], one_ref[head], own_ref[head]], axis=0)


def score_kernel(queries_ref, two_ref, one_ref, own_ref, bias_ref, low_ref, *, group, scaling, first):
    tokens = own_ref.shape[1]
    _, here = places(queries_ref.shape[1], tokens, group)
    count = low_ref.shape[0]

    def scores_of(at):
        return dot(window_of(two_ref, one_ref, own_ref, first + at), queries_ref[first + at], 1, 1)

    scores = scores_of(0)
    for at in range(count):
        ahead = scores_of(at + 1) if at + 1 < count else None
        fold = jnp.where(here, scores[2 * tokens :], scores[0:tokens]) * scaling + bias_ref[0]
        mid = scores[tokens : 2 * tokens] * scaling + bias_ref[1]
        top = jnp.max(jnp.maximum(fold, mid), axis=0, keepdims=True)
        fold = jnp.exp(fold - top)
        mid = jnp.exp(mid - top)
        share = 1.0 / jnp.sum(fold + mid, axis=0, keepdims=True)
        fold = fold * share
        pieces = [jnp.where(here, 0.0, fold), mid * share, jnp.where(here, fold, 0.0)]
        low_ref[at] = jnp.concatenate([piece.astype(LOW) for piece in pieces], axis=0)
        scores = ahead


def forward_kernel(
    shift_ref, near_ref, far_ref, two_ref, one_ref, own_ref, cots_ref, diff_ref, meta_ref, pull_ref,
    send_ref, keep_ref, *, kv, group, tenants, rank, owned,
):
    dim = own_ref.shape[2]
    owner = meta_ref[1:2, :]
    lanes = owner.shape[1]
    hidden = []
    for g in range(kv):
        low = (near_ref if g < kv // 2 else far_ref)[g % (kv // 2)]
        hidden.append(dot(window_of(two_ref, one_ref, own_ref, g), low, 0, 0).astype(LOW))
    hidden = jnp.concatenate(hidden, axis=0)
    on_diff = dot(jnp.concatenate([diff_ref[g] for g in range(kv)], axis=1), hidden, 1, 0)
    lifted = own_terms(on_diff, owner, tenants, rank, group)
    one_hot = (owner == lax.broadcasted_iota(jnp.int32, (tenants, lanes), 0)).astype(WIDE)
    bias = jnp.concatenate([shift_ref[...]] * (8 // rank), axis=0)
    shift = dot(bias, one_hot, 1, 0, lax.Precision.HIGHEST)
    lifted = (lifted + shift).astype(LOW).astype(WIDE)
    rep = lax.axis_size("rep")
    me = lax.axis_index("ctx")
    per_group = group // owned
    span = tenants * rank
    slots = slots_of(lanes, group, owned)
    lift_all = jnp.concatenate(picked_rows(lifted, owner, slots, tenants, rank, group), axis=0)
    on_proj = dot(pull_ref[...], hidden, 1, 1)
    on_rot = dot(lift_all, jnp.concatenate([cots_ref[g] for g in range(kv)], axis=1), 1, 0) - on_proj
    here_rows = span // rep
    for g in range(kv):
        columns = slice(g * dim, (g + 1) * dim)
        for low in range(per_group):
            device = (g ^ (me // per_group)) * per_group + low
            into = send_ref if low % 2 else keep_ref
            for r in range(rep):
                pieces = []
                for h in range(low * owned, (low + 1) * owned):
                    rows = slice(h * span + r * here_rows, h * span + (r + 1) * here_rows)
                    pieces += [on_rot[rows, columns], on_proj[rows, columns]]
                into[reduce_place(dict(ctx=device, rep=r))] = jnp.concatenate(pieces, axis=0).astype(LOW)


def backward_kernel(
    queries_ref, gh_ref, near_ref, far_ref, two_keys, one_keys, own_keys, two_values, one_values, own_values,
    dq_hbm, back_two_ref, back_one_ref, back_own_ref, dq_ref, sems, *, kv, group, scaling,
):
    tokens, dim = own_keys.shape[1:]

    def weight_grad_of(g):
        return dot(window_of(two_values, one_values, own_values, g), gh_ref[g], 1, 1)

    copies = []
    weight_grad = weight_grad_of(0)
    for g in range(kv):
        ahead = weight_grad_of(g + 1) if g + 1 < kv else None
        low = (near_ref if g < kv // 2 else far_ref)[g % (kv // 2)]
        weights = low.astype(WIDE)
        delta = jnp.sum(weights * weight_grad, axis=0, keepdims=True)
        score_grad = (weights * (weight_grad - delta)).astype(LOW)
        query_grad = (dot(window_of(two_keys, one_keys, own_keys, g), score_grad, 0, 0) * scaling).T.reshape(tokens, group, dim)
        if g % 2 == 1:
            heads = slice((g - 1) * group, (g + 1) * group)
            dq_ref[:, heads, :] = jnp.concatenate([before, query_grad], axis=1).astype(LOW)
            copies.append(pltpu.make_async_copy(dq_ref.at[:, heads], dq_hbm.at[:, heads], sems.at[g // 2]))
            copies[-1].start()
        before = query_grad
        key_grad = dot(score_grad, queries_ref[g], 1, 0) * scaling
        value_grad = dot(low, gh_ref[g], 1, 0)
        for place, grad in ((g, key_grad), (kv + g, value_grad)):
            back_two_ref[place] = grad[0:tokens].astype(LOW)
            back_one_ref[place] = grad[tokens : 2 * tokens].astype(LOW)
            back_own_ref[place] = grad[2 * tokens :]
        weight_grad = ahead
    for copy in copies:
        copy.wait()


def finish_kernel(
    own_ref, mate_ref, two_ref, part_ref, *refs, kv, owned,
):
    *other_refs, keys_ref, values_ref, rot_ref, proj_ref, wide_ref = refs
    total = part_ref[0].astype(WIDE)
    for other_ref in other_refs:
        total = total + other_ref[0].astype(WIDE)
    size = rot_ref.shape[0]
    for place in range(owned):
        for at, out in enumerate((rot_ref, proj_ref)):
            row = (2 * place + at) * size
            out[:, place, :] = total[row : row + size]
    tokens = own_ref.shape[1]
    even = (lax.axis_index("ctx") % 2 == 0).astype(WIDE)
    for at, out in enumerate((keys_ref, values_ref)):
        for m in range(kv):
            place = at * kv + m
            total = own_ref[place] + two_ref[place].astype(WIDE) + even * mate_ref[place].astype(WIDE)
            wide_ref[at, pl.ds(m, tokens, stride=kv), :] = total
        out[...] = wide_ref[at].astype(LOW)


def on_device(
    query_rows, key_rows, value_matrix, cotangent, rotation, projection, shift_bias, doc_starts, tenant_ids,
):
    queries = query_rows[0]
    upstream = cotangent[0]
    tokens, heads, dim = queries.shape
    kv = key_rows.shape[2]
    group = heads // kv
    scaling = dim ** (-0.5)
    tenants, rank = rotation.shape[0], rotation.shape[1]
    lanes = tokens * group
    ctx = lax.axis_size("ctx")
    rep = lax.axis_size("rep")
    assert 2 * tokens == DOC_MAX


    rot = rotation.reshape(tenants * rank, heads, dim)
    proj = projection.reshape(tenants * rank, heads, dim)
    sizes = dict(kv=kv, group=group)
    vmem = pl.BlockSpec(memory_space=pltpu.VMEM)

    def call(body, outs, flops, moved, out_specs=None, scratch=(), **fixed):
        def run(*operands):
            return pl.pallas_call(
                lambda *refs: body(*refs, **fixed),
                out_shape=[jax.ShapeDtypeStruct(*out) for out in outs],
                in_specs=[vmem] * len(operands),
                out_specs=out_specs or [vmem] * len(outs),
                scratch_shapes=scratch,
                compiler_params=pltpu.CompilerParams(vmem_limit_bytes=12 * 2**20),
                name=body.__name__,
                cost_estimate=pl.CostEstimate(flops=flops, bytes_accessed=moved, transcendentals=0),
            )(*operands)

        return run

    span = tenants * rank
    here = heads // ctx
    rows = here * 2 * span // rep
    even = jnp.reshape(lax.axis_index("ctx") % 2 == 0, (1, 1, 1))
    key_rows, even = lax.optimization_barrier((key_rows, even))
    own_keys = lax.optimization_barrier(jnp.moveaxis(key_rows[0], 1, 0))
    two_keys = shifted(own_keys, "ctx", 2)
    meta, biases = call(
        place_kernel, [((8, lanes), jnp.int32), ((2, tokens, lanes), WIDE)], 8 * 2**30, 2**20,
        group=group,
    )(jnp.concatenate([doc_starts, tenant_ids], axis=0))
    own_values, meta = lax.optimization_barrier((jnp.moveaxis(value_matrix[0], 1, 0), meta))
    two_values = shifted(own_values, "ctx", 2)
    cots, queries, pulled, pull = call(
        pull_kernel,
        [((kv, lanes, dim), LOW), ((kv, lanes, dim), LOW), ((8, lanes), WIDE), ((span * group, lanes), LOW)],
        2**30, 4 * 2**20, tenants=tenants, rank=rank, owned=here, **sizes,
    )(meta, upstream, rot, queries)
    two_keys, pulled = lax.optimization_barrier((two_keys, pulled))
    one_keys = exchanged(jnp.where(even, own_keys, two_keys), {"ctx": 1})
    grad_hidden, diff = call(
        hidden_grad_kernel, [((kv, lanes, dim), LOW), ((kv, span * group, dim), LOW)],
        2 * 2**30, 4 * 2**20, tenants=tenants, rank=rank, **sizes,
    )(meta, pulled, cots, rot, proj)
    one_keys, grad_hidden = lax.optimization_barrier((one_keys, grad_hidden))

    def weights_of(first):
        return call(
            score_kernel, [((kv // 2, 3 * tokens, lanes), LOW)], 2 * 2**30, 4 * 2**20,
            group=group, scaling=scaling, first=first,
        )(queries, two_keys, one_keys, own_keys, biases)[0]

    near = weights_of(0)
    two_values, near = lax.optimization_barrier((two_values, near))
    one_values = exchanged(jnp.where(even, own_values, two_values), {"ctx": 1})
    far = weights_of(kv // 2)
    one_values, far = lax.optimization_barrier((one_values, far))
    send, keep = call(
        forward_kernel, [((ctx * rep // 2, rows, dim), LOW)] * 2, 4 * 2**30, 10 * 2**20,
        tenants=tenants, rank=rank, owned=here, **sizes,
    )(shift_bias.T, near, far, two_values, one_values, own_values, cots, diff, meta, pull)
    part = (keep.astype(WIDE) + exchanged(send, {"ctx": 1}).astype(WIDE)).astype(LOW)
    near, part = lax.optimization_barrier((near, part))
    window = (2 * kv, tokens, dim)
    d_queries, back_two, back_one, back_own = call(
        backward_kernel,
        [((tokens, heads, dim), LOW), (window, LOW), (window, LOW), (window, WIDE)],
        4 * 2**30, 10 * 2**20,
        scratch=[
            pltpu.VMEM((tokens, heads, dim), LOW), pltpu.SemaphoreType.DMA((kv // 2,)),
        ],
        out_specs=[pl.BlockSpec(memory_space=pltpu.HBM), vmem, vmem, vmem], scaling=scaling, **sizes,
    )(
        queries, grad_hidden, near, far, two_keys, one_keys, own_keys, two_values, one_values, own_values,
    )
    from_mate = exchanged(back_one, {"ctx": 1})
    onward = back_two.astype(WIDE) + jnp.where(even, 0.0, from_mate.astype(WIDE))
    onward = onward.astype(LOW)

    groups = reduce_groups()
    for at, group_bits in enumerate(groups):
        beside = back_own if at == 0 else None
        if at == len(groups) - 1:
            part, onward = lax.optimization_barrier((part, onward))
            from_two = shifted(onward, "ctx", -2)
            beside = from_two
        part, others = scattered(part, group_bits, beside)
        if at < len(groups) - 1:
            part = part.astype(WIDE) + sum(other.astype(WIDE) for other in others)
            part = part.astype(LOW)
    d_keys, d_values, *grads = call(
        finish_kernel, [((tokens * kv, dim), LOW)] * 2 + [((span // rep, here, dim), WIDE)] * 2, 2**20, 2**20,
        scratch=[pltpu.VMEM((2, tokens * kv, dim), WIDE)], kv=kv, owned=here,
    )(back_own, from_mate, from_two, part, *others)
    grads = [grad.reshape(tenants // rep, rank, here, dim) for grad in grads]
    d_keys, d_values = (grad.reshape(key_rows.shape) for grad in (d_keys, d_values))
    return (d_queries[None], d_keys, d_values, grads[0], grads[1])


def solution(mesh):
    rows = P("rep", "ctx", None, None)
    in_specs = (rows, rows, rows, rows, P(), P(), P(), P("rep", None), P("rep", None))
    tenant_rows = P("rep", None, "ctx", None)
    out_specs = (rows, rows, rows, tenant_rows, tenant_rows)
    return jax.shard_map(
        on_device, mesh=mesh, in_specs=in_specs, out_specs=out_specs, check_vma=False
    )
```

```python
import itertools

import jax
import jax.numpy as jnp
import numpy as np
from jax import lax
from jax.experimental import pallas as pl
from jax.experimental.pallas import tpu as pltpu
from jax.sharding import PartitionSpec as P

DOC_MAX = 256
LOW = jnp.bfloat16
WIDE = jnp.float32
far_below = -1e30


def shifted(value, axis, steps):
    count = lax.axis_size(axis)
    return lax.ppermute(value, axis, [(source, (source + steps) % count) for source in range(count)])


def exchanged(value, bits):
    axes = tuple(bits)
    shape = [lax.axis_size(axis) for axis in axes]
    pairs = []
    for source in np.ndindex(*shape):
        target = [at ^ bits[axis] for at, axis in zip(source, axes)]
        pairs.append((np.ravel_multi_index(source, shape), np.ravel_multi_index(target, shape)))
    return lax.ppermute(value, axes, [(int(source), int(target)) for source, target in pairs])


def reduce_groups():
    ctx, rep = lax.axis_size("ctx"), lax.axis_size("rep")
    bits = [{"ctx": 1 << at} for at in range(ctx.bit_length() - 2, 0, -1)]
    bits += [{"rep": 1 << at} for at in range(rep.bit_length() - 1)]
    return [bits[at : at + 2] for at in range(0, len(bits), 2)]


def reduce_place(index):
    place = 0
    for bits in itertools.chain(*reduce_groups()):
        for axis, bit in bits.items():
            place = 2 * place + (index[axis] // bit) % 2
    return place


def scattered(part, group, beside=None):
    count = 1 << len(group)
    size = part.shape[0] // count
    others = []
    for j in range(1, count):
        bits = {}
        for at, pair in enumerate(reversed(group)):
            if (j >> at) & 1:
                bits.update({axis: bits.get(axis, 0) | bit for axis, bit in pair.items()})
        others.append(exchanged(part[j * size : (j + 1) * size], bits))
    if beside is not None:
        others = lax.optimization_barrier((others, beside))[0]
    return part[:size], others


def dot(left, right, left_dim, right_dim, precision=None):
    return lax.dot_general(
        left, right, (((left_dim,), (right_dim,)), ((), ())),
        precision=precision, preferred_element_type=WIDE,
    )


def group_rows(ref, kv_count, group_size):
    rows, _, dim = ref.shape
    wide = 2 * group_size
    parts = []
    for pair in range(kv_count // 2):
        both = ref[:, pair * wide : (pair + 1) * wide, :].astype(WIDE)
        for half in range(2):
            one = both[:, half * group_size : (half + 1) * group_size, :]
            parts.append(one.reshape(rows * group_size, dim).astype(LOW))
    return parts


def lane_head(shape, group_size):
    return lax.broadcasted_iota(jnp.int32, shape, 1) % group_size


def own_terms(maps_by_rows, owner, tenants, low_rank, group_size):
    lanes = maps_by_rows.shape[1]
    same_head = lax.broadcasted_iota(jnp.int32, (group_size, lanes), 0) == lane_head(
        (group_size, lanes), group_size
    )
    span = low_rank * group_size
    total = jnp.zeros((low_rank, group_size, lanes), WIDE)
    for tenant in range(tenants):
        keep = same_head & (owner == tenant)
        block = maps_by_rows[tenant * span : (tenant + 1) * span].reshape(
            low_rank, group_size, lanes
        )
        total = total + jnp.where(keep[None], block, 0.0)
    rows = jnp.sum(total, axis=1)
    rows = jnp.concatenate([rows, rows], axis=0)
    tiles = lanes // 128
    stacked = jnp.concatenate([rows[:, c * 128 : (c + 1) * 128] for c in range(tiles)], axis=0)
    side = lax.broadcasted_iota(jnp.int32, (128, 128), 0) // group_size
    over = lax.broadcasted_iota(jnp.int32, (128, 128), 1) // group_size
    spread = dot(stacked, (side == over).astype(WIDE), 1, 0, lax.Precision.HIGHEST)
    return jnp.concatenate([spread[c * 8 : (c + 1) * 8] for c in range(tiles)], axis=1)


def place_kernel(rows_ref, meta_ref, bias_ref, *, group):
    lanes = meta_ref.shape[1]
    tokens = lanes // group
    row_first = lax.axis_index("ctx") * tokens
    mine = pl.ds(pl.multiple_of(row_first, tokens), tokens)
    row = lax.broadcasted_iota(jnp.int32, (8, tokens), 0)
    both = jnp.where(row == 0, rows_ref[0:1, mine] - row_first, rows_ref[1:2, mine]).astype(WIDE)
    repeat = lax.broadcasted_iota(jnp.int32, (tokens, lanes), 0) == (
        lax.broadcasted_iota(jnp.int32, (tokens, lanes), 1) // group
    )
    meta = dot(both, repeat.astype(WIDE), 1, 0, lax.Precision.HIGHEST).astype(jnp.int32)
    meta_ref[...] = meta
    first = meta[0:1, :]
    key, here = places(lanes, tokens, group)
    bias_ref[0] = jnp.where(jnp.where(here, key, key - 2 * tokens) >= first, 0.0, far_below)
    bias_ref[1] = jnp.where(key - tokens >= first, 0.0, far_below)


def slots_of(lanes, group, owned):
    per_group = group // owned
    head = lane_head((1, lanes), group)
    return head ^ ((lax.axis_index("ctx") % per_group) * owned)


def tenants_of(lanes, tenants, rank):
    row = lax.broadcasted_iota(jnp.int32, (tenants * rank, lanes), 0) // rank
    return row ^ (lax.axis_index("rep") * (tenants // lax.axis_size("rep")))


def picked_rows(rows, owner, slots, tenants, rank, group):
    lanes = owner.shape[1]
    mine = owner == tenants_of(lanes, tenants, rank)
    rows = jnp.where(mine, jnp.concatenate([rows] * (tenants * rank // 8), axis=0), 0.0)
    return [jnp.where(slots == h, rows, 0.0).astype(LOW) for h in range(group)]


def pull_kernel(
    meta_ref, cot_ref, rot_ref, q_ref, cots_ref, queries_ref, pulled_ref, pull_ref,
    *, kv, group, tenants, rank, owned,
):
    owner = meta_ref[1:2, :]
    lanes = owner.shape[1]
    cots = group_rows(cot_ref, kv, group)
    rots = group_rows(rot_ref, kv, group)
    on_rot = dot(jnp.concatenate(rots, axis=1), jnp.concatenate(cots, axis=1), 1, 1)
    pulled = own_terms(on_rot, owner, tenants, rank, group).astype(LOW).astype(WIDE)
    pulled_ref[...] = pulled
    for g, rows in enumerate(group_rows(q_ref, kv, group)):
        queries_ref[g] = rows
        cots_ref[g] = cots[g]
    span = tenants * rank
    slots = slots_of(lanes, group, owned)
    for h, rows in enumerate(picked_rows(pulled, owner, slots, tenants, rank, group)):
        pull_ref[h * span : (h + 1) * span, :] = rows


def hidden_grad_kernel(
    meta_ref, pulled_ref, cots_ref, rot_ref, proj_ref, gh_ref, diff_ref, *, kv, group, tenants, rank,
):
    owner = meta_ref[1:2, :]
    lanes = owner.shape[1]
    dim = cots_ref.shape[2]
    pulled = pulled_ref[...]
    same_head = lax.broadcasted_iota(jnp.int32, (group, lanes), 0) == lane_head((group, lanes), group)
    picked = []
    for tenant in range(tenants):
        keep = same_head & (owner == tenant)
        for k in range(rank):
            picked.append(jnp.where(keep, pulled[k : k + 1], 0.0))
    picked = jnp.concatenate(picked, axis=0).T.astype(LOW)
    rots = group_rows(rot_ref, kv, group)
    projs = group_rows(proj_ref, kv, group)
    diffs = [(proj.astype(WIDE) - rot.astype(WIDE)).astype(LOW) for proj, rot in zip(projs, rots)]
    steered = dot(picked, jnp.concatenate(diffs, axis=1), 1, 0)
    for g in range(kv):
        diff_ref[g] = diffs[g]
        gh_ref[g] = (cots_ref[g].astype(WIDE) + steered[:, g * dim : (g + 1) * dim]).astype(LOW)


def places(lanes, tokens, group):
    key = lax.broadcasted_iota(jnp.int32, (tokens, lanes), 0)
    query = lax.broadcasted_iota(jnp.int32, (tokens, lanes), 1) // group
    return key, key <= query


def window_of(two_ref, one_ref, own_ref, head):
    return jnp.concatenate([two_ref[head], one_ref[head], own_ref[head]], axis=0)


def score_kernel(queries_ref, two_ref, one_ref, own_ref, bias_ref, low_ref, *, group, scaling, first):
    tokens = own_ref.shape[1]
    _, here = places(queries_ref.shape[1], tokens, group)
    count = low_ref.shape[0]

    def scores_of(at):
        return dot(window_of(two_ref, one_ref, own_ref, first + at), queries_ref[first + at], 1, 1)

    scores = scores_of(0)
    for at in range(count):
        ahead = scores_of(at + 1) if at + 1 < count else None
        fold = jnp.where(here, scores[2 * tokens :], scores[0:tokens]) * scaling + bias_ref[0]
        mid = scores[tokens : 2 * tokens] * scaling + bias_ref[1]
        top = jnp.max(jnp.maximum(fold, mid), axis=0, keepdims=True)
        fold = jnp.exp(fold - top)
        mid = jnp.exp(mid - top)
        share = 1.0 / jnp.sum(fold + mid, axis=0, keepdims=True)
        fold = fold * share
        pieces = [jnp.where(here, 0.0, fold), mid * share, jnp.where(here, fold, 0.0)]
        low_ref[at] = jnp.concatenate([piece.astype(LOW) for piece in pieces], axis=0)
        scores = ahead


def forward_kernel(
    shift_ref, near_ref, far_ref, two_ref, one_ref, own_ref, cots_ref, diff_ref, meta_ref, pull_ref,
    send_ref, keep_ref, *, kv, group, tenants, rank, owned,
):
    dim = own_ref.shape[2]
    owner = meta_ref[1:2, :]
    lanes = owner.shape[1]
    hidden = []
    for g in range(kv):
        low = (near_ref if g < kv // 2 else far_ref)[g % (kv // 2)]
        hidden.append(dot(window_of(two_ref, one_ref, own_ref, g), low, 0, 0).astype(LOW))
    hidden = jnp.concatenate(hidden, axis=0)
    on_diff = dot(jnp.concatenate([diff_ref[g] for g in range(kv)], axis=1), hidden, 1, 0)
    lifted = own_terms(on_diff, owner, tenants, rank, group)
    one_hot = (owner == lax.broadcasted_iota(jnp.int32, (tenants, lanes), 0)).astype(WIDE)
    bias = jnp.concatenate([shift_ref[...]] * (8 // rank), axis=0)
    shift = dot(bias, one_hot, 1, 0, lax.Precision.HIGHEST)
    lifted = (lifted + shift).astype(LOW).astype(WIDE)
    rep = lax.axis_size("rep")
    me = lax.axis_index("ctx")
    per_group = group // owned
    span = tenants * rank
    slots = slots_of(lanes, group, owned)
    lift_all = jnp.concatenate(picked_rows(lifted, owner, slots, tenants, rank, group), axis=0)
    on_proj = dot(pull_ref[...], hidden, 1, 1)
    on_rot = dot(lift_all, jnp.concatenate([cots_ref[g] for g in range(kv)], axis=1), 1, 0) - on_proj
    here_rows = span // rep
    for g in range(kv):
        columns = slice(g * dim, (g + 1) * dim)
        for low in range(per_group):
            device = (g ^ (me // per_group)) * per_group + low
            into = send_ref if low % 2 else keep_ref
            for r in range(rep):
                pieces = []
                for h in range(low * owned, (low + 1) * owned):
                    rows = slice(h * span + r * here_rows, h * span + (r + 1) * here_rows)
                    pieces += [on_rot[rows, columns], on_proj[rows, columns]]
                into[reduce_place(dict(ctx=device, rep=r))] = jnp.concatenate(pieces, axis=0).astype(LOW)


def backward_kernel(
    queries_ref, gh_ref, near_ref, far_ref, two_ref, one_ref, own_ref,
    back_two_ref, back_one_ref, back_own_ref, grad_ref, *, kv, scaling,
):
    tokens = own_ref.shape[1]

    def weight_grad_of(g):
        return dot(window_of(two_ref, one_ref, own_ref, g), gh_ref[g], 1, 1)

    weight_grad = weight_grad_of(0)
    for g in range(kv):
        ahead = weight_grad_of(g + 1) if g + 1 < kv else None
        low = (near_ref if g < kv // 2 else far_ref)[g % (kv // 2)]
        weights = low.astype(WIDE)
        delta = jnp.sum(weights * weight_grad, axis=0, keepdims=True)
        score_grad = (weights * (weight_grad - delta)).astype(LOW)
        grad_ref[g] = score_grad
        key_grad = dot(score_grad, queries_ref[g], 1, 0) * scaling
        value_grad = dot(low, gh_ref[g], 1, 0)
        for place, grad in ((g, key_grad), (kv + g, value_grad)):
            back_two_ref[place] = grad[0:tokens].astype(LOW)
            back_one_ref[place] = grad[tokens : 2 * tokens].astype(LOW)
            back_own_ref[place] = grad[2 * tokens :]
        weight_grad = ahead


def query_kernel(
    grad_ref, two_ref, one_ref, own_ref, dq_hbm, dq_ref, sems, *, kv, group, scaling,
):
    tokens, dim = own_ref.shape[1:]
    copies = []
    for g in range(kv):
        query_grad = dot(window_of(two_ref, one_ref, own_ref, g), grad_ref[g], 0, 0) * scaling
        query_grad = query_grad.T.reshape(tokens, group, dim)
        if g % 2 == 1:
            heads = slice((g - 1) * group, (g + 1) * group)
            dq_ref[:, heads, :] = jnp.concatenate([before, query_grad], axis=1).astype(LOW)
            copies.append(pltpu.make_async_copy(dq_ref.at[:, heads], dq_hbm.at[:, heads], sems.at[g // 2]))
            copies[-1].start()
        before = query_grad
    for copy in copies:
        copy.wait()


def finish_kernel(
    own_ref, mate_ref, two_ref, part_ref, *refs, kv, owned,
):
    *other_refs, keys_ref, values_ref, rot_ref, proj_ref, wide_ref = refs
    total = part_ref[0].astype(WIDE)
    for other_ref in other_refs:
        total = total + other_ref[0].astype(WIDE)
    size = rot_ref.shape[0]
    for place in range(owned):
        for at, out in enumerate((rot_ref, proj_ref)):
            row = (2 * place + at) * size
            out[:, place, :] = total[row : row + size]
    tokens = own_ref.shape[1]
    even = (lax.axis_index("ctx") % 2 == 0).astype(WIDE)
    for at, out in enumerate((keys_ref, values_ref)):
        for m in range(kv):
            place = at * kv + m
            total = own_ref[place] + two_ref[place].astype(WIDE) + even * mate_ref[place].astype(WIDE)
            wide_ref[at, pl.ds(m, tokens, stride=kv), :] = total
        out[...] = wide_ref[at].astype(LOW)


def on_device(
    query_rows, key_rows, value_matrix, cotangent, rotation, projection, shift_bias, doc_starts, tenant_ids,
):
    queries = query_rows[0]
    upstream = cotangent[0]
    tokens, heads, dim = queries.shape
    kv = key_rows.shape[2]
    group = heads // kv
    scaling = dim ** (-0.5)
    tenants, rank = rotation.shape[0], rotation.shape[1]
    lanes = tokens * group
    ctx = lax.axis_size("ctx")
    rep = lax.axis_size("rep")
    assert 2 * tokens == DOC_MAX


    rot = rotation.reshape(tenants * rank, heads, dim)
    proj = projection.reshape(tenants * rank, heads, dim)
    sizes = dict(kv=kv, group=group)
    vmem = pl.BlockSpec(memory_space=pltpu.VMEM)

    def call(body, outs, flops, moved, out_specs=None, scratch=(), **fixed):
        def run(*operands):
            return pl.pallas_call(
                lambda *refs: body(*refs, **fixed),
                out_shape=[jax.ShapeDtypeStruct(*out) for out in outs],
                in_specs=[vmem] * len(operands),
                out_specs=out_specs or [vmem] * len(outs),
                scratch_shapes=scratch,
                compiler_params=pltpu.CompilerParams(vmem_limit_bytes=12 * 2**20),
                name=body.__name__,
                cost_estimate=pl.CostEstimate(flops=flops, bytes_accessed=moved, transcendentals=0),
            )(*operands)

        return run

    span = tenants * rank
    here = heads // ctx
    rows = here * 2 * span // rep
    even = jnp.reshape(lax.axis_index("ctx") % 2 == 0, (1, 1, 1))
    key_rows, even = lax.optimization_barrier((key_rows, even))
    own_keys = lax.optimization_barrier(jnp.moveaxis(key_rows[0], 1, 0))
    two_keys = shifted(own_keys, "ctx", 2)
    meta, biases = call(
        place_kernel, [((8, lanes), jnp.int32), ((2, tokens, lanes), WIDE)], 8 * 2**30, 2**20,
        group=group,
    )(jnp.concatenate([doc_starts, tenant_ids], axis=0))
    own_values, meta = lax.optimization_barrier((jnp.moveaxis(value_matrix[0], 1, 0), meta))
    two_values = shifted(own_values, "ctx", 2)
    cots, queries, pulled, pull = call(
        pull_kernel,
        [((kv, lanes, dim), LOW), ((kv, lanes, dim), LOW), ((8, lanes), WIDE), ((span * group, lanes), LOW)],
        2**30, 4 * 2**20, tenants=tenants, rank=rank, owned=here, **sizes,
    )(meta, upstream, rot, queries)
    two_keys, pulled = lax.optimization_barrier((two_keys, pulled))
    one_keys = exchanged(jnp.where(even, own_keys, two_keys), {"ctx": 1})
    grad_hidden, diff = call(
        hidden_grad_kernel, [((kv, lanes, dim), LOW), ((kv, span * group, dim), LOW)],
        2 * 2**30, 4 * 2**20, tenants=tenants, rank=rank, **sizes,
    )(meta, pulled, cots, rot, proj)
    one_keys, grad_hidden = lax.optimization_barrier((one_keys, grad_hidden))

    def weights_of(first):
        return call(
            score_kernel, [((kv // 2, 3 * tokens, lanes), LOW)], 2 * 2**30, 4 * 2**20,
            group=group, scaling=scaling, first=first,
        )(queries, two_keys, one_keys, own_keys, biases)[0]

    near = weights_of(0)
    two_values, near = lax.optimization_barrier((two_values, near))
    one_values = exchanged(jnp.where(even, own_values, two_values), {"ctx": 1})
    far = weights_of(kv // 2)
    one_values, far = lax.optimization_barrier((one_values, far))
    send, keep = call(
        forward_kernel, [((ctx * rep // 2, rows, dim), LOW)] * 2, 4 * 2**30, 10 * 2**20,
        tenants=tenants, rank=rank, owned=here, **sizes,
    )(shift_bias.T, near, far, two_values, one_values, own_values, cots, diff, meta, pull)
    part = (keep.astype(WIDE) + exchanged(send, {"ctx": 1}).astype(WIDE)).astype(LOW)
    near, part = lax.optimization_barrier((near, part))
    window = (2 * kv, tokens, dim)
    back_two, back_one, back_own, score_grad = call(
        backward_kernel, [(window, LOW), (window, LOW), (window, WIDE), ((kv, 3 * tokens, lanes), LOW)],
        4 * 2**30, 10 * 2**20, kv=kv, scaling=scaling,
    )(queries, grad_hidden, near, far, two_values, one_values, own_values)
    d_queries, = call(
        query_kernel, [((tokens, heads, dim), LOW)], 2 * 2**30, 5 * 2**20,
        scratch=[pltpu.VMEM((tokens, heads, dim), LOW), pltpu.SemaphoreType.DMA((kv // 2,))],
        out_specs=[pl.BlockSpec(memory_space=pltpu.HBM)], scaling=scaling, **sizes,
    )(score_grad, two_keys, one_keys, own_keys)
    from_mate = exchanged(back_one, {"ctx": 1})
    onward = back_two.astype(WIDE) + jnp.where(even, 0.0, from_mate.astype(WIDE))
    onward = onward.astype(LOW)

    groups = reduce_groups()
    for at, group_bits in enumerate(groups):
        beside = back_own if at == 0 else None
        if at == len(groups) - 1:
            part, onward = lax.optimization_barrier((part, onward))
            from_two = shifted(onward, "ctx", -2)
            beside = from_two
        part, others = scattered(part, group_bits, beside)
        if at < len(groups) - 1:
            part = part.astype(WIDE) + sum(other.astype(WIDE) for other in others)
            part = part.astype(LOW)
    d_keys, d_values, *grads = call(
        finish_kernel, [((tokens * kv, dim), LOW)] * 2 + [((span // rep, here, dim), WIDE)] * 2, 2**20, 2**20,
        scratch=[pltpu.VMEM((2, tokens * kv, dim), WIDE)], kv=kv, owned=here,
    )(back_own, from_mate, from_two, part, *others)
    grads = [grad.reshape(tenants // rep, rank, here, dim) for grad in grads]
    d_keys, d_values = (grad.reshape(key_rows.shape) for grad in (d_keys, d_values))
    return (d_queries[None], d_keys, d_values, grads[0], grads[1])


def solution(mesh):
    rows = P("rep", "ctx", None, None)
    in_specs = (rows, rows, rows, rows, P(), P(), P(), P("rep", None), P("rep", None))
    tenant_rows = P("rep", None, "ctx", None)
    out_specs = (rows, rows, rows, tenant_rows, tenant_rows)
    return jax.shard_map(
        on_device, mesh=mesh, in_specs=in_specs, out_specs=out_specs, check_vma=False
    )
```

```python
import itertools

import jax
import jax.numpy as jnp
import numpy as np
from jax import lax
from jax.experimental import pallas as pl
from jax.experimental.pallas import tpu as pltpu
from jax.sharding import PartitionSpec as P

DOC_MAX = 256
LOW = jnp.bfloat16
WIDE = jnp.float32
far_below = -1e30


def shifted(value, axis, steps):
    count = lax.axis_size(axis)
    return lax.ppermute(value, axis, [(source, (source + steps) % count) for source in range(count)])


def exchanged(value, bits):
    axes = tuple(bits)
    shape = [lax.axis_size(axis) for axis in axes]
    pairs = []
    for source in np.ndindex(*shape):
        target = [at ^ bits[axis] for at, axis in zip(source, axes)]
        pairs.append((np.ravel_multi_index(source, shape), np.ravel_multi_index(target, shape)))
    return lax.ppermute(value, axes, [(int(source), int(target)) for source, target in pairs])


def reduce_groups():
    ctx, rep = lax.axis_size("ctx"), lax.axis_size("rep")
    bits = [{"ctx": 1 << at} for at in range(ctx.bit_length() - 2, 0, -1)]
    bits += [{"rep": 1 << at} for at in range(rep.bit_length() - 1)]
    return [bits[at : at + 2] for at in range(0, len(bits), 2)]


def reduce_place(index):
    place = 0
    for bits in itertools.chain(*reduce_groups()):
        for axis, bit in bits.items():
            place = 2 * place + (index[axis] // bit) % 2
    return place


def scattered(part, group, beside=None):
    count = 1 << len(group)
    size = part.shape[0] // count
    others = []
    for j in range(1, count):
        bits = {}
        for at, pair in enumerate(reversed(group)):
            if (j >> at) & 1:
                bits.update({axis: bits.get(axis, 0) | bit for axis, bit in pair.items()})
        others.append(exchanged(part[j * size : (j + 1) * size], bits))
    if beside is not None:
        others = lax.optimization_barrier((others, beside))[0]
    return part[:size], others


def dot(left, right, left_dim, right_dim, precision=None):
    return lax.dot_general(
        left, right, (((left_dim,), (right_dim,)), ((), ())),
        precision=precision, preferred_element_type=WIDE,
    )


def group_rows(ref, kv_count, group_size):
    rows, _, dim = ref.shape
    wide = 2 * group_size
    parts = []
    for pair in range(kv_count // 2):
        both = ref[:, pair * wide : (pair + 1) * wide, :].astype(WIDE)
        for half in range(2):
            one = both[:, half * group_size : (half + 1) * group_size, :]
            parts.append(one.reshape(rows * group_size, dim).astype(LOW))
    return parts


def lane_head(shape, group_size):
    return lax.broadcasted_iota(jnp.int32, shape, 1) % group_size


def own_terms(maps_by_rows, owner, tenants, low_rank, group_size):
    lanes = maps_by_rows.shape[1]
    same_head = lax.broadcasted_iota(jnp.int32, (group_size, lanes), 0) == lane_head(
        (group_size, lanes), group_size
    )
    span = low_rank * group_size
    total = jnp.zeros((low_rank, group_size, lanes), WIDE)
    for tenant in range(tenants):
        keep = same_head & (owner == tenant)
        block = maps_by_rows[tenant * span : (tenant + 1) * span].reshape(
            low_rank, group_size, lanes
        )
        total = total + jnp.where(keep[None], block, 0.0)
    rows = jnp.sum(total, axis=1)
    rows = jnp.concatenate([rows, rows], axis=0)
    tiles = lanes // 128
    stacked = jnp.concatenate([rows[:, c * 128 : (c + 1) * 128] for c in range(tiles)], axis=0)
    side = lax.broadcasted_iota(jnp.int32, (128, 128), 0) // group_size
    over = lax.broadcasted_iota(jnp.int32, (128, 128), 1) // group_size
    spread = dot(stacked, (side == over).astype(WIDE), 1, 0, lax.Precision.HIGHEST)
    return jnp.concatenate([spread[c * 8 : (c + 1) * 8] for c in range(tiles)], axis=1)


def place_kernel(rows_ref, meta_ref, bias_ref, *, group):
    lanes = meta_ref.shape[1]
    tokens = lanes // group
    row_first = lax.axis_index("ctx") * tokens
    mine = pl.ds(pl.multiple_of(row_first, tokens), tokens)
    row = lax.broadcasted_iota(jnp.int32, (8, tokens), 0)
    both = jnp.where(row == 0, rows_ref[0:1, mine] - row_first, rows_ref[1:2, mine]).astype(WIDE)
    repeat = lax.broadcasted_iota(jnp.int32, (tokens, lanes), 0) == (
        lax.broadcasted_iota(jnp.int32, (tokens, lanes), 1) // group
    )
    meta = dot(both, repeat.astype(WIDE), 1, 0, lax.Precision.HIGHEST).astype(jnp.int32)
    meta_ref[...] = meta
    first = meta[0:1, :]
    key, here = places(lanes, tokens, group)
    bias_ref[0] = jnp.where(jnp.where(here, key, key - 2 * tokens) >= first, 0.0, far_below)
    bias_ref[1] = jnp.where(key - tokens >= first, 0.0, far_below)


def slots_of(lanes, group, owned):
    per_group = group // owned
    head = lane_head((1, lanes), group)
    return head ^ ((lax.axis_index("ctx") % per_group) * owned)


def tenants_of(lanes, tenants, rank):
    row = lax.broadcasted_iota(jnp.int32, (tenants * rank, lanes), 0) // rank
    return row ^ (lax.axis_index("rep") * (tenants // lax.axis_size("rep")))


def picked_rows(rows, owner, slots, tenants, rank, group):
    lanes = owner.shape[1]
    mine = owner == tenants_of(lanes, tenants, rank)
    rows = jnp.where(mine, jnp.concatenate([rows] * (tenants * rank // 8), axis=0), 0.0)
    return [jnp.where(slots == h, rows, 0.0).astype(LOW) for h in range(group)]


def pull_kernel(
    meta_ref, cot_ref, rot_ref, q_ref, cots_ref, queries_ref, pulled_ref, pull_ref,
    *, kv, group, tenants, rank, owned,
):
    owner = meta_ref[1:2, :]
    lanes = owner.shape[1]
    cots = group_rows(cot_ref, kv, group)
    rots = group_rows(rot_ref, kv, group)
    on_rot = dot(jnp.concatenate(rots, axis=1), jnp.concatenate(cots, axis=1), 1, 1)
    pulled = own_terms(on_rot, owner, tenants, rank, group).astype(LOW).astype(WIDE)
    pulled_ref[...] = pulled
    for g, rows in enumerate(group_rows(q_ref, kv, group)):
        queries_ref[g] = rows
        cots_ref[g] = cots[g]
    span = tenants * rank
    slots = slots_of(lanes, group, owned)
    for h, rows in enumerate(picked_rows(pulled, owner, slots, tenants, rank, group)):
        pull_ref[h * span : (h + 1) * span, :] = rows


def hidden_grad_kernel(
    meta_ref, pulled_ref, cots_ref, rot_ref, proj_ref, gh_ref, diff_ref, *, kv, group, tenants, rank,
):
    owner = meta_ref[1:2, :]
    lanes = owner.shape[1]
    dim = cots_ref.shape[2]
    pulled = pulled_ref[...]
    same_head = lax.broadcasted_iota(jnp.int32, (group, lanes), 0) == lane_head((group, lanes), group)
    picked = []
    for tenant in range(tenants):
        keep = same_head & (owner == tenant)
        for k in range(rank):
            picked.append(jnp.where(keep, pulled[k : k + 1], 0.0))
    picked = jnp.concatenate(picked, axis=0).T.astype(LOW)
    rots = group_rows(rot_ref, kv, group)
    projs = group_rows(proj_ref, kv, group)
    diffs = [(proj.astype(WIDE) - rot.astype(WIDE)).astype(LOW) for proj, rot in zip(projs, rots)]
    steered = dot(picked, jnp.concatenate(diffs, axis=1), 1, 0)
    for g in range(kv):
        diff_ref[g] = diffs[g]
        gh_ref[g] = (cots_ref[g].astype(WIDE) + steered[:, g * dim : (g + 1) * dim]).astype(LOW)


def places(lanes, tokens, group):
    key = lax.broadcasted_iota(jnp.int32, (tokens, lanes), 0)
    query = lax.broadcasted_iota(jnp.int32, (tokens, lanes), 1) // group
    return key, key <= query


def window_of(two_ref, one_ref, own_ref, head):
    return jnp.concatenate([two_ref[head], one_ref[head], own_ref[head]], axis=0)


def weigh(windows_ref, queries_ref, bias_ref, low_ref, group, scaling, first):
    tokens = windows_ref.shape[1] // 3
    _, here = places(queries_ref.shape[1], tokens, group)
    count = low_ref.shape[0]
    scores = dot(windows_ref[first], queries_ref[first], 1, 1)
    for at in range(count):
        ahead = dot(windows_ref[first + at + 1], queries_ref[first + at + 1], 1, 1) if at + 1 < count else None
        fold = jnp.where(here, scores[2 * tokens :], scores[0:tokens]) * scaling + bias_ref[0]
        mid = scores[tokens : 2 * tokens] * scaling + bias_ref[1]
        top = jnp.max(jnp.maximum(fold, mid), axis=0, keepdims=True)
        fold = jnp.exp(fold - top)
        mid = jnp.exp(mid - top)
        share = 1.0 / jnp.sum(fold + mid, axis=0, keepdims=True)
        fold = fold * share
        pieces = [jnp.where(here, 0.0, fold), mid * share, jnp.where(here, fold, 0.0)]
        low_ref[at] = jnp.concatenate([piece.astype(LOW) for piece in pieces], axis=0)
        scores = ahead


def near_kernel(
    queries_ref, two_ref, one_ref, own_ref, bias_ref, low_ref, windows_ref, wide_ref, *, kv, group, scaling,
):
    tokens = own_ref.shape[0] // kv
    for at, ref in enumerate((two_ref, one_ref, own_ref)):
        wide_ref[at] = ref[...].astype(WIDE)
        for m in range(kv):
            rows = wide_ref[at, pl.ds(m, tokens, stride=kv), :]
            windows_ref[m, at * tokens : (at + 1) * tokens, :] = rows.astype(LOW)
    weigh(windows_ref, queries_ref, bias_ref, low_ref, group, scaling, 0)


def far_kernel(queries_ref, windows_ref, bias_ref, low_ref, *, group, scaling, first):
    weigh(windows_ref, queries_ref, bias_ref, low_ref, group, scaling, first)


def forward_kernel(
    shift_ref, near_ref, far_ref, two_ref, one_ref, own_ref, cots_ref, diff_ref, meta_ref, pull_ref,
    send_ref, keep_ref, *, kv, group, tenants, rank, owned,
):
    dim = own_ref.shape[2]
    owner = meta_ref[1:2, :]
    lanes = owner.shape[1]
    hidden = []
    for g in range(kv):
        low = (near_ref if g < kv // 2 else far_ref)[g % (kv // 2)]
        hidden.append(dot(window_of(two_ref, one_ref, own_ref, g), low, 0, 0).astype(LOW))
    hidden = jnp.concatenate(hidden, axis=0)
    on_diff = dot(jnp.concatenate([diff_ref[g] for g in range(kv)], axis=1), hidden, 1, 0)
    lifted = own_terms(on_diff, owner, tenants, rank, group)
    one_hot = (owner == lax.broadcasted_iota(jnp.int32, (tenants, lanes), 0)).astype(WIDE)
    bias = jnp.concatenate([shift_ref[...]] * (8 // rank), axis=0)
    shift = dot(bias, one_hot, 1, 0, lax.Precision.HIGHEST)
    lifted = (lifted + shift).astype(LOW).astype(WIDE)
    rep = lax.axis_size("rep")
    me = lax.axis_index("ctx")
    per_group = group // owned
    span = tenants * rank
    slots = slots_of(lanes, group, owned)
    lift_all = jnp.concatenate(picked_rows(lifted, owner, slots, tenants, rank, group), axis=0)
    on_proj = dot(pull_ref[...], hidden, 1, 1)
    on_rot = dot(lift_all, jnp.concatenate([cots_ref[g] for g in range(kv)], axis=1), 1, 0) - on_proj
    here_rows = span // rep
    for g in range(kv):
        columns = slice(g * dim, (g + 1) * dim)
        for low in range(per_group):
            device = (g ^ (me // per_group)) * per_group + low
            into = send_ref if low % 2 else keep_ref
            for r in range(rep):
                pieces = []
                for h in range(low * owned, (low + 1) * owned):
                    rows = slice(h * span + r * here_rows, h * span + (r + 1) * here_rows)
                    pieces += [on_rot[rows, columns], on_proj[rows, columns]]
                into[reduce_place(dict(ctx=device, rep=r))] = jnp.concatenate(pieces, axis=0).astype(LOW)


def backward_kernel(
    queries_ref, gh_ref, near_ref, far_ref, two_ref, one_ref, own_ref,
    back_two_ref, back_one_ref, back_own_ref, grad_ref, *, kv, scaling,
):
    tokens = own_ref.shape[1]

    def weight_grad_of(g):
        return dot(window_of(two_ref, one_ref, own_ref, g), gh_ref[g], 1, 1)

    weight_grad = weight_grad_of(0)
    for g in range(kv):
        ahead = weight_grad_of(g + 1) if g + 1 < kv else None
        low = (near_ref if g < kv // 2 else far_ref)[g % (kv // 2)]
        weights = low.astype(WIDE)
        delta = jnp.sum(weights * weight_grad, axis=0, keepdims=True)
        score_grad = (weights * (weight_grad - delta)).astype(LOW)
        grad_ref[g] = score_grad
        key_grad = dot(score_grad, queries_ref[g], 1, 0) * scaling
        value_grad = dot(low, gh_ref[g], 1, 0)
        for place, grad in ((g, key_grad), (kv + g, value_grad)):
            back_two_ref[place] = grad[0:tokens].astype(LOW)
            back_one_ref[place] = grad[tokens : 2 * tokens].astype(LOW)
            back_own_ref[place] = grad[2 * tokens :]
        weight_grad = ahead


def query_kernel(
    grad_ref, windows_ref, dq_hbm, dq_ref, sems, *, kv, group, scaling,
):
    tokens, _, dim = dq_ref.shape
    copies = []
    for g in range(kv):
        query_grad = dot(windows_ref[g], grad_ref[g], 0, 0) * scaling
        query_grad = query_grad.T.reshape(tokens, group, dim)
        if g % 2 == 1:
            heads = slice((g - 1) * group, (g + 1) * group)
            dq_ref[:, heads, :] = jnp.concatenate([before, query_grad], axis=1).astype(LOW)
            copies.append(pltpu.make_async_copy(dq_ref.at[:, heads], dq_hbm.at[:, heads], sems.at[g // 2]))
            copies[-1].start()
        before = query_grad
    for copy in copies:
        copy.wait()


def finish_kernel(
    own_ref, mate_ref, two_ref, part_ref, *refs, kv, owned,
):
    *other_refs, keys_ref, values_ref, rot_ref, proj_ref, wide_ref = refs
    total = part_ref[0].astype(WIDE)
    for other_ref in other_refs:
        total = total + other_ref[0].astype(WIDE)
    size = rot_ref.shape[0]
    for place in range(owned):
        for at, out in enumerate((rot_ref, proj_ref)):
            row = (2 * place + at) * size
            out[:, place, :] = total[row : row + size]
    tokens = own_ref.shape[1]
    even = (lax.axis_index("ctx") % 2 == 0).astype(WIDE)
    for at, out in enumerate((keys_ref, values_ref)):
        for m in range(kv):
            place = at * kv + m
            total = own_ref[place] + two_ref[place].astype(WIDE) + even * mate_ref[place].astype(WIDE)
            wide_ref[at, pl.ds(m, tokens, stride=kv), :] = total
        out[...] = wide_ref[at].astype(LOW)


def on_device(
    query_rows, key_rows, value_matrix, cotangent, rotation, projection, shift_bias, doc_starts, tenant_ids,
):
    queries = query_rows[0]
    upstream = cotangent[0]
    tokens, heads, dim = queries.shape
    kv = key_rows.shape[2]
    group = heads // kv
    scaling = dim ** (-0.5)
    tenants, rank = rotation.shape[0], rotation.shape[1]
    lanes = tokens * group
    ctx = lax.axis_size("ctx")
    rep = lax.axis_size("rep")
    assert 2 * tokens == DOC_MAX


    rot = rotation.reshape(tenants * rank, heads, dim)
    proj = projection.reshape(tenants * rank, heads, dim)
    sizes = dict(kv=kv, group=group)
    vmem = pl.BlockSpec(memory_space=pltpu.VMEM)

    def call(body, outs, flops, moved, out_specs=None, scratch=(), **fixed):
        def run(*operands):
            return pl.pallas_call(
                lambda *refs: body(*refs, **fixed),
                out_shape=[jax.ShapeDtypeStruct(*out) for out in outs],
                in_specs=[vmem] * len(operands),
                out_specs=out_specs or [vmem] * len(outs),
                scratch_shapes=scratch,
                compiler_params=pltpu.CompilerParams(vmem_limit_bytes=12 * 2**20),
                name=body.__name__,
                cost_estimate=pl.CostEstimate(flops=flops, bytes_accessed=moved, transcendentals=0),
            )(*operands)

        return run

    span = tenants * rank
    here = heads // ctx
    rows = here * 2 * span // rep
    even = jnp.reshape(lax.axis_index("ctx") % 2 == 0, (1, 1, 1))
    key_rows, even = lax.optimization_barrier((key_rows, even))
    own_keys = key_rows[0]
    two_keys = shifted(own_keys, "ctx", 2)
    meta, biases = call(
        place_kernel, [((8, lanes), jnp.int32), ((2, tokens, lanes), WIDE)], 8 * 2**30, 2**20,
        group=group,
    )(jnp.concatenate([doc_starts, tenant_ids], axis=0))
    own_values, meta = lax.optimization_barrier((jnp.moveaxis(value_matrix[0], 1, 0), meta))
    two_values = shifted(own_values, "ctx", 2)
    cots, queries, pulled, pull = call(
        pull_kernel,
        [((kv, lanes, dim), LOW), ((kv, lanes, dim), LOW), ((8, lanes), WIDE), ((span * group, lanes), LOW)],
        2**30, 4 * 2**20, tenants=tenants, rank=rank, owned=here, **sizes,
    )(meta, upstream, rot, queries)
    two_keys, pulled = lax.optimization_barrier((two_keys, pulled))
    one_keys = exchanged(jnp.where(even, own_keys, two_keys), {"ctx": 1})
    grad_hidden, diff = call(
        hidden_grad_kernel, [((kv, lanes, dim), LOW), ((kv, span * group, dim), LOW)],
        2 * 2**30, 4 * 2**20, tenants=tenants, rank=rank, **sizes,
    )(meta, pulled, cots, rot, proj)
    one_keys, grad_hidden = lax.optimization_barrier((one_keys, grad_hidden))

    flat = (tokens * kv, dim)
    near, windows = call(
        near_kernel, [((kv // 2, 3 * tokens, lanes), LOW), ((kv, 3 * tokens, dim), LOW)], 2 * 2**30, 4 * 2**20,
        scratch=[pltpu.VMEM((3, *flat), WIDE)], scaling=scaling, **sizes,
    )(queries, two_keys.reshape(flat), one_keys.reshape(flat), own_keys.reshape(flat), biases)
    two_values, near = lax.optimization_barrier((two_values, near))
    one_values = exchanged(jnp.where(even, own_values, two_values), {"ctx": 1})
    far, = call(
        far_kernel, [((kv // 2, 3 * tokens, lanes), LOW)], 2 * 2**30, 4 * 2**20,
        group=group, scaling=scaling, first=kv // 2,
    )(queries, windows, biases)
    one_values, far = lax.optimization_barrier((one_values, far))
    send, keep = call(
        forward_kernel, [((ctx * rep // 2, rows, dim), LOW)] * 2, 4 * 2**30, 10 * 2**20,
        tenants=tenants, rank=rank, owned=here, **sizes,
    )(shift_bias.T, near, far, two_values, one_values, own_values, cots, diff, meta, pull)
    part = (keep.astype(WIDE) + exchanged(send, {"ctx": 1}).astype(WIDE)).astype(LOW)
    near, part = lax.optimization_barrier((near, part))
    window = (2 * kv, tokens, dim)
    back_two, back_one, back_own, score_grad = call(
        backward_kernel, [(window, LOW), (window, LOW), (window, WIDE), ((kv, 3 * tokens, lanes), LOW)],
        4 * 2**30, 10 * 2**20, kv=kv, scaling=scaling,
    )(queries, grad_hidden, near, far, two_values, one_values, own_values)
    d_queries, = call(
        query_kernel, [((tokens, heads, dim), LOW)], 2 * 2**30, 5 * 2**20,
        scratch=[pltpu.VMEM((tokens, heads, dim), LOW), pltpu.SemaphoreType.DMA((kv // 2,))],
        out_specs=[pl.BlockSpec(memory_space=pltpu.HBM)], scaling=scaling, **sizes,
    )(score_grad, windows)
    from_mate = exchanged(back_one, {"ctx": 1})
    onward = back_two.astype(WIDE) + jnp.where(even, 0.0, from_mate.astype(WIDE))
    onward = onward.astype(LOW)

    groups = reduce_groups()
    for at, group_bits in enumerate(groups):
        beside = back_own if at == 0 else None
        if at == len(groups) - 1:
            part, onward = lax.optimization_barrier((part, onward))
            from_two = shifted(onward, "ctx", -2)
            beside = from_two
        part, others = scattered(part, group_bits, beside)
        if at < len(groups) - 1:
            part = part.astype(WIDE) + sum(other.astype(WIDE) for other in others)
            part = part.astype(LOW)
    d_keys, d_values, *grads = call(
        finish_kernel, [((tokens * kv, dim), LOW)] * 2 + [((span // rep, here, dim), WIDE)] * 2, 2**20, 2**20,
        scratch=[pltpu.VMEM((2, tokens * kv, dim), WIDE)], kv=kv, owned=here,
    )(back_own, from_mate, from_two, part, *others)
    grads = [grad.reshape(tenants // rep, rank, here, dim) for grad in grads]
    d_keys, d_values = (grad.reshape(key_rows.shape) for grad in (d_keys, d_values))
    return (d_queries[None], d_keys, d_values, grads[0], grads[1])


def solution(mesh):
    rows = P("rep", "ctx", None, None)
    in_specs = (rows, rows, rows, rows, P(), P(), P(), P("rep", None), P("rep", None))
    tenant_rows = P("rep", None, "ctx", None)
    out_specs = (rows, rows, rows, tenant_rows, tenant_rows)
    return jax.shard_map(
        on_device, mesh=mesh, in_specs=in_specs, out_specs=out_specs, check_vma=False
    )
```

```python
import itertools

import jax
import jax.numpy as jnp
import numpy as np
from jax import lax
from jax.experimental import pallas as pl
from jax.experimental.pallas import tpu as pltpu
from jax.sharding import PartitionSpec as P

DOC_MAX = 256
LOW = jnp.bfloat16
WIDE = jnp.float32
far_below = -1e30


def shifted(value, axis, steps):
    count = lax.axis_size(axis)
    return lax.ppermute(value, axis, [(source, (source + steps) % count) for source in range(count)])


def exchanged(value, bits):
    axes = tuple(bits)
    shape = [lax.axis_size(axis) for axis in axes]
    pairs = []
    for source in np.ndindex(*shape):
        target = [at ^ bits[axis] for at, axis in zip(source, axes)]
        pairs.append((np.ravel_multi_index(source, shape), np.ravel_multi_index(target, shape)))
    return lax.ppermute(value, axes, [(int(source), int(target)) for source, target in pairs])


def reduce_groups():
    ctx, rep = lax.axis_size("ctx"), lax.axis_size("rep")
    bits = [{"ctx": 1 << at} for at in range(ctx.bit_length() - 2, 0, -1)]
    bits += [{"rep": 1 << at} for at in range(rep.bit_length() - 1)]
    return [bits[at : at + 2] for at in range(0, len(bits), 2)]


def reduce_place(index):
    place = 0
    for bits in itertools.chain(*reduce_groups()):
        for axis, bit in bits.items():
            place = 2 * place + (index[axis] // bit) % 2
    return place


def scattered(part, group, beside=None):
    count = 1 << len(group)
    size = part.shape[0] // count
    others = []
    for j in range(1, count):
        bits = {}
        for at, pair in enumerate(reversed(group)):
            if (j >> at) & 1:
                bits.update({axis: bits.get(axis, 0) | bit for axis, bit in pair.items()})
        others.append(exchanged(part[j * size : (j + 1) * size], bits))
    if beside is not None:
        others = lax.optimization_barrier((others, beside))[0]
    return part[:size], others


def dot(left, right, left_dim, right_dim, precision=None):
    return lax.dot_general(
        left, right, (((left_dim,), (right_dim,)), ((), ())),
        precision=precision, preferred_element_type=WIDE,
    )


def group_rows(ref, kv_count, group_size):
    rows, _, dim = ref.shape
    wide = 2 * group_size
    parts = []
    for pair in range(kv_count // 2):
        both = ref[:, pair * wide : (pair + 1) * wide, :].astype(WIDE)
        for half in range(2):
            one = both[:, half * group_size : (half + 1) * group_size, :]
            parts.append(one.reshape(rows * group_size, dim).astype(LOW))
    return parts


def lane_head(shape, group_size):
    return lax.broadcasted_iota(jnp.int32, shape, 1) % group_size


def own_terms(maps_by_rows, owner, tenants, low_rank, group_size):
    lanes = maps_by_rows.shape[1]
    same_head = lax.broadcasted_iota(jnp.int32, (group_size, lanes), 0) == lane_head(
        (group_size, lanes), group_size
    )
    span = low_rank * group_size
    total = jnp.zeros((low_rank, group_size, lanes), WIDE)
    for tenant in range(tenants):
        keep = same_head & (owner == tenant)
        block = maps_by_rows[tenant * span : (tenant + 1) * span].reshape(
            low_rank, group_size, lanes
        )
        total = total + jnp.where(keep[None], block, 0.0)
    rows = jnp.sum(total, axis=1)
    rows = jnp.concatenate([rows, rows], axis=0)
    tiles = lanes // 128
    stacked = jnp.concatenate([rows[:, c * 128 : (c + 1) * 128] for c in range(tiles)], axis=0)
    side = lax.broadcasted_iota(jnp.int32, (128, 128), 0) // group_size
    over = lax.broadcasted_iota(jnp.int32, (128, 128), 1) // group_size
    spread = dot(stacked, (side == over).astype(WIDE), 1, 0, lax.Precision.HIGHEST)
    return jnp.concatenate([spread[c * 8 : (c + 1) * 8] for c in range(tiles)], axis=1)


def place_kernel(rows_ref, meta_ref, bias_ref, *, group):
    lanes = meta_ref.shape[1]
    tokens = lanes // group
    row_first = lax.axis_index("ctx") * tokens
    mine = pl.ds(pl.multiple_of(row_first, tokens), tokens)
    row = lax.broadcasted_iota(jnp.int32, (8, tokens), 0)
    both = jnp.where(row == 0, rows_ref[0:1, mine] - row_first, rows_ref[1:2, mine]).astype(WIDE)
    repeat = lax.broadcasted_iota(jnp.int32, (tokens, lanes), 0) == (
        lax.broadcasted_iota(jnp.int32, (tokens, lanes), 1) // group
    )
    meta = dot(both, repeat.astype(WIDE), 1, 0, lax.Precision.HIGHEST).astype(jnp.int32)
    meta_ref[...] = meta
    first = meta[0:1, :]
    key, here = places(lanes, tokens, group)
    bias_ref[0] = jnp.where(jnp.where(here, key, key - 2 * tokens) >= first, 0.0, far_below)
    bias_ref[1] = jnp.where(key - tokens >= first, 0.0, far_below)


def slots_of(lanes, group, owned):
    per_group = group // owned
    head = lane_head((1, lanes), group)
    return head ^ ((lax.axis_index("ctx") % per_group) * owned)


def tenants_of(lanes, tenants, rank):
    row = lax.broadcasted_iota(jnp.int32, (tenants * rank, lanes), 0) // rank
    return row ^ (lax.axis_index("rep") * (tenants // lax.axis_size("rep")))


def picked_rows(rows, owner, slots, tenants, rank, group):
    lanes = owner.shape[1]
    mine = owner == tenants_of(lanes, tenants, rank)
    rows = jnp.where(mine, jnp.concatenate([rows] * (tenants * rank // 8), axis=0), 0.0)
    return [jnp.where(slots == h, rows, 0.0).astype(LOW) for h in range(group)]


def pull_kernel(
    meta_ref, cot_ref, rot_ref, q_ref, cots_ref, queries_ref, pulled_ref, pull_ref,
    *, kv, group, tenants, rank, owned,
):
    owner = meta_ref[1:2, :]
    lanes = owner.shape[1]
    cots = group_rows(cot_ref, kv, group)
    rots = group_rows(rot_ref, kv, group)
    on_rot = dot(jnp.concatenate(rots, axis=1), jnp.concatenate(cots, axis=1), 1, 1)
    pulled = own_terms(on_rot, owner, tenants, rank, group).astype(LOW).astype(WIDE)
    pulled_ref[...] = pulled
    for g, rows in enumerate(group_rows(q_ref, kv, group)):
        queries_ref[g] = rows
        cots_ref[g] = cots[g]
    span = tenants * rank
    slots = slots_of(lanes, group, owned)
    for h, rows in enumerate(picked_rows(pulled, owner, slots, tenants, rank, group)):
        pull_ref[h * span : (h + 1) * span, :] = rows


def hidden_grad_kernel(
    meta_ref, pulled_ref, cots_ref, rot_ref, proj_ref, gh_ref, diff_ref, *, kv, group, tenants, rank,
):
    owner = meta_ref[1:2, :]
    lanes = owner.shape[1]
    dim = cots_ref.shape[2]
    pulled = pulled_ref[...]
    same_head = lax.broadcasted_iota(jnp.int32, (group, lanes), 0) == lane_head((group, lanes), group)
    picked = []
    for tenant in range(tenants):
        keep = same_head & (owner == tenant)
        for k in range(rank):
            picked.append(jnp.where(keep, pulled[k : k + 1], 0.0))
    picked = jnp.concatenate(picked, axis=0).T.astype(LOW)
    rots = group_rows(rot_ref, kv, group)
    projs = group_rows(proj_ref, kv, group)
    diffs = [(proj.astype(WIDE) - rot.astype(WIDE)).astype(LOW) for proj, rot in zip(projs, rots)]
    steered = dot(picked, jnp.concatenate(diffs, axis=1), 1, 0)
    for g in range(kv):
        diff_ref[g] = diffs[g]
        gh_ref[g] = (cots_ref[g].astype(WIDE) + steered[:, g * dim : (g + 1) * dim]).astype(LOW)


def places(lanes, tokens, group):
    key = lax.broadcasted_iota(jnp.int32, (tokens, lanes), 0)
    query = lax.broadcasted_iota(jnp.int32, (tokens, lanes), 1) // group
    return key, key <= query


def window_of(two_ref, one_ref, own_ref, head):
    return jnp.concatenate([two_ref[head], one_ref[head], own_ref[head]], axis=0)


def head_major(ref, wide_ref, outs):
    count = len(outs)
    wide_ref[...] = ref[...].astype(WIDE)
    for m, out in enumerate(outs):
        out[...] = wide_ref[pl.ds(m, out.shape[0], stride=count), :].astype(LOW)


def fold_kernel(
    queries_ref, two_ref, own_ref, bias_ref, fold_ref, stats_ref, two_keys_ref, own_keys_ref, wide_ref,
    *, kv, group, scaling,
):
    tokens = two_keys_ref.shape[1]
    _, here = places(queries_ref.shape[1], tokens, group)
    for at, (ref, keys_ref) in enumerate(((two_ref, two_keys_ref), (own_ref, own_keys_ref))):
        head_major(ref, wide_ref.at[at], [keys_ref.at[m] for m in range(kv)])

    def scores_of(g):
        return dot(jnp.concatenate([two_keys_ref[g], own_keys_ref[g]], axis=0), queries_ref[g], 1, 1)

    scores = scores_of(0)
    for g in range(kv):
        ahead = scores_of(g + 1) if g + 1 < kv else None
        fold = jnp.where(here, scores[tokens:], scores[0:tokens]) * scaling + bias_ref[0]
        top = jnp.max(fold, axis=0, keepdims=True)
        fold = jnp.exp(fold - top)
        fold_ref[g] = fold
        stats_ref[g, 0:1, :] = top
        stats_ref[g, 1:2, :] = jnp.sum(fold, axis=0, keepdims=True)
        scores = ahead


def middle_kernel(
    queries_ref, one_ref, bias_ref, fold_ref, stats_ref, low_ref, one_keys_ref, wide_ref, *, kv, group, scaling,
):
    tokens = one_keys_ref.shape[1]
    _, here = places(queries_ref.shape[1], tokens, group)
    head_major(one_ref, wide_ref, [one_keys_ref.at[m] for m in range(kv)])

    def scores_of(g):
        return dot(one_keys_ref[g], queries_ref[g], 1, 1)

    scores = scores_of(0)
    for g in range(kv):
        ahead = scores_of(g + 1) if g + 1 < kv else None
        mid = scores * scaling + bias_ref[1]
        fold_top = stats_ref[g, 0:1, :]
        top = jnp.maximum(fold_top, jnp.max(mid, axis=0, keepdims=True))
        mid = jnp.exp(mid - top)
        fade = jnp.exp(fold_top - top)
        share = 1.0 / (stats_ref[g, 1:2, :] * fade + jnp.sum(mid, axis=0, keepdims=True))
        fold = fold_ref[g] * (fade * share)
        low_ref[g, 0:tokens, :] = jnp.where(here, 0.0, fold).astype(LOW)
        low_ref[g, tokens : 2 * tokens, :] = (mid * share).astype(LOW)
        low_ref[g, 2 * tokens :, :] = jnp.where(here, fold, 0.0).astype(LOW)
        scores = ahead


def forward_kernel(
    shift_ref, low_ref, two_ref, one_ref, own_ref, cots_ref, diff_ref, meta_ref, pull_ref,
    send_ref, keep_ref, values_ref, wide_ref, *, kv, group, tenants, rank, owned,
):
    dim = own_ref.shape[1]
    tokens = own_ref.shape[0] // kv
    for at, ref in enumerate((two_ref, one_ref, own_ref)):
        rows = slice(at * tokens, (at + 1) * tokens)
        head_major(ref, wide_ref.at[at], [values_ref.at[m, rows] for m in range(kv)])
    owner = meta_ref[1:2, :]
    lanes = owner.shape[1]
    hidden = []
    for g in range(kv):
        hidden.append(dot(values_ref[g], low_ref[g], 0, 0).astype(LOW))
    hidden = jnp.concatenate(hidden, axis=0)
    on_diff = dot(jnp.concatenate([diff_ref[g] for g in range(kv)], axis=1), hidden, 1, 0)
    lifted = own_terms(on_diff, owner, tenants, rank, group)
    one_hot = (owner == lax.broadcasted_iota(jnp.int32, (tenants, lanes), 0)).astype(WIDE)
    bias = jnp.concatenate([shift_ref[...]] * (8 // rank), axis=0)
    shift = dot(bias, one_hot, 1, 0, lax.Precision.HIGHEST)
    lifted = (lifted + shift).astype(LOW).astype(WIDE)
    rep = lax.axis_size("rep")
    me = lax.axis_index("ctx")
    per_group = group // owned
    span = tenants * rank
    slots = slots_of(lanes, group, owned)
    lift_all = jnp.concatenate(picked_rows(lifted, owner, slots, tenants, rank, group), axis=0)
    on_proj = dot(pull_ref[...], hidden, 1, 1)
    on_rot = dot(lift_all, jnp.concatenate([cots_ref[g] for g in range(kv)], axis=1), 1, 0) - on_proj
    here_rows = span // rep
    for g in range(kv):
        columns = slice(g * dim, (g + 1) * dim)
        for low in range(per_group):
            device = (g ^ (me // per_group)) * per_group + low
            into = send_ref if low % 2 else keep_ref
            for r in range(rep):
                pieces = []
                for h in range(low * owned, (low + 1) * owned):
                    rows = slice(h * span + r * here_rows, h * span + (r + 1) * here_rows)
                    pieces += [on_rot[rows, columns], on_proj[rows, columns]]
                into[reduce_place(dict(ctx=device, rep=r))] = jnp.concatenate(pieces, axis=0).astype(LOW)


def backward_kernel(
    queries_ref, gh_ref, low_ref, values_ref, back_two_ref, back_one_ref, back_own_ref, grad_ref, *, kv, scaling,
):
    tokens = back_own_ref.shape[1]

    def weight_grad_of(g):
        return dot(values_ref[g], gh_ref[g], 1, 1)

    weight_grad = weight_grad_of(0)
    for g in range(kv):
        ahead = weight_grad_of(g + 1) if g + 1 < kv else None
        low = low_ref[g]
        weights = low.astype(WIDE)
        delta = jnp.sum(weights * weight_grad, axis=0, keepdims=True)
        score_grad = (weights * (weight_grad - delta)).astype(LOW)
        grad_ref[g] = score_grad
        key_grad = dot(score_grad, queries_ref[g], 1, 0) * scaling
        value_grad = dot(low, gh_ref[g], 1, 0)
        for place, grad in ((g, key_grad), (kv + g, value_grad)):
            back_two_ref[place] = grad[0:tokens].astype(LOW)
            back_one_ref[place] = grad[tokens : 2 * tokens].astype(LOW)
            back_own_ref[place] = grad[2 * tokens :]
        weight_grad = ahead


def query_kernel(
    grad_ref, two_ref, one_ref, own_ref, dq_hbm, dq_ref, sems, *, kv, group, scaling,
):
    tokens, _, dim = dq_ref.shape
    copies = []
    for g in range(kv):
        query_grad = dot(window_of(two_ref, one_ref, own_ref, g), grad_ref[g], 0, 0) * scaling
        query_grad = query_grad.T.reshape(tokens, group, dim)
        if g % 2 == 1:
            heads = slice((g - 1) * group, (g + 1) * group)
            dq_ref[:, heads, :] = jnp.concatenate([before, query_grad], axis=1).astype(LOW)
            copies.append(pltpu.make_async_copy(dq_ref.at[:, heads], dq_hbm.at[:, heads], sems.at[g // 2]))
            copies[-1].start()
        before = query_grad
    for copy in copies:
        copy.wait()


def finish_kernel(
    own_ref, mate_ref, two_ref, part_ref, *refs, kv, owned,
):
    *other_refs, keys_ref, values_ref, rot_ref, proj_ref, wide_ref = refs
    total = part_ref[0].astype(WIDE)
    for other_ref in other_refs:
        total = total + other_ref[0].astype(WIDE)
    size = rot_ref.shape[0]
    for place in range(owned):
        for at, out in enumerate((rot_ref, proj_ref)):
            row = (2 * place + at) * size
            out[:, place, :] = total[row : row + size]
    tokens = own_ref.shape[1]
    even = (lax.axis_index("ctx") % 2 == 0).astype(WIDE)
    for at, out in enumerate((keys_ref, values_ref)):
        for m in range(kv):
            place = at * kv + m
            total = own_ref[place] + two_ref[place].astype(WIDE) + even * mate_ref[place].astype(WIDE)
            wide_ref[at, pl.ds(m, tokens, stride=kv), :] = total
        out[...] = wide_ref[at].astype(LOW)


def on_device(
    query_rows, key_rows, value_matrix, cotangent, rotation, projection, shift_bias, doc_starts, tenant_ids,
):
    queries = query_rows[0]
    upstream = cotangent[0]
    tokens, heads, dim = queries.shape
    kv = key_rows.shape[2]
    group = heads // kv
    scaling = dim ** (-0.5)
    tenants, rank = rotation.shape[0], rotation.shape[1]
    lanes = tokens * group
    ctx = lax.axis_size("ctx")
    rep = lax.axis_size("rep")
    assert 2 * tokens == DOC_MAX


    rot = rotation.reshape(tenants * rank, heads, dim)
    proj = projection.reshape(tenants * rank, heads, dim)
    sizes = dict(kv=kv, group=group)
    vmem = pl.BlockSpec(memory_space=pltpu.VMEM)

    def call(body, outs, flops, moved, out_specs=None, scratch=(), **fixed):
        def run(*operands):
            return pl.pallas_call(
                lambda *refs: body(*refs, **fixed),
                out_shape=[jax.ShapeDtypeStruct(*out) for out in outs],
                in_specs=[vmem] * len(operands),
                out_specs=out_specs or [vmem] * len(outs),
                scratch_shapes=scratch,
                compiler_params=pltpu.CompilerParams(vmem_limit_bytes=12 * 2**20),
                name=body.__name__,
                cost_estimate=pl.CostEstimate(flops=flops, bytes_accessed=moved, transcendentals=0),
            )(*operands)

        return run

    span = tenants * rank
    here = heads // ctx
    rows = here * 2 * span // rep
    even = jnp.reshape(lax.axis_index("ctx") % 2 == 0, (1, 1, 1))
    key_rows, even = lax.optimization_barrier((key_rows, even))
    own_keys = key_rows[0]
    two_keys = shifted(own_keys, "ctx", 2)
    meta, biases = call(
        place_kernel, [((8, lanes), jnp.int32), ((2, tokens, lanes), WIDE)], 8 * 2**30, 2**20,
        group=group,
    )(jnp.concatenate([doc_starts, tenant_ids], axis=0))
    own_values, meta = lax.optimization_barrier((value_matrix[0], meta))
    two_values = shifted(own_values, "ctx", 2)
    cots, queries, pulled, pull = call(
        pull_kernel,
        [((kv, lanes, dim), LOW), ((kv, lanes, dim), LOW), ((8, lanes), WIDE), ((span * group, lanes), LOW)],
        2**30, 4 * 2**20, tenants=tenants, rank=rank, owned=here, **sizes,
    )(meta, upstream, rot, queries)
    grad_hidden, diff = call(
        hidden_grad_kernel, [((kv, lanes, dim), LOW), ((kv, span * group, dim), LOW)],
        2 * 2**30, 4 * 2**20, tenants=tenants, rank=rank, **sizes,
    )(meta, pulled, cots, rot, proj)
    two_keys, grad_hidden = lax.optimization_barrier((two_keys, grad_hidden))
    one_keys = exchanged(jnp.where(even, own_keys, two_keys), {"ctx": 1})
    flat, heads_first = (tokens * kv, dim), ((kv, tokens, dim), LOW)
    fold, stats, two_heads, own_heads = call(
        fold_kernel, [((kv, tokens, lanes), WIDE), ((kv, 2, lanes), WIDE), heads_first, heads_first],
        2 * 2**30, 4 * 2**20, scratch=[pltpu.VMEM((2, *flat), WIDE)], scaling=scaling, **sizes,
    )(queries, two_keys.reshape(flat), own_keys.reshape(flat), biases)
    one_keys, two_values, fold = lax.optimization_barrier((one_keys, two_values, fold))
    one_values = exchanged(jnp.where(even, own_values, two_values), {"ctx": 1})
    low, one_heads = call(
        middle_kernel, [((kv, 3 * tokens, lanes), LOW), heads_first], 2 * 2**30, 4 * 2**20,
        scratch=[pltpu.VMEM(flat, WIDE)], scaling=scaling, **sizes,
    )(queries, one_keys.reshape(flat), biases, fold, stats)
    one_values, low = lax.optimization_barrier((one_values, low))
    send, keep, values = call(
        forward_kernel, [((ctx * rep // 2, rows, dim), LOW)] * 2 + [((kv, 3 * tokens, dim), LOW)],
        4 * 2**30, 10 * 2**20, scratch=[pltpu.VMEM((3, *flat), WIDE)],
        tenants=tenants, rank=rank, owned=here, **sizes,
    )(
        shift_bias.T, low, two_values.reshape(flat), one_values.reshape(flat), own_values.reshape(flat),
        cots, diff, meta, pull,
    )
    part = (keep.astype(WIDE) + exchanged(send, {"ctx": 1}).astype(WIDE)).astype(LOW)
    low, part = lax.optimization_barrier((low, part))
    window = (2 * kv, tokens, dim)
    back_two, back_one, back_own, score_grad = call(
        backward_kernel, [(window, LOW), (window, LOW), (window, WIDE), ((kv, 3 * tokens, lanes), LOW)],
        4 * 2**30, 10 * 2**20, kv=kv, scaling=scaling,
    )(queries, grad_hidden, low, values)
    d_queries, = call(
        query_kernel, [((tokens, heads, dim), LOW)], 2 * 2**30, 5 * 2**20,
        scratch=[pltpu.VMEM((tokens, heads, dim), LOW), pltpu.SemaphoreType.DMA((kv // 2,))],
        out_specs=[pl.BlockSpec(memory_space=pltpu.HBM)], scaling=scaling, **sizes,
    )(score_grad, two_heads, one_heads, own_heads)
    from_mate = exchanged(back_one, {"ctx": 1})
    onward = back_two.astype(WIDE) + jnp.where(even, 0.0, from_mate.astype(WIDE))
    onward = onward.astype(LOW)

    groups = reduce_groups()
    for at, group_bits in enumerate(groups):
        beside = back_own if at == 0 else None
        if at == len(groups) - 1:
            part, onward = lax.optimization_barrier((part, onward))
            from_two = shifted(onward, "ctx", -2)
            beside = from_two
        part, others = scattered(part, group_bits, beside)
        if at < len(groups) - 1:
            part = part.astype(WIDE) + sum(other.astype(WIDE) for other in others)
            part = part.astype(LOW)
    d_keys, d_values, *grads = call(
        finish_kernel, [((tokens * kv, dim), LOW)] * 2 + [((span // rep, here, dim), WIDE)] * 2, 2**20, 2**20,
        scratch=[pltpu.VMEM((2, tokens * kv, dim), WIDE)], kv=kv, owned=here,
    )(back_own, from_mate, from_two, part, *others)
    grads = [grad.reshape(tenants // rep, rank, here, dim) for grad in grads]
    d_keys, d_values = (grad.reshape(key_rows.shape) for grad in (d_keys, d_values))
    return (d_queries[None], d_keys, d_values, grads[0], grads[1])


def solution(mesh):
    rows = P("rep", "ctx", None, None)
    in_specs = (rows, rows, rows, rows, P(), P(), P(), P("rep", None), P("rep", None))
    tenant_rows = P("rep", None, "ctx", None)
    out_specs = (rows, rows, rows, tenant_rows, tenant_rows)
    return jax.shard_map(
        on_device, mesh=mesh, in_specs=in_specs, out_specs=out_specs, check_vma=False
    )
```

```python
import itertools

import jax
import jax.numpy as jnp
import numpy as np
from jax import lax
from jax.experimental import pallas as pl
from jax.experimental.pallas import tpu as pltpu
from jax.sharding import PartitionSpec as P

DOC_MAX = 256
LOW = jnp.bfloat16
WIDE = jnp.float32
far_below = -1e30


def shifted(value, axis, steps):
    count = lax.axis_size(axis)
    return lax.ppermute(value, axis, [(source, (source + steps) % count) for source in range(count)])


def exchanged(value, bits):
    axes = tuple(bits)
    shape = [lax.axis_size(axis) for axis in axes]
    pairs = []
    for source in np.ndindex(*shape):
        target = [at ^ bits[axis] for at, axis in zip(source, axes)]
        pairs.append((np.ravel_multi_index(source, shape), np.ravel_multi_index(target, shape)))
    return lax.ppermute(value, axes, [(int(source), int(target)) for source, target in pairs])


def reduce_groups():
    ctx, rep = lax.axis_size("ctx"), lax.axis_size("rep")
    bits = [{"ctx": 1 << at} for at in range(ctx.bit_length() - 2, 0, -1)]
    bits += [{"rep": 1 << at} for at in range(rep.bit_length() - 1)]
    return [bits[at : at + 2] for at in range(0, len(bits), 2)]


def reduce_place(index):
    place = 0
    for bits in itertools.chain(*reduce_groups()):
        for axis, bit in bits.items():
            place = 2 * place + (index[axis] // bit) % 2
    return place


def scattered(part, group, beside=None):
    count = 1 << len(group)
    size = part.shape[0] // count
    others = []
    for j in range(1, count):
        bits = {}
        for at, pair in enumerate(reversed(group)):
            if (j >> at) & 1:
                bits.update({axis: bits.get(axis, 0) | bit for axis, bit in pair.items()})
        others.append(exchanged(part[j * size : (j + 1) * size], bits))
    if beside is not None:
        others = lax.optimization_barrier((others, beside))[0]
    return part[:size], others


def dot(left, right, left_dim, right_dim, precision=None):
    return lax.dot_general(
        left, right, (((left_dim,), (right_dim,)), ((), ())),
        precision=precision, preferred_element_type=WIDE,
    )


def group_rows(ref, kv_count, group_size):
    rows, _, dim = ref.shape
    wide = 2 * group_size
    parts = []
    for pair in range(kv_count // 2):
        both = ref[:, pair * wide : (pair + 1) * wide, :].astype(WIDE)
        for half in range(2):
            one = both[:, half * group_size : (half + 1) * group_size, :]
            parts.append(one.reshape(rows * group_size, dim).astype(LOW))
    return parts


def lane_head(shape, group_size):
    return lax.broadcasted_iota(jnp.int32, shape, 1) % group_size


def own_terms(maps_by_rows, owner, tenants, low_rank, group_size):
    lanes = maps_by_rows.shape[1]
    same_head = lax.broadcasted_iota(jnp.int32, (group_size, lanes), 0) == lane_head(
        (group_size, lanes), group_size
    )
    span = low_rank * group_size
    total = jnp.zeros((low_rank, group_size, lanes), WIDE)
    for tenant in range(tenants):
        keep = same_head & (owner == tenant)
        block = maps_by_rows[tenant * span : (tenant + 1) * span].reshape(
            low_rank, group_size, lanes
        )
        total = total + jnp.where(keep[None], block, 0.0)
    rows = jnp.sum(total, axis=1)
    rows = jnp.concatenate([rows, rows], axis=0)
    tiles = lanes // 128
    stacked = jnp.concatenate([rows[:, c * 128 : (c + 1) * 128] for c in range(tiles)], axis=0)
    side = lax.broadcasted_iota(jnp.int32, (128, 128), 0) // group_size
    over = lax.broadcasted_iota(jnp.int32, (128, 128), 1) // group_size
    spread = dot(stacked, (side == over).astype(WIDE), 1, 0, lax.Precision.HIGHEST)
    return jnp.concatenate([spread[c * 8 : (c + 1) * 8] for c in range(tiles)], axis=1)


def place_kernel(rows_ref, meta_ref, bias_ref, *, group):
    lanes = meta_ref.shape[1]
    tokens = lanes // group
    row_first = lax.axis_index("ctx") * tokens
    mine = pl.ds(pl.multiple_of(row_first, tokens), tokens)
    row = lax.broadcasted_iota(jnp.int32, (8, tokens), 0)
    both = jnp.where(row == 0, rows_ref[0:1, mine] - row_first, rows_ref[1:2, mine]).astype(WIDE)
    repeat = lax.broadcasted_iota(jnp.int32, (tokens, lanes), 0) == (
        lax.broadcasted_iota(jnp.int32, (tokens, lanes), 1) // group
    )
    meta = dot(both, repeat.astype(WIDE), 1, 0, lax.Precision.HIGHEST).astype(jnp.int32)
    meta_ref[...] = meta
    first = meta[0:1, :]
    key, here = places(lanes, tokens, group)
    bias_ref[0] = jnp.where(jnp.where(here, key, key - 2 * tokens) >= first, 0.0, far_below)
    bias_ref[1] = jnp.where(key - tokens >= first, 0.0, far_below)


def slots_of(lanes, group, owned):
    per_group = group // owned
    head = lane_head((1, lanes), group)
    return head ^ ((lax.axis_index("ctx") % per_group) * owned)


def tenants_of(lanes, tenants, rank):
    row = lax.broadcasted_iota(jnp.int32, (tenants * rank, lanes), 0) // rank
    return row ^ (lax.axis_index("rep") * (tenants // lax.axis_size("rep")))


def picked_rows(rows, owner, slots, tenants, rank, group):
    lanes = owner.shape[1]
    mine = owner == tenants_of(lanes, tenants, rank)
    rows = jnp.where(mine, jnp.concatenate([rows] * (tenants * rank // 8), axis=0), 0.0)
    return [jnp.where(slots == h, rows, 0.0).astype(LOW) for h in range(group)]


def pull_kernel(
    meta_ref, cot_ref, rot_ref, q_ref, cots_ref, queries_ref, pulled_ref, pull_ref,
    *, kv, group, tenants, rank, owned,
):
    owner = meta_ref[1:2, :]
    lanes = owner.shape[1]
    cots = group_rows(cot_ref, kv, group)
    rots = group_rows(rot_ref, kv, group)
    on_rot = dot(jnp.concatenate(rots, axis=1), jnp.concatenate(cots, axis=1), 1, 1)
    pulled = own_terms(on_rot, owner, tenants, rank, group).astype(LOW).astype(WIDE)
    pulled_ref[...] = pulled
    for g, rows in enumerate(group_rows(q_ref, kv, group)):
        queries_ref[g] = rows
        cots_ref[g] = cots[g]
    span = tenants * rank
    slots = slots_of(lanes, group, owned)
    for h, rows in enumerate(picked_rows(pulled, owner, slots, tenants, rank, group)):
        pull_ref[h * span : (h + 1) * span, :] = rows


def hidden_grad_kernel(
    meta_ref, pulled_ref, cots_ref, rot_ref, proj_ref, gh_ref, diff_ref, *, kv, group, tenants, rank,
):
    owner = meta_ref[1:2, :]
    lanes = owner.shape[1]
    dim = cots_ref.shape[2]
    pulled = pulled_ref[...]
    same_head = lax.broadcasted_iota(jnp.int32, (group, lanes), 0) == lane_head((group, lanes), group)
    picked = []
    for tenant in range(tenants):
        keep = same_head & (owner == tenant)
        for k in range(rank):
            picked.append(jnp.where(keep, pulled[k : k + 1], 0.0))
    picked = jnp.concatenate(picked, axis=0).T.astype(LOW)
    rots = group_rows(rot_ref, kv, group)
    projs = group_rows(proj_ref, kv, group)
    diffs = [(proj.astype(WIDE) - rot.astype(WIDE)).astype(LOW) for proj, rot in zip(projs, rots)]
    steered = dot(picked, jnp.concatenate(diffs, axis=1), 1, 0)
    for g in range(kv):
        diff_ref[g] = diffs[g]
        gh_ref[g] = (cots_ref[g].astype(WIDE) + steered[:, g * dim : (g + 1) * dim]).astype(LOW)


def places(lanes, tokens, group):
    key = lax.broadcasted_iota(jnp.int32, (tokens, lanes), 0)
    query = lax.broadcasted_iota(jnp.int32, (tokens, lanes), 1) // group
    return key, key <= query


def window_of(two_ref, one_ref, own_ref, head):
    return jnp.concatenate([two_ref[head], one_ref[head], own_ref[head]], axis=0)


def head_major(ref, wide_ref, outs):
    count = len(outs)
    wide_ref[...] = ref[...].astype(WIDE)
    for m, out in enumerate(outs):
        out[...] = wide_ref[pl.ds(m, out.shape[0], stride=count), :].astype(LOW)


def fold_kernel(
    queries_ref, two_ref, own_ref, bias_ref, fold_ref, stats_ref, two_keys_ref, own_keys_ref, wide_ref,
    *, kv, group, scaling,
):
    tokens = two_keys_ref.shape[1]
    _, here = places(queries_ref.shape[1], tokens, group)
    for at, (ref, keys_ref) in enumerate(((two_ref, two_keys_ref), (own_ref, own_keys_ref))):
        head_major(ref, wide_ref.at[at], [keys_ref.at[m] for m in range(kv)])

    def scores_of(g):
        return dot(jnp.concatenate([two_keys_ref[g], own_keys_ref[g]], axis=0), queries_ref[g], 1, 1)

    scores = scores_of(0)
    for g in range(kv):
        ahead = scores_of(g + 1) if g + 1 < kv else None
        fold = jnp.where(here, scores[tokens:], scores[0:tokens]) * scaling + bias_ref[0]
        top = jnp.max(fold, axis=0, keepdims=True)
        fold = jnp.exp(fold - top)
        fold_ref[g] = fold
        stats_ref[g, 0:1, :] = top
        stats_ref[g, 1:2, :] = jnp.sum(fold, axis=0, keepdims=True)
        scores = ahead


def middle_kernel(
    queries_ref, one_ref, bias_ref, fold_ref, stats_ref, low_ref, one_keys_ref, wide_ref,
    *, kv, group, scaling, first,
):
    tokens = one_keys_ref.shape[1]
    _, here = places(queries_ref.shape[1], tokens, group)
    head_major(one_ref, wide_ref, [one_keys_ref.at[m] for m in range(kv)])
    count = low_ref.shape[0]

    def scores_of(g):
        return dot(one_keys_ref[g], queries_ref[g], 1, 1)

    scores = scores_of(first)
    for at in range(count):
        g = first + at
        ahead = scores_of(g + 1) if at + 1 < count else None
        mid = scores * scaling + bias_ref[1]
        fold_top = stats_ref[g, 0:1, :]
        top = jnp.maximum(fold_top, jnp.max(mid, axis=0, keepdims=True))
        mid = jnp.exp(mid - top)
        fade = jnp.exp(fold_top - top)
        share = 1.0 / (stats_ref[g, 1:2, :] * fade + jnp.sum(mid, axis=0, keepdims=True))
        fold = fold_ref[g] * (fade * share)
        low_ref[at, 0:tokens, :] = jnp.where(here, 0.0, fold).astype(LOW)
        low_ref[at, tokens : 2 * tokens, :] = (mid * share).astype(LOW)
        low_ref[at, 2 * tokens :, :] = jnp.where(here, fold, 0.0).astype(LOW)
        scores = ahead


def half_of(refs, g):
    return refs[g // refs[0].shape[0]].at[g % refs[0].shape[0]]


def hidden_kernel(near_ref, far_ref, two_ref, own_ref, part_ref, two_values_ref, own_values_ref, wide_ref, *, kv):
    tokens, dim = two_values_ref.shape[1:]
    for at, (ref, values_ref) in enumerate(((two_ref, two_values_ref), (own_ref, own_values_ref))):
        head_major(ref, wide_ref.at[at], [values_ref.at[m] for m in range(kv)])
    for g in range(kv):
        low_ref = half_of((near_ref, far_ref), g)
        part_ref[g * dim : (g + 1) * dim, :] = dot(two_values_ref[g], low_ref[0:tokens, :], 0, 0) + dot(
            own_values_ref[g], low_ref[2 * tokens :, :], 0, 0
        )


def sent_slots(group, owned, odd):
    return [slot for slot in range(group) if (slot // owned) % 2 == odd]


def write_parts(into, slots, on_rot, on_proj, kv, group, owned, span, dim):
    rep, me = lax.axis_size("rep"), lax.axis_index("ctx")
    per_group = group // owned
    here_rows = span // rep
    for g in range(kv):
        columns = slice(g * dim, (g + 1) * dim)
        for low in sorted({slot // owned for slot in slots}):
            device = (g ^ (me // per_group)) * per_group + low
            for r in range(rep):
                pieces = []
                for slot in range(low * owned, (low + 1) * owned):
                    first = slots.index(slot) * span + r * here_rows
                    rows = slice(first, first + here_rows)
                    pieces += [on_rot[rows, columns], on_proj[rows, columns]]
                into[reduce_place(dict(ctx=device, rep=r))] = jnp.concatenate(pieces, axis=0).astype(LOW)


def forward_kernel(
    shift_ref, near_ref, far_ref, part_ref, one_ref, cots_ref, diff_ref, meta_ref, pull_ref,
    send_ref, hidden_ref, lift_ref, one_values_ref, wide_ref, *, kv, group, tenants, rank, owned,
):
    tokens, dim = one_values_ref.shape[1:]
    head_major(one_ref, wide_ref, [one_values_ref.at[m] for m in range(kv)])
    owner = meta_ref[1:2, :]
    lanes = owner.shape[1]
    hidden = []
    for g in range(kv):
        low_ref = half_of((near_ref, far_ref), g)
        middle = dot(one_values_ref[g], low_ref[tokens : 2 * tokens, :], 0, 0)
        hidden.append((part_ref[g * dim : (g + 1) * dim, :] + middle).astype(LOW))
    hidden = jnp.concatenate(hidden, axis=0)
    hidden_ref[...] = hidden
    on_diff = dot(jnp.concatenate([diff_ref[g] for g in range(kv)], axis=1), hidden, 1, 0)
    lifted = own_terms(on_diff, owner, tenants, rank, group)
    one_hot = (owner == lax.broadcasted_iota(jnp.int32, (tenants, lanes), 0)).astype(WIDE)
    bias = jnp.concatenate([shift_ref[...]] * (8 // rank), axis=0)
    shift = dot(bias, one_hot, 1, 0, lax.Precision.HIGHEST)
    lifted = (lifted + shift).astype(LOW).astype(WIDE)
    span = tenants * rank
    lifts = picked_rows(lifted, owner, slots_of(lanes, group, owned), tenants, rank, group)
    for at, slot in enumerate(sent_slots(group, owned, 0)):
        lift_ref[at * span : (at + 1) * span, :] = lifts[slot]
    slots = sent_slots(group, owned, 1)
    pulls = [pull_ref[slot * span : (slot + 1) * span, :] for slot in slots]
    on_proj = dot(jnp.concatenate(pulls, axis=0), hidden, 1, 1)
    cots = jnp.concatenate([cots_ref[g] for g in range(kv)], axis=1)
    on_rot = dot(jnp.concatenate([lifts[slot] for slot in slots], axis=0), cots, 1, 0) - on_proj
    write_parts(send_ref, slots, on_rot, on_proj, kv, group, owned, span, dim)


def keep_kernel(hidden_ref, lift_ref, cots_ref, pull_ref, keep_ref, *, kv, group, span, owned):
    dim = cots_ref.shape[2]
    slots = sent_slots(group, owned, 0)
    pulls = [pull_ref[slot * span : (slot + 1) * span, :] for slot in slots]
    on_proj = dot(jnp.concatenate(pulls, axis=0), hidden_ref[...], 1, 1)
    cots = jnp.concatenate([cots_ref[g] for g in range(kv)], axis=1)
    on_rot = dot(lift_ref[...], cots, 1, 0) - on_proj
    write_parts(keep_ref, slots, on_rot, on_proj, kv, group, owned, span, dim)


def backward_kernel(
    queries_ref, gh_ref, near_ref, far_ref, two_ref, one_ref, own_ref, back_two_ref, back_one_ref, back_own_ref, grad_ref,
    *, kv, scaling,
):
    tokens = back_own_ref.shape[1]

    def weight_grad_of(g):
        return dot(window_of(two_ref, one_ref, own_ref, g), gh_ref[g], 1, 1)

    weight_grad = weight_grad_of(0)
    for g in range(kv):
        ahead = weight_grad_of(g + 1) if g + 1 < kv else None
        low = half_of((near_ref, far_ref), g)[...]
        weights = low.astype(WIDE)
        delta = jnp.sum(weights * weight_grad, axis=0, keepdims=True)
        score_grad = (weights * (weight_grad - delta)).astype(LOW)
        grad_ref[g] = score_grad
        key_grad = dot(score_grad, queries_ref[g], 1, 0) * scaling
        value_grad = dot(low, gh_ref[g], 1, 0)
        for place, grad in ((g, key_grad), (kv + g, value_grad)):
            back_two_ref[place] = grad[0:tokens].astype(LOW)
            back_one_ref[place] = grad[tokens : 2 * tokens].astype(LOW)
            back_own_ref[place] = grad[2 * tokens :]
        weight_grad = ahead


def query_kernel(
    grad_ref, two_ref, one_ref, own_ref, dq_hbm, dq_ref, sems, *, kv, group, scaling,
):
    tokens, _, dim = dq_ref.shape
    copies = []
    for g in range(kv):
        query_grad = dot(window_of(two_ref, one_ref, own_ref, g), grad_ref[g], 0, 0) * scaling
        query_grad = query_grad.T.reshape(tokens, group, dim)
        if g % 2 == 1:
            heads = slice((g - 1) * group, (g + 1) * group)
            dq_ref[:, heads, :] = jnp.concatenate([before, query_grad], axis=1).astype(LOW)
            copies.append(pltpu.make_async_copy(dq_ref.at[:, heads], dq_hbm.at[:, heads], sems.at[g // 2]))
            copies[-1].start()
        before = query_grad
    for copy in copies:
        copy.wait()


def finish_kernel(
    own_ref, mate_ref, two_ref, part_ref, *refs, kv, owned,
):
    *other_refs, keys_ref, values_ref, rot_ref, proj_ref, wide_ref = refs
    total = part_ref[0].astype(WIDE)
    for other_ref in other_refs:
        total = total + other_ref[0].astype(WIDE)
    size = rot_ref.shape[0]
    for place in range(owned):
        for at, out in enumerate((rot_ref, proj_ref)):
            row = (2 * place + at) * size
            out[:, place, :] = total[row : row + size]
    tokens = own_ref.shape[1]
    even = (lax.axis_index("ctx") % 2 == 0).astype(WIDE)
    for at, out in enumerate((keys_ref, values_ref)):
        for m in range(kv):
            place = at * kv + m
            total = own_ref[place] + two_ref[place].astype(WIDE) + even * mate_ref[place].astype(WIDE)
            wide_ref[at, pl.ds(m, tokens, stride=kv), :] = total
        out[...] = wide_ref[at].astype(LOW)


def on_device(
    query_rows, key_rows, value_matrix, cotangent, rotation, projection, shift_bias, doc_starts, tenant_ids,
):
    queries = query_rows[0]
    upstream = cotangent[0]
    tokens, heads, dim = queries.shape
    kv = key_rows.shape[2]
    group = heads // kv
    scaling = dim ** (-0.5)
    tenants, rank = rotation.shape[0], rotation.shape[1]
    lanes = tokens * group
    ctx = lax.axis_size("ctx")
    rep = lax.axis_size("rep")
    assert 2 * tokens == DOC_MAX


    rot = rotation.reshape(tenants * rank, heads, dim)
    proj = projection.reshape(tenants * rank, heads, dim)
    sizes = dict(kv=kv, group=group)
    vmem = pl.BlockSpec(memory_space=pltpu.VMEM)

    def call(body, outs, flops, moved, out_specs=None, scratch=(), **fixed):
        def run(*operands):
            return pl.pallas_call(
                lambda *refs: body(*refs, **fixed),
                out_shape=[jax.ShapeDtypeStruct(*out) for out in outs],
                in_specs=[vmem] * len(operands),
                out_specs=out_specs or [vmem] * len(outs),
                scratch_shapes=scratch,
                compiler_params=pltpu.CompilerParams(vmem_limit_bytes=12 * 2**20),
                name=body.__name__,
                cost_estimate=pl.CostEstimate(flops=flops, bytes_accessed=moved, transcendentals=0),
            )(*operands)

        return run

    span = tenants * rank
    here = heads // ctx
    rows = here * 2 * span // rep
    even = jnp.reshape(lax.axis_index("ctx") % 2 == 0, (1, 1, 1))
    key_rows, even = lax.optimization_barrier((key_rows, even))
    own_keys = key_rows[0]
    two_keys = shifted(own_keys, "ctx", 2)
    meta, biases = call(
        place_kernel, [((8, lanes), jnp.int32), ((2, tokens, lanes), WIDE)], 8 * 2**30, 2**20,
        group=group,
    )(jnp.concatenate([doc_starts, tenant_ids], axis=0))
    own_values, meta = lax.optimization_barrier((value_matrix[0], meta))
    two_values = shifted(own_values, "ctx", 2)
    cots, queries, pulled, pull = call(
        pull_kernel,
        [((kv, lanes, dim), LOW), ((kv, lanes, dim), LOW), ((8, lanes), WIDE), ((span * group, lanes), LOW)],
        2**30, 4 * 2**20, tenants=tenants, rank=rank, owned=here, **sizes,
    )(meta, upstream, rot, queries)
    grad_hidden, diff = call(
        hidden_grad_kernel, [((kv, lanes, dim), LOW), ((kv, span * group, dim), LOW)],
        2 * 2**30, 4 * 2**20, tenants=tenants, rank=rank, **sizes,
    )(meta, pulled, cots, rot, proj)
    two_keys, grad_hidden = lax.optimization_barrier((two_keys, grad_hidden))
    one_keys = exchanged(jnp.where(even, own_keys, two_keys), {"ctx": 1})
    flat, heads_first = (tokens * kv, dim), ((kv, tokens, dim), LOW)
    fold, stats, two_heads, own_heads = call(
        fold_kernel, [((kv, tokens, lanes), WIDE), ((kv, 2, lanes), WIDE), heads_first, heads_first],
        2 * 2**30, 4 * 2**20, scratch=[pltpu.VMEM((2, *flat), WIDE)], scaling=scaling, **sizes,
    )(queries, two_keys.reshape(flat), own_keys.reshape(flat), biases)
    one_keys, fold = lax.optimization_barrier((one_keys, fold))

    def weights_of(first):
        return call(
            middle_kernel, [((kv // 2, 3 * tokens, lanes), LOW), heads_first], 2**30, 4 * 2**20,
            scratch=[pltpu.VMEM(flat, WIDE)], scaling=scaling, first=first, **sizes,
        )(queries, one_keys.reshape(flat), biases, fold, stats)

    near, one_heads = weights_of(0)
    two_values, near = lax.optimization_barrier((two_values, near))
    one_values = exchanged(jnp.where(even, own_values, two_values), {"ctx": 1})
    far, _ = weights_of(kv // 2)
    part_hidden, two_sides, own_sides = call(
        hidden_kernel, [((heads // group * dim, lanes), WIDE), heads_first, heads_first], 2**30, 4 * 2**20,
        scratch=[pltpu.VMEM((2, *flat), WIDE)], kv=kv,
    )(near, far, two_values.reshape(flat), own_values.reshape(flat))
    one_values, part_hidden = lax.optimization_barrier((one_values, part_hidden))
    kept = (span * group // 2, lanes)
    send, hidden, lift, one_sides = call(
        forward_kernel,
        [((ctx * rep // 2, rows, dim), LOW), (part_hidden.shape, LOW), (kept, LOW), heads_first],
        3 * 2**30, 10 * 2**20, scratch=[pltpu.VMEM(flat, WIDE)],
        tenants=tenants, rank=rank, owned=here, **sizes,
    )(shift_bias.T, near, far, part_hidden, one_values.reshape(flat), cots, diff, meta, pull)
    keep, = call(
        keep_kernel, [((ctx * rep // 2, rows, dim), LOW)], 2**30, 5 * 2**20, span=span, owned=here, **sizes,
    )(hidden, lift, cots, pull)
    part = (keep.astype(WIDE) + exchanged(send, {"ctx": 1}).astype(WIDE)).astype(LOW)
    near, part = lax.optimization_barrier((near, part))
    window = (2 * kv, tokens, dim)
    back_two, back_one, back_own, score_grad = call(
        backward_kernel, [(window, LOW), (window, LOW), (window, WIDE), ((kv, 3 * tokens, lanes), LOW)],
        4 * 2**30, 10 * 2**20, kv=kv, scaling=scaling,
    )(queries, grad_hidden, near, far, two_sides, one_sides, own_sides)
    d_queries, = call(
        query_kernel, [((tokens, heads, dim), LOW)], 2 * 2**30, 5 * 2**20,
        scratch=[pltpu.VMEM((tokens, heads, dim), LOW), pltpu.SemaphoreType.DMA((kv // 2,))],
        out_specs=[pl.BlockSpec(memory_space=pltpu.HBM)], scaling=scaling, **sizes,
    )(score_grad, two_heads, one_heads, own_heads)
    from_mate = exchanged(back_one, {"ctx": 1})
    onward = back_two.astype(WIDE) + jnp.where(even, 0.0, from_mate.astype(WIDE))
    onward = onward.astype(LOW)

    groups = reduce_groups()
    for at, group_bits in enumerate(groups):
        beside = back_own if at == 0 else None
        if at == len(groups) - 1:
            part, onward = lax.optimization_barrier((part, onward))
            from_two = shifted(onward, "ctx", -2)
            beside = from_two
        part, others = scattered(part, group_bits, beside)
        if at < len(groups) - 1:
            part = part.astype(WIDE) + sum(other.astype(WIDE) for other in others)
            part = part.astype(LOW)
    d_keys, d_values, *grads = call(
        finish_kernel, [((tokens * kv, dim), LOW)] * 2 + [((span // rep, here, dim), WIDE)] * 2, 2**20, 2**20,
        scratch=[pltpu.VMEM((2, tokens * kv, dim), WIDE)], kv=kv, owned=here,
    )(back_own, from_mate, from_two, part, *others)
    grads = [grad.reshape(tenants // rep, rank, here, dim) for grad in grads]
    d_keys, d_values = (grad.reshape(key_rows.shape) for grad in (d_keys, d_values))
    return (d_queries[None], d_keys, d_values, grads[0], grads[1])


def solution(mesh):
    rows = P("rep", "ctx", None, None)
    in_specs = (rows, rows, rows, rows, P(), P(), P(), P("rep", None), P("rep", None))
    tenant_rows = P("rep", None, "ctx", None)
    out_specs = (rows, rows, rows, tenant_rows, tenant_rows)
    return jax.shard_map(
        on_device, mesh=mesh, in_specs=in_specs, out_specs=out_specs, check_vma=False
    )
```

```python
import itertools

import jax
import jax.numpy as jnp
import numpy as np
from jax import lax
from jax.experimental import pallas as pl
from jax.experimental.pallas import tpu as pltpu
from jax.sharding import PartitionSpec as P

DOC_MAX = 256
LOW = jnp.bfloat16
WIDE = jnp.float32
far_below = -1e30


def shifted(value, axis, steps):
    count = lax.axis_size(axis)
    return lax.ppermute(value, axis, [(source, (source + steps) % count) for source in range(count)])


def exchanged(value, bits):
    axes = tuple(bits)
    shape = [lax.axis_size(axis) for axis in axes]
    pairs = []
    for source in np.ndindex(*shape):
        target = [at ^ bits[axis] for at, axis in zip(source, axes)]
        pairs.append((np.ravel_multi_index(source, shape), np.ravel_multi_index(target, shape)))
    return lax.ppermute(value, axes, [(int(source), int(target)) for source, target in pairs])


def reduce_groups():
    ctx, rep = lax.axis_size("ctx"), lax.axis_size("rep")
    bits = [{"ctx": 1 << at} for at in range(ctx.bit_length() - 2, 0, -1)]
    bits += [{"rep": 1 << at} for at in range(rep.bit_length() - 1)]
    return [bits[at : at + 2] for at in range(0, len(bits), 2)]


def reduce_place(index):
    place = 0
    for bits in itertools.chain(*reduce_groups()):
        for axis, bit in bits.items():
            place = 2 * place + (index[axis] // bit) % 2
    return place


def scattered(part, group, beside=None):
    count = 1 << len(group)
    size = part.shape[0] // count
    others = []
    for j in range(1, count):
        bits = {}
        for at, pair in enumerate(reversed(group)):
            if (j >> at) & 1:
                bits.update({axis: bits.get(axis, 0) | bit for axis, bit in pair.items()})
        others.append(exchanged(part[j * size : (j + 1) * size], bits))
    if beside is not None:
        others = lax.optimization_barrier((others, beside))[0]
    return part[:size], others


def dot(left, right, left_dim, right_dim, precision=None):
    return lax.dot_general(
        left, right, (((left_dim,), (right_dim,)), ((), ())),
        precision=precision, preferred_element_type=WIDE,
    )


def group_rows(ref, kv_count, group_size):
    rows, _, dim = ref.shape
    wide = 2 * group_size
    parts = []
    for pair in range(kv_count // 2):
        both = ref[:, pair * wide : (pair + 1) * wide, :].astype(WIDE)
        for half in range(2):
            one = both[:, half * group_size : (half + 1) * group_size, :]
            parts.append(one.reshape(rows * group_size, dim).astype(LOW))
    return parts


def lane_head(shape, group_size):
    return lax.broadcasted_iota(jnp.int32, shape, 1) % group_size


def own_terms(maps_by_rows, owner, tenants, low_rank, group_size):
    lanes = maps_by_rows.shape[1]
    same_head = lax.broadcasted_iota(jnp.int32, (group_size, lanes), 0) == lane_head(
        (group_size, lanes), group_size
    )
    span = low_rank * group_size
    total = jnp.zeros((low_rank, group_size, lanes), WIDE)
    for tenant in range(tenants):
        keep = same_head & (owner == tenant)
        block = maps_by_rows[tenant * span : (tenant + 1) * span].reshape(
            low_rank, group_size, lanes
        )
        total = total + jnp.where(keep[None], block, 0.0)
    rows = jnp.sum(total, axis=1)
    rows = jnp.concatenate([rows, rows], axis=0)
    tiles = lanes // 128
    stacked = jnp.concatenate([rows[:, c * 128 : (c + 1) * 128] for c in range(tiles)], axis=0)
    side = lax.broadcasted_iota(jnp.int32, (128, 128), 0) // group_size
    over = lax.broadcasted_iota(jnp.int32, (128, 128), 1) // group_size
    spread = dot(stacked, (side == over).astype(WIDE), 1, 0, lax.Precision.HIGHEST)
    return jnp.concatenate([spread[c * 8 : (c + 1) * 8] for c in range(tiles)], axis=1)


def place_kernel(rows_ref, meta_ref, bias_ref, *, group):
    lanes = meta_ref.shape[1]
    tokens = lanes // group
    row_first = lax.axis_index("ctx") * tokens
    mine = pl.ds(pl.multiple_of(row_first, tokens), tokens)
    row = lax.broadcasted_iota(jnp.int32, (8, tokens), 0)
    both = jnp.where(row == 0, rows_ref[0:1, mine] - row_first, rows_ref[1:2, mine]).astype(WIDE)
    repeat = lax.broadcasted_iota(jnp.int32, (tokens, lanes), 0) == (
        lax.broadcasted_iota(jnp.int32, (tokens, lanes), 1) // group
    )
    meta = dot(both, repeat.astype(WIDE), 1, 0, lax.Precision.HIGHEST).astype(jnp.int32)
    meta_ref[...] = meta
    first = meta[0:1, :]
    key, here = places(lanes, tokens, group)
    bias_ref[0] = jnp.where(jnp.where(here, key, key - 2 * tokens) >= first, 0.0, far_below)
    bias_ref[1] = jnp.where(key - tokens >= first, 0.0, far_below)


def slots_of(lanes, group, owned):
    per_group = group // owned
    head = lane_head((1, lanes), group)
    return head ^ ((lax.axis_index("ctx") % per_group) * owned)


def tenants_of(lanes, tenants, rank):
    row = lax.broadcasted_iota(jnp.int32, (tenants * rank, lanes), 0) // rank
    return row ^ (lax.axis_index("rep") * (tenants // lax.axis_size("rep")))


def picked_rows(rows, owner, slots, tenants, rank, group):
    lanes = owner.shape[1]
    mine = owner == tenants_of(lanes, tenants, rank)
    rows = jnp.where(mine, jnp.concatenate([rows] * (tenants * rank // 8), axis=0), 0.0)
    return [jnp.where(slots == h, rows, 0.0).astype(LOW) for h in range(group)]


def pull_kernel(
    meta_ref, cot_ref, rot_ref, q_ref, cots_ref, queries_ref, pulled_ref, pull_ref,
    *, kv, group, tenants, rank, owned,
):
    owner = meta_ref[1:2, :]
    lanes = owner.shape[1]
    cots = group_rows(cot_ref, kv, group)
    rots = group_rows(rot_ref, kv, group)
    on_rot = dot(jnp.concatenate(rots, axis=1), jnp.concatenate(cots, axis=1), 1, 1)
    pulled = own_terms(on_rot, owner, tenants, rank, group).astype(LOW).astype(WIDE)
    pulled_ref[...] = pulled
    for g, rows in enumerate(group_rows(q_ref, kv, group)):
        queries_ref[g] = rows
        cots_ref[g] = cots[g]
    span = tenants * rank
    slots = slots_of(lanes, group, owned)
    for h, rows in enumerate(picked_rows(pulled, owner, slots, tenants, rank, group)):
        pull_ref[h * span : (h + 1) * span, :] = rows


def hidden_grad_kernel(
    meta_ref, pulled_ref, cots_ref, rot_ref, proj_ref, gh_ref, diff_ref, *, kv, group, tenants, rank,
):
    owner = meta_ref[1:2, :]
    lanes = owner.shape[1]
    dim = cots_ref.shape[2]
    pulled = pulled_ref[...]
    same_head = lax.broadcasted_iota(jnp.int32, (group, lanes), 0) == lane_head((group, lanes), group)
    picked = []
    for tenant in range(tenants):
        keep = same_head & (owner == tenant)
        for k in range(rank):
            picked.append(jnp.where(keep, pulled[k : k + 1], 0.0))
    picked = jnp.concatenate(picked, axis=0).T.astype(LOW)
    rots = group_rows(rot_ref, kv, group)
    projs = group_rows(proj_ref, kv, group)
    diffs = [(proj.astype(WIDE) - rot.astype(WIDE)).astype(LOW) for proj, rot in zip(projs, rots)]
    steered = dot(picked, jnp.concatenate(diffs, axis=1), 1, 0)
    for g in range(kv):
        diff_ref[g] = diffs[g]
        gh_ref[g] = (cots_ref[g].astype(WIDE) + steered[:, g * dim : (g + 1) * dim]).astype(LOW)


def places(lanes, tokens, group):
    key = lax.broadcasted_iota(jnp.int32, (tokens, lanes), 0)
    query = lax.broadcasted_iota(jnp.int32, (tokens, lanes), 1) // group
    return key, key <= query


def window_of(two_ref, own_ref, one_ref, head):
    return jnp.concatenate([two_ref[head], own_ref[head], one_ref[head]], axis=0)


def head_major(ref, wide_ref, outs):
    count = len(outs)
    wide_ref[...] = ref[...].astype(WIDE)
    for m, out in enumerate(outs):
        out[...] = wide_ref[pl.ds(m, out.shape[0], stride=count), :].astype(LOW)


def fold_kernel(
    queries_ref, two_ref, own_ref, bias_ref, fold_ref, stats_ref, two_keys_ref, own_keys_ref, wide_ref,
    *, kv, group, scaling,
):
    tokens = two_keys_ref.shape[1]
    _, here = places(queries_ref.shape[1], tokens, group)
    for at, (ref, keys_ref) in enumerate(((two_ref, two_keys_ref), (own_ref, own_keys_ref))):
        head_major(ref, wide_ref.at[at], [keys_ref.at[m] for m in range(kv)])

    def scores_of(g):
        return dot(jnp.concatenate([two_keys_ref[g], own_keys_ref[g]], axis=0), queries_ref[g], 1, 1)

    scores = scores_of(0)
    for g in range(kv):
        ahead = scores_of(g + 1) if g + 1 < kv else None
        fold = jnp.where(here, scores[tokens:], scores[0:tokens]) * scaling + bias_ref[0]
        top = jnp.max(fold, axis=0, keepdims=True)
        fold = jnp.exp(fold - top)
        fold_ref[g] = fold
        stats_ref[g, 0:1, :] = top
        stats_ref[g, 1:2, :] = jnp.sum(fold, axis=0, keepdims=True)
        scores = ahead


def near_kernel(
    queries_ref, one_ref, bias_ref, fold_ref, stats_ref, low_ref, one_keys_ref, wide_ref, *, kv, group, scaling,
):
    head_major(one_ref, wide_ref, [one_keys_ref.at[m] for m in range(kv)])
    weigh(queries_ref, one_keys_ref, bias_ref, fold_ref, stats_ref, low_ref, group, scaling, 0)


def far_kernel(
    queries_ref, one_keys_ref, bias_ref, fold_ref, stats_ref, low_ref, *, group, scaling, first,
):
    weigh(queries_ref, one_keys_ref, bias_ref, fold_ref, stats_ref, low_ref, group, scaling, first)


def weigh(queries_ref, one_keys_ref, bias_ref, fold_ref, stats_ref, low_ref, group, scaling, first):
    tokens = one_keys_ref.shape[1]
    _, here = places(queries_ref.shape[1], tokens, group)
    count = low_ref.shape[0]

    def scores_of(g):
        return dot(one_keys_ref[g], queries_ref[g], 1, 1)

    scores = scores_of(first)
    for at in range(count):
        g = first + at
        ahead = scores_of(g + 1) if at + 1 < count else None
        mid = scores * scaling + bias_ref[1]
        fold_top = stats_ref[g, 0:1, :]
        top = jnp.maximum(fold_top, jnp.max(mid, axis=0, keepdims=True))
        mid = jnp.exp(mid - top)
        fade = jnp.exp(fold_top - top)
        share = 1.0 / (stats_ref[g, 1:2, :] * fade + jnp.sum(mid, axis=0, keepdims=True))
        fold = fold_ref[g] * (fade * share)
        low_ref[at, 0:tokens, :] = jnp.where(here, 0.0, fold).astype(LOW)
        low_ref[at, tokens : 2 * tokens, :] = jnp.where(here, fold, 0.0).astype(LOW)
        low_ref[at, 2 * tokens :, :] = (mid * share).astype(LOW)
        scores = ahead


def half_of(refs, g):
    return refs[g // refs[0].shape[0]].at[g % refs[0].shape[0]]


def hidden_kernel(near_ref, far_ref, two_ref, own_ref, part_ref, two_values_ref, own_values_ref, wide_ref, *, kv):
    tokens, dim = two_values_ref.shape[1:]
    for at, (ref, values_ref) in enumerate(((two_ref, two_values_ref), (own_ref, own_values_ref))):
        head_major(ref, wide_ref.at[at], [values_ref.at[m] for m in range(kv)])
    for g in range(kv):
        low_ref = half_of((near_ref, far_ref), g)
        values = jnp.concatenate([two_values_ref[g], own_values_ref[g]], axis=0)
        part_ref[g * dim : (g + 1) * dim, :] = dot(values, low_ref[0 : 2 * tokens, :], 0, 0)


def sent_slots(group, owned, odd):
    return [slot for slot in range(group) if (slot // owned) % 2 == odd]


def write_parts(into, slots, on_rot, on_proj, kv, group, owned, span, dim):
    rep, me = lax.axis_size("rep"), lax.axis_index("ctx")
    per_group = group // owned
    here_rows = span // rep
    for g in range(kv):
        columns = slice(g * dim, (g + 1) * dim)
        for low in sorted({slot // owned for slot in slots}):
            device = (g ^ (me // per_group)) * per_group + low
            for r in range(rep):
                pieces = []
                for slot in range(low * owned, (low + 1) * owned):
                    first = slots.index(slot) * span + r * here_rows
                    rows = slice(first, first + here_rows)
                    pieces += [on_rot[rows, columns], on_proj[rows, columns]]
                into[reduce_place(dict(ctx=device, rep=r))] = jnp.concatenate(pieces, axis=0).astype(LOW)


def forward_kernel(
    shift_ref, near_ref, far_ref, part_ref, one_ref, cots_ref, diff_ref, meta_ref, pull_ref,
    send_ref, hidden_ref, lift_ref, one_values_ref, wide_ref, *, kv, group, tenants, rank, owned,
):
    tokens, dim = one_values_ref.shape[1:]
    head_major(one_ref, wide_ref, [one_values_ref.at[m] for m in range(kv)])
    owner = meta_ref[1:2, :]
    lanes = owner.shape[1]
    hidden = []
    for g in range(kv):
        low_ref = half_of((near_ref, far_ref), g)
        middle = dot(one_values_ref[g], low_ref[2 * tokens :, :], 0, 0)
        hidden.append((part_ref[g * dim : (g + 1) * dim, :] + middle).astype(LOW))
    hidden = jnp.concatenate(hidden, axis=0)
    hidden_ref[...] = hidden
    on_diff = dot(jnp.concatenate([diff_ref[g] for g in range(kv)], axis=1), hidden, 1, 0)
    lifted = own_terms(on_diff, owner, tenants, rank, group)
    one_hot = (owner == lax.broadcasted_iota(jnp.int32, (tenants, lanes), 0)).astype(WIDE)
    bias = jnp.concatenate([shift_ref[...]] * (8 // rank), axis=0)
    shift = dot(bias, one_hot, 1, 0, lax.Precision.HIGHEST)
    lifted = (lifted + shift).astype(LOW).astype(WIDE)
    span = tenants * rank
    lifts = picked_rows(lifted, owner, slots_of(lanes, group, owned), tenants, rank, group)
    for at, slot in enumerate(sent_slots(group, owned, 0)):
        lift_ref[at * span : (at + 1) * span, :] = lifts[slot]
    slots = sent_slots(group, owned, 1)
    pulls = [pull_ref[slot * span : (slot + 1) * span, :] for slot in slots]
    on_proj = dot(jnp.concatenate(pulls, axis=0), hidden, 1, 1)
    cots = jnp.concatenate([cots_ref[g] for g in range(kv)], axis=1)
    on_rot = dot(jnp.concatenate([lifts[slot] for slot in slots], axis=0), cots, 1, 0) - on_proj
    write_parts(send_ref, slots, on_rot, on_proj, kv, group, owned, span, dim)


def keep_kernel(hidden_ref, lift_ref, cots_ref, pull_ref, keep_ref, *, kv, group, span, owned):
    dim = cots_ref.shape[2]
    slots = sent_slots(group, owned, 0)
    pulls = [pull_ref[slot * span : (slot + 1) * span, :] for slot in slots]
    on_proj = dot(jnp.concatenate(pulls, axis=0), hidden_ref[...], 1, 1)
    cots = jnp.concatenate([cots_ref[g] for g in range(kv)], axis=1)
    on_rot = dot(lift_ref[...], cots, 1, 0) - on_proj
    write_parts(keep_ref, slots, on_rot, on_proj, kv, group, owned, span, dim)


def backward_kernel(
    queries_ref, gh_ref, near_ref, far_ref, two_ref, one_ref, own_ref, back_two_ref, back_one_ref, back_own_ref, grad_ref,
    *, kv, scaling,
):
    tokens = back_own_ref.shape[1]

    def weight_grad_of(g):
        return dot(window_of(two_ref, own_ref, one_ref, g), gh_ref[g], 1, 1)

    weight_grad = weight_grad_of(0)
    for g in range(kv):
        ahead = weight_grad_of(g + 1) if g + 1 < kv else None
        low = half_of((near_ref, far_ref), g)[...]
        weights = low.astype(WIDE)
        delta = jnp.sum(weights * weight_grad, axis=0, keepdims=True)
        score_grad = (weights * (weight_grad - delta)).astype(LOW)
        grad_ref[g] = score_grad
        key_grad = dot(score_grad, queries_ref[g], 1, 0) * scaling
        value_grad = dot(low, gh_ref[g], 1, 0)
        for place, grad in ((g, key_grad), (kv + g, value_grad)):
            back_two_ref[place] = grad[0:tokens].astype(LOW)
            back_own_ref[place] = grad[tokens : 2 * tokens]
            back_one_ref[place] = grad[2 * tokens :].astype(LOW)
        weight_grad = ahead


def query_kernel(
    grad_ref, two_ref, one_ref, own_ref, dq_hbm, dq_ref, sems, *, kv, group, scaling,
):
    tokens, _, dim = dq_ref.shape
    copies = []
    for g in range(kv):
        query_grad = dot(window_of(two_ref, own_ref, one_ref, g), grad_ref[g], 0, 0) * scaling
        query_grad = query_grad.T.reshape(tokens, group, dim)
        if g % 2 == 1:
            heads = slice((g - 1) * group, (g + 1) * group)
            dq_ref[:, heads, :] = jnp.concatenate([before, query_grad], axis=1).astype(LOW)
            copies.append(pltpu.make_async_copy(dq_ref.at[:, heads], dq_hbm.at[:, heads], sems.at[g // 2]))
            copies[-1].start()
        before = query_grad
    for copy in copies:
        copy.wait()


def finish_kernel(
    own_ref, mate_ref, two_ref, part_ref, *refs, kv, owned,
):
    *other_refs, keys_ref, values_ref, rot_ref, proj_ref, wide_ref = refs
    total = part_ref[0].astype(WIDE)
    for other_ref in other_refs:
        total = total + other_ref[0].astype(WIDE)
    size = rot_ref.shape[0]
    for place in range(owned):
        for at, out in enumerate((rot_ref, proj_ref)):
            row = (2 * place + at) * size
            out[:, place, :] = total[row : row + size]
    tokens = own_ref.shape[1]
    even = (lax.axis_index("ctx") % 2 == 0).astype(WIDE)
    for at, out in enumerate((keys_ref, values_ref)):
        for m in range(kv):
            place = at * kv + m
            total = own_ref[place] + two_ref[place].astype(WIDE) + even * mate_ref[place].astype(WIDE)
            wide_ref[at, pl.ds(m, tokens, stride=kv), :] = total
        out[...] = wide_ref[at].astype(LOW)


def on_device(
    query_rows, key_rows, value_matrix, cotangent, rotation, projection, shift_bias, doc_starts, tenant_ids,
):
    queries = query_rows[0]
    upstream = cotangent[0]
    tokens, heads, dim = queries.shape
    kv = key_rows.shape[2]
    group = heads // kv
    scaling = dim ** (-0.5)
    tenants, rank = rotation.shape[0], rotation.shape[1]
    lanes = tokens * group
    ctx = lax.axis_size("ctx")
    rep = lax.axis_size("rep")
    assert 2 * tokens == DOC_MAX


    rot = rotation.reshape(tenants * rank, heads, dim)
    proj = projection.reshape(tenants * rank, heads, dim)
    sizes = dict(kv=kv, group=group)
    vmem = pl.BlockSpec(memory_space=pltpu.VMEM)

    def call(body, outs, flops, moved, out_specs=None, scratch=(), **fixed):
        def run(*operands):
            return pl.pallas_call(
                lambda *refs: body(*refs, **fixed),
                out_shape=[jax.ShapeDtypeStruct(*out) for out in outs],
                in_specs=[vmem] * len(operands),
                out_specs=out_specs or [vmem] * len(outs),
                scratch_shapes=scratch,
                compiler_params=pltpu.CompilerParams(vmem_limit_bytes=12 * 2**20),
                name=body.__name__,
                cost_estimate=pl.CostEstimate(flops=flops, bytes_accessed=moved, transcendentals=0),
            )(*operands)

        return run

    span = tenants * rank
    here = heads // ctx
    rows = here * 2 * span // rep
    even = jnp.reshape(lax.axis_index("ctx") % 2 == 0, (1, 1, 1))
    key_rows, even = lax.optimization_barrier((key_rows, even))
    own_keys = key_rows[0]
    two_keys = shifted(own_keys, "ctx", 2)
    meta, biases = call(
        place_kernel, [((8, lanes), jnp.int32), ((2, tokens, lanes), WIDE)], 8 * 2**30, 2**20,
        group=group,
    )(jnp.concatenate([doc_starts, tenant_ids], axis=0))
    own_values = value_matrix[0]
    leaving, meta = lax.optimization_barrier((own_values, meta))
    two_values = shifted(leaving, "ctx", 2)
    cots, queries, pulled, pull = call(
        pull_kernel,
        [((kv, lanes, dim), LOW), ((kv, lanes, dim), LOW), ((8, lanes), WIDE), ((span * group, lanes), LOW)],
        2**30, 4 * 2**20, tenants=tenants, rank=rank, owned=here, **sizes,
    )(meta, upstream, rot, queries)
    grad_hidden, diff = call(
        hidden_grad_kernel, [((kv, lanes, dim), LOW), ((kv, span * group, dim), LOW)],
        2 * 2**30, 4 * 2**20, tenants=tenants, rank=rank, **sizes,
    )(meta, pulled, cots, rot, proj)
    two_keys, grad_hidden = lax.optimization_barrier((two_keys, grad_hidden))
    one_keys = exchanged(jnp.where(even, own_keys, two_keys), {"ctx": 1})
    flat, heads_first = (tokens * kv, dim), ((kv, tokens, dim), LOW)
    fold, stats, two_heads, own_heads = call(
        fold_kernel, [((kv, tokens, lanes), WIDE), ((kv, 2, lanes), WIDE), heads_first, heads_first],
        2 * 2**30, 4 * 2**20, scratch=[pltpu.VMEM((2, *flat), WIDE)], scaling=scaling, **sizes,
    )(queries, two_keys.reshape(flat), own_keys.reshape(flat), biases)
    one_keys, fold = lax.optimization_barrier((one_keys, fold))

    halves = ((kv // 2, 3 * tokens, lanes), LOW)
    near, one_heads = call(
        near_kernel, [halves, heads_first], 2**30, 4 * 2**20,
        scratch=[pltpu.VMEM(flat, WIDE)], scaling=scaling, **sizes,
    )(queries, one_keys.reshape(flat), biases, fold, stats)
    two_values, near = lax.optimization_barrier((two_values, near))
    one_values = exchanged(jnp.where(even, own_values, two_values), {"ctx": 1})
    far, = call(
        far_kernel, [halves], 2**30, 4 * 2**20, group=group, scaling=scaling, first=kv // 2,
    )(queries, one_heads, biases, fold, stats)
    part_hidden, two_sides, own_sides = call(
        hidden_kernel, [((heads // group * dim, lanes), WIDE), heads_first, heads_first], 2**30, 4 * 2**20,
        scratch=[pltpu.VMEM((2, *flat), WIDE)], kv=kv,
    )(near, far, two_values.reshape(flat), own_values.reshape(flat))
    one_values, part_hidden = lax.optimization_barrier((one_values, part_hidden))
    kept = (span * group // 2, lanes)
    send, hidden, lift, one_sides = call(
        forward_kernel,
        [((ctx * rep // 2, rows, dim), LOW), (part_hidden.shape, LOW), (kept, LOW), heads_first],
        3 * 2**30, 10 * 2**20, scratch=[pltpu.VMEM(flat, WIDE)],
        tenants=tenants, rank=rank, owned=here, **sizes,
    )(shift_bias.T, near, far, part_hidden, one_values.reshape(flat), cots, diff, meta, pull)
    keep, = call(
        keep_kernel, [((ctx * rep // 2, rows, dim), LOW)], 2**30, 5 * 2**20, span=span, owned=here, **sizes,
    )(hidden, lift, cots, pull)
    part = (keep.astype(WIDE) + exchanged(send, {"ctx": 1}).astype(WIDE)).astype(LOW)
    near, part = lax.optimization_barrier((near, part))
    window = (2 * kv, tokens, dim)
    back_two, back_one, back_own, score_grad = call(
        backward_kernel, [(window, LOW), (window, LOW), (window, WIDE), ((kv, 3 * tokens, lanes), LOW)],
        4 * 2**30, 10 * 2**20, kv=kv, scaling=scaling,
    )(queries, grad_hidden, near, far, two_sides, one_sides, own_sides)
    d_queries, = call(
        query_kernel, [((tokens, heads, dim), LOW)], 2 * 2**30, 5 * 2**20,
        scratch=[pltpu.VMEM((tokens, heads, dim), LOW), pltpu.SemaphoreType.DMA((kv // 2,))],
        out_specs=[pl.BlockSpec(memory_space=pltpu.HBM)], scaling=scaling, **sizes,
    )(score_grad, two_heads, one_heads, own_heads)
    from_mate = exchanged(back_one, {"ctx": 1})
    onward = back_two.astype(WIDE) + jnp.where(even, 0.0, from_mate.astype(WIDE))
    onward = onward.astype(LOW)

    groups = reduce_groups()
    for at, group_bits in enumerate(groups):
        beside = back_own if at == 0 else None
        if at == len(groups) - 1:
            part, onward = lax.optimization_barrier((part, onward))
            from_two = shifted(onward, "ctx", -2)
            beside = from_two
        part, others = scattered(part, group_bits, beside)
        if at < len(groups) - 1:
            part = part.astype(WIDE) + sum(other.astype(WIDE) for other in others)
            part = part.astype(LOW)
    d_keys, d_values, *grads = call(
        finish_kernel, [((tokens * kv, dim), LOW)] * 2 + [((span // rep, here, dim), WIDE)] * 2, 2**20, 2**20,
        scratch=[pltpu.VMEM((2, tokens * kv, dim), WIDE)], kv=kv, owned=here,
    )(back_own, from_mate, from_two, part, *others)
    grads = [grad.reshape(tenants // rep, rank, here, dim) for grad in grads]
    d_keys, d_values = (grad.reshape(key_rows.shape) for grad in (d_keys, d_values))
    return (d_queries[None], d_keys, d_values, grads[0], grads[1])


def solution(mesh):
    rows = P("rep", "ctx", None, None)
    in_specs = (rows, rows, rows, rows, P(), P(), P(), P("rep", None), P("rep", None))
    tenant_rows = P("rep", None, "ctx", None)
    out_specs = (rows, rows, rows, tenant_rows, tenant_rows)
    return jax.shard_map(
        on_device, mesh=mesh, in_specs=in_specs, out_specs=out_specs, check_vma=False
    )
```

```python
import itertools

import jax
import jax.numpy as jnp
import numpy as np
from jax import lax
from jax.experimental import pallas as pl
from jax.experimental.pallas import tpu as pltpu
from jax.sharding import PartitionSpec as P

DOC_MAX = 256
LOW = jnp.bfloat16
WIDE = jnp.float32
far_below = -1e30


def shifted(value, axis, steps):
    count = lax.axis_size(axis)
    return lax.ppermute(value, axis, [(source, (source + steps) % count) for source in range(count)])


def exchanged(value, bits):
    axes = tuple(bits)
    shape = [lax.axis_size(axis) for axis in axes]
    pairs = []
    for source in np.ndindex(*shape):
        target = [at ^ bits[axis] for at, axis in zip(source, axes)]
        pairs.append((np.ravel_multi_index(source, shape), np.ravel_multi_index(target, shape)))
    return lax.ppermute(value, axes, [(int(source), int(target)) for source, target in pairs])


def reduce_groups():
    ctx, rep = lax.axis_size("ctx"), lax.axis_size("rep")
    bits = [{"ctx": 1 << at} for at in range(ctx.bit_length() - 2, 0, -1)]
    bits += [{"rep": 1 << at} for at in range(rep.bit_length() - 1)]
    return [bits[at : at + 2] for at in range(0, len(bits), 2)]


def reduce_place(index):
    place = 0
    for bits in itertools.chain(*reduce_groups()):
        for axis, bit in bits.items():
            place = 2 * place + (index[axis] // bit) % 2
    return place


def scattered(part, group, beside=None):
    count = 1 << len(group)
    size = part.shape[0] // count
    others = []
    for j in range(1, count):
        bits = {}
        for at, pair in enumerate(reversed(group)):
            if (j >> at) & 1:
                bits.update({axis: bits.get(axis, 0) | bit for axis, bit in pair.items()})
        others.append(exchanged(part[j * size : (j + 1) * size], bits))
    if beside is not None:
        others = lax.optimization_barrier((others, beside))[0]
    return part[:size], others


def dot(left, right, left_dim, right_dim, precision=None):
    return lax.dot_general(
        left, right, (((left_dim,), (right_dim,)), ((), ())),
        precision=precision, preferred_element_type=WIDE,
    )


def group_rows(ref, kv_count, group_size):
    rows, _, dim = ref.shape
    wide = 2 * group_size
    parts = []
    for pair in range(kv_count // 2):
        both = ref[:, pair * wide : (pair + 1) * wide, :].astype(WIDE)
        for half in range(2):
            one = both[:, half * group_size : (half + 1) * group_size, :]
            parts.append(one.reshape(rows * group_size, dim).astype(LOW))
    return parts


def lane_head(shape, group_size):
    return lax.broadcasted_iota(jnp.int32, shape, 1) % group_size


def own_terms(maps_by_rows, owner, tenants, low_rank, group_size):
    lanes = maps_by_rows.shape[1]
    same_head = lax.broadcasted_iota(jnp.int32, (group_size, lanes), 0) == lane_head(
        (group_size, lanes), group_size
    )
    span = low_rank * group_size
    total = jnp.zeros((low_rank, group_size, lanes), WIDE)
    for tenant in range(tenants):
        keep = same_head & (owner == tenant)
        block = maps_by_rows[tenant * span : (tenant + 1) * span].reshape(
            low_rank, group_size, lanes
        )
        total = total + jnp.where(keep[None], block, 0.0)
    rows = jnp.sum(total, axis=1)
    rows = jnp.concatenate([rows, rows], axis=0)
    tiles = lanes // 128
    stacked = jnp.concatenate([rows[:, c * 128 : (c + 1) * 128] for c in range(tiles)], axis=0)
    side = lax.broadcasted_iota(jnp.int32, (128, 128), 0) // group_size
    over = lax.broadcasted_iota(jnp.int32, (128, 128), 1) // group_size
    spread = dot(stacked, (side == over).astype(WIDE), 1, 0, lax.Precision.HIGHEST)
    return jnp.concatenate([spread[c * 8 : (c + 1) * 8] for c in range(tiles)], axis=1)


def place_kernel(rows_ref, meta_ref, bias_ref, *, group):
    lanes = meta_ref.shape[1]
    tokens = lanes // group
    row_first = lax.axis_index("ctx") * tokens
    mine = pl.ds(pl.multiple_of(row_first, tokens), tokens)
    row = lax.broadcasted_iota(jnp.int32, (8, tokens), 0)
    both = jnp.where(row == 0, rows_ref[0:1, mine] - row_first, rows_ref[1:2, mine]).astype(WIDE)
    repeat = lax.broadcasted_iota(jnp.int32, (tokens, lanes), 0) == (
        lax.broadcasted_iota(jnp.int32, (tokens, lanes), 1) // group
    )
    meta = dot(both, repeat.astype(WIDE), 1, 0, lax.Precision.HIGHEST).astype(jnp.int32)
    meta_ref[...] = meta
    first = meta[0:1, :]
    key, here = places(lanes, tokens, group)
    bias_ref[0] = jnp.where(jnp.where(here, key, key - 2 * tokens) >= first, 0.0, far_below)
    bias_ref[1] = jnp.where(key - tokens >= first, 0.0, far_below)


def slots_of(lanes, group, owned):
    per_group = group // owned
    head = lane_head((1, lanes), group)
    return head ^ ((lax.axis_index("ctx") % per_group) * owned)


def tenants_of(lanes, tenants, rank):
    row = lax.broadcasted_iota(jnp.int32, (tenants * rank, lanes), 0) // rank
    return row ^ (lax.axis_index("rep") * (tenants // lax.axis_size("rep")))


def picked_rows(rows, owner, slots, tenants, rank, group):
    lanes = owner.shape[1]
    mine = owner == tenants_of(lanes, tenants, rank)
    rows = jnp.where(mine, jnp.concatenate([rows] * (tenants * rank // 8), axis=0), 0.0)
    return [jnp.where(slots == h, rows, 0.0).astype(LOW) for h in range(group)]


def pull_kernel(
    meta_ref, cot_ref, rot_ref, q_ref, cots_ref, queries_ref, pulled_ref, pull_ref,
    *, kv, group, tenants, rank, owned,
):
    owner = meta_ref[1:2, :]
    lanes = owner.shape[1]
    cots = group_rows(cot_ref, kv, group)
    rots = group_rows(rot_ref, kv, group)
    on_rot = dot(jnp.concatenate(rots, axis=1), jnp.concatenate(cots, axis=1), 1, 1)
    pulled = own_terms(on_rot, owner, tenants, rank, group).astype(LOW).astype(WIDE)
    pulled_ref[...] = pulled
    for g, rows in enumerate(group_rows(q_ref, kv, group)):
        queries_ref[g] = rows
        cots_ref[g] = cots[g]
    span = tenants * rank
    slots = slots_of(lanes, group, owned)
    for h, rows in enumerate(picked_rows(pulled, owner, slots, tenants, rank, group)):
        pull_ref[h * span : (h + 1) * span, :] = rows


def hidden_grad_kernel(
    meta_ref, pulled_ref, cots_ref, rot_ref, proj_ref, gh_ref, diff_ref, *, kv, group, tenants, rank,
):
    owner = meta_ref[1:2, :]
    lanes = owner.shape[1]
    dim = cots_ref.shape[2]
    pulled = pulled_ref[...]
    same_head = lax.broadcasted_iota(jnp.int32, (group, lanes), 0) == lane_head((group, lanes), group)
    picked = []
    for tenant in range(tenants):
        keep = same_head & (owner == tenant)
        for k in range(rank):
            picked.append(jnp.where(keep, pulled[k : k + 1], 0.0))
    picked = jnp.concatenate(picked, axis=0).T.astype(LOW)
    rots = group_rows(rot_ref, kv, group)
    projs = group_rows(proj_ref, kv, group)
    diffs = [(proj.astype(WIDE) - rot.astype(WIDE)).astype(LOW) for proj, rot in zip(projs, rots)]
    steered = dot(picked, jnp.concatenate(diffs, axis=1), 1, 0)
    for g in range(kv):
        diff_ref[g] = diffs[g]
        gh_ref[g] = (cots_ref[g].astype(WIDE) + steered[:, g * dim : (g + 1) * dim]).astype(LOW)


def places(lanes, tokens, group):
    key = lax.broadcasted_iota(jnp.int32, (tokens, lanes), 0)
    query = lax.broadcasted_iota(jnp.int32, (tokens, lanes), 1) // group
    return key, key <= query


def window_of(two_ref, own_ref, one_ref, head):
    return jnp.concatenate([two_ref[head], own_ref[head], one_ref[head]], axis=0)


def head_major(ref, wide_ref, outs):
    count = len(outs)
    wide_ref[...] = ref[...].astype(WIDE)
    for m, out in enumerate(outs):
        out[...] = wide_ref[pl.ds(m, out.shape[0], stride=count), :].astype(LOW)


def fold_kernel(
    queries_ref, two_ref, own_ref, bias_ref, fold_ref, stats_ref, two_keys_ref, own_keys_ref, wide_ref,
    *, kv, group, scaling,
):
    tokens = two_keys_ref.shape[1]
    _, here = places(queries_ref.shape[1], tokens, group)
    for at, (ref, keys_ref) in enumerate(((two_ref, two_keys_ref), (own_ref, own_keys_ref))):
        head_major(ref, wide_ref.at[at], [keys_ref.at[m] for m in range(kv)])

    def scores_of(g):
        return dot(jnp.concatenate([two_keys_ref[g], own_keys_ref[g]], axis=0), queries_ref[g], 1, 1)

    scores = scores_of(0)
    for g in range(kv):
        ahead = scores_of(g + 1) if g + 1 < kv else None
        fold = jnp.where(here, scores[tokens:], scores[0:tokens]) * scaling + bias_ref[0]
        top = jnp.max(fold, axis=0, keepdims=True)
        fold = jnp.exp(fold - top)
        fold_ref[g] = fold
        stats_ref[g, 0:1, :] = top
        stats_ref[g, 1:2, :] = jnp.sum(fold, axis=0, keepdims=True)
        scores = ahead


def near_kernel(
    queries_ref, one_ref, bias_ref, fold_ref, stats_ref, low_ref, one_keys_ref, wide_ref, *, kv, group, scaling,
):
    head_major(one_ref, wide_ref, [one_keys_ref.at[m] for m in range(kv)])
    weigh(queries_ref, one_keys_ref, bias_ref, fold_ref, stats_ref, low_ref, group, scaling, 0)


def far_kernel(
    queries_ref, one_keys_ref, bias_ref, fold_ref, stats_ref, low_ref, *, group, scaling, first,
):
    weigh(queries_ref, one_keys_ref, bias_ref, fold_ref, stats_ref, low_ref, group, scaling, first)


def weigh(queries_ref, one_keys_ref, bias_ref, fold_ref, stats_ref, low_ref, group, scaling, first):
    tokens = one_keys_ref.shape[1]
    _, here = places(queries_ref.shape[1], tokens, group)
    count = low_ref.shape[0]

    def scores_of(g):
        return dot(one_keys_ref[g], queries_ref[g], 1, 1)

    scores = scores_of(first)
    for at in range(count):
        g = first + at
        ahead = scores_of(g + 1) if at + 1 < count else None
        mid = scores * scaling + bias_ref[1]
        fold_top = stats_ref[g, 0:1, :]
        top = jnp.maximum(fold_top, jnp.max(mid, axis=0, keepdims=True))
        mid = jnp.exp(mid - top)
        fade = jnp.exp(fold_top - top)
        share = 1.0 / (stats_ref[g, 1:2, :] * fade + jnp.sum(mid, axis=0, keepdims=True))
        fold = fold_ref[g] * (fade * share)
        low_ref[at, 0:tokens, :] = jnp.where(here, 0.0, fold).astype(LOW)
        low_ref[at, tokens : 2 * tokens, :] = jnp.where(here, fold, 0.0).astype(LOW)
        low_ref[at, 2 * tokens :, :] = (mid * share).astype(LOW)
        scores = ahead


def half_of(refs, g):
    return refs[g // refs[0].shape[0]].at[g % refs[0].shape[0]]


def hidden_kernel(near_ref, far_ref, two_ref, own_ref, part_ref, two_values_ref, own_values_ref, wide_ref, *, kv):
    tokens, dim = two_values_ref.shape[1:]
    for at, (ref, values_ref) in enumerate(((two_ref, two_values_ref), (own_ref, own_values_ref))):
        head_major(ref, wide_ref.at[at], [values_ref.at[m] for m in range(kv)])
    for g in range(kv):
        low_ref = half_of((near_ref, far_ref), g)
        values = jnp.concatenate([two_values_ref[g], own_values_ref[g]], axis=0)
        part_ref[g * dim : (g + 1) * dim, :] = dot(values, low_ref[0 : 2 * tokens, :], 0, 0)


def sent_slots(group, owned, odd):
    return [slot for slot in range(group) if (slot // owned) % 2 == odd]


def write_parts(into, slots, on_rot, on_proj, kv, group, owned, span, dim):
    rep, me = lax.axis_size("rep"), lax.axis_index("ctx")
    per_group = group // owned
    here_rows = span // rep
    for g in range(kv):
        columns = slice(g * dim, (g + 1) * dim)
        for low in sorted({slot // owned for slot in slots}):
            device = (g ^ (me // per_group)) * per_group + low
            for r in range(rep):
                pieces = []
                for slot in range(low * owned, (low + 1) * owned):
                    first = slots.index(slot) * span + r * here_rows
                    rows = slice(first, first + here_rows)
                    pieces += [on_rot[rows, columns], on_proj[rows, columns]]
                into[reduce_place(dict(ctx=device, rep=r))] = jnp.concatenate(pieces, axis=0).astype(LOW)


def forward_kernel(
    shift_ref, near_ref, far_ref, part_ref, one_ref, cots_ref, diff_ref, meta_ref, pull_ref,
    send_ref, hidden_ref, lift_ref, one_values_ref, wide_ref, *, kv, group, tenants, rank, owned,
):
    tokens, dim = one_values_ref.shape[1:]
    head_major(one_ref, wide_ref, [one_values_ref.at[m] for m in range(kv)])
    owner = meta_ref[1:2, :]
    lanes = owner.shape[1]
    hidden = []
    for g in range(kv):
        low_ref = half_of((near_ref, far_ref), g)
        middle = dot(one_values_ref[g], low_ref[2 * tokens :, :], 0, 0)
        hidden.append((part_ref[g * dim : (g + 1) * dim, :] + middle).astype(LOW))
    hidden = jnp.concatenate(hidden, axis=0)
    hidden_ref[...] = hidden
    on_diff = dot(jnp.concatenate([diff_ref[g] for g in range(kv)], axis=1), hidden, 1, 0)
    lifted = own_terms(on_diff, owner, tenants, rank, group)
    one_hot = (owner == lax.broadcasted_iota(jnp.int32, (tenants, lanes), 0)).astype(WIDE)
    bias = jnp.concatenate([shift_ref[...]] * (8 // rank), axis=0)
    shift = dot(bias, one_hot, 1, 0, lax.Precision.HIGHEST)
    lifted = (lifted + shift).astype(LOW).astype(WIDE)
    span = tenants * rank
    lifts = picked_rows(lifted, owner, slots_of(lanes, group, owned), tenants, rank, group)
    for at, slot in enumerate(sent_slots(group, owned, 0)):
        lift_ref[at * span : (at + 1) * span, :] = lifts[slot]
    slots = sent_slots(group, owned, 1)
    pulls = [pull_ref[slot * span : (slot + 1) * span, :] for slot in slots]
    on_proj = dot(jnp.concatenate(pulls, axis=0), hidden, 1, 1)
    cots = jnp.concatenate([cots_ref[g] for g in range(kv)], axis=1)
    on_rot = dot(jnp.concatenate([lifts[slot] for slot in slots], axis=0), cots, 1, 0) - on_proj
    write_parts(send_ref, slots, on_rot, on_proj, kv, group, owned, span, dim)


def keep_kernel(hidden_ref, lift_ref, cots_ref, pull_ref, keep_ref, *, kv, group, span, owned):
    dim = cots_ref.shape[2]
    slots = sent_slots(group, owned, 0)
    pulls = [pull_ref[slot * span : (slot + 1) * span, :] for slot in slots]
    on_proj = dot(jnp.concatenate(pulls, axis=0), hidden_ref[...], 1, 1)
    cots = jnp.concatenate([cots_ref[g] for g in range(kv)], axis=1)
    on_rot = dot(lift_ref[...], cots, 1, 0) - on_proj
    write_parts(keep_ref, slots, on_rot, on_proj, kv, group, owned, span, dim)


def backward_kernel(
    queries_ref, gh_ref, near_ref, far_ref, two_ref, one_ref, own_ref, back_two_ref, back_one_ref, back_own_ref, grad_ref,
    *, kv, scaling,
):
    tokens = back_own_ref.shape[1]

    def weight_grad_of(g):
        return dot(window_of(two_ref, own_ref, one_ref, g), gh_ref[g], 1, 1)

    weight_grad = weight_grad_of(0)
    for g in range(kv):
        ahead = weight_grad_of(g + 1) if g + 1 < kv else None
        low = half_of((near_ref, far_ref), g)[...]
        weights = low.astype(WIDE)
        delta = jnp.sum(weights * weight_grad, axis=0, keepdims=True)
        score_grad = (weights * (weight_grad - delta)).astype(LOW)
        grad_ref[g] = score_grad
        key_grad = dot(score_grad, queries_ref[g], 1, 0) * scaling
        value_grad = dot(low, gh_ref[g], 1, 0)
        for place, grad in ((g, key_grad), (kv + g, value_grad)):
            back_two_ref[place] = grad[0:tokens].astype(LOW)
            back_own_ref[place] = grad[tokens : 2 * tokens]
            back_one_ref[place] = grad[2 * tokens :].astype(LOW)
        weight_grad = ahead


def query_kernel(
    grad_ref, two_ref, one_ref, own_ref, dq_hbm, dq_ref, sems, *, kv, group, scaling,
):
    tokens, _, dim = dq_ref.shape
    copies = []
    for g in range(kv):
        query_grad = dot(window_of(two_ref, own_ref, one_ref, g), grad_ref[g], 0, 0) * scaling
        query_grad = query_grad.T.reshape(tokens, group, dim)
        if g % 2 == 1:
            heads = slice((g - 1) * group, (g + 1) * group)
            dq_ref[:, heads, :] = jnp.concatenate([before, query_grad], axis=1).astype(LOW)
            copies.append(pltpu.make_async_copy(dq_ref.at[:, heads], dq_hbm.at[:, heads], sems.at[g // 2]))
            copies[-1].start()
        before = query_grad
    for copy in copies:
        copy.wait()


def finish_kernel(own_ref, mate_ref, two_ref, part_ref, *refs, kv, owned):
    *other_refs, keys_hbm, values_hbm, rot_hbm, proj_hbm, wide_ref, low_ref, grads_ref, sems = refs
    copies = [
        pltpu.make_async_copy(source, target, sems.at[at])
        for at, (source, target) in enumerate(
            (
                (grads_ref.at[0], rot_hbm), (grads_ref.at[1], proj_hbm),
                (low_ref.at[0], keys_hbm), (low_ref.at[1], values_hbm),
            )
        )
    ]
    total = part_ref[0].astype(WIDE)
    for other_ref in other_refs:
        total = total + other_ref[0].astype(WIDE)
    size = grads_ref.shape[1]
    for at in range(2):
        for place in range(owned):
            row = (2 * place + at) * size
            grads_ref[at, :, place, :] = total[row : row + size]
        copies[at].start()
    tokens = own_ref.shape[1]
    even = (lax.axis_index("ctx") % 2 == 0).astype(WIDE)
    for at in range(2):
        for m in range(kv):
            place = at * kv + m
            total = own_ref[place] + two_ref[place].astype(WIDE) + even * mate_ref[place].astype(WIDE)
            wide_ref[at, pl.ds(m, tokens, stride=kv), :] = total
        low_ref[at] = wide_ref[at].astype(LOW)
        copies[2 + at].start()
    for copy in copies:
        copy.wait()


def on_device(
    query_rows, key_rows, value_matrix, cotangent, rotation, projection, shift_bias, doc_starts, tenant_ids,
):
    queries = query_rows[0]
    upstream = cotangent[0]
    tokens, heads, dim = queries.shape
    kv = key_rows.shape[2]
    group = heads // kv
    scaling = dim ** (-0.5)
    tenants, rank = rotation.shape[0], rotation.shape[1]
    lanes = tokens * group
    ctx = lax.axis_size("ctx")
    rep = lax.axis_size("rep")
    assert 2 * tokens == DOC_MAX


    rot = rotation.reshape(tenants * rank, heads, dim)
    proj = projection.reshape(tenants * rank, heads, dim)
    sizes = dict(kv=kv, group=group)
    vmem = pl.BlockSpec(memory_space=pltpu.VMEM)

    def call(body, outs, flops, moved, out_specs=None, scratch=(), **fixed):
        def run(*operands):
            return pl.pallas_call(
                lambda *refs: body(*refs, **fixed),
                out_shape=[jax.ShapeDtypeStruct(*out) for out in outs],
                in_specs=[vmem] * len(operands),
                out_specs=out_specs or [vmem] * len(outs),
                scratch_shapes=scratch,
                compiler_params=pltpu.CompilerParams(vmem_limit_bytes=12 * 2**20),
                name=body.__name__,
                cost_estimate=pl.CostEstimate(flops=flops, bytes_accessed=moved, transcendentals=0),
            )(*operands)

        return run

    span = tenants * rank
    here = heads // ctx
    rows = here * 2 * span // rep
    even = jnp.reshape(lax.axis_index("ctx") % 2 == 0, (1, 1, 1))
    key_rows, even = lax.optimization_barrier((key_rows, even))
    own_keys = key_rows[0]
    two_keys = shifted(own_keys, "ctx", 2)
    meta, biases = call(
        place_kernel, [((8, lanes), jnp.int32), ((2, tokens, lanes), WIDE)], 8 * 2**30, 2**20,
        group=group,
    )(jnp.concatenate([doc_starts, tenant_ids], axis=0))
    own_values = value_matrix[0]
    leaving, meta = lax.optimization_barrier((own_values, meta))
    two_values = shifted(leaving, "ctx", 2)
    cots, queries, pulled, pull = call(
        pull_kernel,
        [((kv, lanes, dim), LOW), ((kv, lanes, dim), LOW), ((8, lanes), WIDE), ((span * group, lanes), LOW)],
        2**30, 4 * 2**20, tenants=tenants, rank=rank, owned=here, **sizes,
    )(meta, upstream, rot, queries)
    grad_hidden, diff = call(
        hidden_grad_kernel, [((kv, lanes, dim), LOW), ((kv, span * group, dim), LOW)],
        2 * 2**30, 4 * 2**20, tenants=tenants, rank=rank, **sizes,
    )(meta, pulled, cots, rot, proj)
    two_keys, grad_hidden = lax.optimization_barrier((two_keys, grad_hidden))
    one_keys = exchanged(jnp.where(even, own_keys, two_keys), {"ctx": 1})
    flat, heads_first = (tokens * kv, dim), ((kv, tokens, dim), LOW)
    fold, stats, two_heads, own_heads = call(
        fold_kernel, [((kv, tokens, lanes), WIDE), ((kv, 2, lanes), WIDE), heads_first, heads_first],
        2 * 2**30, 4 * 2**20, scratch=[pltpu.VMEM((2, *flat), WIDE)], scaling=scaling, **sizes,
    )(queries, two_keys.reshape(flat), own_keys.reshape(flat), biases)
    one_keys, fold = lax.optimization_barrier((one_keys, fold))

    halves = ((kv // 2, 3 * tokens, lanes), LOW)
    near, one_heads = call(
        near_kernel, [halves, heads_first], 2**30, 4 * 2**20,
        scratch=[pltpu.VMEM(flat, WIDE)], scaling=scaling, **sizes,
    )(queries, one_keys.reshape(flat), biases, fold, stats)
    two_values, near = lax.optimization_barrier((two_values, near))
    one_values = exchanged(jnp.where(even, own_values, two_values), {"ctx": 1})
    far, = call(
        far_kernel, [halves], 2**30, 4 * 2**20, group=group, scaling=scaling, first=kv // 2,
    )(queries, one_heads, biases, fold, stats)
    part_hidden, two_sides, own_sides = call(
        hidden_kernel, [((heads // group * dim, lanes), WIDE), heads_first, heads_first], 2**30, 4 * 2**20,
        scratch=[pltpu.VMEM((2, *flat), WIDE)], kv=kv,
    )(near, far, two_values.reshape(flat), own_values.reshape(flat))
    one_values, part_hidden = lax.optimization_barrier((one_values, part_hidden))
    kept = (span * group // 2, lanes)
    send, hidden, lift, one_sides = call(
        forward_kernel,
        [((ctx * rep // 2, rows, dim), LOW), (part_hidden.shape, LOW), (kept, LOW), heads_first],
        3 * 2**30, 10 * 2**20, scratch=[pltpu.VMEM(flat, WIDE)],
        tenants=tenants, rank=rank, owned=here, **sizes,
    )(shift_bias.T, near, far, part_hidden, one_values.reshape(flat), cots, diff, meta, pull)
    keep, = call(
        keep_kernel, [((ctx * rep // 2, rows, dim), LOW)], 2**30, 5 * 2**20, span=span, owned=here, **sizes,
    )(hidden, lift, cots, pull)
    part = (keep.astype(WIDE) + exchanged(send, {"ctx": 1}).astype(WIDE)).astype(LOW)
    near, part = lax.optimization_barrier((near, part))
    window = (2 * kv, tokens, dim)
    back_two, back_one, back_own, score_grad = call(
        backward_kernel, [(window, LOW), (window, LOW), (window, WIDE), ((kv, 3 * tokens, lanes), LOW)],
        4 * 2**30, 10 * 2**20, kv=kv, scaling=scaling,
    )(queries, grad_hidden, near, far, two_sides, one_sides, own_sides)
    d_queries, = call(
        query_kernel, [((tokens, heads, dim), LOW)], 2 * 2**30, 5 * 2**20,
        scratch=[pltpu.VMEM((tokens, heads, dim), LOW), pltpu.SemaphoreType.DMA((kv // 2,))],
        out_specs=[pl.BlockSpec(memory_space=pltpu.HBM)], scaling=scaling, **sizes,
    )(score_grad, two_heads, one_heads, own_heads)
    from_mate = exchanged(back_one, {"ctx": 1})
    onward = back_two.astype(WIDE) + jnp.where(even, 0.0, from_mate.astype(WIDE))
    onward = onward.astype(LOW)

    groups = reduce_groups()
    for at, group_bits in enumerate(groups):
        beside = back_own if at == 0 else None
        if at == len(groups) - 1:
            part, onward = lax.optimization_barrier((part, onward))
            from_two = shifted(onward, "ctx", -2)
            beside = from_two
        part, others = scattered(part, group_bits, beside)
        if at < len(groups) - 1:
            part = part.astype(WIDE) + sum(other.astype(WIDE) for other in others)
            part = part.astype(LOW)
    d_keys, d_values, *grads = call(
        finish_kernel, [((tokens * kv, dim), LOW)] * 2 + [((span // rep, here, dim), WIDE)] * 2, 2**20, 2**20,
        scratch=[
            pltpu.VMEM((2, tokens * kv, dim), WIDE), pltpu.VMEM((2, tokens * kv, dim), LOW),
            pltpu.VMEM((2, span // rep, here, dim), WIDE), pltpu.SemaphoreType.DMA((4,)),
        ],
        out_specs=[pl.BlockSpec(memory_space=pltpu.HBM)] * 4, kv=kv, owned=here,
    )(back_own, from_mate, from_two, part, *others)
    grads = [grad.reshape(tenants // rep, rank, here, dim) for grad in grads]
    d_keys, d_values = (grad.reshape(key_rows.shape) for grad in (d_keys, d_values))
    return (d_queries[None], d_keys, d_values, grads[0], grads[1])


def solution(mesh):
    rows = P("rep", "ctx", None, None)
    in_specs = (rows, rows, rows, rows, P(), P(), P(), P("rep", None), P("rep", None))
    tenant_rows = P("rep", None, "ctx", None)
    out_specs = (rows, rows, rows, tenant_rows, tenant_rows)
    return jax.shard_map(
        on_device, mesh=mesh, in_specs=in_specs, out_specs=out_specs, check_vma=False
    )
```

```python
import itertools

import jax
import jax.numpy as jnp
import numpy as np
from jax import lax
from jax.experimental import pallas as pl
from jax.experimental.pallas import tpu as pltpu
from jax.sharding import PartitionSpec as P

DOC_MAX = 256
LOW = jnp.bfloat16
WIDE = jnp.float32
far_below = -1e30


def shifted(value, axis, steps):
    count = lax.axis_size(axis)
    return lax.ppermute(value, axis, [(source, (source + steps) % count) for source in range(count)])


def exchanged(value, bits):
    axes = tuple(bits)
    shape = [lax.axis_size(axis) for axis in axes]
    pairs = []
    for source in np.ndindex(*shape):
        target = [at ^ bits[axis] for at, axis in zip(source, axes)]
        pairs.append((np.ravel_multi_index(source, shape), np.ravel_multi_index(target, shape)))
    return lax.ppermute(value, axes, [(int(source), int(target)) for source, target in pairs])


def reduce_groups():
    ctx, rep = lax.axis_size("ctx"), lax.axis_size("rep")
    bits = [{"ctx": 1 << at} for at in range(ctx.bit_length() - 2, 0, -1)]
    bits += [{"rep": 1 << at} for at in range(rep.bit_length() - 1)]
    over_ctx = ctx.bit_length() - 2
    return [bits[at : at + 2] for at in range(0, over_ctx, 2)] + [[bit] for bit in bits[over_ctx:]]


def reduce_place(index):
    place = 0
    for bits in itertools.chain(*reduce_groups()):
        for axis, bit in bits.items():
            place = 2 * place + (index[axis] // bit) % 2
    return place


def scattered(part, group, beside=None):
    count = 1 << len(group)
    size = part.shape[0] // count
    others = []
    for j in range(1, count):
        bits = {}
        for at, pair in enumerate(reversed(group)):
            if (j >> at) & 1:
                bits.update({axis: bits.get(axis, 0) | bit for axis, bit in pair.items()})
        others.append(exchanged(part[j * size : (j + 1) * size], bits))
    if beside is not None:
        others = lax.optimization_barrier((others, beside))[0]
    return part[:size], others


def dot(left, right, left_dim, right_dim, precision=None):
    return lax.dot_general(
        left, right, (((left_dim,), (right_dim,)), ((), ())),
        precision=precision, preferred_element_type=WIDE,
    )


def group_rows(ref, kv_count, group_size):
    rows, _, dim = ref.shape
    wide = 2 * group_size
    parts = []
    for pair in range(kv_count // 2):
        both = ref[:, pair * wide : (pair + 1) * wide, :].astype(WIDE)
        for half in range(2):
            one = both[:, half * group_size : (half + 1) * group_size, :]
            parts.append(one.reshape(rows * group_size, dim).astype(LOW))
    return parts


def lane_head(shape, group_size):
    return lax.broadcasted_iota(jnp.int32, shape, 1) % group_size


def own_terms(maps_by_rows, owner, tenants, low_rank, group_size):
    lanes = maps_by_rows.shape[1]
    same_head = lax.broadcasted_iota(jnp.int32, (group_size, lanes), 0) == lane_head(
        (group_size, lanes), group_size
    )
    span = low_rank * group_size
    total = jnp.zeros((low_rank, group_size, lanes), WIDE)
    for tenant in range(tenants):
        keep = same_head & (owner == tenant)
        block = maps_by_rows[tenant * span : (tenant + 1) * span].reshape(
            low_rank, group_size, lanes
        )
        total = total + jnp.where(keep[None], block, 0.0)
    rows = jnp.sum(total, axis=1)
    rows = jnp.concatenate([rows, rows], axis=0)
    tiles = lanes // 128
    stacked = jnp.concatenate([rows[:, c * 128 : (c + 1) * 128] for c in range(tiles)], axis=0)
    side = lax.broadcasted_iota(jnp.int32, (128, 128), 0) // group_size
    over = lax.broadcasted_iota(jnp.int32, (128, 128), 1) // group_size
    spread = dot(stacked, (side == over).astype(WIDE), 1, 0, lax.Precision.HIGHEST)
    return jnp.concatenate([spread[c * 8 : (c + 1) * 8] for c in range(tiles)], axis=1)


def place_kernel(rows_ref, meta_ref, bias_ref, *, group):
    lanes = meta_ref.shape[1]
    tokens = lanes // group
    row_first = lax.axis_index("ctx") * tokens
    mine = pl.ds(pl.multiple_of(row_first, tokens), tokens)
    row = lax.broadcasted_iota(jnp.int32, (8, tokens), 0)
    both = jnp.where(row == 0, rows_ref[0:1, mine] - row_first, rows_ref[1:2, mine]).astype(WIDE)
    repeat = lax.broadcasted_iota(jnp.int32, (tokens, lanes), 0) == (
        lax.broadcasted_iota(jnp.int32, (tokens, lanes), 1) // group
    )
    meta = dot(both, repeat.astype(WIDE), 1, 0, lax.Precision.HIGHEST).astype(jnp.int32)
    meta_ref[...] = meta
    first = meta[0:1, :]
    key, here = places(lanes, tokens, group)
    bias_ref[0] = jnp.where(jnp.where(here, key, key - 2 * tokens) >= first, 0.0, far_below)
    bias_ref[1] = jnp.where(key - tokens >= first, 0.0, far_below)


def slots_of(lanes, group, owned):
    per_group = group // owned
    head = lane_head((1, lanes), group)
    return head ^ ((lax.axis_index("ctx") % per_group) * owned)


def tenants_of(lanes, tenants, rank):
    row = lax.broadcasted_iota(jnp.int32, (tenants * rank, lanes), 0) // rank
    return row ^ (lax.axis_index("rep") * (tenants // lax.axis_size("rep")))


def picked_rows(rows, owner, slots, tenants, rank, group):
    lanes = owner.shape[1]
    mine = owner == tenants_of(lanes, tenants, rank)
    rows = jnp.where(mine, jnp.concatenate([rows] * (tenants * rank // 8), axis=0), 0.0)
    return [jnp.where(slots == h, rows, 0.0).astype(LOW) for h in range(group)]


def pull_kernel(
    meta_ref, cot_ref, rot_ref, q_ref, cots_ref, queries_ref, pulled_ref, pull_ref,
    *, kv, group, tenants, rank, owned,
):
    owner = meta_ref[1:2, :]
    lanes = owner.shape[1]
    cots = group_rows(cot_ref, kv, group)
    rots = group_rows(rot_ref, kv, group)
    on_rot = dot(jnp.concatenate(rots, axis=1), jnp.concatenate(cots, axis=1), 1, 1)
    pulled = own_terms(on_rot, owner, tenants, rank, group).astype(LOW).astype(WIDE)
    pulled_ref[...] = pulled
    for g, rows in enumerate(group_rows(q_ref, kv, group)):
        queries_ref[g] = rows
        cots_ref[g] = cots[g]
    span = tenants * rank
    slots = slots_of(lanes, group, owned)
    for h, rows in enumerate(picked_rows(pulled, owner, slots, tenants, rank, group)):
        pull_ref[h * span : (h + 1) * span, :] = rows


def hidden_grad_kernel(
    meta_ref, pulled_ref, cots_ref, rot_ref, proj_ref, gh_ref, diff_ref, *, kv, group, tenants, rank,
):
    owner = meta_ref[1:2, :]
    lanes = owner.shape[1]
    dim = cots_ref.shape[2]
    pulled = pulled_ref[...]
    same_head = lax.broadcasted_iota(jnp.int32, (group, lanes), 0) == lane_head((group, lanes), group)
    picked = []
    for tenant in range(tenants):
        keep = same_head & (owner == tenant)
        for k in range(rank):
            picked.append(jnp.where(keep, pulled[k : k + 1], 0.0))
    picked = jnp.concatenate(picked, axis=0).T.astype(LOW)
    rots = group_rows(rot_ref, kv, group)
    projs = group_rows(proj_ref, kv, group)
    diffs = [(proj.astype(WIDE) - rot.astype(WIDE)).astype(LOW) for proj, rot in zip(projs, rots)]
    steered = dot(picked, jnp.concatenate(diffs, axis=1), 1, 0)
    for g in range(kv):
        diff_ref[g] = diffs[g]
        gh_ref[g] = (cots_ref[g].astype(WIDE) + steered[:, g * dim : (g + 1) * dim]).astype(LOW)


def places(lanes, tokens, group):
    key = lax.broadcasted_iota(jnp.int32, (tokens, lanes), 0)
    query = lax.broadcasted_iota(jnp.int32, (tokens, lanes), 1) // group
    return key, key <= query


def window_of(two_ref, own_ref, one_ref, head):
    return jnp.concatenate([two_ref[head], own_ref[head], one_ref[head]], axis=0)


def head_major(ref, wide_ref, outs):
    count = len(outs)
    wide_ref[...] = ref[...].astype(WIDE)
    for m, out in enumerate(outs):
        out[...] = wide_ref[pl.ds(m, out.shape[0], stride=count), :].astype(LOW)


def fold_kernel(
    queries_ref, two_ref, own_ref, bias_ref, fold_ref, stats_ref, two_keys_ref, own_keys_ref, wide_ref,
    *, kv, group, scaling,
):
    tokens = two_keys_ref.shape[1]
    _, here = places(queries_ref.shape[1], tokens, group)
    for at, (ref, keys_ref) in enumerate(((two_ref, two_keys_ref), (own_ref, own_keys_ref))):
        head_major(ref, wide_ref.at[at], [keys_ref.at[m] for m in range(kv)])

    def scores_of(g):
        return dot(jnp.concatenate([two_keys_ref[g], own_keys_ref[g]], axis=0), queries_ref[g], 1, 1)

    scores = scores_of(0)
    for g in range(kv):
        ahead = scores_of(g + 1) if g + 1 < kv else None
        fold = jnp.where(here, scores[tokens:], scores[0:tokens]) * scaling + bias_ref[0]
        top = jnp.max(fold, axis=0, keepdims=True)
        fold = jnp.exp(fold - top)
        fold_ref[g] = fold
        stats_ref[g, 0:1, :] = top
        stats_ref[g, 1:2, :] = jnp.sum(fold, axis=0, keepdims=True)
        scores = ahead


def near_kernel(
    queries_ref, one_ref, bias_ref, fold_ref, stats_ref, low_ref, one_keys_ref, wide_ref, *, kv, group, scaling,
):
    head_major(one_ref, wide_ref, [one_keys_ref.at[m] for m in range(kv)])
    weigh(queries_ref, one_keys_ref, bias_ref, fold_ref, stats_ref, low_ref, group, scaling, 0)


def far_kernel(
    queries_ref, one_keys_ref, bias_ref, fold_ref, stats_ref, low_ref, *, group, scaling, first,
):
    weigh(queries_ref, one_keys_ref, bias_ref, fold_ref, stats_ref, low_ref, group, scaling, first)


def weigh(queries_ref, one_keys_ref, bias_ref, fold_ref, stats_ref, low_ref, group, scaling, first):
    tokens = one_keys_ref.shape[1]
    _, here = places(queries_ref.shape[1], tokens, group)
    count = low_ref.shape[0]

    def scores_of(g):
        return dot(one_keys_ref[g], queries_ref[g], 1, 1)

    scores = scores_of(first)
    for at in range(count):
        g = first + at
        ahead = scores_of(g + 1) if at + 1 < count else None
        mid = scores * scaling + bias_ref[1]
        fold_top = stats_ref[g, 0:1, :]
        top = jnp.maximum(fold_top, jnp.max(mid, axis=0, keepdims=True))
        mid = jnp.exp(mid - top)
        fade = jnp.exp(fold_top - top)
        share = 1.0 / (stats_ref[g, 1:2, :] * fade + jnp.sum(mid, axis=0, keepdims=True))
        fold = fold_ref[g] * (fade * share)
        low_ref[at, 0:tokens, :] = jnp.where(here, 0.0, fold).astype(LOW)
        low_ref[at, tokens : 2 * tokens, :] = jnp.where(here, fold, 0.0).astype(LOW)
        low_ref[at, 2 * tokens :, :] = (mid * share).astype(LOW)
        scores = ahead


def half_of(refs, g):
    return refs[g // refs[0].shape[0]].at[g % refs[0].shape[0]]


def hidden_kernel(near_ref, far_ref, two_ref, own_ref, part_ref, two_values_ref, own_values_ref, wide_ref, *, kv):
    tokens, dim = two_values_ref.shape[1:]
    for at, (ref, values_ref) in enumerate(((two_ref, two_values_ref), (own_ref, own_values_ref))):
        head_major(ref, wide_ref.at[at], [values_ref.at[m] for m in range(kv)])
    for g in range(kv):
        low_ref = half_of((near_ref, far_ref), g)
        values = jnp.concatenate([two_values_ref[g], own_values_ref[g]], axis=0)
        part_ref[g * dim : (g + 1) * dim, :] = dot(values, low_ref[0 : 2 * tokens, :], 0, 0)


def sent_slots(group, owned, odd):
    return [slot for slot in range(group) if (slot // owned) % 2 == odd]


def write_parts(into, slots, on_rot, on_proj, kv, group, owned, span, dim):
    rep, me = lax.axis_size("rep"), lax.axis_index("ctx")
    per_group = group // owned
    here_rows = span // rep
    for g in range(kv):
        columns = slice(g * dim, (g + 1) * dim)
        for low in sorted({slot // owned for slot in slots}):
            device = (g ^ (me // per_group)) * per_group + low
            for r in range(rep):
                pieces = []
                for slot in range(low * owned, (low + 1) * owned):
                    first = slots.index(slot) * span + r * here_rows
                    rows = slice(first, first + here_rows)
                    pieces += [on_rot[rows, columns], on_proj[rows, columns]]
                into[reduce_place(dict(ctx=device, rep=r))] = jnp.concatenate(pieces, axis=0).astype(LOW)


def forward_kernel(
    shift_ref, near_ref, far_ref, part_ref, one_ref, cots_ref, diff_ref, meta_ref, pull_ref,
    send_ref, hidden_ref, lift_ref, one_values_ref, wide_ref, *, kv, group, tenants, rank, owned,
):
    tokens, dim = one_values_ref.shape[1:]
    head_major(one_ref, wide_ref, [one_values_ref.at[m] for m in range(kv)])
    owner = meta_ref[1:2, :]
    lanes = owner.shape[1]
    hidden = []
    for g in range(kv):
        low_ref = half_of((near_ref, far_ref), g)
        middle = dot(one_values_ref[g], low_ref[2 * tokens :, :], 0, 0)
        hidden.append((part_ref[g * dim : (g + 1) * dim, :] + middle).astype(LOW))
    hidden = jnp.concatenate(hidden, axis=0)
    hidden_ref[...] = hidden
    on_diff = dot(jnp.concatenate([diff_ref[g] for g in range(kv)], axis=1), hidden, 1, 0)
    lifted = own_terms(on_diff, owner, tenants, rank, group)
    one_hot = (owner == lax.broadcasted_iota(jnp.int32, (tenants, lanes), 0)).astype(WIDE)
    bias = jnp.concatenate([shift_ref[...]] * (8 // rank), axis=0)
    shift = dot(bias, one_hot, 1, 0, lax.Precision.HIGHEST)
    lifted = (lifted + shift).astype(LOW).astype(WIDE)
    span = tenants * rank
    lifts = picked_rows(lifted, owner, slots_of(lanes, group, owned), tenants, rank, group)
    for at, slot in enumerate(sent_slots(group, owned, 0)):
        lift_ref[at * span : (at + 1) * span, :] = lifts[slot]
    slots = sent_slots(group, owned, 1)
    pulls = [pull_ref[slot * span : (slot + 1) * span, :] for slot in slots]
    on_proj = dot(jnp.concatenate(pulls, axis=0), hidden, 1, 1)
    cots = jnp.concatenate([cots_ref[g] for g in range(kv)], axis=1)
    on_rot = dot(jnp.concatenate([lifts[slot] for slot in slots], axis=0), cots, 1, 0) - on_proj
    write_parts(send_ref, slots, on_rot, on_proj, kv, group, owned, span, dim)


def keep_kernel(hidden_ref, lift_ref, cots_ref, pull_ref, keep_ref, *, kv, group, span, owned):
    dim = cots_ref.shape[2]
    slots = sent_slots(group, owned, 0)
    pulls = [pull_ref[slot * span : (slot + 1) * span, :] for slot in slots]
    on_proj = dot(jnp.concatenate(pulls, axis=0), hidden_ref[...], 1, 1)
    cots = jnp.concatenate([cots_ref[g] for g in range(kv)], axis=1)
    on_rot = dot(lift_ref[...], cots, 1, 0) - on_proj
    write_parts(keep_ref, slots, on_rot, on_proj, kv, group, owned, span, dim)


def backward_kernel(
    queries_ref, gh_ref, near_ref, far_ref, two_ref, one_ref, own_ref, back_two_ref, back_one_ref, back_own_ref, grad_ref,
    *, kv, scaling,
):
    tokens = back_own_ref.shape[1]

    def weight_grad_of(g):
        return dot(window_of(two_ref, own_ref, one_ref, g), gh_ref[g], 1, 1)

    weight_grad = weight_grad_of(0)
    for g in range(kv):
        ahead = weight_grad_of(g + 1) if g + 1 < kv else None
        low = half_of((near_ref, far_ref), g)[...]
        weights = low.astype(WIDE)
        delta = jnp.sum(weights * weight_grad, axis=0, keepdims=True)
        score_grad = (weights * (weight_grad - delta)).astype(LOW)
        grad_ref[g] = score_grad
        key_grad = dot(score_grad, queries_ref[g], 1, 0) * scaling
        value_grad = dot(low, gh_ref[g], 1, 0)
        for place, grad in ((g, key_grad), (kv + g, value_grad)):
            back_two_ref[place] = grad[0:tokens].astype(LOW)
            back_own_ref[place] = grad[tokens : 2 * tokens]
            back_one_ref[place] = grad[2 * tokens :].astype(LOW)
        weight_grad = ahead


def query_kernel(
    grad_ref, two_ref, one_ref, own_ref, dq_hbm, dq_ref, sems, *, kv, group, scaling,
):
    tokens, _, dim = dq_ref.shape
    copies = []
    for g in range(kv):
        query_grad = dot(window_of(two_ref, own_ref, one_ref, g), grad_ref[g], 0, 0) * scaling
        query_grad = query_grad.T.reshape(tokens, group, dim)
        if g % 2 == 1:
            heads = slice((g - 1) * group, (g + 1) * group)
            dq_ref[:, heads, :] = jnp.concatenate([before, query_grad], axis=1).astype(LOW)
            copies.append(pltpu.make_async_copy(dq_ref.at[:, heads], dq_hbm.at[:, heads], sems.at[g // 2]))
            copies[-1].start()
        before = query_grad
    for copy in copies:
        copy.wait()


def finish_kernel(
    own_ref, mate_ref, two_ref, part_ref, *refs, kv, owned,
):
    *other_refs, keys_ref, values_ref, rot_ref, proj_ref, wide_ref = refs
    total = part_ref[0].astype(WIDE)
    for other_ref in other_refs:
        total = total + other_ref[0].astype(WIDE)
    size = rot_ref.shape[0]
    for place in range(owned):
        for at, out in enumerate((rot_ref, proj_ref)):
            row = (2 * place + at) * size
            out[:, place, :] = total[row : row + size]
    tokens = own_ref.shape[1]
    even = (lax.axis_index("ctx") % 2 == 0).astype(WIDE)
    for at, out in enumerate((keys_ref, values_ref)):
        for m in range(kv):
            place = at * kv + m
            total = own_ref[place] + two_ref[place].astype(WIDE) + even * mate_ref[place].astype(WIDE)
            wide_ref[at, pl.ds(m, tokens, stride=kv), :] = total
        out[...] = wide_ref[at].astype(LOW)


def on_device(
    query_rows, key_rows, value_matrix, cotangent, rotation, projection, shift_bias, doc_starts, tenant_ids,
):
    queries = query_rows[0]
    upstream = cotangent[0]
    tokens, heads, dim = queries.shape
    kv = key_rows.shape[2]
    group = heads // kv
    scaling = dim ** (-0.5)
    tenants, rank = rotation.shape[0], rotation.shape[1]
    lanes = tokens * group
    ctx = lax.axis_size("ctx")
    rep = lax.axis_size("rep")
    assert 2 * tokens == DOC_MAX


    rot = rotation.reshape(tenants * rank, heads, dim)
    proj = projection.reshape(tenants * rank, heads, dim)
    sizes = dict(kv=kv, group=group)
    vmem = pl.BlockSpec(memory_space=pltpu.VMEM)

    def call(body, outs, flops, moved, out_specs=None, scratch=(), **fixed):
        def run(*operands):
            return pl.pallas_call(
                lambda *refs: body(*refs, **fixed),
                out_shape=[jax.ShapeDtypeStruct(*out) for out in outs],
                in_specs=[vmem] * len(operands),
                out_specs=out_specs or [vmem] * len(outs),
                scratch_shapes=scratch,
                compiler_params=pltpu.CompilerParams(vmem_limit_bytes=12 * 2**20),
                name=body.__name__,
                cost_estimate=pl.CostEstimate(flops=flops, bytes_accessed=moved, transcendentals=0),
            )(*operands)

        return run

    span = tenants * rank
    here = heads // ctx
    rows = here * 2 * span // rep
    even = jnp.reshape(lax.axis_index("ctx") % 2 == 0, (1, 1, 1))
    key_rows, even = lax.optimization_barrier((key_rows, even))
    own_keys = key_rows[0]
    two_keys = shifted(own_keys, "ctx", 2)
    meta, biases = call(
        place_kernel, [((8, lanes), jnp.int32), ((2, tokens, lanes), WIDE)], 8 * 2**30, 2**20,
        group=group,
    )(jnp.concatenate([doc_starts, tenant_ids], axis=0))
    own_values = value_matrix[0]
    leaving, meta = lax.optimization_barrier((own_values, meta))
    two_values = shifted(leaving, "ctx", 2)
    cots, queries, pulled, pull = call(
        pull_kernel,
        [((kv, lanes, dim), LOW), ((kv, lanes, dim), LOW), ((8, lanes), WIDE), ((span * group, lanes), LOW)],
        2**30, 4 * 2**20, tenants=tenants, rank=rank, owned=here, **sizes,
    )(meta, upstream, rot, queries)
    grad_hidden, diff = call(
        hidden_grad_kernel, [((kv, lanes, dim), LOW), ((kv, span * group, dim), LOW)],
        2 * 2**30, 4 * 2**20, tenants=tenants, rank=rank, **sizes,
    )(meta, pulled, cots, rot, proj)
    two_keys, grad_hidden = lax.optimization_barrier((two_keys, grad_hidden))
    one_keys = exchanged(jnp.where(even, own_keys, two_keys), {"ctx": 1})
    flat, heads_first = (tokens * kv, dim), ((kv, tokens, dim), LOW)
    fold, stats, two_heads, own_heads = call(
        fold_kernel, [((kv, tokens, lanes), WIDE), ((kv, 2, lanes), WIDE), heads_first, heads_first],
        2 * 2**30, 4 * 2**20, scratch=[pltpu.VMEM((2, *flat), WIDE)], scaling=scaling, **sizes,
    )(queries, two_keys.reshape(flat), own_keys.reshape(flat), biases)
    one_keys, fold = lax.optimization_barrier((one_keys, fold))

    halves = ((kv // 2, 3 * tokens, lanes), LOW)
    near, one_heads = call(
        near_kernel, [halves, heads_first], 2**30, 4 * 2**20,
        scratch=[pltpu.VMEM(flat, WIDE)], scaling=scaling, **sizes,
    )(queries, one_keys.reshape(flat), biases, fold, stats)
    two_values, near = lax.optimization_barrier((two_values, near))
    one_values = exchanged(jnp.where(even, own_values, two_values), {"ctx": 1})
    far, = call(
        far_kernel, [halves], 2**30, 4 * 2**20, group=group, scaling=scaling, first=kv // 2,
    )(queries, one_heads, biases, fold, stats)
    part_hidden, two_sides, own_sides = call(
        hidden_kernel, [((heads // group * dim, lanes), WIDE), heads_first, heads_first], 2**30, 4 * 2**20,
        scratch=[pltpu.VMEM((2, *flat), WIDE)], kv=kv,
    )(near, far, two_values.reshape(flat), own_values.reshape(flat))
    one_values, part_hidden = lax.optimization_barrier((one_values, part_hidden))
    kept = (span * group // 2, lanes)
    send, hidden, lift, one_sides = call(
        forward_kernel,
        [((ctx * rep // 2, rows, dim), LOW), (part_hidden.shape, LOW), (kept, LOW), heads_first],
        3 * 2**30, 10 * 2**20, scratch=[pltpu.VMEM(flat, WIDE)],
        tenants=tenants, rank=rank, owned=here, **sizes,
    )(shift_bias.T, near, far, part_hidden, one_values.reshape(flat), cots, diff, meta, pull)
    keep, = call(
        keep_kernel, [((ctx * rep // 2, rows, dim), LOW)], 2**30, 5 * 2**20, span=span, owned=here, **sizes,
    )(hidden, lift, cots, pull)
    part = (keep.astype(WIDE) + exchanged(send, {"ctx": 1}).astype(WIDE)).astype(LOW)
    near, part = lax.optimization_barrier((near, part))
    window = (2 * kv, tokens, dim)
    back_two, back_one, back_own, score_grad = call(
        backward_kernel, [(window, LOW), (window, LOW), (window, WIDE), ((kv, 3 * tokens, lanes), LOW)],
        4 * 2**30, 10 * 2**20, kv=kv, scaling=scaling,
    )(queries, grad_hidden, near, far, two_sides, one_sides, own_sides)
    d_queries, = call(
        query_kernel, [((tokens, heads, dim), LOW)], 2 * 2**30, 5 * 2**20,
        scratch=[pltpu.VMEM((tokens, heads, dim), LOW), pltpu.SemaphoreType.DMA((kv // 2,))],
        out_specs=[pl.BlockSpec(memory_space=pltpu.HBM)], scaling=scaling, **sizes,
    )(score_grad, two_heads, one_heads, own_heads)
    from_mate = exchanged(back_one, {"ctx": 1})
    onward = back_two.astype(WIDE) + jnp.where(even, 0.0, from_mate.astype(WIDE))
    onward = onward.astype(LOW)

    from_two = shifted(onward, "ctx", -2)
    groups = reduce_groups()
    for at, group_bits in enumerate(groups):
        if at == len(groups) - 2:
            part, onward = lax.optimization_barrier((part, onward))
        beside = {0: back_own, len(groups) - 2: onward, len(groups) - 1: from_two}.get(at)
        part, others = scattered(part, group_bits, beside)
        if at < len(groups) - 1:
            part = part.astype(WIDE) + sum(other.astype(WIDE) for other in others)
            part = part.astype(LOW)
    d_keys, d_values, *grads = call(
        finish_kernel, [((tokens * kv, dim), LOW)] * 2 + [((span // rep, here, dim), WIDE)] * 2, 2**20, 2**20,
        scratch=[pltpu.VMEM((2, tokens * kv, dim), WIDE)], kv=kv, owned=here,
    )(back_own, from_mate, from_two, part, *others)
    grads = [grad.reshape(tenants // rep, rank, here, dim) for grad in grads]
    d_keys, d_values = (grad.reshape(key_rows.shape) for grad in (d_keys, d_values))
    return (d_queries[None], d_keys, d_values, grads[0], grads[1])


def solution(mesh):
    rows = P("rep", "ctx", None, None)
    in_specs = (rows, rows, rows, rows, P(), P(), P(), P("rep", None), P("rep", None))
    tenant_rows = P("rep", None, "ctx", None)
    out_specs = (rows, rows, rows, tenant_rows, tenant_rows)
    return jax.shard_map(
        on_device, mesh=mesh, in_specs=in_specs, out_specs=out_specs, check_vma=False
    )
```

```python
import itertools

import jax
import jax.numpy as jnp
import numpy as np
from jax import lax
from jax.experimental import pallas as pl
from jax.experimental.pallas import tpu as pltpu
from jax.sharding import PartitionSpec as P

DOC_MAX = 256
LOW = jnp.bfloat16
WIDE = jnp.float32
far_below = -1e30


def shifted(value, axis, steps):
    count = lax.axis_size(axis)
    return lax.ppermute(value, axis, [(source, (source + steps) % count) for source in range(count)])


def exchanged(value, bits):
    axes = tuple(bits)
    shape = [lax.axis_size(axis) for axis in axes]
    pairs = []
    for source in np.ndindex(*shape):
        target = [at ^ bits[axis] for at, axis in zip(source, axes)]
        pairs.append((np.ravel_multi_index(source, shape), np.ravel_multi_index(target, shape)))
    return lax.ppermute(value, axes, [(int(source), int(target)) for source, target in pairs])


def reduce_groups():
    ctx, rep = lax.axis_size("ctx"), lax.axis_size("rep")
    bits = [{"ctx": 1 << at} for at in range(ctx.bit_length() - 2, 0, -1)]
    bits += [{"rep": 1 << at} for at in range(rep.bit_length() - 1)]
    over_ctx = ctx.bit_length() - 2
    return [bits[at : at + 2] for at in range(0, over_ctx, 2)] + [[bit] for bit in bits[over_ctx:]]


def reduce_place(index):
    place = 0
    for bits in itertools.chain(*reduce_groups()):
        for axis, bit in bits.items():
            place = 2 * place + (index[axis] // bit) % 2
    return place


def scattered(part, group, beside=None):
    count = 1 << len(group)
    size = part.shape[0] // count
    others = []
    for j in ([1, 3, 2] if count == 4 else [1]):
        bits = {}
        for at, pair in enumerate(reversed(group)):
            if (j >> at) & 1:
                bits.update({axis: bits.get(axis, 0) | bit for axis, bit in pair.items()})
        others.append(exchanged(part[j * size : (j + 1) * size], bits))
    if beside is not None:
        others = lax.optimization_barrier((others, beside))[0]
    return part[:size], others


def dot(left, right, left_dim, right_dim, precision=None):
    return lax.dot_general(
        left, right, (((left_dim,), (right_dim,)), ((), ())),
        precision=precision, preferred_element_type=WIDE,
    )


def group_rows(ref, kv_count, group_size):
    rows, _, dim = ref.shape
    wide = 2 * group_size
    parts = []
    for pair in range(kv_count // 2):
        both = ref[:, pair * wide : (pair + 1) * wide, :].astype(WIDE)
        for half in range(2):
            one = both[:, half * group_size : (half + 1) * group_size, :]
            parts.append(one.reshape(rows * group_size, dim).astype(LOW))
    return parts


def lane_head(shape, group_size):
    return lax.broadcasted_iota(jnp.int32, shape, 1) % group_size


def own_terms(maps_by_rows, owner, tenants, low_rank, group_size):
    lanes = maps_by_rows.shape[1]
    same_head = lax.broadcasted_iota(jnp.int32, (group_size, lanes), 0) == lane_head(
        (group_size, lanes), group_size
    )
    span = low_rank * group_size
    total = jnp.zeros((low_rank, group_size, lanes), WIDE)
    for tenant in range(tenants):
        keep = same_head & (owner == tenant)
        block = maps_by_rows[tenant * span : (tenant + 1) * span].reshape(
            low_rank, group_size, lanes
        )
        total = total + jnp.where(keep[None], block, 0.0)
    rows = jnp.sum(total, axis=1)
    rows = jnp.concatenate([rows, rows], axis=0)
    tiles = lanes // 128
    stacked = jnp.concatenate([rows[:, c * 128 : (c + 1) * 128] for c in range(tiles)], axis=0)
    side = lax.broadcasted_iota(jnp.int32, (128, 128), 0) // group_size
    over = lax.broadcasted_iota(jnp.int32, (128, 128), 1) // group_size
    spread = dot(stacked, (side == over).astype(WIDE), 1, 0, lax.Precision.HIGHEST)
    return jnp.concatenate([spread[c * 8 : (c + 1) * 8] for c in range(tiles)], axis=1)


def place_kernel(rows_ref, meta_ref, bias_ref, *, group):
    lanes = meta_ref.shape[1]
    tokens = lanes // group
    row_first = lax.axis_index("ctx") * tokens
    mine = pl.ds(pl.multiple_of(row_first, tokens), tokens)
    row = lax.broadcasted_iota(jnp.int32, (8, tokens), 0)
    both = jnp.where(row == 0, rows_ref[0:1, mine] - row_first, rows_ref[1:2, mine]).astype(WIDE)
    repeat = lax.broadcasted_iota(jnp.int32, (tokens, lanes), 0) == (
        lax.broadcasted_iota(jnp.int32, (tokens, lanes), 1) // group
    )
    meta = dot(both, repeat.astype(WIDE), 1, 0, lax.Precision.HIGHEST).astype(jnp.int32)
    meta_ref[...] = meta
    first = meta[0:1, :]
    key, here = places(lanes, tokens, group)
    bias_ref[0] = jnp.where(jnp.where(here, key, key - 2 * tokens) >= first, 0.0, far_below)
    bias_ref[1] = jnp.where(key - tokens >= first, 0.0, far_below)


def slots_of(lanes, group, owned):
    per_group = group // owned
    head = lane_head((1, lanes), group)
    return head ^ ((lax.axis_index("ctx") % per_group) * owned)


def tenants_of(lanes, tenants, rank):
    row = lax.broadcasted_iota(jnp.int32, (tenants * rank, lanes), 0) // rank
    return row ^ (lax.axis_index("rep") * (tenants // lax.axis_size("rep")))


def picked_rows(rows, owner, slots, tenants, rank, group):
    lanes = owner.shape[1]
    mine = owner == tenants_of(lanes, tenants, rank)
    rows = jnp.where(mine, jnp.concatenate([rows] * (tenants * rank // 8), axis=0), 0.0)
    return [jnp.where(slots == h, rows, 0.0).astype(LOW) for h in range(group)]


def pull_kernel(
    meta_ref, cot_ref, rot_ref, q_ref, cots_ref, queries_ref, pulled_ref, pull_ref,
    *, kv, group, tenants, rank, owned,
):
    owner = meta_ref[1:2, :]
    lanes = owner.shape[1]
    cots = group_rows(cot_ref, kv, group)
    rots = group_rows(rot_ref, kv, group)
    on_rot = dot(jnp.concatenate(rots, axis=1), jnp.concatenate(cots, axis=1), 1, 1)
    pulled = own_terms(on_rot, owner, tenants, rank, group).astype(LOW).astype(WIDE)
    pulled_ref[...] = pulled
    for g, rows in enumerate(group_rows(q_ref, kv, group)):
        queries_ref[g] = rows
        cots_ref[g] = cots[g]
    span = tenants * rank
    slots = slots_of(lanes, group, owned)
    for h, rows in enumerate(picked_rows(pulled, owner, slots, tenants, rank, group)):
        pull_ref[h * span : (h + 1) * span, :] = rows


def hidden_grad_kernel(
    meta_ref, pulled_ref, cots_ref, rot_ref, proj_ref, gh_ref, diff_ref, *, kv, group, tenants, rank,
):
    owner = meta_ref[1:2, :]
    lanes = owner.shape[1]
    dim = cots_ref.shape[2]
    pulled = pulled_ref[...]
    same_head = lax.broadcasted_iota(jnp.int32, (group, lanes), 0) == lane_head((group, lanes), group)
    picked = []
    for tenant in range(tenants):
        keep = same_head & (owner == tenant)
        for k in range(rank):
            picked.append(jnp.where(keep, pulled[k : k + 1], 0.0))
    picked = jnp.concatenate(picked, axis=0).T.astype(LOW)
    rots = group_rows(rot_ref, kv, group)
    projs = group_rows(proj_ref, kv, group)
    diffs = [(proj.astype(WIDE) - rot.astype(WIDE)).astype(LOW) for proj, rot in zip(projs, rots)]
    steered = dot(picked, jnp.concatenate(diffs, axis=1), 1, 0)
    for g in range(kv):
        diff_ref[g] = diffs[g]
        gh_ref[g] = (cots_ref[g].astype(WIDE) + steered[:, g * dim : (g + 1) * dim]).astype(LOW)


def places(lanes, tokens, group):
    key = lax.broadcasted_iota(jnp.int32, (tokens, lanes), 0)
    query = lax.broadcasted_iota(jnp.int32, (tokens, lanes), 1) // group
    return key, key <= query


def window_of(two_ref, own_ref, one_ref, head):
    return jnp.concatenate([two_ref[head], own_ref[head], one_ref[head]], axis=0)


def head_major(ref, wide_ref, outs):
    count = len(outs)
    wide_ref[...] = ref[...].astype(WIDE)
    for m, out in enumerate(outs):
        out[...] = wide_ref[pl.ds(m, out.shape[0], stride=count), :].astype(LOW)


def fold_kernel(
    queries_ref, two_ref, own_ref, bias_ref, fold_ref, stats_ref, two_keys_ref, own_keys_ref, wide_ref,
    *, kv, group, scaling,
):
    tokens = two_keys_ref.shape[1]
    _, here = places(queries_ref.shape[1], tokens, group)
    for at, (ref, keys_ref) in enumerate(((two_ref, two_keys_ref), (own_ref, own_keys_ref))):
        head_major(ref, wide_ref.at[at], [keys_ref.at[m] for m in range(kv)])

    def scores_of(g):
        return dot(jnp.concatenate([two_keys_ref[g], own_keys_ref[g]], axis=0), queries_ref[g], 1, 1)

    scores = scores_of(0)
    for g in range(kv):
        ahead = scores_of(g + 1) if g + 1 < kv else None
        fold = jnp.where(here, scores[tokens:], scores[0:tokens]) * scaling + bias_ref[0]
        top = jnp.max(fold, axis=0, keepdims=True)
        fold = jnp.exp(fold - top)
        fold_ref[g] = fold
        stats_ref[g, 0:1, :] = top
        stats_ref[g, 1:2, :] = jnp.sum(fold, axis=0, keepdims=True)
        scores = ahead


def near_kernel(
    queries_ref, one_ref, bias_ref, fold_ref, stats_ref, low_ref, one_keys_ref, wide_ref, *, kv, group, scaling,
):
    head_major(one_ref, wide_ref, [one_keys_ref.at[m] for m in range(kv)])
    weigh(queries_ref, one_keys_ref, bias_ref, fold_ref, stats_ref, low_ref, group, scaling, 0)


def far_kernel(
    queries_ref, one_keys_ref, bias_ref, fold_ref, stats_ref, low_ref, *, group, scaling, first,
):
    weigh(queries_ref, one_keys_ref, bias_ref, fold_ref, stats_ref, low_ref, group, scaling, first)


def weigh(queries_ref, one_keys_ref, bias_ref, fold_ref, stats_ref, low_ref, group, scaling, first):
    tokens = one_keys_ref.shape[1]
    _, here = places(queries_ref.shape[1], tokens, group)
    count = low_ref.shape[0]

    def scores_of(g):
        return dot(one_keys_ref[g], queries_ref[g], 1, 1)

    scores = scores_of(first)
    for at in range(count):
        g = first + at
        ahead = scores_of(g + 1) if at + 1 < count else None
        mid = scores * scaling + bias_ref[1]
        fold_top = stats_ref[g, 0:1, :]
        top = jnp.maximum(fold_top, jnp.max(mid, axis=0, keepdims=True))
        mid = jnp.exp(mid - top)
        fade = jnp.exp(fold_top - top)
        share = 1.0 / (stats_ref[g, 1:2, :] * fade + jnp.sum(mid, axis=0, keepdims=True))
        fold = fold_ref[g] * (fade * share)
        low_ref[at, 0:tokens, :] = jnp.where(here, 0.0, fold).astype(LOW)
        low_ref[at, tokens : 2 * tokens, :] = jnp.where(here, fold, 0.0).astype(LOW)
        low_ref[at, 2 * tokens :, :] = (mid * share).astype(LOW)
        scores = ahead


def half_of(refs, g):
    return refs[g // refs[0].shape[0]].at[g % refs[0].shape[0]]


def hidden_kernel(near_ref, far_ref, two_ref, own_ref, part_ref, two_values_ref, own_values_ref, wide_ref, *, kv):
    tokens, dim = two_values_ref.shape[1:]
    for at, (ref, values_ref) in enumerate(((two_ref, two_values_ref), (own_ref, own_values_ref))):
        head_major(ref, wide_ref.at[at], [values_ref.at[m] for m in range(kv)])
    for g in range(kv):
        low_ref = half_of((near_ref, far_ref), g)
        values = jnp.concatenate([two_values_ref[g], own_values_ref[g]], axis=0)
        part_ref[g * dim : (g + 1) * dim, :] = dot(values, low_ref[0 : 2 * tokens, :], 0, 0)


def sent_slots(group, owned, odd):
    return [slot for slot in range(group) if (slot // owned) % 2 == odd]


def write_parts(into, slots, on_rot, on_proj, kv, group, owned, span, dim):
    rep, me = lax.axis_size("rep"), lax.axis_index("ctx")
    per_group = group // owned
    here_rows = span // rep
    for g in range(kv):
        columns = slice(g * dim, (g + 1) * dim)
        for low in sorted({slot // owned for slot in slots}):
            device = (g ^ (me // per_group)) * per_group + low
            for r in range(rep):
                pieces = []
                for slot in range(low * owned, (low + 1) * owned):
                    first = slots.index(slot) * span + r * here_rows
                    rows = slice(first, first + here_rows)
                    pieces += [on_rot[rows, columns], on_proj[rows, columns]]
                into[reduce_place(dict(ctx=device, rep=r))] = jnp.concatenate(pieces, axis=0).astype(LOW)


def forward_kernel(
    shift_ref, near_ref, far_ref, part_ref, one_ref, cots_ref, diff_ref, meta_ref, pull_ref,
    send_ref, hidden_ref, lift_ref, one_values_ref, wide_ref, *, kv, group, tenants, rank, owned,
):
    tokens, dim = one_values_ref.shape[1:]
    head_major(one_ref, wide_ref, [one_values_ref.at[m] for m in range(kv)])
    owner = meta_ref[1:2, :]
    lanes = owner.shape[1]
    hidden = []
    for g in range(kv):
        low_ref = half_of((near_ref, far_ref), g)
        middle = dot(one_values_ref[g], low_ref[2 * tokens :, :], 0, 0)
        hidden.append((part_ref[g * dim : (g + 1) * dim, :] + middle).astype(LOW))
    hidden = jnp.concatenate(hidden, axis=0)
    hidden_ref[...] = hidden
    on_diff = dot(jnp.concatenate([diff_ref[g] for g in range(kv)], axis=1), hidden, 1, 0)
    lifted = own_terms(on_diff, owner, tenants, rank, group)
    one_hot = (owner == lax.broadcasted_iota(jnp.int32, (tenants, lanes), 0)).astype(WIDE)
    bias = jnp.concatenate([shift_ref[...]] * (8 // rank), axis=0)
    shift = dot(bias, one_hot, 1, 0, lax.Precision.HIGHEST)
    lifted = (lifted + shift).astype(LOW).astype(WIDE)
    span = tenants * rank
    lifts = picked_rows(lifted, owner, slots_of(lanes, group, owned), tenants, rank, group)
    for at, slot in enumerate(sent_slots(group, owned, 0)):
        lift_ref[at * span : (at + 1) * span, :] = lifts[slot]
    slots = sent_slots(group, owned, 1)
    pulls = [pull_ref[slot * span : (slot + 1) * span, :] for slot in slots]
    on_proj = dot(jnp.concatenate(pulls, axis=0), hidden, 1, 1)
    cots = jnp.concatenate([cots_ref[g] for g in range(kv)], axis=1)
    on_rot = dot(jnp.concatenate([lifts[slot] for slot in slots], axis=0), cots, 1, 0) - on_proj
    write_parts(send_ref, slots, on_rot, on_proj, kv, group, owned, span, dim)


def keep_kernel(hidden_ref, lift_ref, cots_ref, pull_ref, keep_ref, *, kv, group, span, owned):
    dim = cots_ref.shape[2]
    slots = sent_slots(group, owned, 0)
    pulls = [pull_ref[slot * span : (slot + 1) * span, :] for slot in slots]
    on_proj = dot(jnp.concatenate(pulls, axis=0), hidden_ref[...], 1, 1)
    cots = jnp.concatenate([cots_ref[g] for g in range(kv)], axis=1)
    on_rot = dot(lift_ref[...], cots, 1, 0) - on_proj
    write_parts(keep_ref, slots, on_rot, on_proj, kv, group, owned, span, dim)


def backward_kernel(
    queries_ref, gh_ref, near_ref, far_ref, two_ref, one_ref, own_ref, back_two_ref, back_one_ref, back_own_ref, grad_ref,
    *, kv, scaling,
):
    tokens = back_own_ref.shape[1]

    def weight_grad_of(g):
        return dot(window_of(two_ref, own_ref, one_ref, g), gh_ref[g], 1, 1)

    weight_grad = weight_grad_of(0)
    for g in range(kv):
        ahead = weight_grad_of(g + 1) if g + 1 < kv else None
        low = half_of((near_ref, far_ref), g)[...]
        weights = low.astype(WIDE)
        delta = jnp.sum(weights * weight_grad, axis=0, keepdims=True)
        score_grad = (weights * (weight_grad - delta)).astype(LOW)
        grad_ref[g] = score_grad
        key_grad = dot(score_grad, queries_ref[g], 1, 0) * scaling
        value_grad = dot(low, gh_ref[g], 1, 0)
        for place, grad in ((g, key_grad), (kv + g, value_grad)):
            back_two_ref[place] = grad[0:tokens].astype(LOW)
            back_own_ref[place] = grad[tokens : 2 * tokens]
            back_one_ref[place] = grad[2 * tokens :].astype(LOW)
        weight_grad = ahead


def query_kernel(
    grad_ref, two_ref, one_ref, own_ref, dq_hbm, dq_ref, sems, *, kv, group, scaling,
):
    tokens, _, dim = dq_ref.shape
    copies = []
    for g in range(kv):
        query_grad = dot(window_of(two_ref, own_ref, one_ref, g), grad_ref[g], 0, 0) * scaling
        query_grad = query_grad.T.reshape(tokens, group, dim)
        if g % 2 == 1:
            heads = slice((g - 1) * group, (g + 1) * group)
            dq_ref[:, heads, :] = jnp.concatenate([before, query_grad], axis=1).astype(LOW)
            copies.append(pltpu.make_async_copy(dq_ref.at[:, heads], dq_hbm.at[:, heads], sems.at[g // 2]))
            copies[-1].start()
        before = query_grad
    for copy in copies:
        copy.wait()


def finish_kernel(
    own_ref, mate_ref, two_ref, part_ref, *refs, kv, owned,
):
    *other_refs, keys_ref, values_ref, rot_ref, proj_ref, wide_ref = refs
    total = part_ref[0].astype(WIDE)
    for other_ref in other_refs:
        total = total + other_ref[0].astype(WIDE)
    size = rot_ref.shape[0]
    for place in range(owned):
        for at, out in enumerate((rot_ref, proj_ref)):
            row = (2 * place + at) * size
            out[:, place, :] = total[row : row + size]
    tokens = own_ref.shape[1]
    even = (lax.axis_index("ctx") % 2 == 0).astype(WIDE)
    for at, out in enumerate((keys_ref, values_ref)):
        for m in range(kv):
            place = at * kv + m
            total = own_ref[place] + two_ref[place].astype(WIDE) + even * mate_ref[place].astype(WIDE)
            wide_ref[at, pl.ds(m, tokens, stride=kv), :] = total
        out[...] = wide_ref[at].astype(LOW)


def on_device(
    query_rows, key_rows, value_matrix, cotangent, rotation, projection, shift_bias, doc_starts, tenant_ids,
):
    queries = query_rows[0]
    upstream = cotangent[0]
    tokens, heads, dim = queries.shape
    kv = key_rows.shape[2]
    group = heads // kv
    scaling = dim ** (-0.5)
    tenants, rank = rotation.shape[0], rotation.shape[1]
    lanes = tokens * group
    ctx = lax.axis_size("ctx")
    rep = lax.axis_size("rep")
    assert 2 * tokens == DOC_MAX


    rot = rotation.reshape(tenants * rank, heads, dim)
    proj = projection.reshape(tenants * rank, heads, dim)
    sizes = dict(kv=kv, group=group)
    vmem = pl.BlockSpec(memory_space=pltpu.VMEM)

    def call(body, outs, flops, moved, out_specs=None, scratch=(), **fixed):
        def run(*operands):
            return pl.pallas_call(
                lambda *refs: body(*refs, **fixed),
                out_shape=[jax.ShapeDtypeStruct(*out) for out in outs],
                in_specs=[vmem] * len(operands),
                out_specs=out_specs or [vmem] * len(outs),
                scratch_shapes=scratch,
                compiler_params=pltpu.CompilerParams(vmem_limit_bytes=12 * 2**20),
                name=body.__name__,
                cost_estimate=pl.CostEstimate(flops=flops, bytes_accessed=moved, transcendentals=0),
            )(*operands)

        return run

    span = tenants * rank
    here = heads // ctx
    rows = here * 2 * span // rep
    even = jnp.reshape(lax.axis_index("ctx") % 2 == 0, (1, 1, 1))
    key_rows, even = lax.optimization_barrier((key_rows, even))
    own_keys = key_rows[0]
    two_keys = shifted(own_keys, "ctx", 2)
    meta, biases = call(
        place_kernel, [((8, lanes), jnp.int32), ((2, tokens, lanes), WIDE)], 8 * 2**30, 2**20,
        group=group,
    )(jnp.concatenate([doc_starts, tenant_ids], axis=0))
    own_values = value_matrix[0]
    leaving, meta = lax.optimization_barrier((own_values, meta))
    two_values = shifted(leaving, "ctx", 2)
    cots, queries, pulled, pull = call(
        pull_kernel,
        [((kv, lanes, dim), LOW), ((kv, lanes, dim), LOW), ((8, lanes), WIDE), ((span * group, lanes), LOW)],
        2**30, 4 * 2**20, tenants=tenants, rank=rank, owned=here, **sizes,
    )(meta, upstream, rot, queries)
    grad_hidden, diff = call(
        hidden_grad_kernel, [((kv, lanes, dim), LOW), ((kv, span * group, dim), LOW)],
        2 * 2**30, 4 * 2**20, tenants=tenants, rank=rank, **sizes,
    )(meta, pulled, cots, rot, proj)
    two_keys, grad_hidden = lax.optimization_barrier((two_keys, grad_hidden))
    one_keys = exchanged(jnp.where(even, own_keys, two_keys), {"ctx": 1})
    flat, heads_first = (tokens * kv, dim), ((kv, tokens, dim), LOW)
    fold, stats, two_heads, own_heads = call(
        fold_kernel, [((kv, tokens, lanes), WIDE), ((kv, 2, lanes), WIDE), heads_first, heads_first],
        2 * 2**30, 4 * 2**20, scratch=[pltpu.VMEM((2, *flat), WIDE)], scaling=scaling, **sizes,
    )(queries, two_keys.reshape(flat), own_keys.reshape(flat), biases)
    one_keys, fold = lax.optimization_barrier((one_keys, fold))

    halves = ((kv // 2, 3 * tokens, lanes), LOW)
    near, one_heads = call(
        near_kernel, [halves, heads_first], 2**30, 4 * 2**20,
        scratch=[pltpu.VMEM(flat, WIDE)], scaling=scaling, **sizes,
    )(queries, one_keys.reshape(flat), biases, fold, stats)
    two_values, near = lax.optimization_barrier((two_values, near))
    one_values = exchanged(jnp.where(even, own_values, two_values), {"ctx": 1})
    far, = call(
        far_kernel, [halves], 2**30, 4 * 2**20, group=group, scaling=scaling, first=kv // 2,
    )(queries, one_heads, biases, fold, stats)
    part_hidden, two_sides, own_sides = call(
        hidden_kernel, [((heads // group * dim, lanes), WIDE), heads_first, heads_first], 2**30, 4 * 2**20,
        scratch=[pltpu.VMEM((2, *flat), WIDE)], kv=kv,
    )(near, far, two_values.reshape(flat), own_values.reshape(flat))
    one_values, part_hidden = lax.optimization_barrier((one_values, part_hidden))
    kept = (span * group // 2, lanes)
    send, hidden, lift, one_sides = call(
        forward_kernel,
        [((ctx * rep // 2, rows, dim), LOW), (part_hidden.shape, LOW), (kept, LOW), heads_first],
        3 * 2**30, 10 * 2**20, scratch=[pltpu.VMEM(flat, WIDE)],
        tenants=tenants, rank=rank, owned=here, **sizes,
    )(shift_bias.T, near, far, part_hidden, one_values.reshape(flat), cots, diff, meta, pull)
    keep, = call(
        keep_kernel, [((ctx * rep // 2, rows, dim), LOW)], 2**30, 5 * 2**20, span=span, owned=here, **sizes,
    )(hidden, lift, cots, pull)
    part = (keep.astype(WIDE) + exchanged(send, {"ctx": 1}).astype(WIDE)).astype(LOW)
    near, part = lax.optimization_barrier((near, part))
    window = (2 * kv, tokens, dim)
    back_two, back_one, back_own, score_grad = call(
        backward_kernel, [(window, LOW), (window, LOW), (window, WIDE), ((kv, 3 * tokens, lanes), LOW)],
        4 * 2**30, 10 * 2**20, kv=kv, scaling=scaling,
    )(queries, grad_hidden, near, far, two_sides, one_sides, own_sides)
    d_queries, = call(
        query_kernel, [((tokens, heads, dim), LOW)], 2 * 2**30, 5 * 2**20,
        scratch=[pltpu.VMEM((tokens, heads, dim), LOW), pltpu.SemaphoreType.DMA((kv // 2,))],
        out_specs=[pl.BlockSpec(memory_space=pltpu.HBM)], scaling=scaling, **sizes,
    )(score_grad, two_heads, one_heads, own_heads)
    from_mate = exchanged(back_one, {"ctx": 1})
    onward = back_two.astype(WIDE) + jnp.where(even, 0.0, from_mate.astype(WIDE))
    onward = onward.astype(LOW)

    from_two = shifted(onward, "ctx", -2)
    groups = reduce_groups()
    for at, group_bits in enumerate(groups):
        if at == len(groups) - 2:
            part, onward = lax.optimization_barrier((part, onward))
        beside = {0: back_own, len(groups) - 2: onward, len(groups) - 1: from_two}.get(at)
        part, others = scattered(part, group_bits, beside)
        if at < len(groups) - 1:
            part = part.astype(WIDE) + sum(other.astype(WIDE) for other in others)
            part = part.astype(LOW)
    d_keys, d_values, *grads = call(
        finish_kernel, [((tokens * kv, dim), LOW)] * 2 + [((span // rep, here, dim), WIDE)] * 2, 2**20, 2**20,
        scratch=[pltpu.VMEM((2, tokens * kv, dim), WIDE)], kv=kv, owned=here,
    )(back_own, from_mate, from_two, part, *others)
    grads = [grad.reshape(tenants // rep, rank, here, dim) for grad in grads]
    d_keys, d_values = (grad.reshape(key_rows.shape) for grad in (d_keys, d_values))
    return (d_queries[None], d_keys, d_values, grads[0], grads[1])


def solution(mesh):
    rows = P("rep", "ctx", None, None)
    in_specs = (rows, rows, rows, rows, P(), P(), P(), P("rep", None), P("rep", None))
    tenant_rows = P("rep", None, "ctx", None)
    out_specs = (rows, rows, rows, tenant_rows, tenant_rows)
    return jax.shard_map(
        on_device, mesh=mesh, in_specs=in_specs, out_specs=out_specs, check_vma=False
    )
```
